32 devices in a mesh: groups: 2 (over x), inst: 4 (over y, core), tp: 4 (over z).
Axes of the slice: x: 2, y: 2, z: 4, core: 2. Of those that a mesh axis runs over, the one named last changes fastest.
Arguments:
- kv_cache: bfloat16 [384, 2, 256, 512], P(('groups', 'inst'), None, None, 'tp'), parts along dimension 0, may hold values from -110 to 110
- hidden: bfloat16 [384, 4096], P(('groups', 'inst')), parts along dimension 0, may hold values from -18 to 18
- lengths: int32 [384], P('groups'), parts along dimension 0, may hold values from 1 to 254, as said below
- source: int32 [384], P('groups'), parts along dimension 0, may hold values from 0 to 191, as said below
- norm_gain: float32 [4096], replicated, may hold values from 0.1 to 1.9
- query_weight: bfloat16 [4096, 2048], P(None, 'tp'), may hold values from -0.09375 to 0.09375
- keyval_weight: bfloat16 [4096, 2, 512], P(None, None, 'tp'), may hold values from -0.09375 to 0.09375
- out_weight: bfloat16 [2048, 4096], P('tp'), may hold values from -0.125 to 0.125
Outputs:
- final_hidden: bfloat16 [384, 4096], P(('groups', 'inst')), parts along dimension 0
- final_cache: bfloat16 [384, 2, 256, 512], P(('groups', 'inst'), None, None, 'tp'), parts along dimension 0
The draws below stay inside these ranges and needn't reach their ends.
There are 2 independent parts, one for each index of `groups`. The reference program is written for one: setup_inputs(seed, part) draws one part's arguments, and reference() takes and returns one part's arrays. A program takes and returns all parts, laid end to end along the dimension named above; an argument that names none is the same for every part. Nothing has to cross between parts.
Inputs may be any that keep to these rules, and one draw needn't show every extreme that they name: `source`: A permutation of the slots. In each instance exactly 4 slots take a request from another instance; from one instance to another exactly 2 requests move or none; the other slots keep their own request. `lengths`: positions from a slot's length on hold stale entries.
All inputs are finite; a program needn't handle non-finite values.
Results may differ from the reference program's by a relative error of at most 0.012.
The reference program's roundings to bfloat16 on the way count: a program that leaves them out, or rounds other values in their place, can miss the bound.
Values may be sent and summed in bfloat16 or wider, within the bound.
No kernel may reach another device: no remote copies, remote signals or barrier semaphores. Data moves between devices by JAX's collectives and lax.ppermute only.
A program may use at most 128 MiB of HBM per device.

```python
import jax
import jax.numpy as jnp
from jax import lax

D = 4096
QPK = 4
HD = 128
STEPS = 2
MOVE = 2
SLOTS = 48
CAP = 256
KV_HEADS = 4
HEADS = 16
ROUNDS = 2
REQS = 192


def draw_kv_cache(key, part):
    key = jax.random.fold_in(key, 21)
    first = jax.random.fold_in(key, 0)
    shape = (REQS, 2, CAP, KV_HEADS * HD)
    base = jax.random.truncated_normal(first, -4.0, 4.0, shape, jnp.float32)
    return base.astype(jnp.bfloat16)


def draw_hidden(key, part):
    key = jax.random.fold_in(key, 22)
    first, second, third = jax.random.split(key, 3)
    row_scale = 10.0 ** jax.random.uniform(second, (REQS, 1), jnp.float32, -0.5, 0.5)
    col_scale = 2.0 ** jax.random.uniform(third, (1, D), jnp.float32, -1.0, 1.0)
    noise = jax.random.truncated_normal(first, -4.0, 4.0, (REQS, D), jnp.float32)
    return (0.7 * row_scale * col_scale * noise).astype(jnp.bfloat16)


def draw_lengths(key, part):
    key = jax.random.fold_in(key, 23)
    first, second, third = jax.random.split(key, 3)
    instances = REQS // SLOTS
    upper = jax.random.randint(first, (instances, 1), CAP // 4, CAP - STEPS + 1)
    upper = jnp.broadcast_to(upper, (instances, SLOTS)).reshape(REQS)
    drawn = jax.random.randint(second, (REQS,), 1, upper + 1)
    picked = jax.random.randint(third, (), 0, REQS)
    drawn = drawn.at[picked].set(CAP - STEPS)
    drawn = drawn.at[(picked + 1) % REQS].set(1)
    return drawn.astype(jnp.int32)


def draw_source(key, part):
    key = jax.random.fold_in(key, 24)
    first, second = jax.random.split(key, 2)
    instances = REQS // SLOTS
    sigma = jax.random.permutation(first, instances)
    inverse = jnp.zeros((instances,), jnp.int32).at[sigma].set(jnp.arange(instances, dtype=jnp.int32))
    slot_keys = jax.random.split(second, instances)
    orders = jax.vmap(lambda single: jax.random.permutation(single, SLOTS))(slot_keys)
    result = jnp.arange(REQS, dtype=jnp.int32)
    targets = jnp.arange(instances, dtype=jnp.int32)
    for round_idx in range(ROUNDS):
        senders = inverse[(sigma - round_idx - 1) % instances]
        for member in range(MOVE):
            column = round_idx * MOVE + member
            receive_slot = targets * SLOTS + orders[:, column]
            send_slot = senders * SLOTS + orders[senders, column]
            result = result.at[receive_slot].set(send_slot.astype(jnp.int32))
    return result.astype(jnp.int32)


def block_levels(key, shape, pieces, low, largest):
    factor_of, own = 1.0, jax.random.fold_in(key, 6)
    for dim, shards_of in pieces:
        heights = jnp.exp(jax.random.uniform(jax.random.fold_in(own, dim), (shards_of,), jnp.float32, low / len(pieces), largest / len(pieces)))
        factor_of = factor_of * jnp.repeat(heights, shape[dim] // shards_of).reshape([-1 if axis == dim else 1 for axis in range(len(shape))])
    return factor_of


def gaussian(rng, dims, deviation, bound, cuts=(), held_as=jnp.bfloat16):
    level = block_levels(rng, dims, cuts, -0.22, 0.18) if cuts else 1.0
    array = jax.random.normal(rng, dims, jnp.float32) * deviation * level
    return jnp.minimum(jnp.maximum(array, -bound), bound).astype(held_as)


def setup_inputs(seed: int = 0, part: int = 0) -> dict:
    arg_keys = jax.random.split(jax.random.key(seed), 9)
    part_keys = jax.random.split(jax.random.fold_in(arg_keys[8], part), 9)
    return {
        "kv_cache": draw_kv_cache(jax.random.fold_in(jax.random.fold_in(arg_keys[8], part), 71), part),
        "hidden": draw_hidden(jax.random.fold_in(jax.random.fold_in(arg_keys[8], part), 71), part),
        "lengths": draw_lengths(jax.random.fold_in(jax.random.fold_in(arg_keys[8], part), 71), part),
        "source": draw_source(jax.random.fold_in(jax.random.fold_in(arg_keys[8], part), 71), part),
        "norm_gain": jnp.clip(1.0 + 0.18 * jax.random.normal(arg_keys[4], (D,), jnp.float32), 0.1, 1.9),
        "query_weight": gaussian(arg_keys[5], (D, HEADS * HD), D ** -0.5, 0.09375, ((1, 4),)),
        "keyval_weight": gaussian(arg_keys[6], (D, 2, KV_HEADS * HD), D ** -0.5, 0.09375, ((2, 4),)),
        "out_weight": gaussian(arg_keys[7], (HEADS * HD, D), (HEADS * HD) ** -0.5, 0.125, ((0, 4),)),
    }


EPS = 1e-05
THETA = 500000.0

def rotate(inputs, position):
    halfway = inputs.shape[-1] // 2
    frequency = THETA ** (-(jnp.arange(halfway, dtype=jnp.float32) * 2.0) / inputs.shape[-1])
    angles = position.astype(jnp.float32)[:, None] * frequency[None, :]
    cosine = jnp.concatenate([jnp.cos(angles), jnp.cos(angles)], axis=-1)
    sine_part = jnp.concatenate([jnp.sin(angles), jnp.sin(angles)], axis=-1)
    target = (inputs.shape[0],) + (1,) * (inputs.ndim - 2) + (inputs.shape[-1],)
    cosine = cosine.reshape(target)
    sine_part = sine_part.reshape(target)
    turned = jnp.concatenate([-inputs[..., halfway:], inputs[..., :halfway]], axis=-1)
    return inputs * cosine + turned * sine_part

def decode_step(current, stored, position, norm_gain, query_weight, keyval_weight, out_weight):
    batch_rows = current.shape[0]
    widened = current.astype(jnp.float32)
    normed = (widened * lax.rsqrt(lax.optimization_barrier(jnp.mean(widened * widened, axis=-1, keepdims=True)) + EPS) * norm_gain).astype(jnp.bfloat16)
    queries = jnp.dot(normed, query_weight, preferred_element_type=jnp.float32).reshape(batch_rows, KV_HEADS, QPK, HD)
    queries = lax.optimization_barrier(rotate(queries, position).astype(jnp.bfloat16))
    new_rows = jnp.dot(normed, keyval_weight.reshape(D, 2 * KV_HEADS * HD), preferred_element_type=jnp.float32)
    new_rows = new_rows.reshape(batch_rows, 2, KV_HEADS, HD)
    new_rows = jnp.stack([rotate(new_rows[:, 0], position), new_rows[:, 1]], axis=1).astype(jnp.bfloat16)
    new_rows = new_rows.reshape(batch_rows, 2, 1, KV_HEADS * HD)
    placed = (jnp.arange(CAP, dtype=jnp.int32)[None, :] == position[:, None])[:, None, :, None]
    stored = jnp.where(placed, new_rows, stored)
    key_rows = stored[:, 0].reshape(batch_rows, CAP, KV_HEADS, HD).astype(jnp.float32)
    value_rows = stored[:, 1].reshape(batch_rows, CAP, KV_HEADS, HD).astype(jnp.float32)
    scores = jnp.einsum('rgjd,rcgd->rgjc', queries.astype(jnp.float32), key_rows) * HD ** (-0.5)
    visible = (jnp.arange(CAP, dtype=jnp.int32)[None, :] <= position[:, None])[:, None, None, :]
    scores = jnp.where(visible, scores, -jnp.inf)
    highest = lax.optimization_barrier(jnp.max(scores, axis=-1, keepdims=True))
    weight = jnp.exp(scores - highest)
    weight = weight / lax.optimization_barrier(jnp.sum(weight, axis=-1, keepdims=True))
    weight16 = lax.optimization_barrier(weight.astype(jnp.bfloat16))
    attended = jnp.einsum('rgjc,rcgd->rgjd', weight16.astype(jnp.float32), value_rows)
    attended = attended.astype(jnp.bfloat16).reshape(batch_rows, KV_HEADS * QPK * HD)
    head_part = jnp.dot(attended, out_weight, preferred_element_type=jnp.float32)
    return ((widened + head_part).astype(jnp.bfloat16), stored)

def reference(kv_cache, hidden, lengths, source, norm_gain, query_weight, keyval_weight, out_weight):
    stored = jnp.take(kv_cache, source, axis=0)
    current = jnp.take(hidden, source, axis=0)
    position = jnp.take(lengths, source, axis=0)
    for turn_idx in range(STEPS):
        current, stored = decode_step(current, stored, position + turn_idx, norm_gain, query_weight, keyval_weight, out_weight)
    return (current, stored)
```

```python
import functools

import jax
import jax.numpy as jnp
import numpy as np
from jax import lax
from jax.experimental import pallas as pl
from jax.experimental.pallas import tpu as pltpu
from jax.sharding import PartitionSpec as P

MOVE = 2
EPS = 1e-05
THETA = 500000.0
HD = 128
GROUP = 8
PIECE = 16
CHUNK = 8

F32 = jnp.float32
BF16 = jnp.bfloat16
I32 = jnp.int32

ANY = pl.BlockSpec(memory_space=pl.ANY)
VMEM = pl.BlockSpec(memory_space=pltpu.VMEM)
SMEM = pl.BlockSpec(memory_space=pltpu.SMEM)


def params(mib):
    return pltpu.CompilerParams(vmem_limit_bytes=mib * 1024 * 1024)


def cost(flops, nbytes):
    return pl.CostEstimate(flops=flops, bytes_accessed=nbytes, transcendentals=0)


def angle_tables(positions):
    frequency = THETA ** (-(np.arange(HD // 2, dtype=np.float64) * 2.0) / HD)
    angles = np.arange(positions, dtype=np.float64)[:, None] * frequency[None, :]
    cosine = np.concatenate([np.cos(angles), np.cos(angles)], axis=-1)
    sine = np.concatenate([-np.sin(angles), np.sin(angles)], axis=-1)
    return cosine.astype(np.float32), sine.astype(np.float32)


def turn(x, cosine, sine):
    return x * cosine + pltpu.roll(x, HD // 2, 1) * sine


def gather_angles(position_of, slots, cos_ref, sin_ref, cos_rows, sin_rows):
    for s in range(slots):
        p = position_of(s)
        cos_rows[s : s + 1, :] = cos_ref[pl.ds(p, 1), :]
        sin_rows[s : s + 1, :] = sin_ref[pl.ds(p, 1), :]


def spread_normed(normed3, spread, slots, width):
    blocks = width // HD
    row = lax.broadcasted_iota(I32, (HD, 4 * HD), 0)
    col = lax.broadcasted_iota(I32, (HD, 4 * HD), 1)
    goal = jnp.where(col < 2 * HD, 2 * row, 2 * row + 1 + 2 * HD)
    places = jnp.where(col == goal, 1.0, 0.0).astype(BF16)
    spread_all = jnp.dot(
        normed3[...].reshape(blocks * slots, HD), places, preferred_element_type=F32
    ).astype(BF16)
    spread[:, 0:slots, :] = spread_all[:, : 2 * HD].reshape(blocks, slots, 2 * HD)
    spread[:, slots:, :] = spread_all[:, 2 * HD :].reshape(blocks, slots, 2 * HD)


def project(normed3, spread, wq, wkv, wq_copies, wkv_copies, slots, width):
    pieces = len(wq_copies)
    depth = width // pieces
    query = None
    pair = None
    for c in range(pieces):
        wkv_copies[c].wait()
        for b in range(c * depth // HD, (c + 1) * depth // HD):
            part = jnp.dot(
                spread[b], wkv[b * 2 * HD : (b + 1) * 2 * HD, :], preferred_element_type=F32
            )
            pair = part if pair is None else pair + part
    for c in range(pieces):
        wq_copies[c].wait()
        for b in range(c * depth // (2 * HD), (c + 1) * depth // (2 * HD)):
            block = jnp.concatenate([normed3[2 * b], normed3[2 * b + 1]], axis=1)
            part = jnp.dot(
                block, wq[b * 2 * HD : (b + 1) * 2 * HD, :], preferred_element_type=F32
            )
            query = part if query is None else query + part
    return query, pair[:slots], pair[slots:]


def weight_copies(src, dst, sem, pieces):
    depth = src.shape[0] // pieces
    copies = [
        pltpu.make_async_copy(
            src.at[pl.ds(c * depth, depth)], dst.at[pl.ds(c * depth, depth)], sem.at[c]
        )
        for c in range(pieces)
    ]
    return copies


def put_row(cache, place, p, key_row, value_row):
    base = pl.multiple_of((jnp.maximum(p, 0) // PIECE) * PIECE, PIECE)
    hit = lax.broadcasted_iota(I32, (PIECE, HD), 0) + base == p
    for which, new in ((0, key_row), (1, value_row)):
        old = cache[place, which, pl.ds(base, PIECE), :].astype(F32)
        cache[place, which, pl.ds(base, PIECE), :] = jnp.where(hit, new, old).astype(BF16)


def attend(cache, places, positions, query_rows):
    cap = cache.shape[2]
    col = lax.broadcasted_iota(I32, (GROUP, cap), 1)
    scores = [
        lax.dot_general(
            rows.astype(BF16),
            cache[place, 0],
            (((1,), (1,)), ((), ())),
            preferred_element_type=F32,
        )
        for place, rows in zip(places, query_rows)
    ]
    probs = []
    for score, p in zip(scores, positions):
        score = jnp.where(col <= p, score * HD**-0.5, -jnp.inf)
        weight = jnp.exp(score - jnp.max(score, axis=-1, keepdims=True))
        weight = weight / jnp.sum(weight, axis=-1, keepdims=True)
        probs.append(weight.astype(BF16))
    return [
        jnp.dot(prob, cache[place, 1], preferred_element_type=F32)
        for place, prob in zip(places, probs)
    ]


def norm_into(normed3, pieces, gains, firsts, total_width):
    square = None
    for piece in pieces:
        part = jnp.sum(piece * piece, axis=-1, keepdims=True)
        square = part if square is None else square + part
    factor = lax.rsqrt(square / total_width + EPS)
    for piece, gain, first in zip(pieces, gains, firsts):
        normed = (piece * factor * gain).astype(BF16)
        for i in range(piece.shape[1] // HD):
            normed3[first + i] = normed[:, i * HD : (i + 1) * HD]


def first_kernel(
    peers, slots, heads, shard,
    meta, source_s, lengths_s, source_v, hidden, gain, cos_ref, sin_ref, wq_hbm, wkv_hbm, cache_hbm,
    query_out, newkey_out, newvalue_out, plan, *rest,
):
    others = peers - 1
    moving = others * MOVE
    boxes, notes = rest[:others], rest[others : 2 * others]
    (wq, wkv, normed3, spread, cos_rows, sin_rows, leaving, hidden32,
     wq_sem, wkv_sem, in_sem, out_sem) = rest[2 * others :]
    width = hidden.shape[1]
    me, me_tp = meta[0], meta[1]
    wq_copies = weight_copies(wq_hbm, wq, wq_sem, 4)
    wkv_copies = weight_copies(wkv_hbm, wkv, wkv_sem, 4)
    for copy in wkv_copies + wq_copies:
        copy.start()

    low = me * slots
    src = source_v[...]
    index = lax.broadcasted_iota(I32, src.shape, 1)
    mine_goes = (src >= low) & (src < low + slots)
    mine_comes = (index >= low) & (index < low + slots)
    index_f = index.astype(F32)
    send_slots = []
    for k in range(1, peers):
        to = lax.rem(me + k, peers) * slots
        sent = mine_goes & (index >= to) & (index < to + slots)
        origin = lax.rem(me + peers - k, peers) * slots
        taken = mine_comes & (src >= origin) & (src < origin + slots)
        for m in range(MOVE):
            at = (k - 1) * MOVE + m
            if m == 0:
                j = jnp.min(jnp.where(sent, index_f, 1e6)).astype(I32)
                r = jnp.min(jnp.where(taken, index_f, 1e6)).astype(I32)
            else:
                j = jnp.max(jnp.where(sent, index_f, -1.0)).astype(I32)
                r = jnp.max(jnp.where(taken, index_f, -1.0)).astype(I32)
            known = (j >= 0) & (j < src.shape[1])
            slot = source_s[jnp.where(known, j, 0)] - low
            slot = jnp.where(known, slot, 0)
            send_slots.append(slot)
            plan[at] = jnp.where((r >= 0) & (r < src.shape[1]), r - low, -1)
            pltpu.make_async_copy(cache_hbm.at[slot], leaving.at[at], in_sem.at[at]).start()

    wide = hidden[...].astype(F32)
    hidden32[...] = wide
    norm_into(normed3, [wide], [gain[...]], [0], width)
    spread_normed(normed3, spread, slots, width)
    gather_angles(lambda s: lengths_s[low + s], slots, cos_ref, sin_ref, cos_rows, sin_rows)
    query, key, value = project(normed3, spread, wq, wkv, wq_copies, wkv_copies, slots, width)
    cosine, sine = cos_rows[...], sin_rows[...]
    query_out[...] = jnp.zeros(query_out.shape, F32)
    for g in range(heads):
        turned = turn(query[:, g * HD : (g + 1) * HD], cosine, sine)
        query_out[pl.ds(g, slots, stride=GROUP), :] = turned.astype(BF16).astype(F32)
    newkey_out[...] = turn(key, cosine, sine).astype(BF16).astype(F32)
    newvalue_out[...] = value.astype(BF16).astype(F32)

    positions = [lengths_s[low + slot] for slot in send_slots]
    for at, slot in enumerate(send_slots):
        pltpu.make_async_copy(cache_hbm.at[slot], leaving.at[at], in_sem.at[at]).wait()
        put_row(
            leaving, at, positions[at],
            newkey_out[pl.ds(slot, 1), :], newvalue_out[pl.ds(slot, 1), :],
        )
    for k in range(others):
        pltpu.make_async_copy(
            leaving.at[pl.ds(k * MOVE, MOVE)], boxes[k], out_sem.at[k]
        ).start()
    rows = [query_out[pl.ds(pl.multiple_of(slot * GROUP, GROUP), GROUP), :] for slot in send_slots]
    attended = attend(leaving, list(range(moving)), positions, rows)
    column = pl.multiple_of(me_tp * shard, shard)
    for at, slot in enumerate(send_slots):
        note = notes[at // MOVE]
        m = at % MOVE
        for g in range(heads):
            note[m : m + 1, g * HD : (g + 1) * HD] = attended[at][g : g + 1, :]
        note[m : m + 1, heads * HD :] = hidden32[pl.ds(slot, 1), pl.ds(column, shard)]
    for k in range(others):
        pltpu.make_async_copy(
            leaving.at[pl.ds(k * MOVE, MOVE)], boxes[k], out_sem.at[k]
        ).wait()


def attend_all(buffer, places, positions, query_of, attended_rows, slots):
    for c in range(slots // CHUNK):
        span = range(c * CHUNK, (c + 1) * CHUNK)
        got = attend(
            buffer,
            [places[s] for s in span],
            [positions[s] for s in span],
            [query_of(s) for s in span],
        )
        for s, rows in zip(span, got):
            attended_rows[s * GROUP : (s + 1) * GROUP, :] = rows


def attend_kernel(
    slots, heads, meta, lengths_s, query, newkey, newvalue, cache_hbm, out,
    buffer, attended_rows, in_sem,
):
    low = meta[0] * slots

    def copy_in(c):
        span = pl.ds(c * CHUNK, CHUNK)
        return pltpu.make_async_copy(cache_hbm.at[span], buffer.at[span], in_sem.at[c])

    for c in range(slots // CHUNK):
        copy_in(c).start()
    for c in range(slots // CHUNK):
        copy_in(c).wait()
        span = list(range(c * CHUNK, (c + 1) * CHUNK))
        positions = [lengths_s[low + s] for s in span]
        for s, p in zip(span, positions):
            put_row(buffer, s, p, newkey[s : s + 1, :], newvalue[s : s + 1, :])
        got = attend(
            buffer, span, positions, [query[s * GROUP : (s + 1) * GROUP, :] for s in span]
        )
        for s, rows in zip(span, got):
            attended_rows[s * GROUP : (s + 1) * GROUP, :] = rows
    for g in range(heads):
        out[:, g * HD : (g + 1) * HD] = attended_rows[pl.ds(g, slots, stride=GROUP), :].astype(BF16)


def project_out(attended, wo, wo_hbm, wo_sem, own, sends, me_tp, peers_tp):
    shard = own.shape[1]
    for k in list(range(1, peers_tp)) + [0]:
        out_copy(wo, wo_hbm, wo_sem, me_tp, peers_tp, shard, k).wait()
        part = jnp.dot(attended, wo[k], preferred_element_type=F32)
        if k == 0:
            own[...] = part
        else:
            sends[k - 1][...] = part.astype(BF16)


def out_copy(wo, wo_hbm, wo_sem, me_tp, peers_tp, shard, k):
    column = pl.multiple_of(lax.rem(me_tp + k, peers_tp) * shard, shard)
    return pltpu.make_async_copy(wo_hbm.at[:, pl.ds(column, shard)], wo.at[k], wo_sem.at[k])


def out_kernel(peers, peers_tp, meta, plan, attended, wo_hbm, *rest):
    notes = rest[: peers - 1]
    own = rest[peers - 1]
    sends = rest[peers : peers + peers_tp - 1]
    wo, wo_sem = rest[peers + peers_tp - 1 :]
    me_tp = meta[1]
    shard = own.shape[1]
    for k in list(range(1, peers_tp)) + [0]:
        out_copy(wo, wo_hbm, wo_sem, me_tp, peers_tp, shard, k).start()
    rows = attended[...].astype(F32)
    index = lax.broadcasted_iota(I32, rows.shape, 0)
    for at in range((peers - 1) * MOVE):
        note = notes[at // MOVE][at % MOVE : at % MOVE + 1, : rows.shape[1]]
        rows = jnp.where(index == plan[at], note, rows)
    project_out(rows.astype(BF16), wo, wo_hbm, wo_sem, own, sends, me_tp, peers_tp)


def sum_kernel(peers, peers_tp, heads, meta, plan, hidden, own, *rest):
    got, notes, out = rest[: peers_tp - 1], rest[peers_tp - 1 : -1], rest[-1]
    shard = own.shape[1]
    total = own[...]
    for part in got:
        total = total + part[...].astype(F32)
    if notes:
        column = pl.multiple_of(meta[1] * shard, shard)
        residual = hidden[:, pl.ds(column, shard)].astype(F32)
        index = lax.broadcasted_iota(I32, residual.shape, 0)
        for at in range((peers - 1) * MOVE):
            note = notes[at // MOVE][at % MOVE : at % MOVE + 1, heads * HD :]
            residual = jnp.where(index == plan[at], note, residual)
    else:
        residual = hidden[...].astype(F32)
    out[...] = (residual + total).astype(BF16)


def load_slots(slots, peers, cache_hbm, box_hbm, buffer, in_sem):
    copies = []
    for c in range(slots // CHUNK):
        span = pl.ds(c * CHUNK, CHUNK)
        copies.append(pltpu.make_async_copy(cache_hbm.at[span], buffer.at[span], in_sem.at[c]))
    for k in range(peers - 1):
        copies.append(
            pltpu.make_async_copy(
                box_hbm[k],
                buffer.at[pl.ds(slots + k * MOVE, MOVE)],
                in_sem.at[slots // CHUNK + k],
            )
        )
    return copies


def map_places(slots, peers, plan, place):
    for s in range(slots):
        place[s] = s
    for at in range((peers - 1) * MOVE):
        taker = plan[at]

        @pl.when(taker >= 0)
        def _():
            place[taker] = slots + at


def second_kernel(
    peers, peers_tp, slots, heads,
    meta, source_s, lengths_s, plan, gain, cos_ref, sin_ref, newkey1, newvalue1,
    wq_hbm, wkv_hbm, wo_hbm, cache_hbm, *rest,
):
    blocks, rest = rest[:peers_tp], rest[peers_tp:]
    box_hbm, rest = rest[: peers - 1], rest[peers - 1 :]
    newkey, newvalue, own = rest[:3]
    sends, rest = rest[3 : 2 + peers_tp], rest[2 + peers_tp :]
    (wq, wkv, wo, normed3, spread, cos_rows, sin_rows, buffer, query_rows, attended_rows, place,
     wq_sem, wkv_sem, wo_sem, in_sem) = rest
    me, me_tp = meta[0], meta[1]
    low = me * slots
    width = gain.shape[1]
    shard = own.shape[1]
    wq_copies = weight_copies(wq_hbm, wq, wq_sem, 4)
    wkv_copies = weight_copies(wkv_hbm, wkv, wkv_sem, 4)
    cache_copies = load_slots(slots, peers, cache_hbm, box_hbm, buffer, in_sem)
    for copy in wkv_copies + wq_copies + cache_copies[::-1]:
        copy.start()
    for k in list(range(1, peers_tp)) + [0]:
        out_copy(wo, wo_hbm, wo_sem, me_tp, peers_tp, shard, k).start()

    map_places(slots, peers, plan, place)
    firsts = [lax.rem(me_tp + peers_tp - k, peers_tp) for k in range(peers_tp)]
    norm_into(
        normed3,
        [block[...].astype(F32) for block in blocks],
        [gain[:, pl.ds(pl.multiple_of(first * shard, shard), shard)] for first in firsts],
        [first * (shard // HD) for first in firsts],
        width,
    )
    spread_normed(normed3, spread, slots, width)
    lengths = [lengths_s[source_s[low + s]] for s in range(slots)]
    gather_angles(lambda s: lengths[s] + 1, slots, cos_ref, sin_ref, cos_rows, sin_rows)
    query, key, value = project(normed3, spread, wq, wkv, wq_copies, wkv_copies, slots, width)
    cosine, sine = cos_rows[...], sin_rows[...]
    query_rows[...] = jnp.zeros(query_rows.shape, F32)
    for g in range(heads):
        turned = turn(query[:, g * HD : (g + 1) * HD], cosine, sine)
        query_rows[pl.ds(g, slots, stride=GROUP), :] = turned.astype(BF16).astype(F32)
    newkey[...] = turn(key, cosine, sine).astype(BF16).astype(F32)
    newvalue[...] = value.astype(BF16).astype(F32)

    for copy in cache_copies[::-1]:
        copy.wait()
    for c in range(slots // CHUNK):
        span = list(range(c * CHUNK, (c + 1) * CHUNK))
        places = [place[s] for s in span]
        for s, at in zip(span, places):
            first = jnp.where(at < slots, lengths[s], -1)
            put_row(buffer, at, first, newkey1[s : s + 1, :], newvalue1[s : s + 1, :])
            put_row(buffer, at, lengths[s] + 1, newkey[s : s + 1, :], newvalue[s : s + 1, :])
        got = attend(
            buffer, places, [lengths[s] + 1 for s in span],
            [query_rows[s * GROUP : (s + 1) * GROUP, :] for s in span],
        )
        for s, rows in zip(span, got):
            attended_rows[s * GROUP : (s + 1) * GROUP, :] = rows
    attended = jnp.concatenate(
        [attended_rows[pl.ds(g, slots, stride=GROUP), :].astype(BF16) for g in range(heads)], axis=1
    )
    project_out(attended, wo, wo_hbm, wo_sem, own, sends, me_tp, peers_tp)


def cache_kernel(
    peers, slots, meta, source_s, lengths_s, plan, newkey1, newvalue1, newkey2, newvalue2,
    cache_hbm, *rest,
):
    box_hbm, rest = rest[: peers - 1], rest[peers - 1 :]
    out_hbm, buffer, place, in_sem, out_sem = rest
    low = meta[0] * slots
    cache_copies = load_slots(slots, peers, cache_hbm, box_hbm, buffer, in_sem)
    for copy in cache_copies:
        copy.start()
    map_places(slots, peers, plan, place)
    chunks = slots // CHUNK
    for copy in cache_copies[chunks:]:
        copy.wait()
    outs = []
    for c in range(chunks):
        cache_copies[c].wait()
        for s in range(c * CHUNK, (c + 1) * CHUNK):
            at = place[s]
            length = lengths_s[source_s[low + s]]
            first = jnp.where(at < slots, length, -1)
            put_row(buffer, at, first, newkey1[s : s + 1, :], newvalue1[s : s + 1, :])
            put_row(buffer, at, length + 1, newkey2[s : s + 1, :], newvalue2[s : s + 1, :])
            copy = pltpu.make_async_copy(buffer.at[at], out_hbm.at[s], out_sem.at[s])
            copy.start()
            outs.append(copy)
    for copy in outs:
        copy.wait()


def join_kernel(peers_tp, meta, *rest):
    blocks, out = rest[:-1], rest[-1]
    shard = blocks[0].shape[1]
    for k, block in enumerate(blocks):
        first = lax.rem(meta[1] + peers_tp - k, peers_tp)
        out[:, pl.ds(pl.multiple_of(first * shard, shard), shard)] = block[...]


def shifted(x, axis, size, k):
    return lax.ppermute(x, axis, [(i, (i + k) % size) for i in range(size)])


def local(
    tables, kv_cache, hidden, lengths, source, norm_gain, query_weight, keyval_weight, out_weight
):
    peers, peers_tp = lax.axis_size("inst"), lax.axis_size("tp")
    slots, cap = kv_cache.shape[0], kv_cache.shape[2]
    width = hidden.shape[1]
    heads = query_weight.shape[1] // HD
    shard = width // peers_tp
    others, moving = peers - 1, (peers - 1) * MOVE
    blocks = width // HD
    meta = jnp.stack([lax.axis_index("inst"), lax.axis_index("tp")]).astype(I32)
    gain = norm_gain.reshape(1, width)
    wkv = keyval_weight.reshape(2 * width, HD)
    cosine, sine = (jnp.asarray(table) for table in tables)
    row32 = jax.ShapeDtypeStruct((slots, HD), F32)
    note_width = heads * HD + shard
    dma = pltpu.SemaphoreType.DMA
    weights = [
        pltpu.VMEM(query_weight.shape, BF16),
        pltpu.VMEM(wkv.shape, BF16),
    ]
    stages = [
        pltpu.VMEM((blocks, slots, HD), BF16),
        pltpu.VMEM((blocks, 2 * slots, 2 * HD), BF16),
        pltpu.VMEM((slots, HD), F32),
        pltpu.VMEM((slots, HD), F32),
    ]
    flops = 2 * slots * width * (heads + 2) * HD
    cache_bytes = kv_cache.size * 2

    query, newkey1, newvalue1, plan, *rest = pl.pallas_call(
        functools.partial(first_kernel, peers, slots, heads, shard),
        out_shape=[
            jax.ShapeDtypeStruct((slots * GROUP, HD), F32),
            row32,
            row32,
            jax.ShapeDtypeStruct((moving,), I32),
        ]
        + [jax.ShapeDtypeStruct((MOVE,) + kv_cache.shape[1:], BF16)] * others
        + [jax.ShapeDtypeStruct((MOVE, note_width), F32)] * others,
        in_specs=[SMEM] * 3 + [VMEM] * 5 + [ANY] * 3,
        out_specs=[VMEM] * 3 + [SMEM] + [ANY] * others + [VMEM] * others,
        scratch_shapes=weights
        + stages
        + [
            pltpu.VMEM((moving,) + kv_cache.shape[1:], BF16),
            pltpu.VMEM((slots, width), F32),
            dma((4,)),
            dma((4,)),
            dma((moving,)),
            dma((others,)),
        ],
        compiler_params=params(40),
        cost_estimate=cost(flops, (query_weight.size + wkv.size) * 2),
        name="first_step",
    )(meta, source, lengths, source.reshape(1, -1), hidden, gain, cosine, sine, query_weight, wkv,
      kv_cache)
    boxes, notes = rest[:others], rest[others:]
    got_notes = [shifted(note, "inst", peers, k + 1) for k, note in enumerate(notes)]
    got_boxes = [shifted(box, "inst", peers, k + 1) for k, box in enumerate(boxes)]

    attended = pl.pallas_call(
        functools.partial(attend_kernel, slots, heads),
        out_shape=jax.ShapeDtypeStruct((slots, heads * HD), BF16),
        in_specs=[SMEM] * 2 + [VMEM] * 3 + [ANY],
        out_specs=VMEM,
        scratch_shapes=[
            pltpu.VMEM(kv_cache.shape, BF16),
            pltpu.VMEM((slots * GROUP, HD), F32),
            dma((slots // CHUNK,)),
        ],
        compiler_params=params(24),
        cost_estimate=cost(4 * slots * cap * HD * heads, cache_bytes),
        name="attention",
    )(meta, lengths, query, newkey1, newvalue1, kv_cache)

    sent = [jax.ShapeDtypeStruct((slots, shard), F32)]
    sent += [jax.ShapeDtypeStruct((slots, shard), BF16)] * (peers_tp - 1)
    wo_scratch = pltpu.VMEM((peers_tp, heads * HD, shard), BF16)
    own, *sends = pl.pallas_call(
        functools.partial(out_kernel, peers, peers_tp),
        out_shape=sent,
        in_specs=[SMEM] * 2 + [VMEM, ANY] + [VMEM] * others,
        out_specs=[VMEM] * peers_tp,
        scratch_shapes=[wo_scratch, dma((peers_tp,))],
        compiler_params=params(24),
        cost_estimate=cost(2 * slots * width * heads * HD, out_weight.size * 2),
        name="out_projection",
    )(meta, plan, attended, out_weight, *got_notes)

    def summed(residual, own, sends, notes):
        got = [shifted(part, "tp", peers_tp, k + 1) for k, part in enumerate(sends)]
        shard_rows = pl.pallas_call(
            functools.partial(sum_kernel, peers, peers_tp, heads),
            out_shape=jax.ShapeDtypeStruct((slots, shard), BF16),
            in_specs=[SMEM] * 2 + [VMEM] * (2 + len(got) + len(notes)),
            out_specs=VMEM,
            compiler_params=params(16),
            name="sum_terms",
        )(meta, plan, residual, own, *got, *notes)
        return [shard_rows] + [
            shifted(shard_rows, "tp", peers_tp, k) for k in range(1, peers_tp)
        ]

    pieces = summed(hidden, own, sends, got_notes)

    newkey2, newvalue2, own, *sends = pl.pallas_call(
        functools.partial(second_kernel, peers, peers_tp, slots, heads),
        out_shape=[row32, row32] + sent,
        in_specs=[SMEM] * 4 + [VMEM] * 5 + [ANY] * 4 + [VMEM] * peers_tp + [ANY] * others,
        out_specs=[VMEM] * (2 + peers_tp),
        scratch_shapes=weights
        + [wo_scratch]
        + stages
        + [
            pltpu.VMEM((slots + moving,) + kv_cache.shape[1:], BF16),
            pltpu.VMEM((slots * GROUP, HD), F32),
            pltpu.VMEM((slots * GROUP, HD), F32),
            pltpu.SMEM((slots,), I32),
            dma((4,)),
            dma((4,)),
            dma((peers_tp,)),
            dma((slots // CHUNK + others,)),
        ],
        compiler_params=params(48),
        cost_estimate=cost(3 * flops, cache_bytes + (query_weight.size + wkv.size) * 4),
        name="second_step",
    )(meta, source, lengths, plan, gain, cosine, sine, newkey1, newvalue1, query_weight, wkv,
      out_weight, kv_cache, *pieces, *got_boxes)

    pieces = summed(pieces[0], own, sends, [])
    final_cache = pl.pallas_call(
        functools.partial(cache_kernel, peers, slots),
        out_shape=jax.ShapeDtypeStruct(kv_cache.shape, BF16),
        in_specs=[SMEM] * 4 + [VMEM] * 4 + [ANY] * peers,
        out_specs=ANY,
        scratch_shapes=[
            pltpu.VMEM((slots + moving,) + kv_cache.shape[1:], BF16),
            pltpu.SMEM((slots,), I32),
            dma((slots // CHUNK + others,)),
            dma((slots,)),
        ],
        compiler_params=params(24),
        cost_estimate=cost(0, 2 * cache_bytes),
        name="write_cache",
    )(meta, source, lengths, plan, newkey1, newvalue1, newkey2, newvalue2, kv_cache, *got_boxes)
    final_hidden = pl.pallas_call(
        functools.partial(join_kernel, peers_tp),
        out_shape=jax.ShapeDtypeStruct(hidden.shape, BF16),
        in_specs=[SMEM] + [VMEM] * peers_tp,
        out_specs=VMEM,
        compiler_params=params(16),
        name="join",
    )(meta, *pieces)
    return (final_hidden, final_cache)


def solution(mesh):
    def whole(kv_cache, *rest):
        tables = angle_tables(kv_cache.shape[2])
        return jax.shard_map(
            functools.partial(local, tables),
            mesh=mesh,
            in_specs=(
                P(("groups", "inst"), None, None, "tp"),
                P(("groups", "inst"), None),
                P("groups"),
                P("groups"),
                P(),
                P(None, "tp"),
                P(None, None, "tp"),
                P("tp", None),
            ),
            out_specs=(P(("groups", "inst"), None), P(("groups", "inst"), None, None, "tp")),
            check_vma=False,
        )(kv_cache, *rest)

    return whole
```

```python
import functools

import jax
import jax.numpy as jnp
import numpy as np
from jax import lax
from jax.experimental import pallas as pl
from jax.experimental.pallas import tpu as pltpu
from jax.sharding import PartitionSpec as P

MOVE = 2
EPS = 1e-05
THETA = 500000.0
HD = 128
GROUP = 8
PIECE = 16
CHUNK = 8

F32 = jnp.float32
BF16 = jnp.bfloat16
I32 = jnp.int32

ANY = pl.BlockSpec(memory_space=pl.ANY)
VMEM = pl.BlockSpec(memory_space=pltpu.VMEM)
SMEM = pl.BlockSpec(memory_space=pltpu.SMEM)
HBM = pl.BlockSpec(memory_space=pltpu.HBM)


def params(mib):
    return pltpu.CompilerParams(vmem_limit_bytes=mib * 1024 * 1024)


def cost(flops, nbytes):
    return pl.CostEstimate(flops=flops, bytes_accessed=nbytes, transcendentals=0)


def angle_tables(positions):
    frequency = THETA ** (-(np.arange(HD // 2, dtype=np.float64) * 2.0) / HD)
    angles = np.arange(positions, dtype=np.float64)[:, None] * frequency[None, :]
    cosine = np.concatenate([np.cos(angles), np.cos(angles)], axis=-1)
    sine = np.concatenate([-np.sin(angles), np.sin(angles)], axis=-1)
    return cosine.astype(np.float32), sine.astype(np.float32)


def turn(x, cosine, sine):
    return x * cosine + pltpu.roll(x, HD // 2, 1) * sine


def gather_angles(position_of, slots, cos_ref, sin_ref, cos_rows, sin_rows):
    for s in range(slots):
        p = position_of(s)
        cos_rows[s : s + 1, :] = cos_ref[pl.ds(p, 1), :]
        sin_rows[s : s + 1, :] = sin_ref[pl.ds(p, 1), :]


def spread_normed(normed3, spread, slots, width):
    blocks = width // HD
    row = lax.broadcasted_iota(I32, (HD, 4 * HD), 0)
    col = lax.broadcasted_iota(I32, (HD, 4 * HD), 1)
    goal = jnp.where(col < 2 * HD, 2 * row, 2 * row + 1 + 2 * HD)
    places = jnp.where(col == goal, 1.0, 0.0).astype(BF16)
    spread_all = jnp.dot(
        normed3[...].reshape(blocks * slots, HD), places, preferred_element_type=F32
    ).astype(BF16)
    spread[:, 0:slots, :] = spread_all[:, : 2 * HD].reshape(blocks, slots, 2 * HD)
    spread[:, slots:, :] = spread_all[:, 2 * HD :].reshape(blocks, slots, 2 * HD)


def project(normed3, spread, wq, wkv, slots, width, wq_copies=(), wkv_copies=()):
    pieces = max(len(wq_copies), 1)
    depth = width // pieces
    query = None
    pair = None
    for c in range(pieces):
        for copy in wkv_copies[c : c + 1]:
            copy.wait()
        for b in range(c * depth // HD, (c + 1) * depth // HD):
            part = jnp.dot(
                spread[b], wkv[b * 2 * HD : (b + 1) * 2 * HD, :], preferred_element_type=F32
            )
            pair = part if pair is None else pair + part
    for c in range(pieces):
        for copy in wq_copies[c : c + 1]:
            copy.wait()
        for b in range(c * depth // (2 * HD), (c + 1) * depth // (2 * HD)):
            block = jnp.concatenate([normed3[2 * b], normed3[2 * b + 1]], axis=1)
            part = jnp.dot(
                block, wq[b * 2 * HD : (b + 1) * 2 * HD, :], preferred_element_type=F32
            )
            query = part if query is None else query + part
    return query, pair[:slots], pair[slots:]


def weight_copies(src, dst, sem, pieces):
    depth = src.shape[0] // pieces
    copies = [
        pltpu.make_async_copy(
            src.at[pl.ds(c * depth, depth)], dst.at[pl.ds(c * depth, depth)], sem.at[c]
        )
        for c in range(pieces)
    ]
    return copies


def put_row(cache, place, p, key_row, value_row):
    base = pl.multiple_of((jnp.maximum(p, 0) // PIECE) * PIECE, PIECE)
    hit = lax.broadcasted_iota(I32, (PIECE, HD), 0) + base == p
    for which, new in ((0, key_row), (1, value_row)):
        old = cache[place, which, pl.ds(base, PIECE), :].astype(F32)
        cache[place, which, pl.ds(base, PIECE), :] = jnp.where(hit, new, old).astype(BF16)


def attend(cache, places, positions, query_rows):
    cap = cache.shape[2]
    col = lax.broadcasted_iota(I32, (GROUP, cap), 1)
    scores = [
        lax.dot_general(
            rows.astype(BF16),
            cache[place, 0],
            (((1,), (1,)), ((), ())),
            preferred_element_type=F32,
        )
        for place, rows in zip(places, query_rows)
    ]
    probs = []
    for score, p in zip(scores, positions):
        score = jnp.where(col <= p, score * HD**-0.5, -jnp.inf)
        weight = jnp.exp(score - jnp.max(score, axis=-1, keepdims=True))
        weight = weight / jnp.sum(weight, axis=-1, keepdims=True)
        probs.append(weight.astype(BF16))
    return [
        jnp.dot(prob, cache[place, 1], preferred_element_type=F32)
        for place, prob in zip(places, probs)
    ]


def norm_into(normed3, pieces, gains, firsts, total_width):
    square = None
    for piece in pieces:
        part = jnp.sum(piece * piece, axis=-1, keepdims=True)
        square = part if square is None else square + part
    factor = lax.rsqrt(square / total_width + EPS)
    for piece, gain, first in zip(pieces, gains, firsts):
        normed = (piece * factor * gain).astype(BF16)
        for i in range(piece.shape[1] // HD):
            normed3[first + i] = normed[:, i * HD : (i + 1) * HD]


def first_kernel(
    peers, slots, heads, shard,
    meta, source_hbm, lengths_hbm, hidden_hbm, gain_hbm, cos_hbm, sin_hbm, wq_hbm, wkv_hbm,
    cache_hbm, query_out, newkey_out, newvalue_out, plan, *rest,
):
    others = peers - 1
    moving = others * MOVE
    boxes, notes = rest[:others], rest[others : 2 * others]
    (wq, wkv, normed3, spread, cos_rows, sin_rows, leaving, hidden32, source_s, lengths_s, source_v,
     hidden, gain, cos_ref, sin_ref, small_sem, wq_sem, wkv_sem, in_sem, out_sem) = rest[2 * others :]
    width = hidden.shape[1]
    me, me_tp = meta[0], meta[1]
    wq_copies = weight_copies(wq_hbm, wq, wq_sem, 4)
    wkv_copies = weight_copies(wkv_hbm, wkv, wkv_sem, 4)
    small = [
        pltpu.make_async_copy(src, dst, small_sem.at[i])
        for i, (src, dst) in enumerate((
            (source_hbm, source_v), (source_hbm, source_s), (lengths_hbm, lengths_s),
            (hidden_hbm, hidden), (gain_hbm, gain), (cos_hbm, cos_ref), (sin_hbm, sin_ref),
        ))
    ]
    for copy in small + wkv_copies + wq_copies:
        copy.start()
    small[0].wait()
    small[1].wait()

    low = me * slots
    src = source_v[...]
    index = lax.broadcasted_iota(I32, src.shape, 1)
    mine_goes = (src >= low) & (src < low + slots)
    mine_comes = (index >= low) & (index < low + slots)
    index_f = index.astype(F32)
    send_slots = []
    for k in range(1, peers):
        other = jnp.bitwise_xor(me, k) * slots
        sent = mine_goes & (index >= other) & (index < other + slots)
        taken = mine_comes & (src >= other) & (src < other + slots)
        for m in range(MOVE):
            at = (k - 1) * MOVE + m
            if m == 0:
                j = jnp.min(jnp.where(sent, index_f, 1e6)).astype(I32)
                r = jnp.min(jnp.where(taken, index_f, 1e6)).astype(I32)
            else:
                j = jnp.max(jnp.where(sent, index_f, -1.0)).astype(I32)
                r = jnp.max(jnp.where(taken, index_f, -1.0)).astype(I32)
            known = (j >= 0) & (j < src.shape[1])
            slot = source_s[0, jnp.where(known, j, 0)] - low
            slot = jnp.where(known, slot, 0)
            send_slots.append(slot)
            plan[at] = jnp.where((r >= 0) & (r < src.shape[1]), r - low, -1)
            pltpu.make_async_copy(cache_hbm.at[slot], leaving.at[at], in_sem.at[at]).start()

    for copy in small[2:]:
        copy.wait()
    wide = hidden[...].astype(F32)
    hidden32[...] = wide
    norm_into(normed3, [wide], [gain[...]], [0], width)
    spread_normed(normed3, spread, slots, width)
    gather_angles(lambda s: lengths_s[0, low + s], slots, cos_ref, sin_ref, cos_rows, sin_rows)
    query, key, value = project(
        normed3, spread, wq, wkv, slots, width, wq_copies, wkv_copies
    )
    cosine, sine = cos_rows[...], sin_rows[...]
    query_out[...] = jnp.zeros(query_out.shape, F32)
    for g in range(heads):
        turned = turn(query[:, g * HD : (g + 1) * HD], cosine, sine)
        query_out[pl.ds(g, slots, stride=GROUP), :] = turned.astype(BF16).astype(F32)
    newkey_out[...] = turn(key, cosine, sine).astype(BF16).astype(F32)
    newvalue_out[...] = value.astype(BF16).astype(F32)

    positions = [lengths_s[0, low + slot] for slot in send_slots]
    for at, slot in enumerate(send_slots):
        pltpu.make_async_copy(cache_hbm.at[slot], leaving.at[at], in_sem.at[at]).wait()
        put_row(
            leaving, at, positions[at],
            newkey_out[pl.ds(slot, 1), :], newvalue_out[pl.ds(slot, 1), :],
        )
    for k in range(others):
        pltpu.make_async_copy(
            leaving.at[pl.ds(k * MOVE, MOVE)], boxes[k], out_sem.at[k]
        ).start()
    rows = [query_out[pl.ds(pl.multiple_of(slot * GROUP, GROUP), GROUP), :] for slot in send_slots]
    attended = attend(leaving, list(range(moving)), positions, rows)
    column = pl.multiple_of(me_tp * shard, shard)
    for at, slot in enumerate(send_slots):
        note = notes[at // MOVE]
        m = at % MOVE
        for g in range(heads):
            note[m : m + 1, g * HD : (g + 1) * HD] = attended[at][g : g + 1, :]
        note[m : m + 1, heads * HD :] = hidden32[pl.ds(slot, 1), pl.ds(column, shard)]
    for k in range(others):
        pltpu.make_async_copy(
            leaving.at[pl.ds(k * MOVE, MOVE)], boxes[k], out_sem.at[k]
        ).wait()


def attend_kernel(
    slots, heads, meta, lengths_s, query, newkey, newvalue, cache_hbm, out,
    buffer, attended_rows, in_sem,
):
    low = meta[0] * slots

    def copy_in(c):
        span = pl.ds(c * CHUNK, CHUNK)
        return pltpu.make_async_copy(cache_hbm.at[span], buffer.at[span], in_sem.at[c])

    for c in range(slots // CHUNK):
        copy_in(c).start()
    for c in range(slots // CHUNK):
        copy_in(c).wait()
        span = list(range(c * CHUNK, (c + 1) * CHUNK))
        positions = [lengths_s[low + s] for s in span]
        for s, p in zip(span, positions):
            put_row(buffer, s, p, newkey[s : s + 1, :], newvalue[s : s + 1, :])
        got = attend(
            buffer, span, positions, [query[s * GROUP : (s + 1) * GROUP, :] for s in span]
        )
        for s, rows in zip(span, got):
            attended_rows[s * GROUP : (s + 1) * GROUP, :] = rows
    for g in range(heads):
        out[:, g * HD : (g + 1) * HD] = attended_rows[pl.ds(g, slots, stride=GROUP), :].astype(BF16)


def project_out(attended, wo, own, sends, me_tp, peers_tp):
    shard = own.shape[1]
    for k in list(range(peers_tp - 1, 0, -1)) + [0]:
        column = pl.multiple_of(jnp.bitwise_xor(me_tp, k) * shard, shard)
        part = jnp.dot(attended, wo[:, pl.ds(column, shard)], preferred_element_type=F32)
        if k == 0:
            own[...] = part
        else:
            sends[k - 1][...] = part.astype(BF16)


def out_kernel(peers, peers_tp, meta, plan, attended, wo, *rest):
    notes = rest[: peers - 1]
    own = rest[peers - 1]
    sends = rest[peers:]
    rows = attended[...].astype(F32)
    index = lax.broadcasted_iota(I32, rows.shape, 0)
    for at in range((peers - 1) * MOVE):
        note = notes[at // MOVE][at % MOVE : at % MOVE + 1, : rows.shape[1]]
        rows = jnp.where(index == plan[at], note, rows)
    project_out(rows.astype(BF16), wo, own, sends, meta[1], peers_tp)


def sum_kernel(peers, peers_tp, heads, meta, plan, hidden, own, *rest):
    got, notes, out = rest[: peers_tp - 1], rest[peers_tp - 1 : -1], rest[-1]
    shard = own.shape[1]
    total = own[...]
    for part in got:
        total = total + part[...].astype(F32)
    if notes:
        column = pl.multiple_of(meta[1] * shard, shard)
        residual = hidden[:, pl.ds(column, shard)].astype(F32)
        index = lax.broadcasted_iota(I32, residual.shape, 0)
        for at in range((peers - 1) * MOVE):
            note = notes[at // MOVE][at % MOVE : at % MOVE + 1, heads * HD :]
            residual = jnp.where(index == plan[at], note, residual)
    else:
        residual = hidden[...].astype(F32)
    out[...] = (residual + total).astype(BF16)


def load_slots(slots, peers, cache_hbm, box_hbm, buffer, in_sem):
    copies = []
    for c in range(slots // CHUNK):
        span = pl.ds(c * CHUNK, CHUNK)
        copies.append(pltpu.make_async_copy(cache_hbm.at[span], buffer.at[span], in_sem.at[c]))
    for k in range(peers - 1):
        copies.append(
            pltpu.make_async_copy(
                box_hbm[k],
                buffer.at[pl.ds(slots + k * MOVE, MOVE)],
                in_sem.at[slots // CHUNK + k],
            )
        )
    return copies


def map_places(slots, peers, plan, place):
    for s in range(slots):
        place[s] = s
    for at in range((peers - 1) * MOVE):
        taker = plan[at]

        @pl.when(taker >= 0)
        def _():
            place[taker] = slots + at


def second_kernel(
    peers, peers_tp, slots, heads,
    meta, source_s, lengths_s, plan, gain, cos_ref, sin_ref, newkey1, newvalue1,
    wq, wkv, wo, cache_hbm, *rest,
):
    blocks, rest = rest[:peers_tp], rest[peers_tp:]
    box_hbm, rest = rest[: peers - 1], rest[peers - 1 :]
    newkey, newvalue, own = rest[:3]
    sends, rest = rest[3 : 2 + peers_tp], rest[2 + peers_tp :]
    (normed3, spread, cos_rows, sin_rows, buffer, query_rows, attended_rows, place,
     in_sem) = rest
    me, me_tp = meta[0], meta[1]
    low = me * slots
    width = gain.shape[1]
    shard = own.shape[1]
    cache_copies = load_slots(slots, peers, cache_hbm, box_hbm, buffer, in_sem)
    for copy in cache_copies[::-1]:
        copy.start()

    map_places(slots, peers, plan, place)
    firsts = [jnp.bitwise_xor(me_tp, k) for k in range(peers_tp)]
    norm_into(
        normed3,
        [block[...].astype(F32) for block in blocks],
        [gain[:, pl.ds(pl.multiple_of(first * shard, shard), shard)] for first in firsts],
        [first * (shard // HD) for first in firsts],
        width,
    )
    spread_normed(normed3, spread, slots, width)
    lengths = [lengths_s[source_s[low + s]] for s in range(slots)]
    gather_angles(lambda s: lengths[s] + 1, slots, cos_ref, sin_ref, cos_rows, sin_rows)
    query, key, value = project(normed3, spread, wq, wkv, slots, width)
    cosine, sine = cos_rows[...], sin_rows[...]
    query_rows[...] = jnp.zeros(query_rows.shape, F32)
    for g in range(heads):
        turned = turn(query[:, g * HD : (g + 1) * HD], cosine, sine)
        query_rows[pl.ds(g, slots, stride=GROUP), :] = turned.astype(BF16).astype(F32)
    newkey[...] = turn(key, cosine, sine).astype(BF16).astype(F32)
    newvalue[...] = value.astype(BF16).astype(F32)

    for copy in cache_copies[::-1]:
        copy.wait()
    for c in range(slots // CHUNK):
        span = list(range(c * CHUNK, (c + 1) * CHUNK))
        places = [place[s] for s in span]
        for s, at in zip(span, places):
            first = jnp.where(at < slots, lengths[s], -1)
            put_row(buffer, at, first, newkey1[s : s + 1, :], newvalue1[s : s + 1, :])
            put_row(buffer, at, lengths[s] + 1, newkey[s : s + 1, :], newvalue[s : s + 1, :])
        got = attend(
            buffer, places, [lengths[s] + 1 for s in span],
            [query_rows[s * GROUP : (s + 1) * GROUP, :] for s in span],
        )
        for s, rows in zip(span, got):
            attended_rows[s * GROUP : (s + 1) * GROUP, :] = rows
    attended = jnp.concatenate(
        [attended_rows[pl.ds(g, slots, stride=GROUP), :].astype(BF16) for g in range(heads)], axis=1
    )
    project_out(attended, wo, own, sends, me_tp, peers_tp)


def cache_kernel(
    peers, slots, meta, source_s, lengths_s, plan, newkey1, newvalue1, newkey2, newvalue2,
    cache_hbm, *rest,
):
    box_hbm, rest = rest[: peers - 1], rest[peers - 1 :]
    out_hbm, buffer, place, in_sem, out_sem = rest
    low = meta[0] * slots
    cache_copies = load_slots(slots, peers, cache_hbm, box_hbm, buffer, in_sem)
    for copy in cache_copies:
        copy.start()
    map_places(slots, peers, plan, place)
    chunks = slots // CHUNK
    for copy in cache_copies[chunks:]:
        copy.wait()
    outs = []
    for c in range(chunks):
        cache_copies[c].wait()
        for s in range(c * CHUNK, (c + 1) * CHUNK):
            at = place[s]
            length = lengths_s[source_s[low + s]]
            first = jnp.where(at < slots, length, -1)
            put_row(buffer, at, first, newkey1[s : s + 1, :], newvalue1[s : s + 1, :])
            put_row(buffer, at, length + 1, newkey2[s : s + 1, :], newvalue2[s : s + 1, :])
            copy = pltpu.make_async_copy(buffer.at[at], out_hbm.at[s], out_sem.at[s])
            copy.start()
            outs.append(copy)
    for copy in outs:
        copy.wait()


def join_kernel(peers_tp, meta, *rest):
    blocks, out, sem = rest[:-2], rest[-2], rest[-1]
    shard = blocks[0].shape[1]
    copies = []
    for k, block in enumerate(blocks):
        column = pl.multiple_of(jnp.bitwise_xor(meta[1], k) * shard, shard)
        copies.append(pltpu.make_async_copy(block, out.at[:, pl.ds(column, shard)], sem.at[k]))
        copies[-1].start()
    for copy in copies:
        copy.wait()


def swapped(x, axis, size, k):
    return lax.ppermute(x, axis, [(i, i ^ k) for i in range(size)])


def local(
    tables, kv_cache, hidden, lengths, source, norm_gain, query_weight, keyval_weight, out_weight
):
    peers, peers_tp = lax.axis_size("inst"), lax.axis_size("tp")
    slots, cap = kv_cache.shape[0], kv_cache.shape[2]
    width = hidden.shape[1]
    heads = query_weight.shape[1] // HD
    shard = width // peers_tp
    others, moving = peers - 1, (peers - 1) * MOVE
    blocks = width // HD
    meta = jnp.stack([lax.axis_index("inst"), lax.axis_index("tp")]).astype(I32)
    gain = norm_gain.reshape(1, width)
    wkv = keyval_weight.reshape(2 * width, HD)
    cosine, sine = (jnp.asarray(table) for table in tables)
    row32 = jax.ShapeDtypeStruct((slots, HD), F32)
    note_width = heads * HD + shard
    dma = pltpu.SemaphoreType.DMA
    weights = [
        pltpu.VMEM(query_weight.shape, BF16),
        pltpu.VMEM(wkv.shape, BF16),
    ]
    stages = [
        pltpu.VMEM((blocks, slots, HD), BF16),
        pltpu.VMEM((blocks, 2 * slots, 2 * HD), BF16),
        pltpu.VMEM((slots, HD), F32),
        pltpu.VMEM((slots, HD), F32),
    ]
    flops = 2 * slots * width * (heads + 2) * HD
    cache_bytes = kv_cache.size * 2

    query, newkey1, newvalue1, plan, *rest = pl.pallas_call(
        functools.partial(first_kernel, peers, slots, heads, shard),
        out_shape=[
            jax.ShapeDtypeStruct((slots * GROUP, HD), F32),
            row32,
            row32,
            jax.ShapeDtypeStruct((moving,), I32),
        ]
        + [jax.ShapeDtypeStruct((MOVE,) + kv_cache.shape[1:], BF16)] * others
        + [jax.ShapeDtypeStruct((MOVE, note_width), F32)] * others,
        in_specs=[SMEM] + [HBM] * 9,
        out_specs=[VMEM] * 3 + [SMEM] + [ANY] * others + [VMEM] * others,
        scratch_shapes=weights
        + stages
        + [
            pltpu.VMEM((moving,) + kv_cache.shape[1:], BF16),
            pltpu.VMEM((slots, width), F32),
            pltpu.SMEM((1, source.shape[0]), I32),
            pltpu.SMEM((1, source.shape[0]), I32),
            pltpu.VMEM((1, source.shape[0]), I32),
            pltpu.VMEM(hidden.shape, BF16),
            pltpu.VMEM((1, width), F32),
            pltpu.VMEM(cosine.shape, F32),
            pltpu.VMEM(cosine.shape, F32),
            dma((7,)),
            dma((4,)),
            dma((4,)),
            dma((moving,)),
            dma((others,)),
        ],
        compiler_params=params(24),
        cost_estimate=cost(flops, (query_weight.size + wkv.size) * 2),
        name="first_step",
    )(meta, source.reshape(1, -1), lengths.reshape(1, -1), hidden, gain, cosine, sine, query_weight,
      wkv, kv_cache)
    boxes, notes = rest[:others], rest[others:]
    got_notes = [swapped(note, "inst", peers, k + 1) for k, note in enumerate(notes)]
    got_boxes = [swapped(box, "inst", peers, k + 1) for k, box in enumerate(boxes)]

    attended = pl.pallas_call(
        functools.partial(attend_kernel, slots, heads),
        out_shape=jax.ShapeDtypeStruct((slots, heads * HD), BF16),
        in_specs=[SMEM] * 2 + [VMEM] * 3 + [ANY],
        out_specs=VMEM,
        scratch_shapes=[
            pltpu.VMEM(kv_cache.shape, BF16),
            pltpu.VMEM((slots * GROUP, HD), F32),
            dma((slots // CHUNK,)),
        ],
        compiler_params=params(24),
        cost_estimate=cost(4 * slots * cap * HD * heads, cache_bytes),
        name="attention",
    )(meta, lengths, query, newkey1, newvalue1, kv_cache)

    sent = [jax.ShapeDtypeStruct((slots, shard), F32)]
    sent += [jax.ShapeDtypeStruct((slots, shard), BF16)] * (peers_tp - 1)
    own, *sends = pl.pallas_call(
        functools.partial(out_kernel, peers, peers_tp),
        out_shape=sent,
        in_specs=[SMEM] * 2 + [VMEM] * (2 + others),
        out_specs=[VMEM] * peers_tp,
        compiler_params=params(16),
        cost_estimate=cost(2 * slots * width * heads * HD, out_weight.size * 2),
        name="out_projection",
    )(meta, plan, attended, out_weight, *got_notes)

    def summed(residual, own, sends, notes):
        got = [swapped(sends[k - 1], "tp", peers_tp, k) for k in range(peers_tp - 1, 0, -1)]
        shard_rows = pl.pallas_call(
            functools.partial(sum_kernel, peers, peers_tp, heads),
            out_shape=jax.ShapeDtypeStruct((slots, shard), BF16),
            in_specs=[SMEM] * 2 + [VMEM] * (2 + len(got) + len(notes)),
            out_specs=VMEM,
            compiler_params=params(16),
            name="sum_terms",
        )(meta, plan, residual, own, *got, *notes)
        return [shard_rows] + [
            swapped(shard_rows, "tp", peers_tp, k) for k in range(1, peers_tp)
        ]

    pieces = summed(hidden, own, sends, got_notes)

    newkey2, newvalue2, own, *sends = pl.pallas_call(
        functools.partial(second_kernel, peers, peers_tp, slots, heads),
        out_shape=[row32, row32] + sent,
        in_specs=[SMEM] * 4 + [VMEM] * 8 + [ANY] + [VMEM] * peers_tp + [ANY] * others,
        out_specs=[VMEM] * (2 + peers_tp),
        scratch_shapes=stages
        + [
            pltpu.VMEM((slots + moving,) + kv_cache.shape[1:], BF16),
            pltpu.VMEM((slots * GROUP, HD), F32),
            pltpu.VMEM((slots * GROUP, HD), F32),
            pltpu.SMEM((slots,), I32),
            dma((slots // CHUNK + others,)),
        ],
        compiler_params=params(32),
        cost_estimate=cost(3 * flops, cache_bytes + (query_weight.size + wkv.size) * 4),
        name="second_step",
    )(meta, source, lengths, plan, gain, cosine, sine, newkey1, newvalue1, query_weight, wkv,
      out_weight, kv_cache, *pieces, *got_boxes)

    pieces = summed(pieces[0], own, sends, [])
    final_cache = pl.pallas_call(
        functools.partial(cache_kernel, peers, slots),
        out_shape=jax.ShapeDtypeStruct(kv_cache.shape, BF16),
        in_specs=[SMEM] * 4 + [VMEM] * 4 + [ANY] * peers,
        out_specs=ANY,
        scratch_shapes=[
            pltpu.VMEM((slots + moving,) + kv_cache.shape[1:], BF16),
            pltpu.SMEM((slots,), I32),
            dma((slots // CHUNK + others,)),
            dma((slots,)),
        ],
        compiler_params=params(24),
        cost_estimate=cost(0, 2 * cache_bytes),
        name="write_cache",
    )(meta, source, lengths, plan, newkey1, newvalue1, newkey2, newvalue2, kv_cache, *got_boxes)
    final_hidden = pl.pallas_call(
        functools.partial(join_kernel, peers_tp),
        out_shape=jax.ShapeDtypeStruct(hidden.shape, BF16),
        in_specs=[SMEM] + [ANY] * peers_tp,
        out_specs=ANY,
        scratch_shapes=[dma((peers_tp,))],
        compiler_params=params(16),
        name="join",
    )(meta, *pieces)
    return (final_hidden, final_cache)


def solution(mesh):
    def whole(kv_cache, *rest):
        tables = angle_tables(kv_cache.shape[2])
        return jax.shard_map(
            functools.partial(local, tables),
            mesh=mesh,
            in_specs=(
                P(("groups", "inst"), None, None, "tp"),
                P(("groups", "inst"), None),
                P("groups"),
                P("groups"),
                P(),
                P(None, "tp"),
                P(None, None, "tp"),
                P("tp", None),
            ),
            out_specs=(P(("groups", "inst"), None), P(("groups", "inst"), None, None, "tp")),
            check_vma=False,
        )(kv_cache, *rest)

    return whole
```

```python
import functools

import jax
import jax.numpy as jnp
import numpy as np
from jax import lax
from jax.experimental import pallas as pl
from jax.experimental.pallas import tpu as pltpu
from jax.sharding import PartitionSpec as P

MOVE = 2
EPS = 1e-05
THETA = 500000.0
HD = 128
GROUP = 8
PIECE = 16
CHUNK = 8

F32 = jnp.float32
BF16 = jnp.bfloat16
I32 = jnp.int32

ANY = pl.BlockSpec(memory_space=pl.ANY)
VMEM = pl.BlockSpec(memory_space=pltpu.VMEM)
SMEM = pl.BlockSpec(memory_space=pltpu.SMEM)
HBM = pl.BlockSpec(memory_space=pltpu.HBM)


def params(mib):
    return pltpu.CompilerParams(vmem_limit_bytes=mib * 1024 * 1024)


def cost(flops, nbytes):
    return pl.CostEstimate(flops=flops, bytes_accessed=nbytes, transcendentals=0)


def angle_tables(positions):
    frequency = THETA ** (-(np.arange(HD // 2, dtype=np.float64) * 2.0) / HD)
    angles = np.arange(positions, dtype=np.float64)[:, None] * frequency[None, :]
    cosine = np.concatenate([np.cos(angles), np.cos(angles)], axis=-1)
    sine = np.concatenate([-np.sin(angles), np.sin(angles)], axis=-1)
    return cosine.astype(np.float32), sine.astype(np.float32)


def turn(x, cosine, sine):
    return x * cosine + pltpu.roll(x, HD // 2, 1) * sine


def gather_angles(position_of, slots, cos_ref, sin_ref, cos_rows, sin_rows):
    for s in range(slots):
        p = position_of(s)
        cos_rows[s : s + 1, :] = cos_ref[pl.ds(p, 1), :]
        sin_rows[s : s + 1, :] = sin_ref[pl.ds(p, 1), :]


def spread_normed(normed3, spread, slots, width):
    blocks = width // HD
    row = lax.broadcasted_iota(I32, (HD, 4 * HD), 0)
    col = lax.broadcasted_iota(I32, (HD, 4 * HD), 1)
    goal = jnp.where(col < 2 * HD, 2 * row, 2 * row + 1 + 2 * HD)
    places = jnp.where(col == goal, 1.0, 0.0).astype(BF16)
    spread_all = jnp.dot(
        normed3[...].reshape(blocks * slots, HD), places, preferred_element_type=F32
    ).astype(BF16)
    spread[:, 0:slots, :] = spread_all[:, : 2 * HD].reshape(blocks, slots, 2 * HD)
    spread[:, slots:, :] = spread_all[:, 2 * HD :].reshape(blocks, slots, 2 * HD)


def project(normed3, spread, wq, wkv, slots, width, wq_copies=(), wkv_copies=()):
    pieces = max(len(wq_copies), 1)
    depth = width // pieces
    query = None
    pair = None
    for c in range(pieces):
        for copy in wkv_copies[c : c + 1]:
            copy.wait()
        for b in range(c * depth // HD, (c + 1) * depth // HD):
            part = jnp.dot(
                spread[b], wkv[b * 2 * HD : (b + 1) * 2 * HD, :], preferred_element_type=F32
            )
            pair = part if pair is None else pair + part
    for c in range(pieces):
        for copy in wq_copies[c : c + 1]:
            copy.wait()
        for b in range(c * depth // (2 * HD), (c + 1) * depth // (2 * HD)):
            block = jnp.concatenate([normed3[2 * b], normed3[2 * b + 1]], axis=1)
            part = jnp.dot(
                block, wq[b * 2 * HD : (b + 1) * 2 * HD, :], preferred_element_type=F32
            )
            query = part if query is None else query + part
    return query, pair[:slots], pair[slots:]


def weight_copies(src, dst, sem, pieces):
    depth = src.shape[0] // pieces
    copies = [
        pltpu.make_async_copy(
            src.at[pl.ds(c * depth, depth)], dst.at[pl.ds(c * depth, depth)], sem.at[c]
        )
        for c in range(pieces)
    ]
    return copies


def put_row(cache, place, p, key_row, value_row):
    base = pl.multiple_of((jnp.maximum(p, 0) // PIECE) * PIECE, PIECE)
    hit = lax.broadcasted_iota(I32, (PIECE, HD), 0) + base == p
    for which, new in ((0, key_row), (1, value_row)):
        old = cache[place, which, pl.ds(base, PIECE), :].astype(F32)
        cache[place, which, pl.ds(base, PIECE), :] = jnp.where(hit, new, old).astype(BF16)


def attend(cache, places, positions, query_rows):
    cap = cache.shape[2]
    col = lax.broadcasted_iota(I32, (GROUP, cap), 1)
    scores = [
        lax.dot_general(
            rows.astype(BF16),
            cache[place, 0],
            (((1,), (1,)), ((), ())),
            preferred_element_type=F32,
        )
        for place, rows in zip(places, query_rows)
    ]
    probs = []
    for score, p in zip(scores, positions):
        score = jnp.where(col <= p, score * HD**-0.5, -jnp.inf)
        weight = jnp.exp(score - jnp.max(score, axis=-1, keepdims=True))
        weight = weight / jnp.sum(weight, axis=-1, keepdims=True)
        probs.append(weight.astype(BF16))
    return [
        jnp.dot(prob, cache[place, 1], preferred_element_type=F32)
        for place, prob in zip(places, probs)
    ]


def norm_into(normed3, pieces, gains, firsts, total_width):
    square = None
    for piece in pieces:
        part = jnp.sum(piece * piece, axis=-1, keepdims=True)
        square = part if square is None else square + part
    factor = lax.rsqrt(square / total_width + EPS)
    for piece, gain, first in zip(pieces, gains, firsts):
        normed = (piece * factor * gain).astype(BF16)
        for i in range(piece.shape[1] // HD):
            normed3[first + i] = normed[:, i * HD : (i + 1) * HD]


def first_kernel(
    peers, slots, heads, shard,
    meta, source_hbm, lengths_hbm, hidden_hbm, gain_hbm, cos_hbm, sin_hbm, wq_hbm, wkv_hbm,
    cache_hbm, query_out, newkey_out, newvalue_out, plan, *rest,
):
    others = peers - 1
    moving = others * MOVE
    boxes, notes = rest[:others], rest[others : 2 * others]
    (wq, wkv, normed3, spread, cos_rows, sin_rows, leaving, hidden32, source_s, lengths_s, source_v,
     hidden, gain, cos_ref, sin_ref, small_sem, wq_sem, wkv_sem, in_sem, out_sem) = rest[2 * others :]
    width = hidden.shape[1]
    me, me_tp = meta[0], meta[1]
    wq_copies = weight_copies(wq_hbm, wq, wq_sem, 4)
    wkv_copies = weight_copies(wkv_hbm, wkv, wkv_sem, 4)
    small = [
        pltpu.make_async_copy(src, dst, small_sem.at[i])
        for i, (src, dst) in enumerate((
            (source_hbm, source_v), (source_hbm, source_s), (lengths_hbm, lengths_s),
            (hidden_hbm, hidden), (gain_hbm, gain), (cos_hbm, cos_ref), (sin_hbm, sin_ref),
        ))
    ]
    for copy in small + wkv_copies + wq_copies:
        copy.start()
    small[0].wait()
    small[1].wait()

    low = me * slots
    src = source_v[...]
    index = lax.broadcasted_iota(I32, src.shape, 1)
    mine_goes = (src >= low) & (src < low + slots)
    mine_comes = (index >= low) & (index < low + slots)
    index_f = index.astype(F32)
    send_slots = []
    for k in range(1, peers):
        other = jnp.bitwise_xor(me, k) * slots
        sent = mine_goes & (index >= other) & (index < other + slots)
        taken = mine_comes & (src >= other) & (src < other + slots)
        for m in range(MOVE):
            at = (k - 1) * MOVE + m
            if m == 0:
                j = jnp.min(jnp.where(sent, index_f, 1e6)).astype(I32)
                r = jnp.min(jnp.where(taken, index_f, 1e6)).astype(I32)
            else:
                j = jnp.max(jnp.where(sent, index_f, -1.0)).astype(I32)
                r = jnp.max(jnp.where(taken, index_f, -1.0)).astype(I32)
            known = (j >= 0) & (j < src.shape[1])
            slot = source_s[0, jnp.where(known, j, 0)] - low
            slot = jnp.where(known, slot, 0)
            send_slots.append(slot)
            plan[at] = jnp.where((r >= 0) & (r < src.shape[1]), r - low, -1)
            pltpu.make_async_copy(cache_hbm.at[slot], leaving.at[at], in_sem.at[at]).start()

    for copy in small[2:]:
        copy.wait()
    wide = hidden[...].astype(F32)
    hidden32[...] = wide
    norm_into(normed3, [wide], [gain[...]], [0], width)
    spread_normed(normed3, spread, slots, width)
    gather_angles(lambda s: lengths_s[0, low + s], slots, cos_ref, sin_ref, cos_rows, sin_rows)
    query, key, value = project(
        normed3, spread, wq, wkv, slots, width, wq_copies, wkv_copies
    )
    cosine, sine = cos_rows[...], sin_rows[...]
    query_out[...] = jnp.zeros(query_out.shape, F32)
    for g in range(heads):
        turned = turn(query[:, g * HD : (g + 1) * HD], cosine, sine)
        query_out[pl.ds(g, slots, stride=GROUP), :] = turned.astype(BF16).astype(F32)
    newkey_out[...] = turn(key, cosine, sine).astype(BF16).astype(F32)
    newvalue_out[...] = value.astype(BF16).astype(F32)

    positions = [lengths_s[0, low + slot] for slot in send_slots]
    for at, slot in enumerate(send_slots):
        pltpu.make_async_copy(cache_hbm.at[slot], leaving.at[at], in_sem.at[at]).wait()
        put_row(
            leaving, at, positions[at],
            newkey_out[pl.ds(slot, 1), :], newvalue_out[pl.ds(slot, 1), :],
        )
    for k in range(others):
        pltpu.make_async_copy(
            leaving.at[pl.ds(k * MOVE, MOVE)], boxes[k], out_sem.at[k]
        ).start()
    rows = [query_out[pl.ds(pl.multiple_of(slot * GROUP, GROUP), GROUP), :] for slot in send_slots]
    attended = attend(leaving, list(range(moving)), positions, rows)
    column = pl.multiple_of(me_tp * shard, shard)
    for at, slot in enumerate(send_slots):
        note = notes[at // MOVE]
        m = at % MOVE
        for g in range(heads):
            note[m : m + 1, g * HD : (g + 1) * HD] = attended[at][g : g + 1, :]
        note[m : m + 1, heads * HD :] = hidden32[pl.ds(slot, 1), pl.ds(column, shard)]
    for k in range(others):
        pltpu.make_async_copy(
            leaving.at[pl.ds(k * MOVE, MOVE)], boxes[k], out_sem.at[k]
        ).wait()


def attend_kernel(
    slots, heads, meta, lengths_s, query, newkey, newvalue, cache_hbm, out,
    buffer, attended_rows, in_sem,
):
    low = meta[0] * slots

    def copy_in(c):
        span = pl.ds(c * CHUNK, CHUNK)
        return pltpu.make_async_copy(cache_hbm.at[span], buffer.at[span], in_sem.at[c])

    for c in range(slots // CHUNK):
        copy_in(c).start()
    for c in range(slots // CHUNK):
        copy_in(c).wait()
        span = list(range(c * CHUNK, (c + 1) * CHUNK))
        positions = [lengths_s[low + s] for s in span]
        for s, p in zip(span, positions):
            put_row(buffer, s, p, newkey[s : s + 1, :], newvalue[s : s + 1, :])
        got = attend(
            buffer, span, positions, [query[s * GROUP : (s + 1) * GROUP, :] for s in span]
        )
        for s, rows in zip(span, got):
            attended_rows[s * GROUP : (s + 1) * GROUP, :] = rows
    for g in range(heads):
        out[:, g * HD : (g + 1) * HD] = attended_rows[pl.ds(g, slots, stride=GROUP), :].astype(BF16)


def project_out(attended, wo, own, sends, me_tp, peers_tp):
    shard = own.shape[1]
    for k in list(range(peers_tp - 1, 0, -1)) + [0]:
        column = pl.multiple_of(jnp.bitwise_xor(me_tp, k) * shard, shard)
        part = jnp.dot(attended, wo[:, pl.ds(column, shard)], preferred_element_type=F32)
        if k == 0:
            own[...] = part
        else:
            sends[k - 1][...] = part.astype(BF16)


def out_kernel(peers, peers_tp, meta, plan, attended, wo, _box, *rest):
    notes = rest[: peers - 1]
    own = rest[peers - 1]
    sends = rest[peers:]
    rows = attended[...].astype(F32)
    index = lax.broadcasted_iota(I32, rows.shape, 0)
    for at in range((peers - 1) * MOVE):
        note = notes[at // MOVE][at % MOVE : at % MOVE + 1, : rows.shape[1]]
        rows = jnp.where(index == plan[at], note, rows)
    project_out(rows.astype(BF16), wo, own, sends, meta[1], peers_tp)


def sum_kernel(peers, peers_tp, heads, meta, plan, hidden, own, *rest):
    got, notes, out = rest[: peers_tp - 1], rest[peers_tp - 1 : -1], rest[-1]
    shard = own.shape[1]
    total = own[...]
    for part in got:
        total = total + part[...].astype(F32)
    if notes:
        column = pl.multiple_of(meta[1] * shard, shard)
        residual = hidden[:, pl.ds(column, shard)].astype(F32)
        index = lax.broadcasted_iota(I32, residual.shape, 0)
        for at in range((peers - 1) * MOVE):
            note = notes[at // MOVE][at % MOVE : at % MOVE + 1, heads * HD :]
            residual = jnp.where(index == plan[at], note, residual)
    else:
        residual = hidden[...].astype(F32)
    out[...] = (residual + total).astype(BF16)


def load_slots(slots, peers, cache_hbm, box_hbm, buffer, in_sem):
    copies = []
    for c in range(slots // CHUNK):
        span = pl.ds(c * CHUNK, CHUNK)
        copies.append(pltpu.make_async_copy(cache_hbm.at[span], buffer.at[span], in_sem.at[c]))
    for k in range(peers - 1):
        copies.append(
            pltpu.make_async_copy(
                box_hbm[k],
                buffer.at[pl.ds(slots + k * MOVE, MOVE)],
                in_sem.at[slots // CHUNK + k],
            )
        )
    return copies


def map_places(slots, peers, plan, place):
    for s in range(slots):
        place[s] = s
    for at in range((peers - 1) * MOVE):
        taker = plan[at]

        @pl.when(taker >= 0)
        def _():
            place[taker] = slots + at


def second_kernel(
    peers, peers_tp, slots, heads,
    meta, source_s, lengths_s, plan, gain, cos_ref, sin_ref, newkey1, newvalue1,
    wq, wkv, wo, cache_hbm, *rest,
):
    blocks, rest = rest[:peers_tp], rest[peers_tp:]
    box_hbm, rest = rest[: peers - 1], rest[peers - 1 :]
    newkey, newvalue, own = rest[:3]
    sends, rest = rest[3 : 2 + peers_tp], rest[2 + peers_tp :]
    (normed3, spread, cos_rows, sin_rows, buffer, query_rows, attended_rows, place,
     in_sem) = rest
    me, me_tp = meta[0], meta[1]
    low = me * slots
    width = gain.shape[1]
    shard = own.shape[1]
    cache_copies = load_slots(slots, peers, cache_hbm, box_hbm, buffer, in_sem)
    for copy in cache_copies[::-1]:
        copy.start()

    map_places(slots, peers, plan, place)
    firsts = [jnp.bitwise_xor(me_tp, k) for k in range(peers_tp)]
    norm_into(
        normed3,
        [block[...].astype(F32) for block in blocks],
        [gain[:, pl.ds(pl.multiple_of(first * shard, shard), shard)] for first in firsts],
        [first * (shard // HD) for first in firsts],
        width,
    )
    spread_normed(normed3, spread, slots, width)
    lengths = [lengths_s[source_s[low + s]] for s in range(slots)]
    gather_angles(lambda s: lengths[s] + 1, slots, cos_ref, sin_ref, cos_rows, sin_rows)
    query, key, value = project(normed3, spread, wq, wkv, slots, width)
    cosine, sine = cos_rows[...], sin_rows[...]
    query_rows[...] = jnp.zeros(query_rows.shape, F32)
    for g in range(heads):
        turned = turn(query[:, g * HD : (g + 1) * HD], cosine, sine)
        query_rows[pl.ds(g, slots, stride=GROUP), :] = turned.astype(BF16).astype(F32)
    newkey[...] = turn(key, cosine, sine).astype(BF16).astype(F32)
    newvalue[...] = value.astype(BF16).astype(F32)

    for copy in cache_copies[::-1]:
        copy.wait()
    for c in range(slots // CHUNK):
        span = list(range(c * CHUNK, (c + 1) * CHUNK))
        places = [place[s] for s in span]
        for s, at in zip(span, places):
            first = jnp.where(at < slots, lengths[s], -1)
            put_row(buffer, at, first, newkey1[s : s + 1, :], newvalue1[s : s + 1, :])
            put_row(buffer, at, lengths[s] + 1, newkey[s : s + 1, :], newvalue[s : s + 1, :])
        got = attend(
            buffer, places, [lengths[s] + 1 for s in span],
            [query_rows[s * GROUP : (s + 1) * GROUP, :] for s in span],
        )
        for s, rows in zip(span, got):
            attended_rows[s * GROUP : (s + 1) * GROUP, :] = rows
    attended = jnp.concatenate(
        [attended_rows[pl.ds(g, slots, stride=GROUP), :].astype(BF16) for g in range(heads)], axis=1
    )
    project_out(attended, wo, own, sends, me_tp, peers_tp)


def cache_kernel(
    peers, slots, meta, source_s, lengths_s, plan, newkey1, newvalue1, newkey2, newvalue2,
    cache_hbm, *rest,
):
    box_hbm, rest = rest[: peers - 1], rest[peers - 1 :]
    out_hbm, buffer, place, in_sem, out_sem = rest
    low = meta[0] * slots
    cache_copies = load_slots(slots, peers, cache_hbm, box_hbm, buffer, in_sem)
    for copy in cache_copies:
        copy.start()
    map_places(slots, peers, plan, place)
    chunks = slots // CHUNK
    for copy in cache_copies[chunks:]:
        copy.wait()
    outs = []
    for c in range(chunks):
        cache_copies[c].wait()
        for s in range(c * CHUNK, (c + 1) * CHUNK):
            at = place[s]
            length = lengths_s[source_s[low + s]]
            first = jnp.where(at < slots, length, -1)
            put_row(buffer, at, first, newkey1[s : s + 1, :], newvalue1[s : s + 1, :])
            put_row(buffer, at, length + 1, newkey2[s : s + 1, :], newvalue2[s : s + 1, :])
            copy = pltpu.make_async_copy(buffer.at[at], out_hbm.at[s], out_sem.at[s])
            copy.start()
            outs.append(copy)
    for copy in outs:
        copy.wait()


def join_kernel(peers_tp, meta, *rest):
    blocks, out, sem = rest[:-2], rest[-2], rest[-1]
    shard = blocks[0].shape[1]
    copies = []
    for k, block in enumerate(blocks):
        column = pl.multiple_of(jnp.bitwise_xor(meta[1], k) * shard, shard)
        copies.append(pltpu.make_async_copy(block, out.at[:, pl.ds(column, shard)], sem.at[k]))
        copies[-1].start()
    for copy in copies:
        copy.wait()


def swapped(x, axis, size, k):
    return lax.ppermute(x, axis, [(i, i ^ k) for i in range(size)])


def local(
    tables, kv_cache, hidden, lengths, source, norm_gain, query_weight, keyval_weight, out_weight
):
    peers, peers_tp = lax.axis_size("inst"), lax.axis_size("tp")
    slots, cap = kv_cache.shape[0], kv_cache.shape[2]
    width = hidden.shape[1]
    heads = query_weight.shape[1] // HD
    shard = width // peers_tp
    others, moving = peers - 1, (peers - 1) * MOVE
    blocks = width // HD
    meta = jnp.stack([lax.axis_index("inst"), lax.axis_index("tp")]).astype(I32)
    gain = norm_gain.reshape(1, width)
    wkv = keyval_weight.reshape(2 * width, HD)
    cosine, sine = (jnp.asarray(table) for table in tables)
    row32 = jax.ShapeDtypeStruct((slots, HD), F32)
    note_width = heads * HD + shard
    dma = pltpu.SemaphoreType.DMA
    weights = [
        pltpu.VMEM(query_weight.shape, BF16),
        pltpu.VMEM(wkv.shape, BF16),
    ]
    stages = [
        pltpu.VMEM((blocks, slots, HD), BF16),
        pltpu.VMEM((blocks, 2 * slots, 2 * HD), BF16),
        pltpu.VMEM((slots, HD), F32),
        pltpu.VMEM((slots, HD), F32),
    ]
    flops = 2 * slots * width * (heads + 2) * HD
    cache_bytes = kv_cache.size * 2

    query, newkey1, newvalue1, plan, *rest = pl.pallas_call(
        functools.partial(first_kernel, peers, slots, heads, shard),
        out_shape=[
            jax.ShapeDtypeStruct((slots * GROUP, HD), F32),
            row32,
            row32,
            jax.ShapeDtypeStruct((moving,), I32),
        ]
        + [jax.ShapeDtypeStruct((MOVE,) + kv_cache.shape[1:], BF16)] * others
        + [jax.ShapeDtypeStruct((MOVE, note_width), F32)] * others,
        in_specs=[SMEM] + [HBM] * 9,
        out_specs=[VMEM] * 3 + [SMEM] + [ANY] * others + [VMEM] * others,
        scratch_shapes=weights
        + stages
        + [
            pltpu.VMEM((moving,) + kv_cache.shape[1:], BF16),
            pltpu.VMEM((slots, width), F32),
            pltpu.SMEM((1, source.shape[0]), I32),
            pltpu.SMEM((1, source.shape[0]), I32),
            pltpu.VMEM((1, source.shape[0]), I32),
            pltpu.VMEM(hidden.shape, BF16),
            pltpu.VMEM((1, width), F32),
            pltpu.VMEM(cosine.shape, F32),
            pltpu.VMEM(cosine.shape, F32),
            dma((7,)),
            dma((4,)),
            dma((4,)),
            dma((moving,)),
            dma((others,)),
        ],
        compiler_params=params(24),
        cost_estimate=cost(flops, (query_weight.size + wkv.size) * 2),
        name="first_step",
    )(meta, *(
        pltpu.with_memory_space_constraint(x, pltpu.HBM)
        for x in (source.reshape(1, -1), lengths.reshape(1, -1), hidden, gain, cosine, sine,
                  query_weight, wkv, kv_cache)
    ))
    boxes, notes = rest[:others], rest[others:]
    got_notes = [swapped(note, "inst", peers, k + 1) for k, note in enumerate(notes)]
    got_boxes = [swapped(box, "inst", peers, k + 1) for k, box in enumerate(boxes)]

    attended = pl.pallas_call(
        functools.partial(attend_kernel, slots, heads),
        out_shape=jax.ShapeDtypeStruct((slots, heads * HD), BF16),
        in_specs=[SMEM] * 2 + [VMEM] * 3 + [ANY],
        out_specs=VMEM,
        scratch_shapes=[
            pltpu.VMEM(kv_cache.shape, BF16),
            pltpu.VMEM((slots * GROUP, HD), F32),
            dma((slots // CHUNK,)),
        ],
        compiler_params=params(24),
        cost_estimate=cost(4 * slots * cap * HD * heads, cache_bytes),
        name="attention",
    )(meta, lengths, query, newkey1, newvalue1, kv_cache)

    sent = [jax.ShapeDtypeStruct((slots, shard), F32)]
    sent += [jax.ShapeDtypeStruct((slots, shard), BF16)] * (peers_tp - 1)
    own, *sends = pl.pallas_call(
        functools.partial(out_kernel, peers, peers_tp),
        out_shape=sent,
        in_specs=[SMEM] * 2 + [VMEM] * 2 + [ANY] + [VMEM] * others,
        out_specs=[VMEM] * peers_tp,
        compiler_params=params(16),
        cost_estimate=cost(2 * slots * width * heads * HD, out_weight.size * 2),
        name="out_projection",
    )(meta, plan, attended, out_weight, got_boxes[0], *got_notes)

    def summed(residual, own, sends, notes):
        got = [swapped(sends[k - 1], "tp", peers_tp, k) for k in range(peers_tp - 1, 0, -1)]
        shard_rows = pl.pallas_call(
            functools.partial(sum_kernel, peers, peers_tp, heads),
            out_shape=jax.ShapeDtypeStruct((slots, shard), BF16),
            in_specs=[SMEM] * 2 + [VMEM] * (2 + len(got) + len(notes)),
            out_specs=VMEM,
            compiler_params=params(16),
            name="sum_terms",
        )(meta, plan, residual, own, *got, *notes)
        return [shard_rows] + [
            swapped(shard_rows, "tp", peers_tp, k) for k in range(1, peers_tp)
        ]

    pieces = summed(hidden, own, sends, got_notes)

    newkey2, newvalue2, own, *sends = pl.pallas_call(
        functools.partial(second_kernel, peers, peers_tp, slots, heads),
        out_shape=[row32, row32] + sent,
        in_specs=[SMEM] * 4 + [VMEM] * 8 + [ANY] + [VMEM] * peers_tp + [ANY] * others,
        out_specs=[VMEM] * (2 + peers_tp),
        scratch_shapes=stages
        + [
            pltpu.VMEM((slots + moving,) + kv_cache.shape[1:], BF16),
            pltpu.VMEM((slots * GROUP, HD), F32),
            pltpu.VMEM((slots * GROUP, HD), F32),
            pltpu.SMEM((slots,), I32),
            dma((slots // CHUNK + others,)),
        ],
        compiler_params=params(32),
        cost_estimate=cost(3 * flops, cache_bytes + (query_weight.size + wkv.size) * 4),
        name="second_step",
    )(meta, source, lengths, plan, gain, cosine, sine, newkey1, newvalue1, query_weight, wkv,
      out_weight, kv_cache, *pieces, *got_boxes)

    pieces = summed(pieces[0], own, sends, [])
    final_cache = pl.pallas_call(
        functools.partial(cache_kernel, peers, slots),
        out_shape=jax.ShapeDtypeStruct(kv_cache.shape, BF16),
        in_specs=[SMEM] * 4 + [VMEM] * 4 + [ANY] * peers,
        out_specs=ANY,
        scratch_shapes=[
            pltpu.VMEM((slots + moving,) + kv_cache.shape[1:], BF16),
            pltpu.SMEM((slots,), I32),
            dma((slots // CHUNK + others,)),
            dma((slots,)),
        ],
        compiler_params=params(24),
        cost_estimate=cost(0, 2 * cache_bytes),
        name="write_cache",
    )(meta, source, lengths, plan, newkey1, newvalue1, newkey2, newvalue2, kv_cache, *got_boxes)
    final_hidden = pl.pallas_call(
        functools.partial(join_kernel, peers_tp),
        out_shape=jax.ShapeDtypeStruct(hidden.shape, BF16),
        in_specs=[SMEM] + [ANY] * peers_tp,
        out_specs=ANY,
        scratch_shapes=[dma((peers_tp,))],
        compiler_params=params(16),
        name="join",
    )(meta, *pieces)
    return (final_hidden, final_cache)


def solution(mesh):
    def whole(kv_cache, *rest):
        tables = angle_tables(kv_cache.shape[2])
        return jax.shard_map(
            functools.partial(local, tables),
            mesh=mesh,
            in_specs=(
                P(("groups", "inst"), None, None, "tp"),
                P(("groups", "inst"), None),
                P("groups"),
                P("groups"),
                P(),
                P(None, "tp"),
                P(None, None, "tp"),
                P("tp", None),
            ),
            out_specs=(P(("groups", "inst"), None), P(("groups", "inst"), None, None, "tp")),
            check_vma=False,
        )(kv_cache, *rest)

    return whole
```

```python
import functools

import jax
import jax.numpy as jnp
import numpy as np
from jax import lax
from jax.experimental import pallas as pl
from jax.experimental.pallas import tpu as pltpu
from jax.sharding import PartitionSpec as P

MOVE = 2
EPS = 1e-05
THETA = 500000.0
HD = 128
GROUP = 8
PIECE = 16
CHUNK = 8
NOTE = 16

F32 = jnp.float32
BF16 = jnp.bfloat16
I32 = jnp.int32

ANY = pl.BlockSpec(memory_space=pl.ANY)
VMEM = pl.BlockSpec(memory_space=pltpu.VMEM)
SMEM = pl.BlockSpec(memory_space=pltpu.SMEM)
HBM = pl.BlockSpec(memory_space=pltpu.HBM)


def params(mib):
    return pltpu.CompilerParams(vmem_limit_bytes=mib * 1024 * 1024)


def cost(flops, nbytes):
    return pl.CostEstimate(flops=flops, bytes_accessed=nbytes, transcendentals=0)


def angle_tables(positions):
    frequency = THETA ** (-(np.arange(HD // 2, dtype=np.float64) * 2.0) / HD)
    angles = np.arange(positions, dtype=np.float64)[:, None] * frequency[None, :]
    cosine = np.concatenate([np.cos(angles), np.cos(angles)], axis=-1)
    sine = np.concatenate([-np.sin(angles), np.sin(angles)], axis=-1)
    return cosine.astype(np.float32), sine.astype(np.float32)


def turn(x, cosine, sine):
    return x * cosine + pltpu.roll(x, HD // 2, 1) * sine


def gather_angles(position_of, slots, cos_ref, sin_ref, cos_rows, sin_rows):
    for s in range(slots):
        p = position_of(s)
        cos_rows[s : s + 1, :] = cos_ref[pl.ds(p, 1), :]
        sin_rows[s : s + 1, :] = sin_ref[pl.ds(p, 1), :]


def spread_normed(normed3, spread, slots, width):
    blocks = width // HD
    row = lax.broadcasted_iota(I32, (HD, 4 * HD), 0)
    col = lax.broadcasted_iota(I32, (HD, 4 * HD), 1)
    goal = jnp.where(col < 2 * HD, 2 * row, 2 * row + 1 + 2 * HD)
    places = jnp.where(col == goal, 1.0, 0.0).astype(BF16)
    spread_all = jnp.dot(
        normed3[...].reshape(blocks * slots, HD), places, preferred_element_type=F32
    ).astype(BF16)
    spread[:, 0:slots, :] = spread_all[:, : 2 * HD].reshape(blocks, slots, 2 * HD)
    spread[:, slots:, :] = spread_all[:, 2 * HD :].reshape(blocks, slots, 2 * HD)


def project(normed3, spread, wq, wkv, slots, width, wq_copies=(), wkv_copies=()):
    pieces = max(len(wq_copies), 1)
    depth = width // pieces
    query = None
    pair = None
    for c in range(pieces):
        for copy in wkv_copies[c : c + 1]:
            copy.wait()
        for b in range(c * depth // HD, (c + 1) * depth // HD):
            part = jnp.dot(
                spread[b], wkv[b * 2 * HD : (b + 1) * 2 * HD, :], preferred_element_type=F32
            )
            pair = part if pair is None else pair + part
    for c in range(pieces):
        for copy in wq_copies[c : c + 1]:
            copy.wait()
        for b in range(c * depth // (2 * HD), (c + 1) * depth // (2 * HD)):
            block = jnp.concatenate([normed3[2 * b], normed3[2 * b + 1]], axis=1)
            part = jnp.dot(
                block, wq[b * 2 * HD : (b + 1) * 2 * HD, :], preferred_element_type=F32
            )
            query = part if query is None else query + part
    return query, pair[:slots], pair[slots:]


def weight_copies(src, dst, sem, pieces):
    depth = src.shape[0] // pieces
    copies = [
        pltpu.make_async_copy(
            src.at[pl.ds(c * depth, depth)], dst.at[pl.ds(c * depth, depth)], sem.at[c]
        )
        for c in range(pieces)
    ]
    return copies


def put_row(cache, place, p, key_row, value_row):
    base = pl.multiple_of((jnp.maximum(p, 0) // PIECE) * PIECE, PIECE)
    hit = lax.broadcasted_iota(I32, (PIECE, HD), 0) + base == p
    for which, new in ((0, key_row), (1, value_row)):
        old = cache[place, which, pl.ds(base, PIECE), :].astype(F32)
        cache[place, which, pl.ds(base, PIECE), :] = jnp.where(hit, new, old).astype(BF16)


def attend(cache, places, positions, query_rows):
    cap = cache.shape[2]
    col = lax.broadcasted_iota(I32, (GROUP, cap), 1)
    scores = [
        lax.dot_general(
            rows.astype(BF16),
            cache[place, 0],
            (((1,), (1,)), ((), ())),
            preferred_element_type=F32,
        )
        for place, rows in zip(places, query_rows)
    ]
    probs = []
    for score, p in zip(scores, positions):
        score = jnp.where(col <= p, score * HD**-0.5, -jnp.inf)
        weight = jnp.exp(score - jnp.max(score, axis=-1, keepdims=True))
        weight = weight / jnp.sum(weight, axis=-1, keepdims=True)
        probs.append(weight.astype(BF16))
    return [
        jnp.dot(prob, cache[place, 1], preferred_element_type=F32)
        for place, prob in zip(places, probs)
    ]


def norm_into(normed3, pieces, gains, firsts, total_width):
    square = None
    for piece in pieces:
        part = jnp.sum(piece * piece, axis=-1, keepdims=True)
        square = part if square is None else square + part
    factor = lax.rsqrt(square / total_width + EPS)
    for piece, gain, first in zip(pieces, gains, firsts):
        normed = (piece * factor * gain).astype(BF16)
        for i in range(piece.shape[1] // HD):
            normed3[first + i] = normed[:, i * HD : (i + 1) * HD]


def first_kernel(
    peers, slots, heads, shard,
    meta, source_hbm, lengths_hbm, hidden_hbm, gain_hbm, cos_hbm, sin_hbm, wq_hbm, wkv_hbm,
    cache_hbm, query_out, newkey_out, newvalue_out, plan, *rest,
):
    others = peers - 1
    moving = others * MOVE
    box, notes = rest[0], (None,) + rest[1:others]
    (wq, wkv, normed3, spread, cos_rows, sin_rows, leaving, hidden32, source_s, lengths_s, source_v,
     hidden, gain, cos_ref, sin_ref, tail, small_sem, wq_sem, wkv_sem, in_sem,
     box_sem) = rest[others:]
    width = hidden.shape[1]
    me, me_tp = meta[0], meta[1]
    wq_copies = weight_copies(wq_hbm, wq, wq_sem, 4)
    wkv_copies = weight_copies(wkv_hbm, wkv, wkv_sem, 4)
    small = [
        pltpu.make_async_copy(src, dst, small_sem.at[i])
        for i, (src, dst) in enumerate((
            (source_hbm, source_v), (source_hbm, source_s), (lengths_hbm, lengths_s),
            (hidden_hbm, hidden), (gain_hbm, gain), (cos_hbm, cos_ref), (sin_hbm, sin_ref),
        ))
    ]
    for copy in small + wkv_copies + wq_copies:
        copy.start()
    small[0].wait()
    small[1].wait()

    low = me * slots
    src = source_v[...]
    index = lax.broadcasted_iota(I32, src.shape, 1)
    mine_goes = (src >= low) & (src < low + slots)
    mine_comes = (index >= low) & (index < low + slots)
    index_f = index.astype(F32)
    send_slots = []
    for k in range(1, peers):
        other = jnp.bitwise_xor(me, k) * slots
        sent = mine_goes & (index >= other) & (index < other + slots)
        taken = mine_comes & (src >= other) & (src < other + slots)
        for m in range(MOVE):
            at = (k - 1) * MOVE + m
            if m == 0:
                j = jnp.min(jnp.where(sent, index_f, 1e6)).astype(I32)
                r = jnp.min(jnp.where(taken, index_f, 1e6)).astype(I32)
            else:
                j = jnp.max(jnp.where(sent, index_f, -1.0)).astype(I32)
                r = jnp.max(jnp.where(taken, index_f, -1.0)).astype(I32)
            known = (j >= 0) & (j < src.shape[1])
            slot = source_s[0, jnp.where(known, j, 0)] - low
            slot = jnp.where(known, slot, 0)
            send_slots.append(slot)
            plan[at] = jnp.where((r >= 0) & (r < src.shape[1]), r - low, -1)
            plan[moving + at] = slot
            pltpu.make_async_copy(cache_hbm.at[slot], leaving.at[at], in_sem.at[at]).start()

    for copy in small[2:]:
        copy.wait()
    wide = hidden[...].astype(F32)
    hidden32[...] = wide
    norm_into(normed3, [wide], [gain[...]], [0], width)
    spread_normed(normed3, spread, slots, width)
    gather_angles(lambda s: lengths_s[0, low + s], slots, cos_ref, sin_ref, cos_rows, sin_rows)
    query, key, value = project(
        normed3, spread, wq, wkv, slots, width, wq_copies, wkv_copies
    )
    cosine, sine = cos_rows[...], sin_rows[...]
    query_out[...] = jnp.zeros(query_out.shape, F32)
    for g in range(heads):
        turned = turn(query[:, g * HD : (g + 1) * HD], cosine, sine)
        query_out[pl.ds(g, slots, stride=GROUP), :] = turned.astype(BF16).astype(F32)
    newkey_out[...] = turn(key, cosine, sine).astype(BF16).astype(F32)
    newvalue_out[...] = value.astype(BF16).astype(F32)

    positions = [lengths_s[0, low + slot] for slot in send_slots]
    for at, slot in enumerate(send_slots):
        pltpu.make_async_copy(cache_hbm.at[slot], leaving.at[at], in_sem.at[at]).wait()
        put_row(
            leaving, at, positions[at],
            newkey_out[pl.ds(slot, 1), :], newvalue_out[pl.ds(slot, 1), :],
        )
    cap = leaving.shape[2]
    copies = [
        pltpu.make_async_copy(
            leaving.at[pl.ds(0, MOVE)], box.at[:, :, pl.ds(0, cap), :], box_sem.at[0]
        )
    ]
    copies[0].start()
    rows = [query_out[pl.ds(pl.multiple_of(slot * GROUP, GROUP), GROUP), :] for slot in send_slots]
    attended = attend(leaving, list(range(moving)), positions, rows)
    column = pl.multiple_of(me_tp * shard, shard)
    for at, slot in enumerate(send_slots):
        m = at % MOVE
        residual = hidden32[pl.ds(slot, 1), pl.ds(column, shard)]
        if at < MOVE:
            blocks = [attended[at][g : g + 1, :] for g in range(heads)]
            blocks += [residual[:, b * HD : (b + 1) * HD] for b in range(shard // HD)]
            blocks += [jnp.zeros((1, HD), F32)] * (NOTE - len(blocks))
            tail[m] = jnp.concatenate(blocks, axis=0).astype(BF16)
            copies.append(
                pltpu.make_async_copy(
                    tail.at[m], box.at[m, 0, pl.ds(cap, NOTE), :], box_sem.at[1 + m]
                )
            )
            copies[-1].start()
        else:
            note = notes[at // MOVE]
            for g in range(heads):
                note[m : m + 1, g * HD : (g + 1) * HD] = attended[at][g : g + 1, :]
            note[m : m + 1, heads * HD :] = residual
    for copy in copies:
        copy.wait()


def attend_kernel(
    slots, heads, meta, lengths_s, query, newkey, newvalue, cache_hbm, out,
    buffer, attended_rows, in_sem,
):
    low = meta[0] * slots

    def copy_in(c):
        span = pl.ds(c * CHUNK, CHUNK)
        return pltpu.make_async_copy(cache_hbm.at[span], buffer.at[span], in_sem.at[c])

    for c in range(slots // CHUNK):
        copy_in(c).start()
    for c in range(slots // CHUNK):
        copy_in(c).wait()
        span = list(range(c * CHUNK, (c + 1) * CHUNK))
        positions = [lengths_s[low + s] for s in span]
        for s, p in zip(span, positions):
            put_row(buffer, s, p, newkey[s : s + 1, :], newvalue[s : s + 1, :])
        got = attend(
            buffer, span, positions, [query[s * GROUP : (s + 1) * GROUP, :] for s in span]
        )
        for s, rows in zip(span, got):
            attended_rows[s * GROUP : (s + 1) * GROUP, :] = rows
    for g in range(heads):
        out[:, g * HD : (g + 1) * HD] = attended_rows[pl.ds(g, slots, stride=GROUP), :].astype(BF16)


def project_out(attended, wo, residual, own, sends, me_tp, peers_tp):
    shard = own.shape[1]
    for k in list(range(peers_tp - 1, 0, -1)) + [0]:
        column = pl.multiple_of(jnp.bitwise_xor(me_tp, k) * shard, shard)
        part = jnp.dot(attended, wo[:, pl.ds(column, shard)], preferred_element_type=F32)
        if k == 0:
            own[...] = residual + part
        else:
            sends[k - 1][...] = part.astype(BF16)


def out_kernel(
    peers, peers_tp, slots, meta, lengths_s, plan, attended, wo, hidden, newkey, newvalue, box_hbm,
    cache_hbm, *rest,
):
    notes, rest = rest[: peers - 2], rest[peers - 2 :]
    own, sends, boxes = rest[0], rest[1:peers_tp], rest[peers_tp : peers_tp + peers - 2]
    leaving, tail, sem, in_sem, out_sem = rest[peers_tp + peers - 2 :]
    moving = (peers - 1) * MOVE
    send_slots = [plan[moving + at] for at in range(MOVE, moving)]
    packs = [
        pltpu.make_async_copy(cache_hbm.at[slot], leaving.at[i], in_sem.at[i])
        for i, slot in enumerate(send_slots)
    ]
    for pack in packs:
        pack.start()
    shard = own.shape[1]
    cap = box_hbm.shape[2] - NOTE
    copy = pltpu.make_async_copy(box_hbm.at[:, 0, pl.ds(cap, NOTE), :], tail, sem.at[0])
    copy.start()
    rows = attended[...].astype(F32)
    heads = rows.shape[1] // HD
    column = pl.multiple_of(meta[1] * shard, shard)
    residual = hidden[:, pl.ds(column, shard)].astype(F32)
    row_index = lax.broadcasted_iota(I32, rows.shape, 0)
    residual_index = lax.broadcasted_iota(I32, residual.shape, 0)
    copy.wait()
    for at in range((peers - 1) * MOVE):
        m = at % MOVE
        if at < MOVE:
            blocks = tail[m].astype(F32)
            blocks = [blocks[b : b + 1, :] for b in range(heads + shard // HD)]
            note = jnp.concatenate(blocks, axis=1)
        else:
            note = notes[at // MOVE - 1][m : m + 1, :]
        rows = jnp.where(row_index == plan[at], note[:, : heads * HD], rows)
        residual = jnp.where(residual_index == plan[at], note[:, heads * HD :], residual)
    for pack in packs:
        pack.wait()
    for i, slot in enumerate(send_slots):
        put_row(
            leaving, i, lengths_s[meta[0] * slots + slot],
            newkey[pl.ds(slot, 1), :], newvalue[pl.ds(slot, 1), :],
        )
    outs = [
        pltpu.make_async_copy(leaving.at[pl.ds(k * MOVE, MOVE)], out, out_sem.at[k])
        for k, out in enumerate(boxes)
    ]
    for out in outs:
        out.start()
    project_out(rows.astype(BF16), wo, residual, own, sends, meta[1], peers_tp)
    for out in outs:
        out.wait()


def sum_kernel(own, *rest):
    total = own[...]
    for part in rest[:-1]:
        total = total + part[...].astype(F32)
    rest[-1][...] = total.astype(BF16)


def load_slots(slots, peers, cache_hbm, box_hbm, buffer, in_sem):
    copies = []
    for c in range(slots // CHUNK):
        span = pl.ds(c * CHUNK, CHUNK)
        copies.append(pltpu.make_async_copy(cache_hbm.at[span], buffer.at[span], in_sem.at[c]))
    for k in range(peers - 1):
        copies.append(
            pltpu.make_async_copy(
                box_hbm[k].at[:, :, pl.ds(0, cache_hbm.shape[2]), :],
                buffer.at[pl.ds(slots + k * MOVE, MOVE)],
                in_sem.at[slots // CHUNK + k],
            )
        )
    return copies


def map_places(slots, peers, plan, place):
    for s in range(slots):
        place[s] = s
    for at in range((peers - 1) * MOVE):
        taker = plan[at]

        @pl.when(taker >= 0)
        def _():
            place[taker] = slots + at


def second_kernel(
    peers, peers_tp, slots, heads,
    meta, source_s, lengths_s, plan, gain, cos_ref, sin_ref, newkey1, newvalue1,
    wq, wkv, wo, cache_hbm, *rest,
):
    blocks, rest = rest[:peers_tp], rest[peers_tp:]
    box_hbm, rest = rest[: peers - 1], rest[peers - 1 :]
    newkey, newvalue, own = rest[:3]
    sends, rest = rest[3 : 2 + peers_tp], rest[2 + peers_tp :]
    (normed3, spread, cos_rows, sin_rows, buffer, query_rows, attended_rows, place,
     in_sem) = rest
    me, me_tp = meta[0], meta[1]
    low = me * slots
    width = gain.shape[1]
    shard = own.shape[1]
    cache_copies = load_slots(slots, peers, cache_hbm, box_hbm, buffer, in_sem)
    for copy in cache_copies[::-1]:
        copy.start()

    map_places(slots, peers, plan, place)
    firsts = [jnp.bitwise_xor(me_tp, k) for k in range(peers_tp)]
    norm_into(
        normed3,
        [block[...].astype(F32) for block in blocks],
        [gain[:, pl.ds(pl.multiple_of(first * shard, shard), shard)] for first in firsts],
        [first * (shard // HD) for first in firsts],
        width,
    )
    spread_normed(normed3, spread, slots, width)
    lengths = [lengths_s[source_s[low + s]] for s in range(slots)]
    gather_angles(lambda s: lengths[s] + 1, slots, cos_ref, sin_ref, cos_rows, sin_rows)
    query, key, value = project(normed3, spread, wq, wkv, slots, width)
    cosine, sine = cos_rows[...], sin_rows[...]
    query_rows[...] = jnp.zeros(query_rows.shape, F32)
    for g in range(heads):
        turned = turn(query[:, g * HD : (g + 1) * HD], cosine, sine)
        query_rows[pl.ds(g, slots, stride=GROUP), :] = turned.astype(BF16).astype(F32)
    newkey[...] = turn(key, cosine, sine).astype(BF16).astype(F32)
    newvalue[...] = value.astype(BF16).astype(F32)

    for copy in cache_copies[::-1]:
        copy.wait()
    for c in range(slots // CHUNK):
        span = list(range(c * CHUNK, (c + 1) * CHUNK))
        places = [place[s] for s in span]
        for s, at in zip(span, places):
            first = jnp.where(at < slots, lengths[s], -1)
            put_row(buffer, at, first, newkey1[s : s + 1, :], newvalue1[s : s + 1, :])
            put_row(buffer, at, lengths[s] + 1, newkey[s : s + 1, :], newvalue[s : s + 1, :])
        got = attend(
            buffer, places, [lengths[s] + 1 for s in span],
            [query_rows[s * GROUP : (s + 1) * GROUP, :] for s in span],
        )
        for s, rows in zip(span, got):
            attended_rows[s * GROUP : (s + 1) * GROUP, :] = rows
    attended = jnp.concatenate(
        [attended_rows[pl.ds(g, slots, stride=GROUP), :].astype(BF16) for g in range(heads)], axis=1
    )
    project_out(attended, wo, blocks[0][...].astype(F32), own, sends, me_tp, peers_tp)


def cache_kernel(
    peers, slots, meta, source_s, lengths_s, plan, newkey1, newvalue1, newkey2, newvalue2,
    cache_hbm, *rest,
):
    box_hbm, rest = rest[: peers - 1], rest[peers - 1 :]
    out_hbm, buffer, place, in_sem, out_sem = rest
    low = meta[0] * slots
    cache_copies = load_slots(slots, peers, cache_hbm, box_hbm, buffer, in_sem)
    for copy in cache_copies:
        copy.start()
    map_places(slots, peers, plan, place)
    chunks = slots // CHUNK
    for copy in cache_copies[chunks:]:
        copy.wait()
    outs = []
    for c in range(chunks):
        cache_copies[c].wait()
        for s in range(c * CHUNK, (c + 1) * CHUNK):
            at = place[s]
            length = lengths_s[source_s[low + s]]
            first = jnp.where(at < slots, length, -1)
            put_row(buffer, at, first, newkey1[s : s + 1, :], newvalue1[s : s + 1, :])
            put_row(buffer, at, length + 1, newkey2[s : s + 1, :], newvalue2[s : s + 1, :])
            copy = pltpu.make_async_copy(buffer.at[at], out_hbm.at[s], out_sem.at[s])
            copy.start()
            outs.append(copy)
    for copy in outs:
        copy.wait()


def join_kernel(peers_tp, meta, *rest):
    blocks, out, sem = rest[:-2], rest[-2], rest[-1]
    shard = blocks[0].shape[1]
    copies = []
    for k, block in enumerate(blocks):
        column = pl.multiple_of(jnp.bitwise_xor(meta[1], k) * shard, shard)
        copies.append(pltpu.make_async_copy(block, out.at[:, pl.ds(column, shard)], sem.at[k]))
        copies[-1].start()
    for copy in copies:
        copy.wait()


def swapped(x, axis, size, k):
    return lax.ppermute(x, axis, [(i, i ^ k) for i in range(size)])


def local(
    tables, kv_cache, hidden, lengths, source, norm_gain, query_weight, keyval_weight, out_weight
):
    peers, peers_tp = lax.axis_size("inst"), lax.axis_size("tp")
    slots, cap = kv_cache.shape[0], kv_cache.shape[2]
    width = hidden.shape[1]
    heads = query_weight.shape[1] // HD
    shard = width // peers_tp
    others, moving = peers - 1, (peers - 1) * MOVE
    blocks = width // HD
    meta = jnp.stack([lax.axis_index("inst"), lax.axis_index("tp")]).astype(I32)
    gain = norm_gain.reshape(1, width)
    wkv = keyval_weight.reshape(2 * width, HD)
    cosine, sine = (jnp.asarray(table) for table in tables)
    row32 = jax.ShapeDtypeStruct((slots, HD), F32)
    note_width = heads * HD + shard
    dma = pltpu.SemaphoreType.DMA
    weights = [
        pltpu.VMEM(query_weight.shape, BF16),
        pltpu.VMEM(wkv.shape, BF16),
    ]
    stages = [
        pltpu.VMEM((blocks, slots, HD), BF16),
        pltpu.VMEM((blocks, 2 * slots, 2 * HD), BF16),
        pltpu.VMEM((slots, HD), F32),
        pltpu.VMEM((slots, HD), F32),
    ]
    flops = 2 * slots * width * (heads + 2) * HD
    cache_bytes = kv_cache.size * 2

    query, newkey1, newvalue1, plan, *notes = pl.pallas_call(
        functools.partial(first_kernel, peers, slots, heads, shard),
        out_shape=[
            jax.ShapeDtypeStruct((slots * GROUP, HD), F32),
            row32,
            row32,
            jax.ShapeDtypeStruct((2 * moving,), I32),
        ]
        + [jax.ShapeDtypeStruct((MOVE, 2, cap + NOTE, HD), BF16)]
        + [jax.ShapeDtypeStruct((MOVE, note_width), F32)] * (others - 1),
        in_specs=[SMEM] + [HBM] * 9,
        out_specs=[VMEM] * 3 + [SMEM, ANY] + [VMEM] * (others - 1),
        scratch_shapes=weights
        + stages
        + [
            pltpu.VMEM((moving,) + kv_cache.shape[1:], BF16),
            pltpu.VMEM((slots, width), F32),
            pltpu.SMEM((1, source.shape[0]), I32),
            pltpu.SMEM((1, source.shape[0]), I32),
            pltpu.VMEM((1, source.shape[0]), I32),
            pltpu.VMEM(hidden.shape, BF16),
            pltpu.VMEM((1, width), F32),
            pltpu.VMEM(cosine.shape, F32),
            pltpu.VMEM(cosine.shape, F32),
            pltpu.VMEM((MOVE, NOTE, HD), BF16),
            dma((7,)),
            dma((4,)),
            dma((4,)),
            dma((moving,)),
            dma((1 + MOVE,)),
        ],
        compiler_params=params(24),
        cost_estimate=cost(flops, (query_weight.size + wkv.size) * 2),
        name="first_step",
    )(meta, *(
        pltpu.with_memory_space_constraint(x, pltpu.HBM)
        for x in (source.reshape(1, -1), lengths.reshape(1, -1), hidden, gain, cosine, sine,
                  query_weight, wkv, kv_cache)
    ))
    got_notes = [swapped(note, "inst", peers, k + 1) for k, note in enumerate(notes)]

    attended = pl.pallas_call(
        functools.partial(attend_kernel, slots, heads),
        out_shape=jax.ShapeDtypeStruct((slots, heads * HD), BF16),
        in_specs=[SMEM] * 2 + [VMEM] * 3 + [ANY],
        out_specs=VMEM,
        scratch_shapes=[
            pltpu.VMEM(kv_cache.shape, BF16),
            pltpu.VMEM((slots * GROUP, HD), F32),
            dma((slots // CHUNK,)),
        ],
        compiler_params=params(24),
        cost_estimate=cost(4 * slots * cap * HD * heads, cache_bytes),
        name="attention",
    )(meta, lengths, query, newkey1, newvalue1, kv_cache)

    sent = [jax.ShapeDtypeStruct((slots, shard), F32)]
    sent += [jax.ShapeDtypeStruct((slots, shard), BF16)] * (peers_tp - 1)
    own, *rest = pl.pallas_call(
        functools.partial(out_kernel, peers, peers_tp, slots),
        out_shape=sent
        + [jax.ShapeDtypeStruct((MOVE,) + kv_cache.shape[1:], BF16)] * (others - 1),
        in_specs=[SMEM] * 3 + [VMEM] * 5 + [ANY] * 2 + [VMEM] * (others - 1),
        out_specs=[VMEM] * peers_tp + [ANY] * (others - 1),
        scratch_shapes=[
            pltpu.VMEM((moving - MOVE,) + kv_cache.shape[1:], BF16),
            pltpu.VMEM((MOVE, NOTE, HD), BF16),
            dma((1,)),
            dma((moving - MOVE,)),
            dma((others - 1,)),
        ],
        compiler_params=params(20),
        cost_estimate=cost(2 * slots * width * heads * HD, out_weight.size * 2),
        name="out_projection",
    )(meta, lengths, plan, attended, out_weight, hidden, newkey1, newvalue1, got_notes[0], kv_cache,
      *got_notes[1:])
    sends, boxes = rest[: peers_tp - 1], rest[peers_tp - 1 :]
    got_boxes = got_notes[:1] + [swapped(box, "inst", peers, k + 2) for k, box in enumerate(boxes)]

    def summed(own, sends):
        got = [swapped(sends[k - 1], "tp", peers_tp, k) for k in range(peers_tp - 1, 0, -1)]
        shard_rows = pl.pallas_call(
            sum_kernel,
            out_shape=jax.ShapeDtypeStruct((slots, shard), BF16),
            in_specs=[VMEM] * peers_tp,
            out_specs=VMEM,
            compiler_params=params(16),
            name="sum_terms",
        )(own, *got)
        return [shard_rows] + [
            swapped(shard_rows, "tp", peers_tp, k) for k in range(1, peers_tp)
        ]

    pieces = summed(own, sends)

    newkey2, newvalue2, own, *sends = pl.pallas_call(
        functools.partial(second_kernel, peers, peers_tp, slots, heads),
        out_shape=[row32, row32] + sent,
        in_specs=[SMEM] * 4 + [VMEM] * 8 + [ANY] + [VMEM] * peers_tp + [ANY] * others,
        out_specs=[VMEM] * (2 + peers_tp),
        scratch_shapes=stages
        + [
            pltpu.VMEM((slots + moving,) + kv_cache.shape[1:], BF16),
            pltpu.VMEM((slots * GROUP, HD), F32),
            pltpu.VMEM((slots * GROUP, HD), F32),
            pltpu.SMEM((slots,), I32),
            dma((slots // CHUNK + others,)),
        ],
        compiler_params=params(32),
        cost_estimate=cost(3 * flops, cache_bytes + (query_weight.size + wkv.size) * 4),
        name="second_step",
    )(meta, source, lengths, plan, gain, cosine, sine, newkey1, newvalue1, query_weight, wkv,
      out_weight, kv_cache, *pieces, *got_boxes)

    pieces = summed(own, sends)
    final_cache = pl.pallas_call(
        functools.partial(cache_kernel, peers, slots),
        out_shape=jax.ShapeDtypeStruct(kv_cache.shape, BF16),
        in_specs=[SMEM] * 4 + [VMEM] * 4 + [ANY] * peers,
        out_specs=ANY,
        scratch_shapes=[
            pltpu.VMEM((slots + moving,) + kv_cache.shape[1:], BF16),
            pltpu.SMEM((slots,), I32),
            dma((slots // CHUNK + others,)),
            dma((slots,)),
        ],
        compiler_params=params(24),
        cost_estimate=cost(0, 2 * cache_bytes),
        name="write_cache",
    )(meta, source, lengths, plan, newkey1, newvalue1, newkey2, newvalue2, kv_cache, *got_boxes)
    final_hidden = pl.pallas_call(
        functools.partial(join_kernel, peers_tp),
        out_shape=jax.ShapeDtypeStruct(hidden.shape, BF16),
        in_specs=[SMEM] + [ANY] * peers_tp,
        out_specs=ANY,
        scratch_shapes=[dma((peers_tp,))],
        compiler_params=params(16),
        name="join",
    )(meta, *pieces)
    return (final_hidden, final_cache)


def solution(mesh):
    def whole(kv_cache, *rest):
        tables = angle_tables(kv_cache.shape[2])
        return jax.shard_map(
            functools.partial(local, tables),
            mesh=mesh,
            in_specs=(
                P(("groups", "inst"), None, None, "tp"),
                P(("groups", "inst"), None),
                P("groups"),
                P("groups"),
                P(),
                P(None, "tp"),
                P(None, None, "tp"),
                P("tp", None),
            ),
            out_specs=(P(("groups", "inst"), None), P(("groups", "inst"), None, None, "tp")),
            check_vma=False,
        )(kv_cache, *rest)

    return whole
```

```python
import functools

import jax
import jax.numpy as jnp
import numpy as np
from jax import lax
from jax.experimental import pallas as pl
from jax.experimental.pallas import tpu as pltpu
from jax.sharding import PartitionSpec as P

MOVE = 2
EPS = 1e-05
THETA = 500000.0
HD = 128
GROUP = 8
PIECE = 16
CHUNK = 8
NOTE = 16

F32 = jnp.float32
BF16 = jnp.bfloat16
I32 = jnp.int32

ANY = pl.BlockSpec(memory_space=pl.ANY)
VMEM = pl.BlockSpec(memory_space=pltpu.VMEM)
SMEM = pl.BlockSpec(memory_space=pltpu.SMEM)
HBM = pl.BlockSpec(memory_space=pltpu.HBM)


def params(mib):
    return pltpu.CompilerParams(vmem_limit_bytes=mib * 1024 * 1024)


def cost(flops, nbytes):
    return pl.CostEstimate(flops=flops, bytes_accessed=nbytes, transcendentals=0)


def angle_tables(positions):
    frequency = THETA ** (-(np.arange(HD // 2, dtype=np.float64) * 2.0) / HD)
    angles = np.arange(positions, dtype=np.float64)[:, None] * frequency[None, :]
    cosine = np.concatenate([np.cos(angles), np.cos(angles)], axis=-1)
    sine = np.concatenate([-np.sin(angles), np.sin(angles)], axis=-1)
    return cosine.astype(np.float32), sine.astype(np.float32)


def turn(x, cosine, sine):
    return x * cosine + pltpu.roll(x, HD // 2, 1) * sine


def gather_angles(position_of, slots, cos_ref, sin_ref, cos_rows, sin_rows):
    for s in range(slots):
        p = position_of(s)
        cos_rows[s : s + 1, :] = cos_ref[pl.ds(p, 1), :]
        sin_rows[s : s + 1, :] = sin_ref[pl.ds(p, 1), :]


def spread_normed(normed3, spread, slots, width):
    blocks = width // HD
    row = lax.broadcasted_iota(I32, (HD, 4 * HD), 0)
    col = lax.broadcasted_iota(I32, (HD, 4 * HD), 1)
    goal = jnp.where(col < 2 * HD, 2 * row, 2 * row + 1 + 2 * HD)
    places = jnp.where(col == goal, 1.0, 0.0).astype(BF16)
    spread_all = jnp.dot(
        normed3[...].reshape(blocks * slots, HD), places, preferred_element_type=F32
    ).astype(BF16)
    spread[:, 0:slots, :] = spread_all[:, : 2 * HD].reshape(blocks, slots, 2 * HD)
    spread[:, slots:, :] = spread_all[:, 2 * HD :].reshape(blocks, slots, 2 * HD)


def project(normed3, spread, wq, wkv, slots, width, wq_copies=(), wkv_copies=()):
    pieces = max(len(wq_copies), 1)
    depth = width // pieces
    query = None
    pair = None
    for c in range(pieces):
        for copy in wkv_copies[c : c + 1]:
            copy.wait()
        for b in range(c * depth // HD, (c + 1) * depth // HD):
            part = jnp.dot(
                spread[b], wkv[b * 2 * HD : (b + 1) * 2 * HD, :], preferred_element_type=F32
            )
            pair = part if pair is None else pair + part
    for c in range(pieces):
        for copy in wq_copies[c : c + 1]:
            copy.wait()
        for b in range(c * depth // (2 * HD), (c + 1) * depth // (2 * HD)):
            block = jnp.concatenate([normed3[2 * b], normed3[2 * b + 1]], axis=1)
            part = jnp.dot(
                block, wq[b * 2 * HD : (b + 1) * 2 * HD, :], preferred_element_type=F32
            )
            query = part if query is None else query + part
    return query, pair[:slots], pair[slots:]


def weight_copies(src, dst, sem, pieces):
    depth = src.shape[0] // pieces
    copies = [
        pltpu.make_async_copy(
            src.at[pl.ds(c * depth, depth)], dst.at[pl.ds(c * depth, depth)], sem.at[c]
        )
        for c in range(pieces)
    ]
    return copies


def put_row(cache, place, p, key_row, value_row):
    base = pl.multiple_of((jnp.maximum(p, 0) // PIECE) * PIECE, PIECE)
    hit = lax.broadcasted_iota(I32, (PIECE, HD), 0) + base == p
    for which, new in ((0, key_row), (1, value_row)):
        old = cache[place, which, pl.ds(base, PIECE), :].astype(F32)
        cache[place, which, pl.ds(base, PIECE), :] = jnp.where(hit, new, old).astype(BF16)


def attend(cache, places, positions, query_rows):
    cap = cache.shape[2]
    col = lax.broadcasted_iota(I32, (GROUP, cap), 1)
    scores = [
        lax.dot_general(
            rows.astype(BF16),
            cache[place, 0],
            (((1,), (1,)), ((), ())),
            preferred_element_type=F32,
        )
        for place, rows in zip(places, query_rows)
    ]
    probs = []
    for score, p in zip(scores, positions):
        score = jnp.where(col <= p, score * HD**-0.5, -jnp.inf)
        weight = jnp.exp(score - jnp.max(score, axis=-1, keepdims=True))
        weight = weight / jnp.sum(weight, axis=-1, keepdims=True)
        probs.append(weight.astype(BF16))
    return [
        jnp.dot(prob, cache[place, 1], preferred_element_type=F32)
        for place, prob in zip(places, probs)
    ]


def norm_into(normed3, pieces, gains, firsts, total_width):
    square = None
    for piece in pieces:
        part = jnp.sum(piece * piece, axis=-1, keepdims=True)
        square = part if square is None else square + part
    factor = lax.rsqrt(square / total_width + EPS)
    for piece, gain, first in zip(pieces, gains, firsts):
        normed = (piece * factor * gain).astype(BF16)
        for i in range(piece.shape[1] // HD):
            normed3[first + i] = normed[:, i * HD : (i + 1) * HD]


def first_kernel(
    peers, slots, heads, shard,
    meta, source_hbm, lengths_hbm, hidden_hbm, gain_hbm, cos_hbm, sin_hbm, wq_hbm, wkv_hbm,
    cache_hbm, query_out, newkey_out, newvalue_out, plan, *rest,
):
    others = peers - 1
    moving = others * MOVE
    box, notes = rest[0], (None,) + rest[1:others]
    (wq, wkv, normed3, spread, cos_rows, sin_rows, leaving, hidden32, source_s, lengths_s, source_v,
     hidden, gain, cos_ref, sin_ref, tail, small_sem, wq_sem, wkv_sem, in_sem,
     box_sem) = rest[others:]
    width = hidden.shape[1]
    me, me_tp = meta[0], meta[1]
    wq_copies = weight_copies(wq_hbm, wq, wq_sem, 4)
    wkv_copies = weight_copies(wkv_hbm, wkv, wkv_sem, 4)
    small = [
        pltpu.make_async_copy(src, dst, small_sem.at[i])
        for i, (src, dst) in enumerate((
            (source_hbm, source_v), (source_hbm, source_s), (lengths_hbm, lengths_s),
            (hidden_hbm, hidden), (gain_hbm, gain), (cos_hbm, cos_ref), (sin_hbm, sin_ref),
        ))
    ]
    for copy in small + wkv_copies + wq_copies:
        copy.start()
    small[0].wait()
    small[1].wait()

    low = me * slots
    src = source_v[...]
    index = lax.broadcasted_iota(I32, src.shape, 1)
    mine_goes = (src >= low) & (src < low + slots)
    mine_comes = (index >= low) & (index < low + slots)
    index_f = index.astype(F32)
    send_slots = []
    for k in range(1, peers):
        other = jnp.bitwise_xor(me, k) * slots
        sent = mine_goes & (index >= other) & (index < other + slots)
        taken = mine_comes & (src >= other) & (src < other + slots)
        for m in range(MOVE):
            at = (k - 1) * MOVE + m
            if m == 0:
                j = jnp.min(jnp.where(sent, index_f, 1e6)).astype(I32)
                r = jnp.min(jnp.where(taken, index_f, 1e6)).astype(I32)
            else:
                j = jnp.max(jnp.where(sent, index_f, -1.0)).astype(I32)
                r = jnp.max(jnp.where(taken, index_f, -1.0)).astype(I32)
            known = (j >= 0) & (j < src.shape[1])
            slot = source_s[0, jnp.where(known, j, 0)] - low
            slot = jnp.where(known, slot, 0)
            send_slots.append(slot)
            plan[at] = jnp.where((r >= 0) & (r < src.shape[1]), r - low, -1)
            plan[moving + at] = slot
            pltpu.make_async_copy(cache_hbm.at[slot], leaving.at[at], in_sem.at[at]).start()

    for copy in small[2:]:
        copy.wait()
    wide = hidden[...].astype(F32)
    hidden32[...] = wide
    norm_into(normed3, [wide], [gain[...]], [0], width)
    spread_normed(normed3, spread, slots, width)
    gather_angles(lambda s: lengths_s[0, low + s], slots, cos_ref, sin_ref, cos_rows, sin_rows)
    query, key, value = project(
        normed3, spread, wq, wkv, slots, width, wq_copies, wkv_copies
    )
    cosine, sine = cos_rows[...], sin_rows[...]
    query_out[...] = jnp.zeros(query_out.shape, F32)
    for g in range(heads):
        turned = turn(query[:, g * HD : (g + 1) * HD], cosine, sine)
        query_out[pl.ds(g, slots, stride=GROUP), :] = turned.astype(BF16).astype(F32)
    newkey_out[...] = turn(key, cosine, sine).astype(BF16).astype(F32)
    newvalue_out[...] = value.astype(BF16).astype(F32)

    positions = [lengths_s[0, low + slot] for slot in send_slots]
    for at, slot in enumerate(send_slots):
        pltpu.make_async_copy(cache_hbm.at[slot], leaving.at[at], in_sem.at[at]).wait()
        put_row(
            leaving, at, positions[at],
            newkey_out[pl.ds(slot, 1), :], newvalue_out[pl.ds(slot, 1), :],
        )
    cap = leaving.shape[2]
    copies = [
        pltpu.make_async_copy(
            leaving.at[pl.ds(0, MOVE)], box.at[:, :, pl.ds(0, cap), :], box_sem.at[0]
        )
    ]
    copies[0].start()
    rows = [query_out[pl.ds(pl.multiple_of(slot * GROUP, GROUP), GROUP), :] for slot in send_slots]
    attended = attend(leaving, list(range(moving)), positions, rows)
    column = pl.multiple_of(me_tp * shard, shard)
    for at, slot in enumerate(send_slots):
        m = at % MOVE
        residual = hidden32[pl.ds(slot, 1), pl.ds(column, shard)]
        if at < MOVE:
            blocks = [attended[at][g : g + 1, :] for g in range(heads)]
            blocks += [residual[:, b * HD : (b + 1) * HD] for b in range(shard // HD)]
            blocks += [jnp.zeros((1, HD), F32)] * (NOTE - len(blocks))
            tail[m] = jnp.concatenate(blocks, axis=0).astype(BF16)
            copies.append(
                pltpu.make_async_copy(
                    tail.at[m], box.at[m, 0, pl.ds(cap, NOTE), :], box_sem.at[1 + m]
                )
            )
            copies[-1].start()
        else:
            note = notes[at // MOVE]
            for g in range(heads):
                note[m : m + 1, g * HD : (g + 1) * HD] = attended[at][g : g + 1, :]
            note[m : m + 1, heads * HD :] = residual
    for copy in copies:
        copy.wait()


def attend_kernel(
    slots, heads, meta, lengths_s, query, newkey, newvalue, cache_hbm, out,
    buffer, attended_rows, in_sem,
):
    low = meta[0] * slots

    def copy_in(c):
        span = pl.ds(c * CHUNK, CHUNK)
        return pltpu.make_async_copy(cache_hbm.at[span], buffer.at[span], in_sem.at[c])

    for c in range(slots // CHUNK):
        copy_in(c).start()
    for c in range(slots // CHUNK):
        copy_in(c).wait()
        span = list(range(c * CHUNK, (c + 1) * CHUNK))
        positions = [lengths_s[low + s] for s in span]
        for s, p in zip(span, positions):
            put_row(buffer, s, p, newkey[s : s + 1, :], newvalue[s : s + 1, :])
        got = attend(
            buffer, span, positions, [query[s * GROUP : (s + 1) * GROUP, :] for s in span]
        )
        for s, rows in zip(span, got):
            attended_rows[s * GROUP : (s + 1) * GROUP, :] = rows
    for g in range(heads):
        out[:, g * HD : (g + 1) * HD] = attended_rows[pl.ds(g, slots, stride=GROUP), :].astype(BF16)


def project_out(attended, wo, residual, own, sends, me_tp, peers_tp):
    shard = own.shape[1]
    for k in list(range(peers_tp - 1, 0, -1)) + [0]:
        column = pl.multiple_of(jnp.bitwise_xor(me_tp, k) * shard, shard)
        part = jnp.dot(attended, wo[:, pl.ds(column, shard)], preferred_element_type=F32)
        if k == 0:
            own[...] = residual + part
        else:
            sends[k - 1][...] = part.astype(BF16)


def is_odd(meta):
    return lax.rem(meta[0], 2) == 1


def out_kernel(
    peers, peers_tp, slots, meta, lengths_s, plan, attended, wo, hidden, newkey, newvalue, box_hbm,
    cache_hbm, *rest,
):
    notes, rest = rest[: peers - 2], rest[peers - 2 :]
    own, sends, boxes = rest[0], rest[1:peers_tp], rest[peers_tp : peers_tp + peers - 2]
    final_hbm, leaving, tail, sem, in_sem, out_sem, early_sem = rest[peers_tp + peers - 2 :]
    early = [
        pltpu.make_async_copy(
            cache_hbm.at[pl.ds(c * CHUNK, CHUNK)], final_hbm.at[pl.ds(c * CHUNK, CHUNK)],
            early_sem.at[c],
        )
        for c in range(slots // CHUNK)
    ]

    @pl.when(is_odd(meta))
    def _():
        for copy in early:
            copy.start()

    moving = (peers - 1) * MOVE
    send_slots = [plan[moving + at] for at in range(MOVE, moving)]
    packs = [
        pltpu.make_async_copy(cache_hbm.at[slot], leaving.at[i], in_sem.at[i])
        for i, slot in enumerate(send_slots)
    ]
    for pack in packs:
        pack.start()
    shard = own.shape[1]
    cap = box_hbm.shape[2] - NOTE
    copy = pltpu.make_async_copy(box_hbm.at[:, 0, pl.ds(cap, NOTE), :], tail, sem.at[0])
    copy.start()
    rows = attended[...].astype(F32)
    heads = rows.shape[1] // HD
    column = pl.multiple_of(meta[1] * shard, shard)
    residual = hidden[:, pl.ds(column, shard)].astype(F32)
    row_index = lax.broadcasted_iota(I32, rows.shape, 0)
    residual_index = lax.broadcasted_iota(I32, residual.shape, 0)
    copy.wait()
    for at in range((peers - 1) * MOVE):
        m = at % MOVE
        if at < MOVE:
            blocks = tail[m].astype(F32)
            blocks = [blocks[b : b + 1, :] for b in range(heads + shard // HD)]
            note = jnp.concatenate(blocks, axis=1)
        else:
            note = notes[at // MOVE - 1][m : m + 1, :]
        rows = jnp.where(row_index == plan[at], note[:, : heads * HD], rows)
        residual = jnp.where(residual_index == plan[at], note[:, heads * HD :], residual)
    for pack in packs:
        pack.wait()
    for i, slot in enumerate(send_slots):
        put_row(
            leaving, i, lengths_s[meta[0] * slots + slot],
            newkey[pl.ds(slot, 1), :], newvalue[pl.ds(slot, 1), :],
        )
    outs = [
        pltpu.make_async_copy(leaving.at[pl.ds(k * MOVE, MOVE)], out, out_sem.at[k])
        for k, out in enumerate(boxes)
    ]
    for out in outs:
        out.start()

    @pl.when(is_odd(meta))
    def _():
        for copy in early:
            copy.wait()

    project_out(rows.astype(BF16), wo, residual, own, sends, meta[1], peers_tp)
    for out in outs:
        out.wait()


def sum_kernel(own, *rest):
    total = own[...]
    for part in rest[:-1]:
        total = total + part[...].astype(F32)
    rest[-1][...] = total.astype(BF16)


def load_slots(slots, peers, cache_hbm, box_hbm, buffer, in_sem):
    copies = []
    for c in range(slots // CHUNK):
        span = pl.ds(c * CHUNK, CHUNK)
        copies.append(pltpu.make_async_copy(cache_hbm.at[span], buffer.at[span], in_sem.at[c]))
    for k in range(peers - 1):
        copies.append(
            pltpu.make_async_copy(
                box_hbm[k].at[:, :, pl.ds(0, cache_hbm.shape[2]), :],
                buffer.at[pl.ds(slots + k * MOVE, MOVE)],
                in_sem.at[slots // CHUNK + k],
            )
        )
    return copies


def map_places(slots, peers, plan, place):
    for s in range(slots):
        place[s] = s
    for at in range((peers - 1) * MOVE):
        taker = plan[at]

        @pl.when(taker >= 0)
        def _():
            place[taker] = slots + at


def second_kernel(
    peers, peers_tp, slots, heads,
    meta, source_s, lengths_s, plan, gain, cos_ref, sin_ref, newkey1, newvalue1,
    wq, wkv, wo, cache_hbm, *rest,
):
    blocks, rest = rest[:peers_tp], rest[peers_tp:]
    box_hbm, rest = rest[: peers - 1], rest[peers - 1 :]
    newkey, newvalue, own = rest[:3]
    sends, rest = rest[3 : 2 + peers_tp], rest[2 + peers_tp :]
    (normed3, spread, cos_rows, sin_rows, buffer, query_rows, attended_rows, place,
     in_sem) = rest
    me, me_tp = meta[0], meta[1]
    low = me * slots
    width = gain.shape[1]
    shard = own.shape[1]
    cache_copies = load_slots(slots, peers, cache_hbm, box_hbm, buffer, in_sem)
    for copy in cache_copies[::-1]:
        copy.start()

    map_places(slots, peers, plan, place)
    firsts = [jnp.bitwise_xor(me_tp, k) for k in range(peers_tp)]
    norm_into(
        normed3,
        [block[...].astype(F32) for block in blocks],
        [gain[:, pl.ds(pl.multiple_of(first * shard, shard), shard)] for first in firsts],
        [first * (shard // HD) for first in firsts],
        width,
    )
    spread_normed(normed3, spread, slots, width)
    lengths = [lengths_s[source_s[low + s]] for s in range(slots)]
    gather_angles(lambda s: lengths[s] + 1, slots, cos_ref, sin_ref, cos_rows, sin_rows)
    query, key, value = project(normed3, spread, wq, wkv, slots, width)
    cosine, sine = cos_rows[...], sin_rows[...]
    query_rows[...] = jnp.zeros(query_rows.shape, F32)
    for g in range(heads):
        turned = turn(query[:, g * HD : (g + 1) * HD], cosine, sine)
        query_rows[pl.ds(g, slots, stride=GROUP), :] = turned.astype(BF16).astype(F32)
    newkey[...] = turn(key, cosine, sine).astype(BF16).astype(F32)
    newvalue[...] = value.astype(BF16).astype(F32)

    for copy in cache_copies[::-1]:
        copy.wait()
    for c in range(slots // CHUNK):
        span = list(range(c * CHUNK, (c + 1) * CHUNK))
        places = [place[s] for s in span]
        for s, at in zip(span, places):
            first = jnp.where(at < slots, lengths[s], -1)
            put_row(buffer, at, first, newkey1[s : s + 1, :], newvalue1[s : s + 1, :])
            put_row(buffer, at, lengths[s] + 1, newkey[s : s + 1, :], newvalue[s : s + 1, :])
        got = attend(
            buffer, places, [lengths[s] + 1 for s in span],
            [query_rows[s * GROUP : (s + 1) * GROUP, :] for s in span],
        )
        for s, rows in zip(span, got):
            attended_rows[s * GROUP : (s + 1) * GROUP, :] = rows
    attended = jnp.concatenate(
        [attended_rows[pl.ds(g, slots, stride=GROUP), :].astype(BF16) for g in range(heads)], axis=1
    )
    project_out(attended, wo, blocks[0][...].astype(F32), own, sends, me_tp, peers_tp)


def cache_kernel(
    peers, slots, meta, source_s, lengths_s, plan, newkey1, newvalue1, newkey2, newvalue2,
    cache_hbm, *rest,
):
    box_hbm, rest = rest[: peers - 1], rest[peers - 1 :]
    _, out_hbm, buffer, place, in_sem, out_sem = rest
    low = meta[0] * slots
    cap = cache_hbm.shape[2]
    odd = is_odd(meta)
    cache_copies = load_slots(slots, peers, cache_hbm, box_hbm, buffer, in_sem)
    for copy in cache_copies:
        copy.start()
    map_places(slots, peers, plan, place)
    chunks = slots // CHUNK
    for copy in cache_copies[chunks:]:
        copy.wait()
    outs = []
    for c in range(chunks):
        cache_copies[c].wait()
        for s in range(c * CHUNK, (c + 1) * CHUNK):
            at = place[s]
            length = lengths_s[source_s[low + s]]
            kept = at < slots
            first = jnp.where(kept, length, -1)
            put_row(buffer, at, first, newkey1[s : s + 1, :], newvalue1[s : s + 1, :])
            put_row(buffer, at, length + 1, newkey2[s : s + 1, :], newvalue2[s : s + 1, :])
            base = pl.multiple_of(jnp.minimum((length // PIECE) * PIECE, cap - 2 * PIECE), PIECE)
            window = (slice(None), pl.ds(base, 2 * PIECE), slice(None))
            whole = pltpu.make_async_copy(buffer.at[at], out_hbm.at[s], out_sem.at[s])
            part = pltpu.make_async_copy(
                buffer.at[at].at[window], out_hbm.at[s].at[window], out_sem.at[s]
            )
            copied = odd & kept
            outs.append((copied, whole, part))
            pl.when(copied)(part.start)
            pl.when(jnp.logical_not(copied))(whole.start)
    for copied, whole, part in outs:
        pl.when(copied)(part.wait)
        pl.when(jnp.logical_not(copied))(whole.wait)


def join_kernel(peers_tp, meta, *rest):
    blocks, out, sem = rest[:-2], rest[-2], rest[-1]
    shard = blocks[0].shape[1]
    copies = []
    for k, block in enumerate(blocks):
        column = pl.multiple_of(jnp.bitwise_xor(meta[1], k) * shard, shard)
        copies.append(pltpu.make_async_copy(block, out.at[:, pl.ds(column, shard)], sem.at[k]))
        copies[-1].start()
    for copy in copies:
        copy.wait()


def swapped(x, axis, size, k):
    return lax.ppermute(x, axis, [(i, i ^ k) for i in range(size)])


def local(
    tables, kv_cache, hidden, lengths, source, norm_gain, query_weight, keyval_weight, out_weight
):
    peers, peers_tp = lax.axis_size("inst"), lax.axis_size("tp")
    slots, cap = kv_cache.shape[0], kv_cache.shape[2]
    width = hidden.shape[1]
    heads = query_weight.shape[1] // HD
    shard = width // peers_tp
    others, moving = peers - 1, (peers - 1) * MOVE
    blocks = width // HD
    meta = jnp.stack([lax.axis_index("inst"), lax.axis_index("tp")]).astype(I32)
    gain = norm_gain.reshape(1, width)
    wkv = keyval_weight.reshape(2 * width, HD)
    cosine, sine = (jnp.asarray(table) for table in tables)
    row32 = jax.ShapeDtypeStruct((slots, HD), F32)
    note_width = heads * HD + shard
    dma = pltpu.SemaphoreType.DMA
    weights = [
        pltpu.VMEM(query_weight.shape, BF16),
        pltpu.VMEM(wkv.shape, BF16),
    ]
    stages = [
        pltpu.VMEM((blocks, slots, HD), BF16),
        pltpu.VMEM((blocks, 2 * slots, 2 * HD), BF16),
        pltpu.VMEM((slots, HD), F32),
        pltpu.VMEM((slots, HD), F32),
    ]
    flops = 2 * slots * width * (heads + 2) * HD
    cache_bytes = kv_cache.size * 2

    query, newkey1, newvalue1, plan, *notes = pl.pallas_call(
        functools.partial(first_kernel, peers, slots, heads, shard),
        out_shape=[
            jax.ShapeDtypeStruct((slots * GROUP, HD), F32),
            row32,
            row32,
            jax.ShapeDtypeStruct((2 * moving,), I32),
        ]
        + [jax.ShapeDtypeStruct((MOVE, 2, cap + NOTE, HD), BF16)]
        + [jax.ShapeDtypeStruct((MOVE, note_width), F32)] * (others - 1),
        in_specs=[SMEM] + [HBM] * 9,
        out_specs=[VMEM] * 3 + [SMEM, ANY] + [VMEM] * (others - 1),
        scratch_shapes=weights
        + stages
        + [
            pltpu.VMEM((moving,) + kv_cache.shape[1:], BF16),
            pltpu.VMEM((slots, width), F32),
            pltpu.SMEM((1, source.shape[0]), I32),
            pltpu.SMEM((1, source.shape[0]), I32),
            pltpu.VMEM((1, source.shape[0]), I32),
            pltpu.VMEM(hidden.shape, BF16),
            pltpu.VMEM((1, width), F32),
            pltpu.VMEM(cosine.shape, F32),
            pltpu.VMEM(cosine.shape, F32),
            pltpu.VMEM((MOVE, NOTE, HD), BF16),
            dma((7,)),
            dma((4,)),
            dma((4,)),
            dma((moving,)),
            dma((1 + MOVE,)),
        ],
        compiler_params=params(24),
        cost_estimate=cost(flops, (query_weight.size + wkv.size) * 2),
        name="first_step",
    )(meta, *(
        pltpu.with_memory_space_constraint(x, pltpu.HBM)
        for x in (source.reshape(1, -1), lengths.reshape(1, -1), hidden, gain, cosine, sine,
                  query_weight, wkv, kv_cache)
    ))
    got_notes = [swapped(note, "inst", peers, k + 1) for k, note in enumerate(notes)]

    attended = pl.pallas_call(
        functools.partial(attend_kernel, slots, heads),
        out_shape=jax.ShapeDtypeStruct((slots, heads * HD), BF16),
        in_specs=[SMEM] * 2 + [VMEM] * 3 + [ANY],
        out_specs=VMEM,
        scratch_shapes=[
            pltpu.VMEM(kv_cache.shape, BF16),
            pltpu.VMEM((slots * GROUP, HD), F32),
            dma((slots // CHUNK,)),
        ],
        compiler_params=params(24),
        cost_estimate=cost(4 * slots * cap * HD * heads, cache_bytes),
        name="attention",
    )(meta, lengths, query, newkey1, newvalue1, kv_cache)

    sent = [jax.ShapeDtypeStruct((slots, shard), F32)]
    sent += [jax.ShapeDtypeStruct((slots, shard), BF16)] * (peers_tp - 1)
    own, *rest = pl.pallas_call(
        functools.partial(out_kernel, peers, peers_tp, slots),
        out_shape=sent
        + [jax.ShapeDtypeStruct((MOVE,) + kv_cache.shape[1:], BF16)] * (others - 1)
        + [pltpu.HBM(kv_cache.shape, BF16)],
        in_specs=[SMEM] * 3 + [VMEM] * 5 + [ANY] * 2 + [VMEM] * (others - 1),
        out_specs=[VMEM] * peers_tp + [ANY] * (others - 1) + [HBM],
        scratch_shapes=[
            pltpu.VMEM((moving - MOVE,) + kv_cache.shape[1:], BF16),
            pltpu.VMEM((MOVE, NOTE, HD), BF16),
            dma((1,)),
            dma((moving - MOVE,)),
            dma((others - 1,)),
            dma((slots // CHUNK,)),
        ],
        compiler_params=params(20),
        cost_estimate=cost(2 * slots * width * heads * HD, out_weight.size * 2),
        name="out_projection",
    )(meta, lengths, plan, attended, out_weight, hidden, newkey1, newvalue1, got_notes[0], kv_cache,
      *got_notes[1:])
    sends, boxes, final_cache = rest[: peers_tp - 1], rest[peers_tp - 1 : -1], rest[-1]
    got_boxes = got_notes[:1] + [swapped(box, "inst", peers, k + 2) for k, box in enumerate(boxes)]

    def summed(own, sends):
        got = [swapped(sends[k - 1], "tp", peers_tp, k) for k in range(peers_tp - 1, 0, -1)]
        shard_rows = pl.pallas_call(
            sum_kernel,
            out_shape=jax.ShapeDtypeStruct((slots, shard), BF16),
            in_specs=[VMEM] * peers_tp,
            out_specs=VMEM,
            compiler_params=params(16),
            name="sum_terms",
        )(own, *got)
        return [shard_rows] + [
            swapped(shard_rows, "tp", peers_tp, k) for k in range(1, peers_tp)
        ]

    pieces = summed(own, sends)

    newkey2, newvalue2, own, *sends = pl.pallas_call(
        functools.partial(second_kernel, peers, peers_tp, slots, heads),
        out_shape=[row32, row32] + sent,
        in_specs=[SMEM] * 4 + [VMEM] * 8 + [ANY] + [VMEM] * peers_tp + [ANY] * others,
        out_specs=[VMEM] * (2 + peers_tp),
        scratch_shapes=stages
        + [
            pltpu.VMEM((slots + moving,) + kv_cache.shape[1:], BF16),
            pltpu.VMEM((slots * GROUP, HD), F32),
            pltpu.VMEM((slots * GROUP, HD), F32),
            pltpu.SMEM((slots,), I32),
            dma((slots // CHUNK + others,)),
        ],
        compiler_params=params(32),
        cost_estimate=cost(3 * flops, cache_bytes + (query_weight.size + wkv.size) * 4),
        name="second_step",
    )(meta, source, lengths, plan, gain, cosine, sine, newkey1, newvalue1, query_weight, wkv,
      out_weight, kv_cache, *pieces, *got_boxes)

    pieces = summed(own, sends)
    final_cache = pl.pallas_call(
        functools.partial(cache_kernel, peers, slots),
        out_shape=jax.ShapeDtypeStruct(kv_cache.shape, BF16),
        in_specs=[SMEM] * 4 + [VMEM] * 4 + [ANY] * peers + [HBM],
        out_specs=HBM,
        input_output_aliases={8 + peers: 0},
        scratch_shapes=[
            pltpu.VMEM((slots + moving,) + kv_cache.shape[1:], BF16),
            pltpu.SMEM((slots,), I32),
            dma((slots // CHUNK + others,)),
            dma((slots,)),
        ],
        compiler_params=params(24),
        cost_estimate=cost(0, 2 * cache_bytes),
        name="write_cache",
    )(meta, source, lengths, plan, newkey1, newvalue1, newkey2, newvalue2, kv_cache, *got_boxes,
      final_cache)
    final_hidden = pl.pallas_call(
        functools.partial(join_kernel, peers_tp),
        out_shape=jax.ShapeDtypeStruct(hidden.shape, BF16),
        in_specs=[SMEM] + [ANY] * peers_tp,
        out_specs=ANY,
        scratch_shapes=[dma((peers_tp,))],
        compiler_params=params(16),
        name="join",
    )(meta, *pieces)
    return (final_hidden, final_cache)


def solution(mesh):
    def whole(kv_cache, *rest):
        tables = angle_tables(kv_cache.shape[2])
        return jax.shard_map(
            functools.partial(local, tables),
            mesh=mesh,
            in_specs=(
                P(("groups", "inst"), None, None, "tp"),
                P(("groups", "inst"), None),
                P("groups"),
                P("groups"),
                P(),
                P(None, "tp"),
                P(None, None, "tp"),
                P("tp", None),
            ),
            out_specs=(P(("groups", "inst"), None), P(("groups", "inst"), None, None, "tp")),
            check_vma=False,
        )(kv_cache, *rest)

    return whole
```

```python
import functools

import jax
import jax.numpy as jnp
import numpy as np
from jax import lax
from jax.experimental import pallas as pl
from jax.experimental.pallas import tpu as pltpu
from jax.sharding import PartitionSpec as P

MOVE = 2
EPS = 1e-05
THETA = 500000.0
HD = 128
GROUP = 8
PIECE = 16
CHUNK = 8

F32 = jnp.float32
BF16 = jnp.bfloat16
I32 = jnp.int32

ANY = pl.BlockSpec(memory_space=pl.ANY)
VMEM = pl.BlockSpec(memory_space=pltpu.VMEM)
SMEM = pl.BlockSpec(memory_space=pltpu.SMEM)
HBM = pl.BlockSpec(memory_space=pltpu.HBM)


def params(mib):
    return pltpu.CompilerParams(vmem_limit_bytes=mib * 1024 * 1024)


def cost(flops, nbytes):
    return pl.CostEstimate(flops=flops, bytes_accessed=nbytes, transcendentals=0)


def angle_tables(positions):
    frequency = THETA ** (-(np.arange(HD // 2, dtype=np.float64) * 2.0) / HD)
    angles = np.arange(positions, dtype=np.float64)[:, None] * frequency[None, :]
    cosine = np.concatenate([np.cos(angles), np.cos(angles)], axis=-1)
    sine = np.concatenate([-np.sin(angles), np.sin(angles)], axis=-1)
    return np.stack([cosine, sine]).astype(np.float32)


def turn(x, cosine, sine):
    return x * cosine + pltpu.roll(x, HD // 2, 1) * sine


def gather_angles(position_of, slots, table, cos_rows, sin_rows):
    for s in range(slots):
        p = position_of(s)
        cos_rows[s : s + 1, :] = table[0, pl.ds(p, 1), :]
        sin_rows[s : s + 1, :] = table[1, pl.ds(p, 1), :]


def spread_normed(normed3, spread, slots, width):
    blocks = width // HD
    row = lax.broadcasted_iota(I32, (HD, 4 * HD), 0)
    col = lax.broadcasted_iota(I32, (HD, 4 * HD), 1)
    goal = jnp.where(col < 2 * HD, 2 * row, 2 * row + 1 + 2 * HD)
    places = jnp.where(col == goal, 1.0, 0.0).astype(BF16)
    spread_all = jnp.dot(
        normed3[...].reshape(blocks * slots, HD), places, preferred_element_type=F32
    ).astype(BF16)
    spread[:, 0:slots, :] = spread_all[:, : 2 * HD].reshape(blocks, slots, 2 * HD)
    spread[:, slots:, :] = spread_all[:, 2 * HD :].reshape(blocks, slots, 2 * HD)


def project(normed3, spread, wq, wkv, slots, width):
    query = None
    pair = None
    for b in range(width // HD):
        part = jnp.dot(
            spread[b], wkv[b * 2 * HD : (b + 1) * 2 * HD, :], preferred_element_type=F32
        )
        pair = part if pair is None else pair + part
    for b in range(width // (2 * HD)):
        block = jnp.concatenate([normed3[2 * b], normed3[2 * b + 1]], axis=1)
        part = jnp.dot(block, wq[b * 2 * HD : (b + 1) * 2 * HD, :], preferred_element_type=F32)
        query = part if query is None else query + part
    return query, pair[:slots], pair[slots:]


def put_row(cache, place, p, key_row, value_row):
    base = pl.multiple_of((jnp.maximum(p, 0) // PIECE) * PIECE, PIECE)
    hit = lax.broadcasted_iota(I32, (PIECE, HD), 0) + base == p
    for which, new in ((0, key_row), (1, value_row)):
        old = cache[place, which, pl.ds(base, PIECE), :].astype(F32)
        cache[place, which, pl.ds(base, PIECE), :] = jnp.where(hit, new, old).astype(BF16)


def attend(cache, places, positions, query_rows):
    cap = cache.shape[2]
    col = lax.broadcasted_iota(I32, (GROUP, cap), 1)
    scores = [
        lax.dot_general(
            rows.astype(BF16),
            cache[place, 0],
            (((1,), (1,)), ((), ())),
            preferred_element_type=F32,
        )
        for place, rows in zip(places, query_rows)
    ]
    probs = []
    for score, p in zip(scores, positions):
        score = jnp.where(col <= p, score * HD**-0.5, -jnp.inf)
        weight = jnp.exp(score - jnp.max(score, axis=-1, keepdims=True))
        weight = weight / jnp.sum(weight, axis=-1, keepdims=True)
        probs.append(weight.astype(BF16))
    return [
        jnp.dot(prob, cache[place, 1], preferred_element_type=F32)
        for place, prob in zip(places, probs)
    ]


def norm_into(normed3, pieces, gains, firsts, total_width):
    square = None
    for piece in pieces:
        part = jnp.sum(piece * piece, axis=-1, keepdims=True)
        square = part if square is None else square + part
    factor = lax.rsqrt(square / total_width + EPS)
    for piece, gain, first in zip(pieces, gains, firsts):
        normed = (piece * factor * gain).astype(BF16)
        for i in range(piece.shape[1] // HD):
            normed3[first + i] = normed[:, i * HD : (i + 1) * HD]


def pack_kernel(
    peers, slots, meta, source_hbm, lengths_hbm, gain_hbm, table_hbm, hidden_hbm, cache_hbm,
    plan, lengths_out, gain_out, table_out, hidden_out, *rest,
):
    moving = (peers - 1) * MOVE
    boxes, (source_s, source_v, leaving, small_sem, in_sem, out_sem) = rest[:-6], rest[-6:]
    pairs = [
        (source_hbm, source_v), (source_hbm, source_s), (lengths_hbm, lengths_out),
        (gain_hbm, gain_out), (table_hbm, table_out), (hidden_hbm, hidden_out),
    ]
    small = [
        pltpu.make_async_copy(src, dst, small_sem.at[i]) for i, (src, dst) in enumerate(pairs)
    ]
    for copy in small:
        copy.start()
    for copy in small[:2]:
        copy.wait()
    low = meta[0] * slots
    src = source_v[...]
    index = lax.broadcasted_iota(I32, src.shape, 1)
    mine_goes = (src >= low) & (src < low + slots)
    mine_comes = (index >= low) & (index < low + slots)
    index_f = index.astype(F32)
    copies = []
    for k in range(1, peers):
        other = jnp.bitwise_xor(meta[0], k) * slots
        sent = mine_goes & (index >= other) & (index < other + slots)
        taken = mine_comes & (src >= other) & (src < other + slots)
        for m in range(MOVE):
            at = (k - 1) * MOVE + m
            if m == 0:
                j = jnp.min(jnp.where(sent, index_f, 1e6)).astype(I32)
                r = jnp.min(jnp.where(taken, index_f, 1e6)).astype(I32)
            else:
                j = jnp.max(jnp.where(sent, index_f, -1.0)).astype(I32)
                r = jnp.max(jnp.where(taken, index_f, -1.0)).astype(I32)
            known = (j >= 0) & (j < src.shape[1])
            slot = source_s[0, jnp.where(known, j, 0)] - low
            slot = jnp.where(known, slot, 0)
            plan[at] = jnp.where((r >= 0) & (r < src.shape[1]), r - low, -1)
            plan[moving + at] = slot
            copies.append(
                pltpu.make_async_copy(cache_hbm.at[slot], leaving.at[at], in_sem.at[at])
            )
            copies[-1].start()
    for copy in copies:
        copy.wait()
    outs = []
    for i, box in enumerate(boxes):
        outs.append(pltpu.make_async_copy(leaving.at[pl.ds(i * MOVE, MOVE)], box, out_sem.at[i]))
        outs[-1].start()
    for copy in outs + small[2:]:
        copy.wait()


def first_kernel(
    peers, slots, heads, shard,
    meta, lengths_s, plan, hidden, gain, table, wq, wkv, cache_hbm, _box,
    query_out, newkey_out, newvalue_out, *rest,
):
    others = peers - 1
    moving = others * MOVE
    notes = rest[:others]
    normed3, spread, cos_rows, sin_rows, leaving, hidden32, in_sem = rest[others:]
    width = hidden.shape[1]
    low = meta[0] * slots
    send_slots = [plan[moving + at] for at in range(moving)]
    copies = [
        pltpu.make_async_copy(cache_hbm.at[slot], leaving.at[at], in_sem.at[at])
        for at, slot in enumerate(send_slots)
    ]
    for copy in copies:
        copy.start()
    wide = hidden[...].astype(F32)
    hidden32[...] = wide
    norm_into(normed3, [wide], [gain[...]], [0], width)
    spread_normed(normed3, spread, slots, width)
    gather_angles(lambda s: lengths_s[0, low + s], slots, table, cos_rows, sin_rows)
    query, key, value = project(normed3, spread, wq, wkv, slots, width)
    cosine, sine = cos_rows[...], sin_rows[...]
    query_out[...] = jnp.zeros(query_out.shape, F32)
    for g in range(heads):
        turned = turn(query[:, g * HD : (g + 1) * HD], cosine, sine)
        query_out[pl.ds(g, slots, stride=GROUP), :] = turned.astype(BF16).astype(F32)
    newkey_out[...] = turn(key, cosine, sine).astype(BF16).astype(F32)
    newvalue_out[...] = value.astype(BF16).astype(F32)

    for copy in copies:
        copy.wait()
    positions = [lengths_s[0, low + slot] for slot in send_slots]
    column = pl.multiple_of(meta[1] * shard, shard)
    for at, slot in enumerate(send_slots):
        key_row, value_row = newkey_out[pl.ds(slot, 1), :], newvalue_out[pl.ds(slot, 1), :]
        put_row(leaving, at, positions[at], key_row, value_row)
        note, m = notes[at // MOVE], at % MOVE
        note[m : m + 1, heads * HD : (heads + 1) * HD] = key_row
        note[m : m + 1, (heads + 1) * HD : (heads + 2) * HD] = value_row
        note[m : m + 1, (heads + 2) * HD :] = hidden32[pl.ds(slot, 1), pl.ds(column, shard)]
    rows = [query_out[pl.ds(pl.multiple_of(slot * GROUP, GROUP), GROUP), :] for slot in send_slots]
    attended = attend(leaving, list(range(moving)), positions, rows)
    for at, got in enumerate(attended):
        note, m = notes[at // MOVE], at % MOVE
        for g in range(heads):
            note[m : m + 1, g * HD : (g + 1) * HD] = got[g : g + 1, :]


def attend_kernel(
    slots, heads, meta, lengths_s, query, newkey, newvalue, cache_hbm, out,
    buffer, attended_rows, in_sem,
):
    low = meta[0] * slots

    def copy_in(c):
        span = pl.ds(c * CHUNK, CHUNK)
        return pltpu.make_async_copy(cache_hbm.at[span], buffer.at[span], in_sem.at[c])

    for c in range(slots // CHUNK):
        copy_in(c).start()
    for c in range(slots // CHUNK):
        copy_in(c).wait()
        span = list(range(c * CHUNK, (c + 1) * CHUNK))
        positions = [lengths_s[0, low + s] for s in span]
        for s, p in zip(span, positions):
            put_row(buffer, s, p, newkey[s : s + 1, :], newvalue[s : s + 1, :])
        got = attend(
            buffer, span, positions, [query[s * GROUP : (s + 1) * GROUP, :] for s in span]
        )
        for s, rows in zip(span, got):
            attended_rows[s * GROUP : (s + 1) * GROUP, :] = rows
    for g in range(heads):
        out[:, g * HD : (g + 1) * HD] = attended_rows[pl.ds(g, slots, stride=GROUP), :].astype(BF16)


def project_out(attended, wo, residual, own, sends, me_tp, peers_tp):
    shard = own.shape[1]
    for k in list(range(peers_tp - 1, 0, -1)) + [0]:
        column = pl.multiple_of(jnp.bitwise_xor(me_tp, k) * shard, shard)
        part = jnp.dot(attended, wo[:, pl.ds(column, shard)], preferred_element_type=F32)
        if k == 0:
            own[...] = residual + part
        else:
            sends[k - 1][...] = part.astype(BF16)


def is_odd(meta):
    return lax.rem(meta[0], 2) == 1


def out_kernel(
    peers, peers_tp, slots, meta, plan, attended, wo, hidden, newkey, newvalue, cache_hbm, *rest,
):
    notes, rest = rest[: peers - 1], rest[peers - 1 :]
    own, sends, (newkey_out, newvalue_out, final_hbm, early_sem) = (
        rest[0], rest[1:peers_tp], rest[peers_tp:]
    )
    early = [
        pltpu.make_async_copy(
            cache_hbm.at[pl.ds(c * CHUNK, CHUNK)], final_hbm.at[pl.ds(c * CHUNK, CHUNK)],
            early_sem.at[c],
        )
        for c in range(slots // CHUNK)
    ]

    @pl.when(is_odd(meta))
    def _():
        for copy in early:
            copy.start()

    shard = own.shape[1]
    column = pl.multiple_of(meta[1] * shard, shard)
    width = attended.shape[1]
    parts = [
        attended[...].astype(F32), newkey[...], newvalue[...],
        hidden[:, pl.ds(column, shard)].astype(F32),
    ]
    firsts = [0, width, width + HD, width + 2 * HD, width + 2 * HD + shard]
    for at in range((peers - 1) * MOVE):
        m = at % MOVE
        note = notes[at // MOVE][m : m + 1, :]
        for i, part in enumerate(parts):
            hit = lax.broadcasted_iota(I32, part.shape, 0) == plan[at]
            parts[i] = jnp.where(hit, note[:, firsts[i] : firsts[i + 1]], part)
    rows, newkey_out[...], newvalue_out[...], residual = parts

    @pl.when(is_odd(meta))
    def _():
        for copy in early:
            copy.wait()

    project_out(rows.astype(BF16), wo, residual, own, sends, meta[1], peers_tp)


def sum_kernel(own, *rest):
    total = own[...]
    for part in rest[:-1]:
        total = total + part[...].astype(F32)
    rest[-1][...] = total.astype(BF16)


def load_slots(slots, peers, cache_hbm, boxes, buffer, in_sem):
    copies = []
    for c in range(slots // CHUNK):
        span = pl.ds(c * CHUNK, CHUNK)
        copies.append(pltpu.make_async_copy(cache_hbm.at[span], buffer.at[span], in_sem.at[c]))
    for k, box in enumerate(boxes):
        copies.append(
            pltpu.make_async_copy(
                box,
                buffer.at[pl.ds(slots + k * MOVE, MOVE)],
                in_sem.at[slots // CHUNK + k],
            )
        )
    return copies


def map_places(slots, peers, plan, place):
    for s in range(slots):
        place[s] = s
    for at in range((peers - 1) * MOVE):
        taker = plan[at]

        @pl.when(taker >= 0)
        def _():
            place[taker] = slots + at


def second_kernel(
    peers, peers_tp, slots, heads,
    meta, source_s, lengths_s, plan, gain, table, newkey1, newvalue1,
    wq, wkv, wo, cache_hbm, *rest,
):
    blocks, rest = rest[:peers_tp], rest[peers_tp:]
    box_hbm, rest = rest[: peers - 1], rest[peers - 1 :]
    newkey, newvalue, own = rest[:3]
    sends, rest = rest[3 : 2 + peers_tp], rest[2 + peers_tp :]
    (normed3, spread, cos_rows, sin_rows, buffer, query_rows, attended_rows, place,
     in_sem) = rest
    me, me_tp = meta[0], meta[1]
    low = me * slots
    width = gain.shape[1]
    shard = own.shape[1]
    cache_copies = load_slots(slots, peers, cache_hbm, box_hbm, buffer, in_sem)
    for copy in cache_copies[::-1]:
        copy.start()

    map_places(slots, peers, plan, place)
    firsts = [jnp.bitwise_xor(me_tp, k) for k in range(peers_tp)]
    norm_into(
        normed3,
        [block[...].astype(F32) for block in blocks],
        [gain[:, pl.ds(pl.multiple_of(first * shard, shard), shard)] for first in firsts],
        [first * (shard // HD) for first in firsts],
        width,
    )
    spread_normed(normed3, spread, slots, width)
    lengths = [lengths_s[0, source_s[low + s]] for s in range(slots)]
    gather_angles(lambda s: lengths[s] + 1, slots, table, cos_rows, sin_rows)
    query, key, value = project(normed3, spread, wq, wkv, slots, width)
    cosine, sine = cos_rows[...], sin_rows[...]
    query_rows[...] = jnp.zeros(query_rows.shape, F32)
    for g in range(heads):
        turned = turn(query[:, g * HD : (g + 1) * HD], cosine, sine)
        query_rows[pl.ds(g, slots, stride=GROUP), :] = turned.astype(BF16).astype(F32)
    newkey[...] = turn(key, cosine, sine).astype(BF16).astype(F32)
    newvalue[...] = value.astype(BF16).astype(F32)

    for copy in cache_copies[::-1]:
        copy.wait()
    for c in range(slots // CHUNK):
        span = list(range(c * CHUNK, (c + 1) * CHUNK))
        places = [place[s] for s in span]
        for s, at in zip(span, places):
            put_row(buffer, at, lengths[s], newkey1[s : s + 1, :], newvalue1[s : s + 1, :])
            put_row(buffer, at, lengths[s] + 1, newkey[s : s + 1, :], newvalue[s : s + 1, :])
        got = attend(
            buffer, places, [lengths[s] + 1 for s in span],
            [query_rows[s * GROUP : (s + 1) * GROUP, :] for s in span],
        )
        for s, rows in zip(span, got):
            attended_rows[s * GROUP : (s + 1) * GROUP, :] = rows
    attended = jnp.concatenate(
        [attended_rows[pl.ds(g, slots, stride=GROUP), :].astype(BF16) for g in range(heads)], axis=1
    )
    project_out(attended, wo, blocks[0][...].astype(F32), own, sends, me_tp, peers_tp)


def cache_kernel(
    peers, slots, meta, source_s, lengths_s, plan, newkey1, newvalue1, newkey2, newvalue2,
    cache_hbm, *rest,
):
    box_hbm, rest = rest[: peers - 1], rest[peers - 1 :]
    _, out_hbm, buffer, place, in_sem, out_sem = rest
    low = meta[0] * slots
    cap = cache_hbm.shape[2]
    odd = is_odd(meta)
    cache_copies = load_slots(slots, peers, cache_hbm, box_hbm, buffer, in_sem)
    for copy in cache_copies:
        copy.start()
    map_places(slots, peers, plan, place)
    chunks = slots // CHUNK
    for copy in cache_copies[chunks:]:
        copy.wait()
    outs = []
    for c in range(chunks):
        cache_copies[c].wait()
        for s in range(c * CHUNK, (c + 1) * CHUNK):
            at = place[s]
            length = lengths_s[0, source_s[low + s]]
            kept = at < slots
            put_row(buffer, at, length, newkey1[s : s + 1, :], newvalue1[s : s + 1, :])
            put_row(buffer, at, length + 1, newkey2[s : s + 1, :], newvalue2[s : s + 1, :])
            base = pl.multiple_of(jnp.minimum((length // PIECE) * PIECE, cap - 2 * PIECE), PIECE)
            window = (slice(None), pl.ds(base, 2 * PIECE), slice(None))
            whole = pltpu.make_async_copy(buffer.at[at], out_hbm.at[s], out_sem.at[s])
            part = pltpu.make_async_copy(
                buffer.at[at].at[window], out_hbm.at[s].at[window], out_sem.at[s]
            )
            copied = odd & kept
            outs.append((copied, whole, part))
            pl.when(copied)(part.start)
            pl.when(jnp.logical_not(copied))(whole.start)
    for copied, whole, part in outs:
        pl.when(copied)(part.wait)
        pl.when(jnp.logical_not(copied))(whole.wait)


def join_kernel(peers_tp, meta, *rest):
    blocks, out, sem = rest[:-2], rest[-2], rest[-1]
    shard = blocks[0].shape[1]
    copies = []
    for k, block in enumerate(blocks):
        column = pl.multiple_of(jnp.bitwise_xor(meta[1], k) * shard, shard)
        copies.append(pltpu.make_async_copy(block, out.at[:, pl.ds(column, shard)], sem.at[k]))
        copies[-1].start()
    for copy in copies:
        copy.wait()


def swapped(x, axis, size, k):
    return lax.ppermute(x, axis, [(i, i ^ k) for i in range(size)])


def local(
    table, kv_cache, hidden, lengths, source, norm_gain, query_weight, keyval_weight, out_weight
):
    peers, peers_tp = lax.axis_size("inst"), lax.axis_size("tp")
    slots, cap = kv_cache.shape[0], kv_cache.shape[2]
    width = hidden.shape[1]
    heads = query_weight.shape[1] // HD
    shard = width // peers_tp
    others, moving = peers - 1, (peers - 1) * MOVE
    blocks = width // HD
    meta = jnp.stack([lax.axis_index("inst"), lax.axis_index("tp")]).astype(I32)
    wkv = keyval_weight.reshape(2 * width, HD)
    row32 = jax.ShapeDtypeStruct((slots, HD), F32)
    note_width = (heads + 2) * HD + shard
    dma = pltpu.SemaphoreType.DMA
    stages = [
        pltpu.VMEM((blocks, slots, HD), BF16),
        pltpu.VMEM((blocks, 2 * slots, 2 * HD), BF16),
        pltpu.VMEM((slots, HD), F32),
        pltpu.VMEM((slots, HD), F32),
    ]
    flops = 2 * slots * width * (heads + 2) * HD
    cache_bytes = kv_cache.size * 2

    slot_shape = kv_cache.shape[1:]
    plan, lengths, gain, table, hidden, *boxes = pl.pallas_call(
        functools.partial(pack_kernel, peers, slots),
        out_shape=[
            jax.ShapeDtypeStruct((2 * moving,), I32),
            jax.ShapeDtypeStruct((1, source.shape[0]), I32),
            jax.ShapeDtypeStruct((1, width), F32),
            jax.ShapeDtypeStruct((2, cap, HD), F32),
            jax.ShapeDtypeStruct(hidden.shape, BF16),
        ]
        + [jax.ShapeDtypeStruct((MOVE,) + slot_shape, BF16)] * others,
        in_specs=[SMEM] + [HBM] * 6,
        out_specs=[SMEM] * 2 + [VMEM] * 3 + [ANY] * others,
        scratch_shapes=[
            pltpu.SMEM((1, source.shape[0]), I32),
            pltpu.VMEM((1, source.shape[0]), I32),
            pltpu.VMEM((moving,) + slot_shape, BF16),
            dma((6,)),
            dma((moving,)),
            dma((others,)),
        ],
        compiler_params=params(10),
        cost_estimate=cost(1, 2 * cache_bytes),
        name="pack",
    )(meta, *(
        pltpu.with_memory_space_constraint(x, pltpu.HBM)
        for x in (source.reshape(1, -1), lengths.reshape(1, -1), norm_gain.reshape(1, width),
                  jnp.asarray(table), hidden, kv_cache)
    ))
    got_boxes = [swapped(box, "inst", peers, k + 1) for k, box in enumerate(boxes)]

    query, newkey1, newvalue1, *notes = pl.pallas_call(
        functools.partial(first_kernel, peers, slots, heads, shard),
        out_shape=[jax.ShapeDtypeStruct((slots * GROUP, HD), F32), row32, row32]
        + [jax.ShapeDtypeStruct((MOVE, note_width), F32)] * others,
        in_specs=[SMEM] * 3 + [VMEM] * 5 + [HBM, ANY],
        out_specs=[VMEM] * (3 + others),
        scratch_shapes=stages
        + [
            pltpu.VMEM((moving,) + slot_shape, BF16),
            pltpu.VMEM((slots, width), F32),
            dma((moving,)),
        ],
        compiler_params=params(24),
        cost_estimate=cost(flops, (query_weight.size + wkv.size) * 2),
        name="first_step",
    )(meta, lengths, plan, hidden, gain, table, query_weight, wkv,
      pltpu.with_memory_space_constraint(kv_cache, pltpu.HBM), got_boxes[0])
    got_notes = [swapped(note, "inst", peers, k + 1) for k, note in enumerate(notes)]

    attended = pl.pallas_call(
        functools.partial(attend_kernel, slots, heads),
        out_shape=jax.ShapeDtypeStruct((slots, heads * HD), BF16),
        in_specs=[SMEM] * 2 + [VMEM] * 3 + [ANY],
        out_specs=VMEM,
        scratch_shapes=[
            pltpu.VMEM(kv_cache.shape, BF16),
            pltpu.VMEM((slots * GROUP, HD), F32),
            dma((slots // CHUNK,)),
        ],
        compiler_params=params(24),
        cost_estimate=cost(4 * slots * cap * HD * heads, cache_bytes),
        name="attention",
    )(meta, lengths, query, newkey1, newvalue1, kv_cache)

    sent = [jax.ShapeDtypeStruct((slots, shard), F32)]
    sent += [jax.ShapeDtypeStruct((slots, shard), BF16)] * (peers_tp - 1)
    own, *rest = pl.pallas_call(
        functools.partial(out_kernel, peers, peers_tp, slots),
        out_shape=sent + [row32, row32, pltpu.HBM(kv_cache.shape, BF16)],
        in_specs=[SMEM] * 2 + [VMEM] * 5 + [ANY] + [VMEM] * others,
        out_specs=[VMEM] * (peers_tp + 2) + [HBM],
        scratch_shapes=[dma((slots // CHUNK,))],
        compiler_params=params(20),
        cost_estimate=cost(2 * slots * width * heads * HD, out_weight.size * 2),
        name="out_projection",
    )(meta, plan, attended, out_weight, hidden, newkey1, newvalue1, kv_cache, *got_notes)
    sends, (newkey1, newvalue1, final_cache) = rest[: peers_tp - 1], rest[peers_tp - 1 :]

    def summed(own, sends):
        got = [swapped(sends[k - 1], "tp", peers_tp, k) for k in range(peers_tp - 1, 0, -1)]
        shard_rows = pl.pallas_call(
            sum_kernel,
            out_shape=jax.ShapeDtypeStruct((slots, shard), BF16),
            in_specs=[VMEM] * peers_tp,
            out_specs=VMEM,
            compiler_params=params(16),
            name="sum_terms",
        )(own, *got)
        return [shard_rows] + [
            swapped(shard_rows, "tp", peers_tp, k) for k in range(1, peers_tp)
        ]

    pieces = summed(own, sends)

    newkey2, newvalue2, own, *sends = pl.pallas_call(
        functools.partial(second_kernel, peers, peers_tp, slots, heads),
        out_shape=[row32, row32] + sent,
        in_specs=[SMEM] * 4 + [VMEM] * 7 + [ANY] + [VMEM] * peers_tp + [ANY] * others,
        out_specs=[VMEM] * (2 + peers_tp),
        scratch_shapes=stages
        + [
            pltpu.VMEM((slots + moving,) + kv_cache.shape[1:], BF16),
            pltpu.VMEM((slots * GROUP, HD), F32),
            pltpu.VMEM((slots * GROUP, HD), F32),
            pltpu.SMEM((slots,), I32),
            dma((slots // CHUNK + others,)),
        ],
        compiler_params=params(32),
        cost_estimate=cost(3 * flops, cache_bytes + (query_weight.size + wkv.size) * 4),
        name="second_step",
    )(meta, source, lengths, plan, gain, table, newkey1, newvalue1, query_weight, wkv,
      out_weight, kv_cache, *pieces, *got_boxes)

    pieces = summed(own, sends)
    final_cache = pl.pallas_call(
        functools.partial(cache_kernel, peers, slots),
        out_shape=jax.ShapeDtypeStruct(kv_cache.shape, BF16),
        in_specs=[SMEM] * 4 + [VMEM] * 4 + [ANY] * peers + [HBM],
        out_specs=HBM,
        input_output_aliases={8 + peers: 0},
        scratch_shapes=[
            pltpu.VMEM((slots + moving,) + kv_cache.shape[1:], BF16),
            pltpu.SMEM((slots,), I32),
            dma((slots // CHUNK + others,)),
            dma((slots,)),
        ],
        compiler_params=params(24),
        cost_estimate=cost(0, 2 * cache_bytes),
        name="write_cache",
    )(meta, source, lengths, plan, newkey1, newvalue1, newkey2, newvalue2, kv_cache, *got_boxes,
      final_cache)
    final_hidden = pl.pallas_call(
        functools.partial(join_kernel, peers_tp),
        out_shape=jax.ShapeDtypeStruct(hidden.shape, BF16),
        in_specs=[SMEM] + [ANY] * peers_tp,
        out_specs=ANY,
        scratch_shapes=[dma((peers_tp,))],
        compiler_params=params(16),
        name="join",
    )(meta, *pieces)
    return (final_hidden, final_cache)


def solution(mesh):
    def whole(kv_cache, *rest):
        table = angle_tables(kv_cache.shape[2])
        return jax.shard_map(
            functools.partial(local, table),
            mesh=mesh,
            in_specs=(
                P(("groups", "inst"), None, None, "tp"),
                P(("groups", "inst"), None),
                P("groups"),
                P("groups"),
                P(),
                P(None, "tp"),
                P(None, None, "tp"),
                P("tp", None),
            ),
            out_specs=(P(("groups", "inst"), None), P(("groups", "inst"), None, None, "tp")),
            check_vma=False,
        )(kv_cache, *rest)

    return whole
```

```python
import functools

import jax
import jax.numpy as jnp
import numpy as np
from jax import lax
from jax.experimental import pallas as pl
from jax.experimental.pallas import tpu as pltpu
from jax.sharding import PartitionSpec as P

MOVE = 2
EPS = 1e-05
THETA = 500000.0
HD = 128
GROUP = 8
PIECE = 16
CHUNK = 8
NOTE = 16

F32 = jnp.float32
BF16 = jnp.bfloat16
I32 = jnp.int32

ANY = pl.BlockSpec(memory_space=pl.ANY)
VMEM = pl.BlockSpec(memory_space=pltpu.VMEM)
SMEM = pl.BlockSpec(memory_space=pltpu.SMEM)
HBM = pl.BlockSpec(memory_space=pltpu.HBM)


def params(mib):
    return pltpu.CompilerParams(vmem_limit_bytes=mib * 1024 * 1024)


def cost(flops, nbytes):
    return pl.CostEstimate(flops=flops, bytes_accessed=nbytes, transcendentals=0)


def angle_tables(positions):
    frequency = THETA ** (-(np.arange(HD // 2, dtype=np.float64) * 2.0) / HD)
    angles = np.arange(positions, dtype=np.float64)[:, None] * frequency[None, :]
    cosine = np.concatenate([np.cos(angles), np.cos(angles)], axis=-1)
    sine = np.concatenate([-np.sin(angles), np.sin(angles)], axis=-1)
    return cosine.astype(np.float32), sine.astype(np.float32)


def turn(x, cosine, sine):
    return x * cosine + pltpu.roll(x, HD // 2, 1) * sine


def gather_angles(position_of, slots, cos_ref, sin_ref, cos_rows, sin_rows):
    for s in range(slots):
        p = position_of(s)
        cos_rows[s : s + 1, :] = cos_ref[pl.ds(p, 1), :]
        sin_rows[s : s + 1, :] = sin_ref[pl.ds(p, 1), :]


def spread_normed(normed3, spread, slots, width):
    blocks = width // HD
    row = lax.broadcasted_iota(I32, (HD, 4 * HD), 0)
    col = lax.broadcasted_iota(I32, (HD, 4 * HD), 1)
    goal = jnp.where(col < 2 * HD, 2 * row, 2 * row + 1 + 2 * HD)
    places = jnp.where(col == goal, 1.0, 0.0).astype(BF16)
    spread_all = jnp.dot(
        normed3[...].reshape(blocks * slots, HD), places, preferred_element_type=F32
    ).astype(BF16)
    spread[:, 0:slots, :] = spread_all[:, : 2 * HD].reshape(blocks, slots, 2 * HD)
    spread[:, slots:, :] = spread_all[:, 2 * HD :].reshape(blocks, slots, 2 * HD)


def project(normed3, spread, wq, wkv, slots, width, wq_copies=(), wkv_copies=()):
    pieces = max(len(wq_copies), 1)
    depth = width // pieces
    query = None
    pair = None
    for c in range(pieces):
        for copy in wkv_copies[c : c + 1]:
            copy.wait()
        for b in range(c * depth // HD, (c + 1) * depth // HD):
            part = jnp.dot(
                spread[b], wkv[b * 2 * HD : (b + 1) * 2 * HD, :], preferred_element_type=F32
            )
            pair = part if pair is None else pair + part
    for c in range(pieces):
        for copy in wq_copies[c : c + 1]:
            copy.wait()
        for b in range(c * depth // (2 * HD), (c + 1) * depth // (2 * HD)):
            block = jnp.concatenate([normed3[2 * b], normed3[2 * b + 1]], axis=1)
            part = jnp.dot(
                block, wq[b * 2 * HD : (b + 1) * 2 * HD, :], preferred_element_type=F32
            )
            query = part if query is None else query + part
    return query, pair[:slots], pair[slots:]


def weight_copies(src, dst, sem, pieces):
    depth = src.shape[0] // pieces
    copies = [
        pltpu.make_async_copy(
            src.at[pl.ds(c * depth, depth)], dst.at[pl.ds(c * depth, depth)], sem.at[c]
        )
        for c in range(pieces)
    ]
    return copies


def put_row(cache, place, p, key_row, value_row):
    base = pl.multiple_of((jnp.maximum(p, 0) // PIECE) * PIECE, PIECE)
    hit = lax.broadcasted_iota(I32, (PIECE, HD), 0) + base == p
    for which, new in ((0, key_row), (1, value_row)):
        old = cache[place, which, pl.ds(base, PIECE), :].astype(F32)
        cache[place, which, pl.ds(base, PIECE), :] = jnp.where(hit, new, old).astype(BF16)


def attend(cache, places, positions, query_rows):
    cap = cache.shape[2]
    col = lax.broadcasted_iota(I32, (GROUP, cap), 1)
    scores = [
        lax.dot_general(
            rows.astype(BF16),
            cache[place, 0],
            (((1,), (1,)), ((), ())),
            preferred_element_type=F32,
        )
        for place, rows in zip(places, query_rows)
    ]
    probs = []
    for score, p in zip(scores, positions):
        score = jnp.where(col <= p, score * HD**-0.5, -jnp.inf)
        weight = jnp.exp(score - jnp.max(score, axis=-1, keepdims=True))
        weight = weight / jnp.sum(weight, axis=-1, keepdims=True)
        probs.append(weight.astype(BF16))
    return [
        jnp.dot(prob, cache[place, 1], preferred_element_type=F32)
        for place, prob in zip(places, probs)
    ]


def norm_into(normed3, pieces, gains, firsts, total_width):
    square = None
    for piece in pieces:
        part = jnp.sum(piece * piece, axis=-1, keepdims=True)
        square = part if square is None else square + part
    factor = lax.rsqrt(square / total_width + EPS)
    for piece, gain, first in zip(pieces, gains, firsts):
        normed = (piece * factor * gain).astype(BF16)
        for i in range(piece.shape[1] // HD):
            normed3[first + i] = normed[:, i * HD : (i + 1) * HD]


def first_kernel(
    peers, slots, heads, shard,
    meta, source_hbm, lengths_hbm, hidden_hbm, gain_hbm, cos_hbm, sin_hbm, wq_hbm, wkv_hbm,
    cache_hbm, query_out, newkey_out, newvalue_out, plan, *rest,
):
    others = peers - 1
    moving = others * MOVE
    box, notes = rest[0], (None,) + rest[1:others]
    (wq, wkv, normed3, spread, cos_rows, sin_rows, leaving, hidden32, source_s, lengths_s, source_v,
     hidden, gain, cos_ref, sin_ref, tail, small_sem, wq_sem, wkv_sem, in_sem,
     box_sem) = rest[others:]
    width = hidden.shape[1]
    me, me_tp = meta[0], meta[1]
    wq_copies = weight_copies(wq_hbm, wq, wq_sem, 4)
    wkv_copies = weight_copies(wkv_hbm, wkv, wkv_sem, 4)
    small = [
        pltpu.make_async_copy(src, dst, small_sem.at[i])
        for i, (src, dst) in enumerate((
            (source_hbm, source_v), (source_hbm, source_s), (lengths_hbm, lengths_s),
            (hidden_hbm, hidden), (gain_hbm, gain), (cos_hbm, cos_ref), (sin_hbm, sin_ref),
        ))
    ]
    for copy in small + wkv_copies + wq_copies:
        copy.start()
    small[0].wait()
    small[1].wait()

    low = me * slots
    src = source_v[...]
    index = lax.broadcasted_iota(I32, src.shape, 1)
    mine_goes = (src >= low) & (src < low + slots)
    mine_comes = (index >= low) & (index < low + slots)
    index_f = index.astype(F32)
    send_slots = []
    for k in range(1, peers):
        other = jnp.bitwise_xor(me, k) * slots
        sent = mine_goes & (index >= other) & (index < other + slots)
        taken = mine_comes & (src >= other) & (src < other + slots)
        for m in range(MOVE):
            at = (k - 1) * MOVE + m
            if m == 0:
                j = jnp.min(jnp.where(sent, index_f, 1e6)).astype(I32)
                r = jnp.min(jnp.where(taken, index_f, 1e6)).astype(I32)
            else:
                j = jnp.max(jnp.where(sent, index_f, -1.0)).astype(I32)
                r = jnp.max(jnp.where(taken, index_f, -1.0)).astype(I32)
            known = (j >= 0) & (j < src.shape[1])
            slot = source_s[0, jnp.where(known, j, 0)] - low
            slot = jnp.where(known, slot, 0)
            send_slots.append(slot)
            plan[at] = jnp.where((r >= 0) & (r < src.shape[1]), r - low, -1)
            plan[moving + at] = slot
            pltpu.make_async_copy(cache_hbm.at[slot], leaving.at[at], in_sem.at[at]).start()

    for copy in small[2:]:
        copy.wait()
    wide = hidden[...].astype(F32)
    hidden32[...] = wide
    norm_into(normed3, [wide], [gain[...]], [0], width)
    spread_normed(normed3, spread, slots, width)
    gather_angles(lambda s: lengths_s[0, low + s], slots, cos_ref, sin_ref, cos_rows, sin_rows)
    query, key, value = project(
        normed3, spread, wq, wkv, slots, width, wq_copies, wkv_copies
    )
    cosine, sine = cos_rows[...], sin_rows[...]
    query_out[...] = jnp.zeros(query_out.shape, F32)
    for g in range(heads):
        turned = turn(query[:, g * HD : (g + 1) * HD], cosine, sine)
        query_out[pl.ds(g, slots, stride=GROUP), :] = turned.astype(BF16).astype(F32)
    newkey_out[...] = turn(key, cosine, sine).astype(BF16).astype(F32)
    newvalue_out[...] = value.astype(BF16).astype(F32)

    positions = [lengths_s[0, low + slot] for slot in send_slots]
    for at, slot in enumerate(send_slots):
        pltpu.make_async_copy(cache_hbm.at[slot], leaving.at[at], in_sem.at[at]).wait()
        put_row(
            leaving, at, positions[at],
            newkey_out[pl.ds(slot, 1), :], newvalue_out[pl.ds(slot, 1), :],
        )
    cap = leaving.shape[2]
    copies = [
        pltpu.make_async_copy(
            leaving.at[pl.ds(0, MOVE)], box.at[:, :, pl.ds(0, cap), :], box_sem.at[0]
        )
    ]
    copies[0].start()
    rows = [query_out[pl.ds(pl.multiple_of(slot * GROUP, GROUP), GROUP), :] for slot in send_slots]
    attended = attend(leaving, list(range(moving)), positions, rows)
    column = pl.multiple_of(me_tp * shard, shard)
    for at, slot in enumerate(send_slots):
        m = at % MOVE
        residual = hidden32[pl.ds(slot, 1), pl.ds(column, shard)]
        if at < MOVE:
            blocks = [attended[at][g : g + 1, :] for g in range(heads)]
            blocks += [residual[:, b * HD : (b + 1) * HD] for b in range(shard // HD)]
            blocks += [jnp.zeros((1, HD), F32)] * (NOTE - len(blocks))
            tail[m] = jnp.concatenate(blocks, axis=0).astype(BF16)
            copies.append(
                pltpu.make_async_copy(
                    tail.at[m], box.at[m, 0, pl.ds(cap, NOTE), :], box_sem.at[1 + m]
                )
            )
            copies[-1].start()
        else:
            note = notes[at // MOVE]
            for g in range(heads):
                note[m : m + 1, g * HD : (g + 1) * HD] = attended[at][g : g + 1, :]
            note[m : m + 1, heads * HD :] = residual
    for copy in copies:
        copy.wait()


def attend_kernel(
    slots, heads, meta, lengths_s, query, newkey, newvalue, cache_hbm, out,
    buffer, attended_rows, in_sem,
):
    low = meta[0] * slots

    def copy_in(c):
        span = pl.ds(c * CHUNK, CHUNK)
        return pltpu.make_async_copy(cache_hbm.at[span], buffer.at[span], in_sem.at[c])

    for c in range(slots // CHUNK):
        copy_in(c).start()
    for c in range(slots // CHUNK):
        copy_in(c).wait()
        span = list(range(c * CHUNK, (c + 1) * CHUNK))
        positions = [lengths_s[low + s] for s in span]
        for s, p in zip(span, positions):
            put_row(buffer, s, p, newkey[s : s + 1, :], newvalue[s : s + 1, :])
        got = attend(
            buffer, span, positions, [query[s * GROUP : (s + 1) * GROUP, :] for s in span]
        )
        for s, rows in zip(span, got):
            attended_rows[s * GROUP : (s + 1) * GROUP, :] = rows
    for g in range(heads):
        out[:, g * HD : (g + 1) * HD] = attended_rows[pl.ds(g, slots, stride=GROUP), :].astype(BF16)


def project_out(attended, wo, residual, own, sends, me_tp, peers_tp):
    shard = own.shape[1]
    for k in list(range(peers_tp - 1, 0, -1)) + [0]:
        column = pl.multiple_of(jnp.bitwise_xor(me_tp, k) * shard, shard)
        part = jnp.dot(attended, wo[:, pl.ds(column, shard)], preferred_element_type=F32)
        if k == 0:
            own[...] = residual + part
        else:
            sends[k - 1][...] = part.astype(BF16)


def out_kernel(
    peers, peers_tp, slots, meta, lengths_s, plan, attended, wo, hidden, newkey, newvalue, box_hbm,
    cache_hbm, *rest,
):
    notes, rest = rest[: peers - 2], rest[peers - 2 :]
    own, sends, boxes = rest[0], rest[1:peers_tp], rest[peers_tp : peers_tp + peers - 2]
    leaving, tail, sem, in_sem, out_sem = rest[peers_tp + peers - 2 :]
    moving = (peers - 1) * MOVE
    send_slots = [plan[moving + at] for at in range(MOVE, moving)]
    packs = [
        pltpu.make_async_copy(cache_hbm.at[slot], leaving.at[i], in_sem.at[i])
        for i, slot in enumerate(send_slots)
    ]
    for pack in packs:
        pack.start()
    shard = own.shape[1]
    cap = box_hbm.shape[2] - NOTE
    copy = pltpu.make_async_copy(box_hbm.at[:, 0, pl.ds(cap, NOTE), :], tail, sem.at[0])
    copy.start()
    rows = attended[...].astype(F32)
    heads = rows.shape[1] // HD
    column = pl.multiple_of(meta[1] * shard, shard)
    residual = hidden[:, pl.ds(column, shard)].astype(F32)
    row_index = lax.broadcasted_iota(I32, rows.shape, 0)
    residual_index = lax.broadcasted_iota(I32, residual.shape, 0)
    copy.wait()
    for at in range((peers - 1) * MOVE):
        m = at % MOVE
        if at < MOVE:
            blocks = tail[m].astype(F32)
            blocks = [blocks[b : b + 1, :] for b in range(heads + shard // HD)]
            note = jnp.concatenate(blocks, axis=1)
        else:
            note = notes[at // MOVE - 1][m : m + 1, :]
        rows = jnp.where(row_index == plan[at], note[:, : heads * HD], rows)
        residual = jnp.where(residual_index == plan[at], note[:, heads * HD :], residual)
    for pack in packs:
        pack.wait()
    for i, slot in enumerate(send_slots):
        put_row(
            leaving, i, lengths_s[meta[0] * slots + slot],
            newkey[pl.ds(slot, 1), :], newvalue[pl.ds(slot, 1), :],
        )
    outs = [
        pltpu.make_async_copy(leaving.at[pl.ds(k * MOVE, MOVE)], out, out_sem.at[k])
        for k, out in enumerate(boxes)
    ]
    for out in outs:
        out.start()
    project_out(rows.astype(BF16), wo, residual, own, sends, meta[1], peers_tp)
    for out in outs:
        out.wait()


def sum_kernel(own, *rest):
    total = own[...]
    for part in rest[:-1]:
        total = total + part[...].astype(F32)
    rest[-1][...] = total.astype(BF16)


def load_slots(slots, peers, cache_hbm, box_hbm, buffer, in_sem):
    copies = []
    for c in range(slots // CHUNK):
        span = pl.ds(c * CHUNK, CHUNK)
        copies.append(pltpu.make_async_copy(cache_hbm.at[span], buffer.at[span], in_sem.at[c]))
    for k in range(peers - 1):
        copies.append(
            pltpu.make_async_copy(
                box_hbm[k].at[:, :, pl.ds(0, cache_hbm.shape[2]), :],
                buffer.at[pl.ds(slots + k * MOVE, MOVE)],
                in_sem.at[slots // CHUNK + k],
            )
        )
    return copies


def map_places(slots, peers, plan, place):
    for s in range(slots):
        place[s] = s
    for at in range((peers - 1) * MOVE):
        taker = plan[at]

        @pl.when(taker >= 0)
        def _():
            place[taker] = slots + at


def second_kernel(
    peers, peers_tp, slots, heads,
    meta, source_s, lengths_s, plan, gain, cos_ref, sin_ref, newkey1, newvalue1,
    wq, wkv, wo, cache_hbm, *rest,
):
    blocks, rest = rest[0], rest[1:]
    box_hbm, rest = rest[: peers - 1], rest[peers - 1 :]
    newkey, newvalue, own = rest[:3]
    sends, rest = rest[3 : 2 + peers_tp], rest[2 + peers_tp :]
    (normed3, spread, cos_rows, sin_rows, buffer, query_rows, attended_rows, place,
     in_sem) = rest
    me, me_tp = meta[0], meta[1]
    low = me * slots
    width = gain.shape[1]
    shard = own.shape[1]
    cache_copies = load_slots(slots, peers, cache_hbm, box_hbm, buffer, in_sem)
    for copy in cache_copies[::-1]:
        copy.start()

    map_places(slots, peers, plan, place)
    norm_into(
        normed3,
        [blocks[k].astype(F32) for k in range(peers_tp)],
        [gain[:, k * shard : (k + 1) * shard] for k in range(peers_tp)],
        [k * (shard // HD) for k in range(peers_tp)],
        width,
    )
    spread_normed(normed3, spread, slots, width)
    lengths = [lengths_s[source_s[low + s]] for s in range(slots)]
    gather_angles(lambda s: lengths[s] + 1, slots, cos_ref, sin_ref, cos_rows, sin_rows)
    query, key, value = project(normed3, spread, wq, wkv, slots, width)
    cosine, sine = cos_rows[...], sin_rows[...]
    query_rows[...] = jnp.zeros(query_rows.shape, F32)
    for g in range(heads):
        turned = turn(query[:, g * HD : (g + 1) * HD], cosine, sine)
        query_rows[pl.ds(g, slots, stride=GROUP), :] = turned.astype(BF16).astype(F32)
    newkey[...] = turn(key, cosine, sine).astype(BF16).astype(F32)
    newvalue[...] = value.astype(BF16).astype(F32)

    for copy in cache_copies[::-1]:
        copy.wait()
    for c in range(slots // CHUNK):
        span = list(range(c * CHUNK, (c + 1) * CHUNK))
        places = [place[s] for s in span]
        for s, at in zip(span, places):
            first = jnp.where(at < slots, lengths[s], -1)
            put_row(buffer, at, first, newkey1[s : s + 1, :], newvalue1[s : s + 1, :])
            put_row(buffer, at, lengths[s] + 1, newkey[s : s + 1, :], newvalue[s : s + 1, :])
        got = attend(
            buffer, places, [lengths[s] + 1 for s in span],
            [query_rows[s * GROUP : (s + 1) * GROUP, :] for s in span],
        )
        for s, rows in zip(span, got):
            attended_rows[s * GROUP : (s + 1) * GROUP, :] = rows
    attended = jnp.concatenate(
        [attended_rows[pl.ds(g, slots, stride=GROUP), :].astype(BF16) for g in range(heads)], axis=1
    )
    project_out(attended, wo, blocks[me_tp].astype(F32), own, sends, me_tp, peers_tp)


def cache_kernel(
    peers, slots, meta, source_s, lengths_s, plan, newkey1, newvalue1, newkey2, newvalue2,
    cache_hbm, *rest,
):
    box_hbm, rest = rest[: peers - 1], rest[peers - 1 :]
    out_hbm, buffer, place, in_sem, out_sem = rest
    low = meta[0] * slots
    cache_copies = load_slots(slots, peers, cache_hbm, box_hbm, buffer, in_sem)
    for copy in cache_copies:
        copy.start()
    map_places(slots, peers, plan, place)
    chunks = slots // CHUNK
    for copy in cache_copies[chunks:]:
        copy.wait()
    outs = []
    for c in range(chunks):
        cache_copies[c].wait()
        for s in range(c * CHUNK, (c + 1) * CHUNK):
            at = place[s]
            length = lengths_s[source_s[low + s]]
            first = jnp.where(at < slots, length, -1)
            put_row(buffer, at, first, newkey1[s : s + 1, :], newvalue1[s : s + 1, :])
            put_row(buffer, at, length + 1, newkey2[s : s + 1, :], newvalue2[s : s + 1, :])
            copy = pltpu.make_async_copy(buffer.at[at], out_hbm.at[s], out_sem.at[s])
            copy.start()
            outs.append(copy)
    for copy in outs:
        copy.wait()


def swapped(x, axis, size, k):
    return lax.ppermute(x, axis, [(i, i ^ k) for i in range(size)])


def local(
    tables, kv_cache, hidden, lengths, source, norm_gain, query_weight, keyval_weight, out_weight
):
    peers, peers_tp = lax.axis_size("inst"), lax.axis_size("tp")
    slots, cap = kv_cache.shape[0], kv_cache.shape[2]
    width = hidden.shape[1]
    heads = query_weight.shape[1] // HD
    shard = width // peers_tp
    others, moving = peers - 1, (peers - 1) * MOVE
    blocks = width // HD
    meta = jnp.stack([lax.axis_index("inst"), lax.axis_index("tp")]).astype(I32)
    gain = norm_gain.reshape(1, width)
    wkv = keyval_weight.reshape(2 * width, HD)
    cosine, sine = (jnp.asarray(table) for table in tables)
    row32 = jax.ShapeDtypeStruct((slots, HD), F32)
    note_width = heads * HD + shard
    dma = pltpu.SemaphoreType.DMA
    weights = [
        pltpu.VMEM(query_weight.shape, BF16),
        pltpu.VMEM(wkv.shape, BF16),
    ]
    stages = [
        pltpu.VMEM((blocks, slots, HD), BF16),
        pltpu.VMEM((blocks, 2 * slots, 2 * HD), BF16),
        pltpu.VMEM((slots, HD), F32),
        pltpu.VMEM((slots, HD), F32),
    ]
    flops = 2 * slots * width * (heads + 2) * HD
    cache_bytes = kv_cache.size * 2

    query, newkey1, newvalue1, plan, *notes = pl.pallas_call(
        functools.partial(first_kernel, peers, slots, heads, shard),
        out_shape=[
            jax.ShapeDtypeStruct((slots * GROUP, HD), F32),
            row32,
            row32,
            jax.ShapeDtypeStruct((2 * moving,), I32),
        ]
        + [jax.ShapeDtypeStruct((MOVE, 2, cap + NOTE, HD), BF16)]
        + [jax.ShapeDtypeStruct((MOVE, note_width), F32)] * (others - 1),
        in_specs=[SMEM] + [HBM] * 9,
        out_specs=[VMEM] * 3 + [SMEM, ANY] + [VMEM] * (others - 1),
        scratch_shapes=weights
        + stages
        + [
            pltpu.VMEM((moving,) + kv_cache.shape[1:], BF16),
            pltpu.VMEM((slots, width), F32),
            pltpu.SMEM((1, source.shape[0]), I32),
            pltpu.SMEM((1, source.shape[0]), I32),
            pltpu.VMEM((1, source.shape[0]), I32),
            pltpu.VMEM(hidden.shape, BF16),
            pltpu.VMEM((1, width), F32),
            pltpu.VMEM(cosine.shape, F32),
            pltpu.VMEM(cosine.shape, F32),
            pltpu.VMEM((MOVE, NOTE, HD), BF16),
            dma((7,)),
            dma((4,)),
            dma((4,)),
            dma((moving,)),
            dma((1 + MOVE,)),
        ],
        compiler_params=params(24),
        cost_estimate=cost(flops, (query_weight.size + wkv.size) * 2),
        name="first_step",
    )(meta, *(
        pltpu.with_memory_space_constraint(x, pltpu.HBM)
        for x in (source.reshape(1, -1), lengths.reshape(1, -1), hidden, gain, cosine, sine,
                  query_weight, wkv, kv_cache)
    ))
    got_notes = [swapped(note, "inst", peers, k + 1) for k, note in enumerate(notes)]

    attended = pl.pallas_call(
        functools.partial(attend_kernel, slots, heads),
        out_shape=jax.ShapeDtypeStruct((slots, heads * HD), BF16),
        in_specs=[SMEM] * 2 + [VMEM] * 3 + [ANY],
        out_specs=VMEM,
        scratch_shapes=[
            pltpu.VMEM(kv_cache.shape, BF16),
            pltpu.VMEM((slots * GROUP, HD), F32),
            dma((slots // CHUNK,)),
        ],
        compiler_params=params(24),
        cost_estimate=cost(4 * slots * cap * HD * heads, cache_bytes),
        name="attention",
    )(meta, lengths, query, newkey1, newvalue1, kv_cache)

    sent = [jax.ShapeDtypeStruct((slots, shard), F32)]
    sent += [jax.ShapeDtypeStruct((slots, shard), BF16)] * (peers_tp - 1)
    own, *rest = pl.pallas_call(
        functools.partial(out_kernel, peers, peers_tp, slots),
        out_shape=sent
        + [jax.ShapeDtypeStruct((MOVE,) + kv_cache.shape[1:], BF16)] * (others - 1),
        in_specs=[SMEM] * 3 + [VMEM] * 5 + [ANY] * 2 + [VMEM] * (others - 1),
        out_specs=[VMEM] * peers_tp + [ANY] * (others - 1),
        scratch_shapes=[
            pltpu.VMEM((moving - MOVE,) + kv_cache.shape[1:], BF16),
            pltpu.VMEM((MOVE, NOTE, HD), BF16),
            dma((1,)),
            dma((moving - MOVE,)),
            dma((others - 1,)),
        ],
        compiler_params=params(20),
        cost_estimate=cost(2 * slots * width * heads * HD, out_weight.size * 2),
        name="out_projection",
    )(meta, lengths, plan, attended, out_weight, hidden, newkey1, newvalue1, got_notes[0], kv_cache,
      *got_notes[1:])
    sends, boxes = rest[: peers_tp - 1], rest[peers_tp - 1 :]
    got_boxes = got_notes[:1] + [swapped(box, "inst", peers, k + 2) for k, box in enumerate(boxes)]

    def summed(own, sends, **gather):
        got = [swapped(sends[k - 1], "tp", peers_tp, k) for k in range(peers_tp - 1, 0, -1)]
        shard_rows = pl.pallas_call(
            sum_kernel,
            out_shape=jax.ShapeDtypeStruct((slots, shard), BF16),
            in_specs=[VMEM] * peers_tp,
            out_specs=VMEM,
            compiler_params=params(16),
            name="sum_terms",
        )(own, *got)
        return lax.all_gather(shard_rows, "tp", **gather)

    pieces = summed(own, sends)

    newkey2, newvalue2, own, *sends = pl.pallas_call(
        functools.partial(second_kernel, peers, peers_tp, slots, heads),
        out_shape=[row32, row32] + sent,
        in_specs=[SMEM] * 4 + [VMEM] * 8 + [ANY, VMEM] + [ANY] * others,
        out_specs=[VMEM] * (2 + peers_tp),
        scratch_shapes=stages
        + [
            pltpu.VMEM((slots + moving,) + kv_cache.shape[1:], BF16),
            pltpu.VMEM((slots * GROUP, HD), F32),
            pltpu.VMEM((slots * GROUP, HD), F32),
            pltpu.SMEM((slots,), I32),
            dma((slots // CHUNK + others,)),
        ],
        compiler_params=params(32),
        cost_estimate=cost(3 * flops, cache_bytes + (query_weight.size + wkv.size) * 4),
        name="second_step",
    )(meta, source, lengths, plan, gain, cosine, sine, newkey1, newvalue1, query_weight, wkv,
      out_weight, kv_cache, pieces, *got_boxes)

    final_hidden = summed(own, sends, axis=1, tiled=True)
    final_cache = pl.pallas_call(
        functools.partial(cache_kernel, peers, slots),
        out_shape=jax.ShapeDtypeStruct(kv_cache.shape, BF16),
        in_specs=[SMEM] * 4 + [VMEM] * 4 + [ANY] * peers,
        out_specs=ANY,
        scratch_shapes=[
            pltpu.VMEM((slots + moving,) + kv_cache.shape[1:], BF16),
            pltpu.SMEM((slots,), I32),
            dma((slots // CHUNK + others,)),
            dma((slots,)),
        ],
        compiler_params=params(24),
        cost_estimate=cost(0, 2 * cache_bytes),
        name="write_cache",
    )(meta, source, lengths, plan, newkey1, newvalue1, newkey2, newvalue2, kv_cache, *got_boxes)
    return (final_hidden, final_cache)


def solution(mesh):
    def whole(kv_cache, *rest):
        tables = angle_tables(kv_cache.shape[2])
        return jax.shard_map(
            functools.partial(local, tables),
            mesh=mesh,
            in_specs=(
                P(("groups", "inst"), None, None, "tp"),
                P(("groups", "inst"), None),
                P("groups"),
                P("groups"),
                P(),
                P(None, "tp"),
                P(None, None, "tp"),
                P("tp", None),
            ),
            out_specs=(P(("groups", "inst"), None), P(("groups", "inst"), None, None, "tp")),
            check_vma=False,
        )(kv_cache, *rest)

    return whole
```

```python
import functools

import jax
import jax.numpy as jnp
import numpy as np
from jax import lax
from jax.experimental import pallas as pl
from jax.experimental.pallas import tpu as pltpu
from jax.sharding import PartitionSpec as P

MOVE = 2
EPS = 1e-05
THETA = 500000.0
HD = 128
GROUP = 8
PIECE = 16
CHUNK = 8
NOTE = 16

F32 = jnp.float32
BF16 = jnp.bfloat16
I32 = jnp.int32

ANY = pl.BlockSpec(memory_space=pl.ANY)
VMEM = pl.BlockSpec(memory_space=pltpu.VMEM)
SMEM = pl.BlockSpec(memory_space=pltpu.SMEM)
HBM = pl.BlockSpec(memory_space=pltpu.HBM)


def params(mib):
    return pltpu.CompilerParams(vmem_limit_bytes=mib * 1024 * 1024)


def cost(flops, nbytes):
    return pl.CostEstimate(flops=flops, bytes_accessed=nbytes, transcendentals=0)


def angle_tables(positions):
    frequency = THETA ** (-(np.arange(HD // 2, dtype=np.float64) * 2.0) / HD)
    angles = np.arange(positions, dtype=np.float64)[:, None] * frequency[None, :]
    cosine = np.concatenate([np.cos(angles), np.cos(angles)], axis=-1)
    sine = np.concatenate([-np.sin(angles), np.sin(angles)], axis=-1)
    return cosine.astype(np.float32), sine.astype(np.float32)


def turn(x, cosine, sine):
    return x * cosine + pltpu.roll(x, HD // 2, 1) * sine


def gather_angles(position_of, slots, cos_ref, sin_ref, cos_rows, sin_rows):
    for s in range(slots):
        p = position_of(s)
        cos_rows[s : s + 1, :] = cos_ref[pl.ds(p, 1), :]
        sin_rows[s : s + 1, :] = sin_ref[pl.ds(p, 1), :]


def spread_normed(normed3, spread, slots, width):
    blocks = width // HD
    row = lax.broadcasted_iota(I32, (HD, 4 * HD), 0)
    col = lax.broadcasted_iota(I32, (HD, 4 * HD), 1)
    goal = jnp.where(col < 2 * HD, 2 * row, 2 * row + 1 + 2 * HD)
    places = jnp.where(col == goal, 1.0, 0.0).astype(BF16)
    spread_all = jnp.dot(
        normed3[...].reshape(blocks * slots, HD), places, preferred_element_type=F32
    ).astype(BF16)
    spread[:, 0:slots, :] = spread_all[:, : 2 * HD].reshape(blocks, slots, 2 * HD)
    spread[:, slots:, :] = spread_all[:, 2 * HD :].reshape(blocks, slots, 2 * HD)


def project(normed3, spread, wq, wkv, slots, width, wq_copies=(), wkv_copies=()):
    pieces = max(len(wq_copies), 1)
    depth = width // pieces
    query = None
    pair = None
    for c in range(pieces):
        for copy in wkv_copies[c : c + 1]:
            copy.wait()
        for b in range(c * depth // HD, (c + 1) * depth // HD):
            part = jnp.dot(
                spread[b], wkv[b * 2 * HD : (b + 1) * 2 * HD, :], preferred_element_type=F32
            )
            pair = part if pair is None else pair + part
    for c in range(pieces):
        for copy in wq_copies[c : c + 1]:
            copy.wait()
        for b in range(c * depth // (2 * HD), (c + 1) * depth // (2 * HD)):
            block = jnp.concatenate([normed3[2 * b], normed3[2 * b + 1]], axis=1)
            part = jnp.dot(
                block, wq[b * 2 * HD : (b + 1) * 2 * HD, :], preferred_element_type=F32
            )
            query = part if query is None else query + part
    return query, pair[:slots], pair[slots:]


def weight_copies(src, dst, sem, pieces):
    depth = src.shape[0] // pieces
    copies = [
        pltpu.make_async_copy(
            src.at[pl.ds(c * depth, depth)], dst.at[pl.ds(c * depth, depth)], sem.at[c]
        )
        for c in range(pieces)
    ]
    return copies


def put_row(cache, place, p, key_row, value_row):
    base = pl.multiple_of((jnp.maximum(p, 0) // PIECE) * PIECE, PIECE)
    hit = lax.broadcasted_iota(I32, (PIECE, HD), 0) + base == p
    for which, new in ((0, key_row), (1, value_row)):
        old = cache[place, which, pl.ds(base, PIECE), :].astype(F32)
        cache[place, which, pl.ds(base, PIECE), :] = jnp.where(hit, new, old).astype(BF16)


def attend(cache, places, positions, query_rows):
    cap = cache.shape[2]
    col = lax.broadcasted_iota(I32, (GROUP, cap), 1)
    scores = [
        lax.dot_general(
            rows.astype(BF16),
            cache[place, 0],
            (((1,), (1,)), ((), ())),
            preferred_element_type=F32,
        )
        for place, rows in zip(places, query_rows)
    ]
    probs = []
    for score, p in zip(scores, positions):
        score = jnp.where(col <= p, score * HD**-0.5, -jnp.inf)
        weight = jnp.exp(score - jnp.max(score, axis=-1, keepdims=True))
        weight = weight / jnp.sum(weight, axis=-1, keepdims=True)
        probs.append(weight.astype(BF16))
    return [
        jnp.dot(prob, cache[place, 1], preferred_element_type=F32)
        for place, prob in zip(places, probs)
    ]


def norm_into(normed3, pieces, gains, firsts, total_width):
    square = None
    for piece in pieces:
        part = jnp.sum(piece * piece, axis=-1, keepdims=True)
        square = part if square is None else square + part
    factor = lax.rsqrt(square / total_width + EPS)
    for piece, gain, first in zip(pieces, gains, firsts):
        normed = (piece * factor * gain).astype(BF16)
        for i in range(piece.shape[1] // HD):
            normed3[first + i] = normed[:, i * HD : (i + 1) * HD]


def first_kernel(
    peers, slots, heads, shard,
    meta, source_hbm, lengths_hbm, hidden_hbm, gain_hbm, cos_hbm, sin_hbm, wq_hbm, wkv_hbm,
    cache_hbm, query_out, newkey_out, newvalue_out, plan, *rest,
):
    others = peers - 1
    moving = others * MOVE
    box, notes = rest[0], (None,) + rest[1:others]
    (wq, wkv, normed3, spread, cos_rows, sin_rows, leaving, hidden32, source_s, lengths_s, source_v,
     hidden, gain, cos_ref, sin_ref, tail, small_sem, wq_sem, wkv_sem, in_sem,
     box_sem) = rest[others:]
    width = hidden.shape[1]
    me, me_tp = meta[0], meta[1]
    wq_copies = weight_copies(wq_hbm, wq, wq_sem, 4)
    wkv_copies = weight_copies(wkv_hbm, wkv, wkv_sem, 4)
    small = [
        pltpu.make_async_copy(src, dst, small_sem.at[i])
        for i, (src, dst) in enumerate((
            (source_hbm, source_v), (source_hbm, source_s), (lengths_hbm, lengths_s),
            (hidden_hbm, hidden), (gain_hbm, gain), (cos_hbm, cos_ref), (sin_hbm, sin_ref),
        ))
    ]
    for copy in small + wkv_copies + wq_copies:
        copy.start()
    small[0].wait()
    small[1].wait()

    low = me * slots
    src = source_v[...]
    index = lax.broadcasted_iota(I32, src.shape, 1)
    mine_goes = (src >= low) & (src < low + slots)
    mine_comes = (index >= low) & (index < low + slots)
    index_f = index.astype(F32)
    send_slots = []
    for k in range(1, peers):
        other = jnp.bitwise_xor(me, k) * slots
        sent = mine_goes & (index >= other) & (index < other + slots)
        taken = mine_comes & (src >= other) & (src < other + slots)
        for m in range(MOVE):
            at = (k - 1) * MOVE + m
            if m == 0:
                j = jnp.min(jnp.where(sent, index_f, 1e6)).astype(I32)
                r = jnp.min(jnp.where(taken, index_f, 1e6)).astype(I32)
            else:
                j = jnp.max(jnp.where(sent, index_f, -1.0)).astype(I32)
                r = jnp.max(jnp.where(taken, index_f, -1.0)).astype(I32)
            known = (j >= 0) & (j < src.shape[1])
            slot = source_s[0, jnp.where(known, j, 0)] - low
            slot = jnp.where(known, slot, 0)
            send_slots.append(slot)
            plan[at] = jnp.where((r >= 0) & (r < src.shape[1]), r - low, -1)
            plan[moving + at] = slot
            pltpu.make_async_copy(cache_hbm.at[slot], leaving.at[at], in_sem.at[at]).start()

    for copy in small[2:]:
        copy.wait()
    wide = hidden[...].astype(F32)
    hidden32[...] = wide
    norm_into(normed3, [wide], [gain[...]], [0], width)
    spread_normed(normed3, spread, slots, width)
    gather_angles(lambda s: lengths_s[0, low + s], slots, cos_ref, sin_ref, cos_rows, sin_rows)
    query, key, value = project(
        normed3, spread, wq, wkv, slots, width, wq_copies, wkv_copies
    )
    cosine, sine = cos_rows[...], sin_rows[...]
    query_out[...] = jnp.zeros(query_out.shape, F32)
    for g in range(heads):
        turned = turn(query[:, g * HD : (g + 1) * HD], cosine, sine)
        query_out[pl.ds(g, slots, stride=GROUP), :] = turned.astype(BF16).astype(F32)
    newkey_out[...] = turn(key, cosine, sine).astype(BF16).astype(F32)
    newvalue_out[...] = value.astype(BF16).astype(F32)

    positions = [lengths_s[0, low + slot] for slot in send_slots]
    for at, slot in enumerate(send_slots):
        pltpu.make_async_copy(cache_hbm.at[slot], leaving.at[at], in_sem.at[at]).wait()
        put_row(
            leaving, at, positions[at],
            newkey_out[pl.ds(slot, 1), :], newvalue_out[pl.ds(slot, 1), :],
        )
    cap = leaving.shape[2]
    copies = [
        pltpu.make_async_copy(
            leaving.at[pl.ds(0, MOVE)], box.at[:, :, pl.ds(0, cap), :], box_sem.at[0]
        )
    ]
    copies[0].start()
    rows = [query_out[pl.ds(pl.multiple_of(slot * GROUP, GROUP), GROUP), :] for slot in send_slots]
    attended = attend(leaving, list(range(moving)), positions, rows)
    column = pl.multiple_of(me_tp * shard, shard)
    for at, slot in enumerate(send_slots):
        m = at % MOVE
        residual = hidden32[pl.ds(slot, 1), pl.ds(column, shard)]
        if at < MOVE:
            blocks = [attended[at][g : g + 1, :] for g in range(heads)]
            blocks += [residual[:, b * HD : (b + 1) * HD] for b in range(shard // HD)]
            blocks += [jnp.zeros((1, HD), F32)] * (NOTE - len(blocks))
            tail[m] = jnp.concatenate(blocks, axis=0).astype(BF16)
            copies.append(
                pltpu.make_async_copy(
                    tail.at[m], box.at[m, 0, pl.ds(cap, NOTE), :], box_sem.at[1 + m]
                )
            )
            copies[-1].start()
        else:
            note = notes[at // MOVE]
            for g in range(heads):
                note[m : m + 1, g * HD : (g + 1) * HD] = attended[at][g : g + 1, :]
            note[m : m + 1, heads * HD :] = residual
    for copy in copies:
        copy.wait()


def attend_kernel(
    slots, heads, meta, lengths_s, query, newkey, newvalue, cache_hbm, out,
    buffer, attended_rows, in_sem,
):
    low = meta[0] * slots

    def copy_in(c):
        span = pl.ds(c * CHUNK, CHUNK)
        return pltpu.make_async_copy(cache_hbm.at[span], buffer.at[span], in_sem.at[c])

    for c in range(slots // CHUNK):
        copy_in(c).start()
    for c in range(slots // CHUNK):
        copy_in(c).wait()
        span = list(range(c * CHUNK, (c + 1) * CHUNK))
        positions = [lengths_s[low + s] for s in span]
        for s, p in zip(span, positions):
            put_row(buffer, s, p, newkey[s : s + 1, :], newvalue[s : s + 1, :])
        got = attend(
            buffer, span, positions, [query[s * GROUP : (s + 1) * GROUP, :] for s in span]
        )
        for s, rows in zip(span, got):
            attended_rows[s * GROUP : (s + 1) * GROUP, :] = rows
    for g in range(heads):
        out[:, g * HD : (g + 1) * HD] = attended_rows[pl.ds(g, slots, stride=GROUP), :].astype(BF16)


def project_out(attended, wo, residual, own, sends, me_tp, peers_tp):
    shard = own.shape[1]
    for k in list(range(peers_tp - 1, 0, -1)) + [0]:
        column = pl.multiple_of(jnp.bitwise_xor(me_tp, k) * shard, shard)
        part = jnp.dot(attended, wo[:, pl.ds(column, shard)], preferred_element_type=F32)
        if k == 0:
            own[...] = residual + part
        else:
            sends[k - 1][...] = part.astype(BF16)


def out_kernel(
    peers, peers_tp, meta, plan, attended, wo, hidden, box_hbm, *rest,
):
    notes, rest = rest[: peers - 2], rest[peers - 2 :]
    own, sends, (tail, sem) = rest[0], rest[1:peers_tp], rest[peers_tp:]
    shard = own.shape[1]
    cap = box_hbm.shape[2] - NOTE
    copy = pltpu.make_async_copy(box_hbm.at[:, 0, pl.ds(cap, NOTE), :], tail, sem.at[0])
    copy.start()
    rows = attended[...].astype(F32)
    heads = rows.shape[1] // HD
    column = pl.multiple_of(meta[1] * shard, shard)
    residual = hidden[:, pl.ds(column, shard)].astype(F32)
    row_index = lax.broadcasted_iota(I32, rows.shape, 0)
    residual_index = lax.broadcasted_iota(I32, residual.shape, 0)
    copy.wait()
    for at in range((peers - 1) * MOVE):
        m = at % MOVE
        if at < MOVE:
            blocks = tail[m].astype(F32)
            blocks = [blocks[b : b + 1, :] for b in range(heads + shard // HD)]
            note = jnp.concatenate(blocks, axis=1)
        else:
            note = notes[at // MOVE - 1][m : m + 1, :]
        rows = jnp.where(row_index == plan[at], note[:, : heads * HD], rows)
        residual = jnp.where(residual_index == plan[at], note[:, heads * HD :], residual)
    project_out(rows.astype(BF16), wo, residual, own, sends, meta[1], peers_tp)


def pack_kernel(slots, meta, lengths_s, plan, newkey, newvalue, cache_hbm, _own, *rest):
    boxes, (leaving, in_sem, out_sem) = rest[:-3], rest[-3:]
    moving = plan.shape[0] // 2
    send_slots = [plan[moving + at] for at in range(MOVE, moving)]
    packs = [
        pltpu.make_async_copy(cache_hbm.at[slot], leaving.at[i], in_sem.at[i])
        for i, slot in enumerate(send_slots)
    ]
    for pack in packs:
        pack.start()
    for pack in packs:
        pack.wait()
    for i, slot in enumerate(send_slots):
        put_row(
            leaving, i, lengths_s[meta[0] * slots + slot],
            newkey[pl.ds(slot, 1), :], newvalue[pl.ds(slot, 1), :],
        )
    outs = [
        pltpu.make_async_copy(leaving.at[pl.ds(k * MOVE, MOVE)], out, out_sem.at[k])
        for k, out in enumerate(boxes)
    ]
    for out in outs:
        out.start()
    for out in outs:
        out.wait()


def sum_kernel(own, *rest):
    total = own[...]
    for part in rest[:-1]:
        total = total + part[...].astype(F32)
    rest[-1][...] = total.astype(BF16)


def load_slots(slots, peers, cache_hbm, box_hbm, buffer, in_sem):
    copies = []
    for c in range(slots // CHUNK):
        span = pl.ds(c * CHUNK, CHUNK)
        copies.append(pltpu.make_async_copy(cache_hbm.at[span], buffer.at[span], in_sem.at[c]))
    for k in range(peers - 1):
        copies.append(
            pltpu.make_async_copy(
                box_hbm[k].at[:, :, pl.ds(0, cache_hbm.shape[2]), :],
                buffer.at[pl.ds(slots + k * MOVE, MOVE)],
                in_sem.at[slots // CHUNK + k],
            )
        )
    return copies


def map_places(slots, peers, plan, place):
    for s in range(slots):
        place[s] = s
    for at in range((peers - 1) * MOVE):
        taker = plan[at]

        @pl.when(taker >= 0)
        def _():
            place[taker] = slots + at


def second_kernel(
    peers, peers_tp, slots, heads,
    meta, source_s, lengths_s, plan, gain, cos_ref, sin_ref, newkey1, newvalue1,
    wq, wkv, wo, cache_hbm, *rest,
):
    blocks, rest = rest[:peers_tp], rest[peers_tp:]
    box_hbm, rest = rest[: peers - 1], rest[peers - 1 :]
    newkey, newvalue, own = rest[:3]
    sends, rest = rest[3 : 2 + peers_tp], rest[2 + peers_tp :]
    (normed3, spread, cos_rows, sin_rows, buffer, query_rows, attended_rows, place,
     in_sem) = rest
    me, me_tp = meta[0], meta[1]
    low = me * slots
    width = gain.shape[1]
    shard = own.shape[1]
    cache_copies = load_slots(slots, peers, cache_hbm, box_hbm, buffer, in_sem)
    for copy in cache_copies[::-1]:
        copy.start()

    map_places(slots, peers, plan, place)
    firsts = [jnp.bitwise_xor(me_tp, k) for k in range(peers_tp)]
    norm_into(
        normed3,
        [block[...].astype(F32) for block in blocks],
        [gain[:, pl.ds(pl.multiple_of(first * shard, shard), shard)] for first in firsts],
        [first * (shard // HD) for first in firsts],
        width,
    )
    spread_normed(normed3, spread, slots, width)
    lengths = [lengths_s[source_s[low + s]] for s in range(slots)]
    gather_angles(lambda s: lengths[s] + 1, slots, cos_ref, sin_ref, cos_rows, sin_rows)
    query, key, value = project(normed3, spread, wq, wkv, slots, width)
    cosine, sine = cos_rows[...], sin_rows[...]
    query_rows[...] = jnp.zeros(query_rows.shape, F32)
    for g in range(heads):
        turned = turn(query[:, g * HD : (g + 1) * HD], cosine, sine)
        query_rows[pl.ds(g, slots, stride=GROUP), :] = turned.astype(BF16).astype(F32)
    newkey[...] = turn(key, cosine, sine).astype(BF16).astype(F32)
    newvalue[...] = value.astype(BF16).astype(F32)

    for copy in cache_copies[::-1]:
        copy.wait()
    for c in range(slots // CHUNK):
        span = list(range(c * CHUNK, (c + 1) * CHUNK))
        places = [place[s] for s in span]
        for s, at in zip(span, places):
            first = jnp.where(at < slots, lengths[s], -1)
            put_row(buffer, at, first, newkey1[s : s + 1, :], newvalue1[s : s + 1, :])
            put_row(buffer, at, lengths[s] + 1, newkey[s : s + 1, :], newvalue[s : s + 1, :])
        got = attend(
            buffer, places, [lengths[s] + 1 for s in span],
            [query_rows[s * GROUP : (s + 1) * GROUP, :] for s in span],
        )
        for s, rows in zip(span, got):
            attended_rows[s * GROUP : (s + 1) * GROUP, :] = rows
    attended = jnp.concatenate(
        [attended_rows[pl.ds(g, slots, stride=GROUP), :].astype(BF16) for g in range(heads)], axis=1
    )
    project_out(attended, wo, blocks[0][...].astype(F32), own, sends, me_tp, peers_tp)


def cache_kernel(
    peers, slots, meta, source_s, lengths_s, plan, newkey1, newvalue1, newkey2, newvalue2,
    cache_hbm, *rest,
):
    box_hbm, rest = rest[: peers - 1], rest[peers - 1 :]
    out_hbm, buffer, place, in_sem, out_sem = rest
    low = meta[0] * slots
    cache_copies = load_slots(slots, peers, cache_hbm, box_hbm, buffer, in_sem)
    for copy in cache_copies:
        copy.start()
    map_places(slots, peers, plan, place)
    chunks = slots // CHUNK
    for copy in cache_copies[chunks:]:
        copy.wait()
    outs = []
    for c in range(chunks):
        cache_copies[c].wait()
        for s in range(c * CHUNK, (c + 1) * CHUNK):
            at = place[s]
            length = lengths_s[source_s[low + s]]
            first = jnp.where(at < slots, length, -1)
            put_row(buffer, at, first, newkey1[s : s + 1, :], newvalue1[s : s + 1, :])
            put_row(buffer, at, length + 1, newkey2[s : s + 1, :], newvalue2[s : s + 1, :])
            copy = pltpu.make_async_copy(buffer.at[at], out_hbm.at[s], out_sem.at[s])
            copy.start()
            outs.append(copy)
    for copy in outs:
        copy.wait()


def join_kernel(peers_tp, meta, *rest):
    blocks, out, sem = rest[:-2], rest[-2], rest[-1]
    shard = blocks[0].shape[1]
    copies = []
    for k, block in enumerate(blocks):
        column = pl.multiple_of(jnp.bitwise_xor(meta[1], k) * shard, shard)
        copies.append(pltpu.make_async_copy(block, out.at[:, pl.ds(column, shard)], sem.at[k]))
        copies[-1].start()
    for copy in copies:
        copy.wait()


def swapped(x, axis, size, k):
    return lax.ppermute(x, axis, [(i, i ^ k) for i in range(size)])


def local(
    tables, kv_cache, hidden, lengths, source, norm_gain, query_weight, keyval_weight, out_weight
):
    peers, peers_tp = lax.axis_size("inst"), lax.axis_size("tp")
    slots, cap = kv_cache.shape[0], kv_cache.shape[2]
    width = hidden.shape[1]
    heads = query_weight.shape[1] // HD
    shard = width // peers_tp
    others, moving = peers - 1, (peers - 1) * MOVE
    blocks = width // HD
    meta = jnp.stack([lax.axis_index("inst"), lax.axis_index("tp")]).astype(I32)
    gain = norm_gain.reshape(1, width)
    wkv = keyval_weight.reshape(2 * width, HD)
    cosine, sine = (jnp.asarray(table) for table in tables)
    row32 = jax.ShapeDtypeStruct((slots, HD), F32)
    note_width = heads * HD + shard
    dma = pltpu.SemaphoreType.DMA
    weights = [
        pltpu.VMEM(query_weight.shape, BF16),
        pltpu.VMEM(wkv.shape, BF16),
    ]
    stages = [
        pltpu.VMEM((blocks, slots, HD), BF16),
        pltpu.VMEM((blocks, 2 * slots, 2 * HD), BF16),
        pltpu.VMEM((slots, HD), F32),
        pltpu.VMEM((slots, HD), F32),
    ]
    flops = 2 * slots * width * (heads + 2) * HD
    cache_bytes = kv_cache.size * 2

    query, newkey1, newvalue1, plan, *notes = pl.pallas_call(
        functools.partial(first_kernel, peers, slots, heads, shard),
        out_shape=[
            jax.ShapeDtypeStruct((slots * GROUP, HD), F32),
            row32,
            row32,
            jax.ShapeDtypeStruct((2 * moving,), I32),
        ]
        + [jax.ShapeDtypeStruct((MOVE, 2, cap + NOTE, HD), BF16)]
        + [jax.ShapeDtypeStruct((MOVE, note_width), F32)] * (others - 1),
        in_specs=[SMEM] + [HBM] * 9,
        out_specs=[VMEM] * 3 + [SMEM, ANY] + [VMEM] * (others - 1),
        scratch_shapes=weights
        + stages
        + [
            pltpu.VMEM((moving,) + kv_cache.shape[1:], BF16),
            pltpu.VMEM((slots, width), F32),
            pltpu.SMEM((1, source.shape[0]), I32),
            pltpu.SMEM((1, source.shape[0]), I32),
            pltpu.VMEM((1, source.shape[0]), I32),
            pltpu.VMEM(hidden.shape, BF16),
            pltpu.VMEM((1, width), F32),
            pltpu.VMEM(cosine.shape, F32),
            pltpu.VMEM(cosine.shape, F32),
            pltpu.VMEM((MOVE, NOTE, HD), BF16),
            dma((7,)),
            dma((4,)),
            dma((4,)),
            dma((moving,)),
            dma((1 + MOVE,)),
        ],
        compiler_params=params(24),
        cost_estimate=cost(flops, (query_weight.size + wkv.size) * 2),
        name="first_step",
    )(meta, *(
        pltpu.with_memory_space_constraint(x, pltpu.HBM)
        for x in (source.reshape(1, -1), lengths.reshape(1, -1), hidden, gain, cosine, sine,
                  query_weight, wkv, kv_cache)
    ))
    got_notes = [swapped(note, "inst", peers, k + 1) for k, note in enumerate(notes)]

    attended = pl.pallas_call(
        functools.partial(attend_kernel, slots, heads),
        out_shape=jax.ShapeDtypeStruct((slots, heads * HD), BF16),
        in_specs=[SMEM] * 2 + [VMEM] * 3 + [ANY],
        out_specs=VMEM,
        scratch_shapes=[
            pltpu.VMEM(kv_cache.shape, BF16),
            pltpu.VMEM((slots * GROUP, HD), F32),
            dma((slots // CHUNK,)),
        ],
        compiler_params=params(24),
        cost_estimate=cost(4 * slots * cap * HD * heads, cache_bytes),
        name="attention",
    )(meta, lengths, query, newkey1, newvalue1, kv_cache)

    sent = [jax.ShapeDtypeStruct((slots, shard), F32)]
    sent += [jax.ShapeDtypeStruct((slots, shard), BF16)] * (peers_tp - 1)
    own, *sends = pl.pallas_call(
        functools.partial(out_kernel, peers, peers_tp),
        out_shape=sent,
        in_specs=[SMEM] * 2 + [VMEM] * 3 + [ANY] + [VMEM] * (others - 1),
        out_specs=[VMEM] * peers_tp,
        scratch_shapes=[pltpu.VMEM((MOVE, NOTE, HD), BF16), dma((1,))],
        compiler_params=params(16),
        cost_estimate=cost(2 * slots * width * heads * HD, out_weight.size * 2),
        name="out_projection",
    )(meta, plan, attended, out_weight, hidden, *got_notes)
    boxes = pl.pallas_call(
        functools.partial(pack_kernel, slots),
        out_shape=[jax.ShapeDtypeStruct((MOVE,) + kv_cache.shape[1:], BF16)] * (others - 1),
        in_specs=[SMEM] * 3 + [VMEM] * 2 + [ANY] * 2,
        out_specs=[ANY] * (others - 1),
        scratch_shapes=[
            pltpu.VMEM((moving - MOVE,) + kv_cache.shape[1:], BF16),
            dma((moving - MOVE,)),
            dma((others - 1,)),
        ],
        compiler_params=params(16),
        cost_estimate=cost(1, cache_bytes),
        name="pack",
    )(meta, lengths, plan, newkey1, newvalue1, kv_cache, own)
    got_boxes = got_notes[:1] + [swapped(box, "inst", peers, k + 2) for k, box in enumerate(boxes)]

    def summed(own, sends):
        got = [swapped(sends[k - 1], "tp", peers_tp, k) for k in range(peers_tp - 1, 0, -1)]
        shard_rows = pl.pallas_call(
            sum_kernel,
            out_shape=jax.ShapeDtypeStruct((slots, shard), BF16),
            in_specs=[VMEM] * peers_tp,
            out_specs=VMEM,
            compiler_params=params(16),
            name="sum_terms",
        )(own, *got)
        blocks = {0: shard_rows}
        far = peers_tp // 2
        while far:
            blocks |= {k + far: swapped(blocks[k], "tp", peers_tp, far) for k in blocks}
            far //= 2
        return [blocks[k] for k in range(peers_tp)]

    pieces = summed(own, sends)

    newkey2, newvalue2, own, *sends = pl.pallas_call(
        functools.partial(second_kernel, peers, peers_tp, slots, heads),
        out_shape=[row32, row32] + sent,
        in_specs=[SMEM] * 4 + [VMEM] * 8 + [ANY] + [VMEM] * peers_tp + [ANY] * others,
        out_specs=[VMEM] * (2 + peers_tp),
        scratch_shapes=stages
        + [
            pltpu.VMEM((slots + moving,) + kv_cache.shape[1:], BF16),
            pltpu.VMEM((slots * GROUP, HD), F32),
            pltpu.VMEM((slots * GROUP, HD), F32),
            pltpu.SMEM((slots,), I32),
            dma((slots // CHUNK + others,)),
        ],
        compiler_params=params(32),
        cost_estimate=cost(3 * flops, cache_bytes + (query_weight.size + wkv.size) * 4),
        name="second_step",
    )(meta, source, lengths, plan, gain, cosine, sine, newkey1, newvalue1, query_weight, wkv,
      out_weight, kv_cache, *pieces, *got_boxes)

    pieces = summed(own, sends)
    final_cache = pl.pallas_call(
        functools.partial(cache_kernel, peers, slots),
        out_shape=jax.ShapeDtypeStruct(kv_cache.shape, BF16),
        in_specs=[SMEM] * 4 + [VMEM] * 4 + [ANY] * peers,
        out_specs=ANY,
        scratch_shapes=[
            pltpu.VMEM((slots + moving,) + kv_cache.shape[1:], BF16),
            pltpu.SMEM((slots,), I32),
            dma((slots // CHUNK + others,)),
            dma((slots,)),
        ],
        compiler_params=params(24),
        cost_estimate=cost(0, 2 * cache_bytes),
        name="write_cache",
    )(meta, source, lengths, plan, newkey1, newvalue1, newkey2, newvalue2, kv_cache, *got_boxes)
    final_hidden = pl.pallas_call(
        functools.partial(join_kernel, peers_tp),
        out_shape=jax.ShapeDtypeStruct(hidden.shape, BF16),
        in_specs=[SMEM] + [ANY] * peers_tp,
        out_specs=ANY,
        scratch_shapes=[dma((peers_tp,))],
        compiler_params=params(16),
        name="join",
    )(meta, *pieces)
    return (final_hidden, final_cache)


def solution(mesh):
    def whole(kv_cache, *rest):
        tables = angle_tables(kv_cache.shape[2])
        return jax.shard_map(
            functools.partial(local, tables),
            mesh=mesh,
            in_specs=(
                P(("groups", "inst"), None, None, "tp"),
                P(("groups", "inst"), None),
                P("groups"),
                P("groups"),
                P(),
                P(None, "tp"),
                P(None, None, "tp"),
                P("tp", None),
            ),
            out_specs=(P(("groups", "inst"), None), P(("groups", "inst"), None, None, "tp")),
            check_vma=False,
        )(kv_cache, *rest)

    return whole
```

```python
import functools

import jax
import jax.numpy as jnp
import numpy as np
from jax import lax
from jax.experimental import pallas as pl
from jax.experimental.pallas import tpu as pltpu
from jax.sharding import PartitionSpec as P

MOVE = 2
EPS = 1e-05
THETA = 500000.0
HD = 128
GROUP = 8
PIECE = 16
CHUNK = 8
BATCH = 16
NOTE = 16

F32 = jnp.float32
BF16 = jnp.bfloat16
I32 = jnp.int32

ANY = pl.BlockSpec(memory_space=pl.ANY)
VMEM = pl.BlockSpec(memory_space=pltpu.VMEM)
SMEM = pl.BlockSpec(memory_space=pltpu.SMEM)
HBM = pl.BlockSpec(memory_space=pltpu.HBM)


def params(mib):
    return pltpu.CompilerParams(vmem_limit_bytes=mib * 1024 * 1024)


def cost(flops, nbytes):
    return pl.CostEstimate(flops=flops, bytes_accessed=nbytes, transcendentals=0)


def angle_tables(positions):
    frequency = THETA ** (-(np.arange(HD // 2, dtype=np.float64) * 2.0) / HD)
    angles = np.arange(positions, dtype=np.float64)[:, None] * frequency[None, :]
    cosine = np.concatenate([np.cos(angles), np.cos(angles)], axis=-1)
    sine = np.concatenate([-np.sin(angles), np.sin(angles)], axis=-1)
    return cosine.astype(np.float32), sine.astype(np.float32)


def turn(x, cosine, sine):
    return x * cosine + pltpu.roll(x, HD // 2, 1) * sine


def gather_angles(position_of, slots, cos_ref, sin_ref, cos_rows, sin_rows):
    for s in range(slots):
        p = position_of(s)
        cos_rows[s : s + 1, :] = cos_ref[pl.ds(p, 1), :]
        sin_rows[s : s + 1, :] = sin_ref[pl.ds(p, 1), :]


def spread_normed(normed3, spread, slots, width):
    blocks = width // HD
    row = lax.broadcasted_iota(I32, (HD, 4 * HD), 0)
    col = lax.broadcasted_iota(I32, (HD, 4 * HD), 1)
    goal = jnp.where(col < 2 * HD, 2 * row, 2 * row + 1 + 2 * HD)
    places = jnp.where(col == goal, 1.0, 0.0).astype(BF16)
    spread_all = jnp.dot(
        normed3[...].reshape(blocks * slots, HD), places, preferred_element_type=F32
    ).astype(BF16)
    spread[:, 0:slots, :] = spread_all[:, : 2 * HD].reshape(blocks, slots, 2 * HD)
    spread[:, slots:, :] = spread_all[:, 2 * HD :].reshape(blocks, slots, 2 * HD)


def project(normed3, spread, wq, wkv, slots, width, wq_copies=(), wkv_copies=()):
    pieces = max(len(wq_copies), 1)
    depth = width // pieces
    query = None
    pair = None
    for c in range(pieces):
        for copy in wkv_copies[c : c + 1]:
            copy.wait()
        for b in range(c * depth // HD, (c + 1) * depth // HD):
            part = jnp.dot(
                spread[b], wkv[b * 2 * HD : (b + 1) * 2 * HD, :], preferred_element_type=F32
            )
            pair = part if pair is None else pair + part
    for c in range(pieces):
        for copy in wq_copies[c : c + 1]:
            copy.wait()
        for b in range(c * depth // (2 * HD), (c + 1) * depth // (2 * HD)):
            block = jnp.concatenate([normed3[2 * b], normed3[2 * b + 1]], axis=1)
            part = jnp.dot(
                block, wq[b * 2 * HD : (b + 1) * 2 * HD, :], preferred_element_type=F32
            )
            query = part if query is None else query + part
    return query, pair[:slots], pair[slots:]


def weight_copies(src, dst, sem, pieces):
    depth = src.shape[0] // pieces
    copies = [
        pltpu.make_async_copy(
            src.at[pl.ds(c * depth, depth)], dst.at[pl.ds(c * depth, depth)], sem.at[c]
        )
        for c in range(pieces)
    ]
    return copies


def put_row(cache, place, p, key_row, value_row):
    base = pl.multiple_of((jnp.maximum(p, 0) // PIECE) * PIECE, PIECE)
    hit = lax.broadcasted_iota(I32, (PIECE, HD), 0) + base == p
    for which, new in ((0, key_row), (1, value_row)):
        old = cache[place, which, pl.ds(base, PIECE), :].astype(F32)
        cache[place, which, pl.ds(base, PIECE), :] = jnp.where(hit, new, old).astype(BF16)


def attend(cache, places, positions, query_rows):
    cap = cache.shape[2]
    col = lax.broadcasted_iota(I32, (GROUP, cap), 1)
    scores = [
        lax.dot_general(
            rows.astype(BF16),
            cache[place, 0],
            (((1,), (1,)), ((), ())),
            preferred_element_type=F32,
        )
        for place, rows in zip(places, query_rows)
    ]
    probs = []
    for score, p in zip(scores, positions):
        score = jnp.where(col <= p, score * HD**-0.5, -jnp.inf)
        weight = jnp.exp(score - jnp.max(score, axis=-1, keepdims=True))
        weight = weight / jnp.sum(weight, axis=-1, keepdims=True)
        probs.append(weight.astype(BF16))
    return [
        jnp.dot(prob, cache[place, 1], preferred_element_type=F32)
        for place, prob in zip(places, probs)
    ]


def norm_into(normed3, pieces, gains, firsts, total_width):
    square = None
    for piece in pieces:
        part = jnp.sum(piece * piece, axis=-1, keepdims=True)
        square = part if square is None else square + part
    factor = lax.rsqrt(square / total_width + EPS)
    for piece, gain, first in zip(pieces, gains, firsts):
        normed = (piece * factor * gain).astype(BF16)
        for i in range(piece.shape[1] // HD):
            normed3[first + i] = normed[:, i * HD : (i + 1) * HD]


def first_kernel(
    peers, slots, heads, shard,
    meta, source_hbm, lengths_hbm, hidden_hbm, gain_hbm, cos_hbm, sin_hbm, wq_hbm, wkv_hbm,
    cache_hbm, query_out, newkey_out, newvalue_out, plan, *rest,
):
    others = peers - 1
    moving = others * MOVE
    cache, box, notes = rest[0], rest[1], (None,) + rest[2 : others + 1]
    (wq, wkv, normed3, spread, cos_rows, sin_rows, leaving, hidden32, source_s, lengths_s, source_v,
     hidden, gain, cos_ref, sin_ref, tail, small_sem, wq_sem, wkv_sem, in_sem,
     box_sem, cache_sem) = rest[others + 1 :]
    width = hidden.shape[1]
    me, me_tp = meta[0], meta[1]
    wq_copies = weight_copies(wq_hbm, wq, wq_sem, 4)
    wkv_copies = weight_copies(wkv_hbm, wkv, wkv_sem, 4)
    small = [
        pltpu.make_async_copy(src, dst, small_sem.at[i])
        for i, (src, dst) in enumerate((
            (source_hbm, source_v), (source_hbm, source_s), (lengths_hbm, lengths_s),
            (hidden_hbm, hidden), (gain_hbm, gain), (cos_hbm, cos_ref), (sin_hbm, sin_ref),
        ))
    ]
    for copy in small + wkv_copies + wq_copies:
        copy.start()
    loads = [
        pltpu.make_async_copy(
            cache_hbm.at[pl.ds(c * CHUNK, CHUNK)], cache.at[pl.ds(c * CHUNK, CHUNK)], cache_sem.at[c]
        )
        for c in range(slots // CHUNK)
    ]
    for copy in small:
        copy.wait()
    wide = hidden[...].astype(F32)
    hidden32[...] = wide
    norm_into(normed3, [wide], [gain[...]], [0], width)
    spread_normed(normed3, spread, slots, width)
    low = me * slots
    src = source_v[...]
    index = lax.broadcasted_iota(I32, src.shape, 1)
    mine_goes = (src >= low) & (src < low + slots)
    mine_comes = (index >= low) & (index < low + slots)
    index_f = index.astype(F32)
    send_slots = []
    for k in range(1, peers):
        other = jnp.bitwise_xor(me, k) * slots
        sent = mine_goes & (index >= other) & (index < other + slots)
        taken = mine_comes & (src >= other) & (src < other + slots)
        for m in range(MOVE):
            at = (k - 1) * MOVE + m
            if m == 0:
                j = jnp.min(jnp.where(sent, index_f, 1e6)).astype(I32)
                r = jnp.min(jnp.where(taken, index_f, 1e6)).astype(I32)
            else:
                j = jnp.max(jnp.where(sent, index_f, -1.0)).astype(I32)
                r = jnp.max(jnp.where(taken, index_f, -1.0)).astype(I32)
            known = (j >= 0) & (j < src.shape[1])
            slot = source_s[0, jnp.where(known, j, 0)] - low
            slot = jnp.where(known, slot, 0)
            send_slots.append(slot)
            plan[at] = jnp.where((r >= 0) & (r < src.shape[1]), r - low, -1)
            plan[moving + at] = slot
            pltpu.make_async_copy(cache_hbm.at[slot], leaving.at[at], in_sem.at[at]).start()
    for copy in loads:
        copy.start()

    gather_angles(lambda s: lengths_s[0, low + s], slots, cos_ref, sin_ref, cos_rows, sin_rows)
    query, key, value = project(
        normed3, spread, wq, wkv, slots, width, wq_copies, wkv_copies
    )
    cosine, sine = cos_rows[...], sin_rows[...]
    query_out[...] = jnp.zeros(query_out.shape, F32)
    for g in range(heads):
        turned = turn(query[:, g * HD : (g + 1) * HD], cosine, sine)
        query_out[pl.ds(g, slots, stride=GROUP), :] = turned.astype(BF16).astype(F32)
    newkey_out[...] = turn(key, cosine, sine).astype(BF16).astype(F32)
    newvalue_out[...] = value.astype(BF16).astype(F32)

    positions = [lengths_s[0, low + slot] for slot in send_slots]
    for at, slot in enumerate(send_slots):
        pltpu.make_async_copy(cache_hbm.at[slot], leaving.at[at], in_sem.at[at]).wait()
        put_row(
            leaving, at, positions[at],
            newkey_out[pl.ds(slot, 1), :], newvalue_out[pl.ds(slot, 1), :],
        )
    cap = leaving.shape[2]
    copies = [
        pltpu.make_async_copy(
            leaving.at[pl.ds(0, MOVE)], box.at[:, :, pl.ds(0, cap), :], box_sem.at[0]
        )
    ]
    copies[0].start()
    rows = [query_out[pl.ds(pl.multiple_of(slot * GROUP, GROUP), GROUP), :] for slot in send_slots]
    attended = attend(leaving, list(range(moving)), positions, rows)
    column = pl.multiple_of(me_tp * shard, shard)
    for at, slot in enumerate(send_slots):
        m = at % MOVE
        residual = hidden32[pl.ds(slot, 1), pl.ds(column, shard)]
        if at < MOVE:
            blocks = [attended[at][g : g + 1, :] for g in range(heads)]
            blocks += [residual[:, b * HD : (b + 1) * HD] for b in range(shard // HD)]
            blocks += [jnp.zeros((1, HD), F32)] * (NOTE - len(blocks))
            tail[m] = jnp.concatenate(blocks, axis=0).astype(BF16)
            copies.append(
                pltpu.make_async_copy(
                    tail.at[m], box.at[m, 0, pl.ds(cap, NOTE), :], box_sem.at[1 + m]
                )
            )
            copies[-1].start()
        else:
            note = notes[at // MOVE]
            for g in range(heads):
                note[m : m + 1, g * HD : (g + 1) * HD] = attended[at][g : g + 1, :]
            note[m : m + 1, heads * HD :] = residual
    for copy in copies + loads:
        copy.wait()


def attend_slots(cache, places, positions, query, attended_rows, heads):
    slots = len(places)
    for first in range(0, slots, BATCH):
        span = range(first, first + BATCH)
        got = attend(
            cache,
            [places[s] for s in span],
            [positions[s] for s in span],
            [query[s * GROUP : (s + 1) * GROUP, :] for s in span],
        )
        for s, rows in zip(span, got):
            attended_rows[s * GROUP : (s + 1) * GROUP, :] = rows
    return jnp.concatenate(
        [attended_rows[pl.ds(g, slots, stride=GROUP), :] for g in range(heads)], axis=1
    )


def attend_kernel(
    slots, heads, meta, lengths_s, query, newkey, newvalue, _, out, cache, attended_rows,
):
    low = meta[0] * slots
    positions = [lengths_s[low + s] for s in range(slots)]
    for s, p in enumerate(positions):
        put_row(cache, s, p, newkey[s : s + 1, :], newvalue[s : s + 1, :])
    out[...] = attend_slots(
        cache, list(range(slots)), positions, query, attended_rows, heads
    ).astype(BF16)


def project_out(attended, wo, residual, own, sends, me_tp, peers_tp):
    shard = own.shape[1]
    for k in list(range(peers_tp - 1, 0, -1)) + [0]:
        column = pl.multiple_of(jnp.bitwise_xor(me_tp, k) * shard, shard)
        part = jnp.dot(attended, wo[:, pl.ds(column, shard)], preferred_element_type=F32)
        if k == 0:
            own[...] = residual + part
        else:
            sends[k - 1][...] = part.astype(BF16)


def out_kernel(
    peers, peers_tp, meta, plan, attended, wo, hidden, box_hbm, *rest,
):
    notes, rest = rest[: peers - 2], rest[peers - 2 :]
    own, sends, (tail, sem) = rest[0], rest[1:peers_tp], rest[peers_tp:]
    shard = own.shape[1]
    cap = box_hbm.shape[2] - NOTE
    copy = pltpu.make_async_copy(box_hbm.at[:, 0, pl.ds(cap, NOTE), :], tail, sem.at[0])
    copy.start()
    rows = attended[...].astype(F32)
    heads = rows.shape[1] // HD
    column = pl.multiple_of(meta[1] * shard, shard)
    residual = hidden[:, pl.ds(column, shard)].astype(F32)
    row_index = lax.broadcasted_iota(I32, rows.shape, 0)
    residual_index = lax.broadcasted_iota(I32, residual.shape, 0)
    copy.wait()
    for at in range((peers - 1) * MOVE):
        m = at % MOVE
        if at < MOVE:
            blocks = tail[m].astype(F32)
            blocks = [blocks[b : b + 1, :] for b in range(heads + shard // HD)]
            note = jnp.concatenate(blocks, axis=1)
        else:
            note = notes[at // MOVE - 1][m : m + 1, :]
        rows = jnp.where(row_index == plan[at], note[:, : heads * HD], rows)
        residual = jnp.where(residual_index == plan[at], note[:, heads * HD :], residual)
    project_out(rows.astype(BF16), wo, residual, own, sends, meta[1], peers_tp)


def pack_kernel(plan, cache, _own, *rest):
    boxes, out_sem = rest[:-1], rest[-1]
    moving = plan.shape[0] // 2
    packs = [
        pltpu.make_async_copy(
            cache.at[plan[moving + at]], boxes[at // MOVE - 1].at[at % MOVE], out_sem.at[at - MOVE]
        )
        for at in range(MOVE, moving)
    ]
    for pack in packs:
        pack.start()
    for pack in packs:
        pack.wait()


def sum_kernel(own, *rest):
    total = own[...]
    for part in rest[:-1]:
        total = total + part[...].astype(F32)
    rest[-1][...] = total.astype(BF16)


def map_places(slots, peers, plan, place):
    for s in range(slots):
        place[s] = s
    for at in range((peers - 1) * MOVE):
        taker = plan[at]

        @pl.when(taker >= 0)
        def _():
            place[taker] = slots + at


def second_kernel(
    peers, peers_tp, slots, heads,
    meta, source_s, lengths_s, plan, gain, cos_ref, sin_ref, wq, wkv, wo, _, *rest,
):
    blocks, rest = rest[:peers_tp], rest[peers_tp:]
    box_hbm, rest = rest[: peers - 1], rest[peers - 1 :]
    own, sends, cache = rest[0], rest[1:peers_tp], rest[peers_tp]
    (normed3, spread, cos_rows, sin_rows, query_rows, attended_rows, place,
     in_sem) = rest[peers_tp + 1 :]
    me, me_tp = meta[0], meta[1]
    low = me * slots
    width = gain.shape[1]
    shard = own.shape[1]
    loads = [
        pltpu.make_async_copy(
            box.at[:, :, pl.ds(0, cache.shape[2]), :],
            cache.at[pl.ds(slots + k * MOVE, MOVE)],
            in_sem.at[k],
        )
        for k, box in enumerate(box_hbm)
    ]
    for copy in loads:
        copy.start()

    map_places(slots, peers, plan, place)
    firsts = [jnp.bitwise_xor(me_tp, k) for k in range(peers_tp)]
    norm_into(
        normed3,
        [block[...].astype(F32) for block in blocks],
        [gain[:, pl.ds(pl.multiple_of(first * shard, shard), shard)] for first in firsts],
        [first * (shard // HD) for first in firsts],
        width,
    )
    spread_normed(normed3, spread, slots, width)
    positions = [lengths_s[source_s[low + s]] + 1 for s in range(slots)]
    gather_angles(lambda s: positions[s], slots, cos_ref, sin_ref, cos_rows, sin_rows)
    query, key, value = project(normed3, spread, wq, wkv, slots, width)
    cosine, sine = cos_rows[...], sin_rows[...]
    query_rows[...] = jnp.zeros(query_rows.shape, F32)
    for g in range(heads):
        turned = turn(query[:, g * HD : (g + 1) * HD], cosine, sine)
        query_rows[pl.ds(g, slots, stride=GROUP), :] = turned.astype(BF16).astype(F32)
    newkey = turn(key, cosine, sine).astype(BF16).astype(F32)
    newvalue = value.astype(BF16).astype(F32)

    for copy in loads:
        copy.wait()
    places = [place[s] for s in range(slots)]
    for s, (at, p) in enumerate(zip(places, positions)):
        put_row(cache, at, p, newkey[s : s + 1, :], newvalue[s : s + 1, :])
    attended = attend_slots(cache, places, positions, query_rows, attended_rows, heads)
    project_out(
        attended.astype(BF16), wo, blocks[0][...].astype(F32), own, sends, me_tp, peers_tp
    )


def cache_kernel(peers, slots, plan, cache, out_hbm, place, out_sem):
    map_places(slots, peers, plan, place)
    copies = [
        pltpu.make_async_copy(cache.at[place[s]], out_hbm.at[s], out_sem.at[s])
        for s in range(slots)
    ]
    for copy in copies:
        copy.start()
    for copy in copies:
        copy.wait()


def join_kernel(peers_tp, meta, *rest):
    blocks, out, sem = rest[:-2], rest[-2], rest[-1]
    shard = blocks[0].shape[1]
    copies = []
    for k, block in enumerate(blocks):
        column = pl.multiple_of(jnp.bitwise_xor(meta[1], k) * shard, shard)
        copies.append(pltpu.make_async_copy(block, out.at[:, pl.ds(column, shard)], sem.at[k]))
        copies[-1].start()
    for copy in copies:
        copy.wait()


def swapped(x, axis, size, k):
    return lax.ppermute(x, axis, [(i, i ^ k) for i in range(size)])


def local(
    tables, kv_cache, hidden, lengths, source, norm_gain, query_weight, keyval_weight, out_weight
):
    peers, peers_tp = lax.axis_size("inst"), lax.axis_size("tp")
    slots, cap = kv_cache.shape[0], kv_cache.shape[2]
    width = hidden.shape[1]
    heads = query_weight.shape[1] // HD
    shard = width // peers_tp
    others, moving = peers - 1, (peers - 1) * MOVE
    blocks = width // HD
    meta = jnp.stack([lax.axis_index("inst"), lax.axis_index("tp")]).astype(I32)
    gain = norm_gain.reshape(1, width)
    wkv = keyval_weight.reshape(2 * width, HD)
    cosine, sine = (jnp.asarray(table) for table in tables)
    row32 = jax.ShapeDtypeStruct((slots, HD), F32)
    note_width = heads * HD + shard
    dma = pltpu.SemaphoreType.DMA
    weights = [
        pltpu.VMEM(query_weight.shape, BF16),
        pltpu.VMEM(wkv.shape, BF16),
    ]
    stages = [
        pltpu.VMEM((blocks, slots, HD), BF16),
        pltpu.VMEM((blocks, 2 * slots, 2 * HD), BF16),
        pltpu.VMEM((slots, HD), F32),
        pltpu.VMEM((slots, HD), F32),
    ]
    flops = 2 * slots * width * (heads + 2) * HD
    cache_bytes = kv_cache.size * 2
    held = jax.ShapeDtypeStruct((slots + moving,) + kv_cache.shape[1:], BF16)

    query, newkey1, newvalue1, plan, cache, *notes = pl.pallas_call(
        functools.partial(first_kernel, peers, slots, heads, shard),
        out_shape=[
            jax.ShapeDtypeStruct((slots * GROUP, HD), F32),
            row32,
            row32,
            jax.ShapeDtypeStruct((2 * moving,), I32),
            held,
        ]
        + [jax.ShapeDtypeStruct((MOVE, 2, cap + NOTE, HD), BF16)]
        + [jax.ShapeDtypeStruct((MOVE, note_width), F32)] * (others - 1),
        in_specs=[SMEM] + [HBM] * 9,
        out_specs=[VMEM] * 3 + [SMEM, VMEM, ANY] + [VMEM] * (others - 1),
        scratch_shapes=weights
        + stages
        + [
            pltpu.VMEM((moving,) + kv_cache.shape[1:], BF16),
            pltpu.VMEM((slots, width), F32),
            pltpu.SMEM((1, source.shape[0]), I32),
            pltpu.SMEM((1, source.shape[0]), I32),
            pltpu.VMEM((1, source.shape[0]), I32),
            pltpu.VMEM(hidden.shape, BF16),
            pltpu.VMEM((1, width), F32),
            pltpu.VMEM(cosine.shape, F32),
            pltpu.VMEM(cosine.shape, F32),
            pltpu.VMEM((MOVE, NOTE, HD), BF16),
            dma((7,)),
            dma((4,)),
            dma((4,)),
            dma((moving,)),
            dma((1 + MOVE,)),
            dma((slots // CHUNK,)),
        ],
        compiler_params=params(24),
        cost_estimate=cost(flops, (query_weight.size + wkv.size) * 2),
        name="first_step",
    )(meta, *(
        pltpu.with_memory_space_constraint(x, pltpu.HBM)
        for x in (source.reshape(1, -1), lengths.reshape(1, -1), hidden, gain, cosine, sine,
                  query_weight, wkv, kv_cache)
    ))
    got_notes = [swapped(note, "inst", peers, k + 1) for k, note in enumerate(notes)]

    attended, cache = pl.pallas_call(
        functools.partial(attend_kernel, slots, heads),
        out_shape=[jax.ShapeDtypeStruct((slots, heads * HD), BF16), held],
        in_specs=[SMEM] * 2 + [VMEM] * 4,
        out_specs=[VMEM] * 2,
        scratch_shapes=[pltpu.VMEM((slots * GROUP, HD), F32)],
        input_output_aliases={5: 1},
        compiler_params=params(12),
        cost_estimate=cost(4 * slots * cap * HD * heads, cache_bytes),
        name="attention",
    )(meta, lengths, query, newkey1, newvalue1, cache)

    sent = [jax.ShapeDtypeStruct((slots, shard), F32)]
    sent += [jax.ShapeDtypeStruct((slots, shard), BF16)] * (peers_tp - 1)
    own, *sends = pl.pallas_call(
        functools.partial(out_kernel, peers, peers_tp),
        out_shape=sent,
        in_specs=[SMEM] * 2 + [VMEM] * 3 + [ANY] + [VMEM] * (others - 1),
        out_specs=[VMEM] * peers_tp,
        scratch_shapes=[pltpu.VMEM((MOVE, NOTE, HD), BF16), dma((1,))],
        compiler_params=params(16),
        cost_estimate=cost(2 * slots * width * heads * HD, out_weight.size * 2),
        name="out_projection",
    )(meta, plan, attended, out_weight, hidden, *got_notes)
    boxes = pl.pallas_call(
        pack_kernel,
        out_shape=[jax.ShapeDtypeStruct((MOVE,) + kv_cache.shape[1:], BF16)] * (others - 1),
        in_specs=[SMEM, VMEM, ANY],
        out_specs=[ANY] * (others - 1),
        scratch_shapes=[dma((moving - MOVE,))],
        compiler_params=params(16),
        cost_estimate=cost(1, 1 * cache_bytes),
        name="pack",
    )(plan, cache, own)
    got_boxes = got_notes[:1] + [swapped(box, "inst", peers, k + 2) for k, box in enumerate(boxes)]

    def summed(own, sends, passed_on):
        got = [swapped(sends[k - 1], "tp", peers_tp, k) for k in range(peers_tp - 1, 0, -1)]
        shard_rows = pl.pallas_call(
            sum_kernel,
            out_shape=jax.ShapeDtypeStruct((slots, shard), BF16),
            in_specs=[VMEM] * peers_tp,
            out_specs=VMEM,
            compiler_params=params(16),
            name="sum_terms",
        )(own, *got)
        blocks = {0: shard_rows}
        if not passed_on:
            blocks |= {k: swapped(shard_rows, "tp", peers_tp, k) for k in range(1, peers_tp)}
        far = peers_tp // 2 if passed_on else 0
        while far:
            blocks |= {k + far: swapped(blocks[k], "tp", peers_tp, far) for k in blocks}
            far //= 2
        return [blocks[k] for k in range(peers_tp)]

    pieces = summed(own, sends, True)

    own, *sends, cache = pl.pallas_call(
        functools.partial(second_kernel, peers, peers_tp, slots, heads),
        out_shape=sent + [held],
        in_specs=[SMEM] * 4 + [VMEM] * (7 + peers_tp) + [ANY] * others,
        out_specs=[VMEM] * (1 + peers_tp),
        scratch_shapes=stages
        + [
            pltpu.VMEM((slots * GROUP, HD), F32),
            pltpu.VMEM((slots * GROUP, HD), F32),
            pltpu.SMEM((slots,), I32),
            dma((others,)),
        ],
        input_output_aliases={10: peers_tp},
        compiler_params=params(16),
        cost_estimate=cost(3 * flops, cache_bytes + (query_weight.size + wkv.size) * 4),
        name="second_step",
    )(meta, source, lengths, plan, gain, cosine, sine, query_weight, wkv, out_weight, cache,
      *pieces, *got_boxes)

    pieces = summed(own, sends, False)
    final_cache = pl.pallas_call(
        functools.partial(cache_kernel, peers, slots),
        out_shape=jax.ShapeDtypeStruct(kv_cache.shape, BF16),
        in_specs=[SMEM, VMEM],
        out_specs=ANY,
        scratch_shapes=[pltpu.SMEM((slots,), I32), dma((slots,))],
        compiler_params=params(16),
        cost_estimate=cost(0, 2 * cache_bytes),
        name="write_cache",
    )(plan, cache)
    final_hidden = pl.pallas_call(
        functools.partial(join_kernel, peers_tp),
        out_shape=jax.ShapeDtypeStruct(hidden.shape, BF16),
        in_specs=[SMEM] + [ANY] * peers_tp,
        out_specs=ANY,
        scratch_shapes=[dma((peers_tp,))],
        compiler_params=params(16),
        name="join",
    )(meta, *pieces)
    return (final_hidden, final_cache)


def solution(mesh):
    def whole(kv_cache, *rest):
        tables = angle_tables(kv_cache.shape[2])
        return jax.shard_map(
            functools.partial(local, tables),
            mesh=mesh,
            in_specs=(
                P(("groups", "inst"), None, None, "tp"),
                P(("groups", "inst"), None),
                P("groups"),
                P("groups"),
                P(),
                P(None, "tp"),
                P(None, None, "tp"),
                P("tp", None),
            ),
            out_specs=(P(("groups", "inst"), None), P(("groups", "inst"), None, None, "tp")),
            check_vma=False,
        )(kv_cache, *rest)

    return whole
```

```python
import functools

import jax
import jax.numpy as jnp
import numpy as np
from jax import lax
from jax.experimental import pallas as pl
from jax.experimental.pallas import tpu as pltpu
from jax.sharding import PartitionSpec as P

MOVE = 2
EPS = 1e-05
THETA = 500000.0
HD = 128
GROUP = 8
PIECE = 16
CHUNK = 8
BATCH = 16
NOTE = 16

F32 = jnp.float32
BF16 = jnp.bfloat16
I32 = jnp.int32

ANY = pl.BlockSpec(memory_space=pl.ANY)
VMEM = pl.BlockSpec(memory_space=pltpu.VMEM)
SMEM = pl.BlockSpec(memory_space=pltpu.SMEM)
HBM = pl.BlockSpec(memory_space=pltpu.HBM)


def params(mib):
    return pltpu.CompilerParams(vmem_limit_bytes=mib * 1024 * 1024)


def cost(flops, nbytes):
    return pl.CostEstimate(flops=flops, bytes_accessed=nbytes, transcendentals=0)


def angle_tables(positions):
    frequency = THETA ** (-(np.arange(HD // 2, dtype=np.float64) * 2.0) / HD)
    angles = np.arange(positions, dtype=np.float64)[:, None] * frequency[None, :]
    cosine = np.concatenate([np.cos(angles), np.cos(angles)], axis=-1)
    sine = np.concatenate([-np.sin(angles), np.sin(angles)], axis=-1)
    return cosine.astype(np.float32), sine.astype(np.float32)


def turn(x, cosine, sine):
    return x * cosine + pltpu.roll(x, HD // 2, 1) * sine


def gather_angles(position_of, slots, cos_ref, sin_ref, cos_rows, sin_rows):
    for s in range(slots):
        p = position_of(s)
        cos_rows[s : s + 1, :] = cos_ref[pl.ds(p, 1), :]
        sin_rows[s : s + 1, :] = sin_ref[pl.ds(p, 1), :]


def spread_normed(normed3, spread, slots, width):
    blocks = width // HD
    row = lax.broadcasted_iota(I32, (HD, 4 * HD), 0)
    col = lax.broadcasted_iota(I32, (HD, 4 * HD), 1)
    goal = jnp.where(col < 2 * HD, 2 * row, 2 * row + 1 + 2 * HD)
    places = jnp.where(col == goal, 1.0, 0.0).astype(BF16)
    spread_all = jnp.dot(
        normed3[...].reshape(blocks * slots, HD), places, preferred_element_type=F32
    ).astype(BF16)
    spread[:, 0:slots, :] = spread_all[:, : 2 * HD].reshape(blocks, slots, 2 * HD)
    spread[:, slots:, :] = spread_all[:, 2 * HD :].reshape(blocks, slots, 2 * HD)


def project_from(normed3, weight, copies=()):
    total = None
    pairs = normed3.shape[0] // 2
    pieces = max(len(copies), 1)
    for b in range(pairs):
        if copies and b % (pairs // pieces) == 0:
            copies[b // (pairs // pieces)].wait()
        block = jnp.concatenate([normed3[2 * b], normed3[2 * b + 1]], axis=1)
        part = jnp.dot(
            block, weight[b * 2 * HD : (b + 1) * 2 * HD, :], preferred_element_type=F32
        )
        total = part if total is None else total + part
    return total


def project_spread(spread, wkv, copies):
    total = None
    blocks = spread.shape[0]
    for b in range(blocks):
        if b % (blocks // len(copies)) == 0:
            copies[b // (blocks // len(copies))].wait()
        part = jnp.dot(
            spread[b], wkv[b * 2 * HD : (b + 1) * 2 * HD, :], preferred_element_type=F32
        )
        total = part if total is None else total + part
    slots = spread.shape[1] // 2
    return total[:slots], total[slots:]


def weight_copies(src, dst, sem, pieces):
    depth = src.shape[0] // pieces
    copies = [
        pltpu.make_async_copy(
            src.at[pl.ds(c * depth, depth)], dst.at[pl.ds(c * depth, depth)], sem.at[c]
        )
        for c in range(pieces)
    ]
    return copies


def put_row(cache, place, p, key_row, value_row):
    base = pl.multiple_of((jnp.maximum(p, 0) // PIECE) * PIECE, PIECE)
    hit = lax.broadcasted_iota(I32, (PIECE, HD), 0) + base == p
    for which, new in ((0, key_row), (1, value_row)):
        old = cache[place, which, pl.ds(base, PIECE), :].astype(F32)
        cache[place, which, pl.ds(base, PIECE), :] = jnp.where(hit, new, old).astype(BF16)


def attend(cache, places, positions, query_rows):
    cap = cache.shape[2]
    col = lax.broadcasted_iota(I32, (GROUP, cap), 1)
    scores = [
        lax.dot_general(
            rows.astype(BF16),
            cache[place, 0],
            (((1,), (1,)), ((), ())),
            preferred_element_type=F32,
        )
        for place, rows in zip(places, query_rows)
    ]
    probs = []
    for score, p in zip(scores, positions):
        score = jnp.where(col <= p, score * HD**-0.5, -jnp.inf)
        weight = jnp.exp(score - jnp.max(score, axis=-1, keepdims=True))
        weight = weight / jnp.sum(weight, axis=-1, keepdims=True)
        probs.append(weight.astype(BF16))
    return [
        jnp.dot(prob, cache[place, 1], preferred_element_type=F32)
        for place, prob in zip(places, probs)
    ]


def norm_into(normed3, pieces, gains, firsts, total_width):
    square = None
    for piece in pieces:
        part = jnp.sum(piece * piece, axis=-1, keepdims=True)
        square = part if square is None else square + part
    factor = lax.rsqrt(square / total_width + EPS)
    for piece, gain, first in zip(pieces, gains, firsts):
        normed = (piece * factor * gain).astype(BF16)
        for i in range(piece.shape[1] // HD):
            normed3[first + i] = normed[:, i * HD : (i + 1) * HD]


def first_kernel(
    peers, slots, heads, shard,
    meta, source_hbm, lengths_hbm, hidden_hbm, gain_hbm, cos_hbm, sin_hbm, wq_hbm, wkv_hbm,
    cache_hbm, query_out, newkey_out, newvalue_out, plan, *rest,
):
    others = peers - 1
    moving = others * MOVE
    cache, box, notes = rest[0], rest[1], (None,) + rest[2 : others + 1]
    (wq, wkv, normed3, spread, cos_rows, sin_rows, leaving, hidden32, source_s, lengths_s, source_v,
     hidden, gain, cos_ref, sin_ref, tail, small_sem, wq_sem, wkv_sem, in_sem,
     box_sem, cache_sem) = rest[others + 1 :]
    width = hidden.shape[1]
    me, me_tp = meta[0], meta[1]
    wq_copies = weight_copies(wq_hbm, wq, wq_sem, 4)
    wkv_copies = weight_copies(wkv_hbm, wkv, wkv_sem, 4)
    small = [
        pltpu.make_async_copy(src, dst, small_sem.at[i])
        for i, (src, dst) in enumerate((
            (source_hbm, source_v), (source_hbm, source_s), (hidden_hbm, hidden), (gain_hbm, gain),
            (lengths_hbm, lengths_s), (cos_hbm, cos_ref), (sin_hbm, sin_ref),
        ))
    ]
    for copy in small[:4] + wkv_copies + wq_copies + small[4:]:
        copy.start()
    loads = [
        pltpu.make_async_copy(
            cache_hbm.at[pl.ds(c * CHUNK, CHUNK)], cache.at[pl.ds(c * CHUNK, CHUNK)], cache_sem.at[c]
        )
        for c in range(slots // CHUNK)
    ]
    for copy in small[:2]:
        copy.wait()

    low = me * slots
    src = source_v[...]
    index = lax.broadcasted_iota(I32, src.shape, 1)
    mine_goes = (src >= low) & (src < low + slots)
    mine_comes = (index >= low) & (index < low + slots)
    index_f = index.astype(F32)
    send_slots = []
    for k in range(1, peers):
        other = jnp.bitwise_xor(me, k) * slots
        sent = mine_goes & (index >= other) & (index < other + slots)
        taken = mine_comes & (src >= other) & (src < other + slots)
        for m in range(MOVE):
            at = (k - 1) * MOVE + m
            if m == 0:
                j = jnp.min(jnp.where(sent, index_f, 1e6)).astype(I32)
                r = jnp.min(jnp.where(taken, index_f, 1e6)).astype(I32)
            else:
                j = jnp.max(jnp.where(sent, index_f, -1.0)).astype(I32)
                r = jnp.max(jnp.where(taken, index_f, -1.0)).astype(I32)
            known = (j >= 0) & (j < src.shape[1])
            slot = source_s[0, jnp.where(known, j, 0)] - low
            slot = jnp.where(known, slot, 0)
            send_slots.append(slot)
            plan[at] = jnp.where((r >= 0) & (r < src.shape[1]), r - low, -1)
            plan[moving + at] = slot
            pltpu.make_async_copy(cache_hbm.at[slot], leaving.at[at], in_sem.at[at]).start()
    for copy in loads:
        copy.start()

    for copy in small[2:4]:
        copy.wait()
    wide = hidden[...].astype(F32)
    hidden32[...] = wide
    norm_into(normed3, [wide], [gain[...]], [0], width)
    spread_normed(normed3, spread, slots, width)
    for copy in small[4:]:
        copy.wait()
    gather_angles(lambda s: lengths_s[0, low + s], slots, cos_ref, sin_ref, cos_rows, sin_rows)
    key, value = project_spread(spread, wkv, wkv_copies)
    query = project_from(normed3, wq, wq_copies)
    cosine, sine = cos_rows[...], sin_rows[...]
    query_out[...] = jnp.zeros(query_out.shape, F32)
    for g in range(heads):
        turned = turn(query[:, g * HD : (g + 1) * HD], cosine, sine)
        query_out[pl.ds(g, slots, stride=GROUP), :] = turned.astype(BF16).astype(F32)
    newkey_out[...] = turn(key, cosine, sine).astype(BF16).astype(F32)
    newvalue_out[...] = value.astype(BF16).astype(F32)

    positions = [lengths_s[0, low + slot] for slot in send_slots]
    for at, slot in enumerate(send_slots):
        pltpu.make_async_copy(cache_hbm.at[slot], leaving.at[at], in_sem.at[at]).wait()
        put_row(
            leaving, at, positions[at],
            newkey_out[pl.ds(slot, 1), :], newvalue_out[pl.ds(slot, 1), :],
        )
    cap = leaving.shape[2]
    copies = [
        pltpu.make_async_copy(
            leaving.at[pl.ds(0, MOVE)], box.at[:, :, pl.ds(0, cap), :], box_sem.at[0]
        )
    ]
    copies[0].start()
    rows = [query_out[pl.ds(pl.multiple_of(slot * GROUP, GROUP), GROUP), :] for slot in send_slots]
    attended = attend(leaving, list(range(moving)), positions, rows)
    column = pl.multiple_of(me_tp * shard, shard)
    for at, slot in enumerate(send_slots):
        m = at % MOVE
        residual = hidden32[pl.ds(slot, 1), pl.ds(column, shard)]
        if at < MOVE:
            blocks = [attended[at][g : g + 1, :] for g in range(heads)]
            blocks += [residual[:, b * HD : (b + 1) * HD] for b in range(shard // HD)]
            blocks += [jnp.zeros((1, HD), F32)] * (NOTE - len(blocks))
            tail[m] = jnp.concatenate(blocks, axis=0).astype(BF16)
            copies.append(
                pltpu.make_async_copy(
                    tail.at[m], box.at[m, 0, pl.ds(cap, NOTE), :], box_sem.at[1 + m]
                )
            )
            copies[-1].start()
        else:
            note = notes[at // MOVE]
            for g in range(heads):
                note[m : m + 1, g * HD : (g + 1) * HD] = attended[at][g : g + 1, :]
            note[m : m + 1, heads * HD :] = residual
    for copy in copies + loads:
        copy.wait()


def attend_slots(cache, places, positions, query, attended_rows, heads):
    slots = len(places)
    for first in range(0, slots, BATCH):
        span = range(first, first + BATCH)
        got = attend(
            cache,
            [places[s] for s in span],
            [positions[s] for s in span],
            [query[s * GROUP : (s + 1) * GROUP, :] for s in span],
        )
        for s, rows in zip(span, got):
            attended_rows[s * GROUP : (s + 1) * GROUP, :] = rows
    return jnp.concatenate(
        [attended_rows[pl.ds(g, slots, stride=GROUP), :] for g in range(heads)], axis=1
    )


def attend_kernel(
    slots, heads, meta, lengths_s, query, newkey, newvalue, _, out, cache, attended_rows,
):
    low = meta[0] * slots
    positions = [lengths_s[low + s] for s in range(slots)]
    for s, p in enumerate(positions):
        put_row(cache, s, p, newkey[s : s + 1, :], newvalue[s : s + 1, :])
    out[...] = attend_slots(
        cache, list(range(slots)), positions, query, attended_rows, heads
    ).astype(BF16)


def project_out(attended, wo, residual, own, sends, me_tp, peers_tp):
    shard = own.shape[1]
    for k in list(range(peers_tp - 1, 0, -1)) + [0]:
        column = pl.multiple_of(jnp.bitwise_xor(me_tp, k) * shard, shard)
        part = jnp.dot(attended, wo[:, pl.ds(column, shard)], preferred_element_type=F32)
        if k == 0:
            own[...] = residual + part
        else:
            sends[k - 1][...] = part.astype(BF16)


def out_kernel(
    peers, peers_tp, meta, plan, attended, wo, hidden, box_hbm, *rest,
):
    notes, rest = rest[: peers - 2], rest[peers - 2 :]
    own, sends, (tail, sem) = rest[0], rest[1:peers_tp], rest[peers_tp:]
    shard = own.shape[1]
    cap = box_hbm.shape[2] - NOTE
    copy = pltpu.make_async_copy(box_hbm.at[:, 0, pl.ds(cap, NOTE), :], tail, sem.at[0])
    copy.start()
    rows = attended[...].astype(F32)
    heads = rows.shape[1] // HD
    column = pl.multiple_of(meta[1] * shard, shard)
    residual = hidden[:, pl.ds(column, shard)].astype(F32)
    row_index = lax.broadcasted_iota(I32, rows.shape, 0)
    residual_index = lax.broadcasted_iota(I32, residual.shape, 0)
    copy.wait()
    for at in range((peers - 1) * MOVE):
        m = at % MOVE
        if at < MOVE:
            blocks = tail[m].astype(F32)
            blocks = [blocks[b : b + 1, :] for b in range(heads + shard // HD)]
            note = jnp.concatenate(blocks, axis=1)
        else:
            note = notes[at // MOVE - 1][m : m + 1, :]
        rows = jnp.where(row_index == plan[at], note[:, : heads * HD], rows)
        residual = jnp.where(residual_index == plan[at], note[:, heads * HD :], residual)
    project_out(rows.astype(BF16), wo, residual, own, sends, meta[1], peers_tp)


def pack_kernel(plan, cache, _own, *rest):
    boxes, out_sem = rest[:-1], rest[-1]
    moving = plan.shape[0] // 2
    packs = [
        pltpu.make_async_copy(
            cache.at[plan[moving + at]], boxes[at // MOVE - 1].at[at % MOVE], out_sem.at[at - MOVE]
        )
        for at in range(MOVE, moving)
    ]
    for pack in packs:
        pack.start()
    for pack in packs:
        pack.wait()


def sum_kernel(own, *rest):
    total = own[...]
    for part in rest[:-1]:
        total = total + part[...].astype(F32)
    rest[-1][...] = total.astype(BF16)


def map_places(slots, peers, plan, place):
    for s in range(slots):
        place[s] = s
    for at in range((peers - 1) * MOVE):
        taker = plan[at]

        @pl.when(taker >= 0)
        def _():
            place[taker] = slots + at


def prepare_kernel(
    peers, slots, meta, source_s, lengths_s, plan, cos_ref, sin_ref, wkv, _,
    weight, cos_rows, sin_rows, place,
):
    map_places(slots, peers, plan, place)
    low = meta[0] * slots
    gather_angles(
        lambda s: lengths_s[source_s[low + s]] + 1, slots, cos_ref, sin_ref, cos_rows, sin_rows
    )
    row = lax.broadcasted_iota(I32, (2 * HD, 2 * HD), 0)
    col = lax.broadcasted_iota(I32, (2 * HD, 2 * HD), 1)
    goal = jnp.where(row < HD, 2 * row, 2 * (row - HD) + 1)
    places = jnp.where(col == goal, 1.0, 0.0).astype(BF16)
    for b in range(weight.shape[0] // HD):
        apart = jnp.dot(
            places, wkv[b * 2 * HD : (b + 1) * 2 * HD, :], preferred_element_type=F32
        ).astype(BF16)
        weight[b * HD : (b + 1) * HD, :HD] = apart[:HD]
        weight[b * HD : (b + 1) * HD, HD:] = apart[HD:]


def second_kernel(
    peers, peers_tp, slots, heads,
    meta, source_s, lengths_s, place, gain, cos_rows, sin_rows, wq, wkv, wo, _, *rest,
):
    blocks, rest = rest[:peers_tp], rest[peers_tp:]
    box_hbm, rest = rest[: peers - 1], rest[peers - 1 :]
    own, sends, cache = rest[0], rest[1:peers_tp], rest[peers_tp]
    normed3, query_rows, attended_rows, in_sem = rest[peers_tp + 1 :]
    me, me_tp = meta[0], meta[1]
    low = me * slots
    width = gain.shape[1]
    shard = own.shape[1]
    loads = [
        pltpu.make_async_copy(
            box.at[:, :, pl.ds(0, cache.shape[2]), :],
            cache.at[pl.ds(slots + k * MOVE, MOVE)],
            in_sem.at[k],
        )
        for k, box in enumerate(box_hbm)
    ]
    for copy in loads:
        copy.start()

    firsts = [jnp.bitwise_xor(me_tp, k) for k in range(peers_tp)]
    norm_into(
        normed3,
        [block[...].astype(F32) for block in blocks],
        [gain[:, pl.ds(pl.multiple_of(first * shard, shard), shard)] for first in firsts],
        [first * (shard // HD) for first in firsts],
        width,
    )
    positions = [lengths_s[source_s[low + s]] + 1 for s in range(slots)]
    query = project_from(normed3, wq)
    pair = project_from(normed3, wkv)
    key, value = pair[:, :HD], pair[:, HD:]
    cosine, sine = cos_rows[...], sin_rows[...]
    query_rows[...] = jnp.zeros(query_rows.shape, F32)
    for g in range(heads):
        turned = turn(query[:, g * HD : (g + 1) * HD], cosine, sine)
        query_rows[pl.ds(g, slots, stride=GROUP), :] = turned.astype(BF16).astype(F32)
    newkey = turn(key, cosine, sine).astype(BF16).astype(F32)
    newvalue = value.astype(BF16).astype(F32)

    for copy in loads:
        copy.wait()
    places = [place[s] for s in range(slots)]
    for s, (at, p) in enumerate(zip(places, positions)):
        put_row(cache, at, p, newkey[s : s + 1, :], newvalue[s : s + 1, :])
    attended = attend_slots(cache, places, positions, query_rows, attended_rows, heads)
    project_out(
        attended.astype(BF16), wo, blocks[0][...].astype(F32), own, sends, me_tp, peers_tp
    )


def cache_kernel(slots, place, cache, out_hbm, out_sem):
    copies = [
        pltpu.make_async_copy(cache.at[place[s]], out_hbm.at[s], out_sem.at[s])
        for s in range(slots)
    ]
    for copy in copies:
        copy.start()
    for copy in copies:
        copy.wait()


def join_kernel(peers_tp, meta, *rest):
    blocks, out, sem = rest[:-2], rest[-2], rest[-1]
    shard = blocks[0].shape[1]
    copies = []
    for k, block in enumerate(blocks):
        column = pl.multiple_of(jnp.bitwise_xor(meta[1], k) * shard, shard)
        copies.append(pltpu.make_async_copy(block, out.at[:, pl.ds(column, shard)], sem.at[k]))
        copies[-1].start()
    for copy in copies:
        copy.wait()


def swapped(x, axis, size, k):
    return lax.ppermute(x, axis, [(i, i ^ k) for i in range(size)])


def local(
    tables, kv_cache, hidden, lengths, source, norm_gain, query_weight, keyval_weight, out_weight
):
    peers, peers_tp = lax.axis_size("inst"), lax.axis_size("tp")
    slots, cap = kv_cache.shape[0], kv_cache.shape[2]
    width = hidden.shape[1]
    heads = query_weight.shape[1] // HD
    shard = width // peers_tp
    others, moving = peers - 1, (peers - 1) * MOVE
    blocks = width // HD
    meta = jnp.stack([lax.axis_index("inst"), lax.axis_index("tp")]).astype(I32)
    gain = norm_gain.reshape(1, width)
    wkv = keyval_weight.reshape(2 * width, HD)
    cosine, sine = (jnp.asarray(table) for table in tables)
    row32 = jax.ShapeDtypeStruct((slots, HD), F32)
    note_width = heads * HD + shard
    dma = pltpu.SemaphoreType.DMA
    weights = [
        pltpu.VMEM(query_weight.shape, BF16),
        pltpu.VMEM(wkv.shape, BF16),
    ]
    stages = [
        pltpu.VMEM((blocks, slots, HD), BF16),
        pltpu.VMEM((blocks, 2 * slots, 2 * HD), BF16),
        pltpu.VMEM((slots, HD), F32),
        pltpu.VMEM((slots, HD), F32),
    ]
    flops = 2 * slots * width * (heads + 2) * HD
    cache_bytes = kv_cache.size * 2
    held = jax.ShapeDtypeStruct((slots + moving,) + kv_cache.shape[1:], BF16)

    query, newkey1, newvalue1, plan, cache, *notes = pl.pallas_call(
        functools.partial(first_kernel, peers, slots, heads, shard),
        out_shape=[
            jax.ShapeDtypeStruct((slots * GROUP, HD), F32),
            row32,
            row32,
            jax.ShapeDtypeStruct((2 * moving,), I32),
            held,
        ]
        + [jax.ShapeDtypeStruct((MOVE, 2, cap + NOTE, HD), BF16)]
        + [jax.ShapeDtypeStruct((MOVE, note_width), F32)] * (others - 1),
        in_specs=[SMEM] + [HBM] * 9,
        out_specs=[VMEM] * 3 + [SMEM, VMEM, ANY] + [VMEM] * (others - 1),
        scratch_shapes=weights
        + stages
        + [
            pltpu.VMEM((moving,) + kv_cache.shape[1:], BF16),
            pltpu.VMEM((slots, width), F32),
            pltpu.SMEM((1, source.shape[0]), I32),
            pltpu.SMEM((1, source.shape[0]), I32),
            pltpu.VMEM((1, source.shape[0]), I32),
            pltpu.VMEM(hidden.shape, BF16),
            pltpu.VMEM((1, width), F32),
            pltpu.VMEM(cosine.shape, F32),
            pltpu.VMEM(cosine.shape, F32),
            pltpu.VMEM((MOVE, NOTE, HD), BF16),
            dma((7,)),
            dma((4,)),
            dma((4,)),
            dma((moving,)),
            dma((1 + MOVE,)),
            dma((slots // CHUNK,)),
        ],
        compiler_params=params(24),
        cost_estimate=cost(flops, (query_weight.size + wkv.size) * 2),
        name="first_step",
    )(meta, *(
        pltpu.with_memory_space_constraint(x, pltpu.HBM)
        for x in (source.reshape(1, -1), lengths.reshape(1, -1), hidden, gain, cosine, sine,
                  query_weight, wkv, kv_cache)
    ))
    got_notes = [swapped(note, "inst", peers, k + 1) for k, note in enumerate(notes)]

    attended, cache = pl.pallas_call(
        functools.partial(attend_kernel, slots, heads),
        out_shape=[jax.ShapeDtypeStruct((slots, heads * HD), BF16), held],
        in_specs=[SMEM] * 2 + [VMEM] * 4,
        out_specs=[VMEM] * 2,
        scratch_shapes=[pltpu.VMEM((slots * GROUP, HD), F32)],
        input_output_aliases={5: 1},
        compiler_params=params(12),
        cost_estimate=cost(4 * slots * cap * HD * heads, cache_bytes),
        name="attention",
    )(meta, lengths, query, newkey1, newvalue1, cache)

    sent = [jax.ShapeDtypeStruct((slots, shard), F32)]
    sent += [jax.ShapeDtypeStruct((slots, shard), BF16)] * (peers_tp - 1)
    own, *sends = pl.pallas_call(
        functools.partial(out_kernel, peers, peers_tp),
        out_shape=sent,
        in_specs=[SMEM] * 2 + [VMEM] * 3 + [ANY] + [VMEM] * (others - 1),
        out_specs=[VMEM] * peers_tp,
        scratch_shapes=[pltpu.VMEM((MOVE, NOTE, HD), BF16), dma((1,))],
        compiler_params=params(16),
        cost_estimate=cost(2 * slots * width * heads * HD, out_weight.size * 2),
        name="out_projection",
    )(meta, plan, attended, out_weight, hidden, *got_notes)
    boxes = pl.pallas_call(
        pack_kernel,
        out_shape=[jax.ShapeDtypeStruct((MOVE,) + kv_cache.shape[1:], BF16)] * (others - 1),
        in_specs=[SMEM, VMEM, ANY],
        out_specs=[ANY] * (others - 1),
        scratch_shapes=[dma((moving - MOVE,))],
        compiler_params=params(16),
        cost_estimate=cost(1, 1 * cache_bytes),
        name="pack",
    )(plan, cache, own)
    got_boxes = got_notes[:1] + [swapped(box, "inst", peers, k + 2) for k, box in enumerate(boxes)]

    def summed(own, sends, passed_on):
        got = [swapped(sends[k - 1], "tp", peers_tp, k) for k in range(peers_tp - 1, 0, -1)]
        shard_rows = pl.pallas_call(
            sum_kernel,
            out_shape=jax.ShapeDtypeStruct((slots, shard), BF16),
            in_specs=[VMEM] * peers_tp,
            out_specs=VMEM,
            compiler_params=params(16),
            name="sum_terms",
        )(own, *got)
        blocks = {0: shard_rows}
        if not passed_on:
            blocks |= {k: swapped(shard_rows, "tp", peers_tp, k) for k in range(1, peers_tp)}
        far = peers_tp // 2 if passed_on else 0
        while far:
            blocks |= {k + far: swapped(blocks[k], "tp", peers_tp, far) for k in blocks}
            far //= 2
        return [blocks[k] for k in range(peers_tp)]

    pieces = summed(own, sends, True)

    weight, cos_rows, sin_rows, place = pl.pallas_call(
        functools.partial(prepare_kernel, peers, slots),
        out_shape=[
            jax.ShapeDtypeStruct((width, 2 * HD), BF16),
            row32,
            row32,
            jax.ShapeDtypeStruct((slots,), I32),
        ],
        in_specs=[SMEM] * 4 + [VMEM] * 3 + [ANY],
        out_specs=[VMEM] * 3 + [SMEM],
        compiler_params=params(16),
        cost_estimate=cost(flops, wkv.size * 4),
        name="prepare",
    )(meta, source, lengths, plan, cosine, sine, wkv, own)

    own, *sends, cache = pl.pallas_call(
        functools.partial(second_kernel, peers, peers_tp, slots, heads),
        out_shape=sent + [held],
        in_specs=[SMEM] * 4 + [VMEM] * (7 + peers_tp) + [ANY] * others,
        out_specs=[VMEM] * (1 + peers_tp),
        scratch_shapes=[
            pltpu.VMEM((blocks, slots, HD), BF16),
            pltpu.VMEM((slots * GROUP, HD), F32),
            pltpu.VMEM((slots * GROUP, HD), F32),
            dma((others,)),
        ],
        input_output_aliases={10: peers_tp},
        compiler_params=params(16),
        cost_estimate=cost(3 * flops, cache_bytes + (query_weight.size + wkv.size) * 4),
        name="second_step",
    )(meta, source, lengths, place, gain, cos_rows, sin_rows, query_weight, weight, out_weight, cache,
      *pieces, *got_boxes)

    pieces = summed(own, sends, False)
    final_cache = pl.pallas_call(
        functools.partial(cache_kernel, slots),
        out_shape=jax.ShapeDtypeStruct(kv_cache.shape, BF16),
        in_specs=[SMEM, VMEM],
        out_specs=ANY,
        scratch_shapes=[dma((slots,))],
        compiler_params=params(16),
        cost_estimate=cost(0, 2 * cache_bytes),
        name="write_cache",
    )(place, cache)
    final_hidden = pl.pallas_call(
        functools.partial(join_kernel, peers_tp),
        out_shape=jax.ShapeDtypeStruct(hidden.shape, BF16),
        in_specs=[SMEM] + [ANY] * peers_tp,
        out_specs=ANY,
        scratch_shapes=[dma((peers_tp,))],
        compiler_params=params(16),
        name="join",
    )(meta, *pieces)
    return (final_hidden, final_cache)


def solution(mesh):
    def whole(kv_cache, *rest):
        tables = angle_tables(kv_cache.shape[2])
        return jax.shard_map(
            functools.partial(local, tables),
            mesh=mesh,
            in_specs=(
                P(("groups", "inst"), None, None, "tp"),
                P(("groups", "inst"), None),
                P("groups"),
                P("groups"),
                P(),
                P(None, "tp"),
                P(None, None, "tp"),
                P("tp", None),
            ),
            out_specs=(P(("groups", "inst"), None), P(("groups", "inst"), None, None, "tp")),
            check_vma=False,
        )(kv_cache, *rest)

    return whole
```

```python
import functools

import jax
import jax.numpy as jnp
import numpy as np
from jax import lax
from jax.experimental import pallas as pl
from jax.experimental.pallas import tpu as pltpu
from jax.sharding import PartitionSpec as P

MOVE = 2
EPS = 1e-05
THETA = 500000.0
HD = 128
GROUP = 8
PIECE = 16
CHUNK = 8
BATCH = 16
NOTE = 16

F32 = jnp.float32
BF16 = jnp.bfloat16
I32 = jnp.int32

ANY = pl.BlockSpec(memory_space=pl.ANY)
VMEM = pl.BlockSpec(memory_space=pltpu.VMEM)
SMEM = pl.BlockSpec(memory_space=pltpu.SMEM)
HBM = pl.BlockSpec(memory_space=pltpu.HBM)


def params(mib):
    return pltpu.CompilerParams(vmem_limit_bytes=mib * 1024 * 1024)


def cost(flops, nbytes):
    return pl.CostEstimate(flops=flops, bytes_accessed=nbytes, transcendentals=0)


def angle_tables(positions):
    frequency = THETA ** (-(np.arange(HD // 2, dtype=np.float64) * 2.0) / HD)
    angles = np.arange(positions, dtype=np.float64)[:, None] * frequency[None, :]
    cosine = np.concatenate([np.cos(angles), np.cos(angles)], axis=-1)
    sine = np.concatenate([-np.sin(angles), np.sin(angles)], axis=-1)
    return cosine.astype(np.float32), sine.astype(np.float32)


def turn(x, cosine, sine):
    return x * cosine + pltpu.roll(x, HD // 2, 1) * sine


def gather_angles(position_of, slots, cos_ref, sin_ref, cos_rows, sin_rows):
    for s in range(slots):
        p = position_of(s)
        cos_rows[s : s + 1, :] = cos_ref[pl.ds(p, 1), :]
        sin_rows[s : s + 1, :] = sin_ref[pl.ds(p, 1), :]


def spread_normed(normed3, spread, slots, width):
    blocks = width // HD
    row = lax.broadcasted_iota(I32, (HD, 4 * HD), 0)
    col = lax.broadcasted_iota(I32, (HD, 4 * HD), 1)
    goal = jnp.where(col < 2 * HD, 2 * row, 2 * row + 1 + 2 * HD)
    places = jnp.where(col == goal, 1.0, 0.0).astype(BF16)
    spread_all = jnp.dot(
        normed3[...].reshape(blocks * slots, HD), places, preferred_element_type=F32
    ).astype(BF16)
    spread[:, 0:slots, :] = spread_all[:, : 2 * HD].reshape(blocks, slots, 2 * HD)
    spread[:, slots:, :] = spread_all[:, 2 * HD :].reshape(blocks, slots, 2 * HD)


def project_from(normed3, weight, copies=()):
    total = None
    pairs = normed3.shape[0] // 2
    pieces = max(len(copies), 1)
    for b in range(pairs):
        if copies and b % (pairs // pieces) == 0:
            copies[b // (pairs // pieces)].wait()
        block = jnp.concatenate([normed3[2 * b], normed3[2 * b + 1]], axis=1)
        part = jnp.dot(
            block, weight[b * 2 * HD : (b + 1) * 2 * HD, :], preferred_element_type=F32
        )
        total = part if total is None else total + part
    return total


def project_spread(spread, wkv, copies):
    total = None
    blocks = spread.shape[0]
    for b in range(blocks):
        if b % (blocks // len(copies)) == 0:
            copies[b // (blocks // len(copies))].wait()
        part = jnp.dot(
            spread[b], wkv[b * 2 * HD : (b + 1) * 2 * HD, :], preferred_element_type=F32
        )
        total = part if total is None else total + part
    slots = spread.shape[1] // 2
    return total[:slots], total[slots:]


def weight_copies(src, dst, sem, pieces):
    depth = src.shape[0] // pieces
    copies = [
        pltpu.make_async_copy(
            src.at[pl.ds(c * depth, depth)], dst.at[pl.ds(c * depth, depth)], sem.at[c]
        )
        for c in range(pieces)
    ]
    return copies


def put_row(cache, place, p, key_row, value_row):
    base = pl.multiple_of((jnp.maximum(p, 0) // PIECE) * PIECE, PIECE)
    hit = lax.broadcasted_iota(I32, (PIECE, HD), 0) + base == p
    for which, new in ((0, key_row), (1, value_row)):
        old = cache[place, which, pl.ds(base, PIECE), :].astype(F32)
        cache[place, which, pl.ds(base, PIECE), :] = jnp.where(hit, new, old).astype(BF16)


def attend(cache, places, positions, query_rows):
    cap = cache.shape[2]
    col = lax.broadcasted_iota(I32, (GROUP, cap), 1)
    scores = [
        lax.dot_general(
            rows.astype(BF16),
            cache[place, 0],
            (((1,), (1,)), ((), ())),
            preferred_element_type=F32,
        )
        for place, rows in zip(places, query_rows)
    ]
    probs = []
    for score, p in zip(scores, positions):
        score = jnp.where(col <= p, score * HD**-0.5, -jnp.inf)
        weight = jnp.exp(score - jnp.max(score, axis=-1, keepdims=True))
        weight = weight / jnp.sum(weight, axis=-1, keepdims=True)
        probs.append(weight.astype(BF16))
    return [
        jnp.dot(prob, cache[place, 1], preferred_element_type=F32)
        for place, prob in zip(places, probs)
    ]


def norm_into(normed3, pieces, gains, firsts, total_width):
    square = None
    for piece in pieces:
        part = jnp.sum(piece * piece, axis=-1, keepdims=True)
        square = part if square is None else square + part
    factor = lax.rsqrt(square / total_width + EPS)
    for piece, gain, first in zip(pieces, gains, firsts):
        normed = (piece * factor * gain).astype(BF16)
        for i in range(piece.shape[1] // HD):
            normed3[first + i] = normed[:, i * HD : (i + 1) * HD]


def first_kernel(
    peers, slots, heads, shard,
    meta, source_hbm, lengths_hbm, hidden_hbm, gain_hbm, cos_hbm, sin_hbm, wq_hbm, wkv_hbm,
    cache_hbm, query_out, newkey_out, newvalue_out, plan, *rest,
):
    others = peers - 1
    moving = others * MOVE
    cache, box, notes = rest[0], rest[1], (None,) + rest[2 : others + 1]
    (wq, wkv, normed3, spread, cos_rows, sin_rows, leaving, hidden32, source_s, lengths_s, source_v,
     hidden, gain, cos_ref, sin_ref, tail, small_sem, wq_sem, wkv_sem, in_sem,
     box_sem, cache_sem) = rest[others + 1 :]
    width = hidden.shape[1]
    me, me_tp = meta[0], meta[1]
    wq_copies = weight_copies(wq_hbm, wq, wq_sem, 4)
    wkv_copies = weight_copies(wkv_hbm, wkv, wkv_sem, 4)
    small = [
        pltpu.make_async_copy(src, dst, small_sem.at[i])
        for i, (src, dst) in enumerate((
            (source_hbm, source_v), (source_hbm, source_s), (hidden_hbm, hidden), (gain_hbm, gain),
            (lengths_hbm, lengths_s), (cos_hbm, cos_ref), (sin_hbm, sin_ref),
        ))
    ]
    for copy in small[:4] + wkv_copies + wq_copies + small[4:]:
        copy.start()
    loads = [
        pltpu.make_async_copy(
            cache_hbm.at[pl.ds(c * CHUNK, CHUNK)], cache.at[pl.ds(c * CHUNK, CHUNK)], cache_sem.at[c]
        )
        for c in range(slots // CHUNK)
    ]
    for copy in small[:2]:
        copy.wait()

    low = me * slots
    src = source_v[...]
    index = lax.broadcasted_iota(I32, src.shape, 1)
    mine_goes = (src >= low) & (src < low + slots)
    mine_comes = (index >= low) & (index < low + slots)
    index_f = index.astype(F32)
    send_slots = []
    for k in range(1, peers):
        other = jnp.bitwise_xor(me, k) * slots
        sent = mine_goes & (index >= other) & (index < other + slots)
        taken = mine_comes & (src >= other) & (src < other + slots)
        for m in range(MOVE):
            at = (k - 1) * MOVE + m
            if m == 0:
                j = jnp.min(jnp.where(sent, index_f, 1e6)).astype(I32)
                r = jnp.min(jnp.where(taken, index_f, 1e6)).astype(I32)
            else:
                j = jnp.max(jnp.where(sent, index_f, -1.0)).astype(I32)
                r = jnp.max(jnp.where(taken, index_f, -1.0)).astype(I32)
            known = (j >= 0) & (j < src.shape[1])
            slot = source_s[0, jnp.where(known, j, 0)] - low
            slot = jnp.where(known, slot, 0)
            send_slots.append(slot)
            plan[at] = jnp.where((r >= 0) & (r < src.shape[1]), r - low, -1)
            plan[moving + at] = slot
            pltpu.make_async_copy(cache_hbm.at[slot], leaving.at[at], in_sem.at[at]).start()
    for copy in loads:
        copy.start()

    for copy in small[2:4]:
        copy.wait()
    wide = hidden[...].astype(F32)
    hidden32[...] = wide
    norm_into(normed3, [wide], [gain[...]], [0], width)
    spread_normed(normed3, spread, slots, width)
    for copy in small[4:]:
        copy.wait()
    gather_angles(lambda s: lengths_s[0, low + s], slots, cos_ref, sin_ref, cos_rows, sin_rows)
    key, value = project_spread(spread, wkv, wkv_copies)
    query = project_from(normed3, wq, wq_copies)
    cosine, sine = cos_rows[...], sin_rows[...]
    query_out[...] = jnp.zeros(query_out.shape, F32)
    for g in range(heads):
        turned = turn(query[:, g * HD : (g + 1) * HD], cosine, sine)
        query_out[pl.ds(g, slots, stride=GROUP), :] = turned.astype(BF16).astype(F32)
    newkey_out[...] = turn(key, cosine, sine).astype(BF16).astype(F32)
    newvalue_out[...] = value.astype(BF16).astype(F32)

    positions = [lengths_s[0, low + slot] for slot in send_slots]
    for at, slot in enumerate(send_slots):
        pltpu.make_async_copy(cache_hbm.at[slot], leaving.at[at], in_sem.at[at]).wait()
        put_row(
            leaving, at, positions[at],
            newkey_out[pl.ds(slot, 1), :], newvalue_out[pl.ds(slot, 1), :],
        )
    cap = leaving.shape[2]
    copies = [
        pltpu.make_async_copy(
            leaving.at[pl.ds(0, MOVE)], box.at[:, :, pl.ds(0, cap), :], box_sem.at[0]
        )
    ]
    copies[0].start()
    rows = [query_out[pl.ds(pl.multiple_of(slot * GROUP, GROUP), GROUP), :] for slot in send_slots]
    attended = attend(leaving, list(range(moving)), positions, rows)
    column = pl.multiple_of(me_tp * shard, shard)
    for at, slot in enumerate(send_slots):
        m = at % MOVE
        residual = hidden32[pl.ds(slot, 1), pl.ds(column, shard)]
        if at < MOVE:
            blocks = [attended[at][g : g + 1, :] for g in range(heads)]
            blocks += [residual[:, b * HD : (b + 1) * HD] for b in range(shard // HD)]
            blocks += [jnp.zeros((1, HD), F32)] * (NOTE - len(blocks))
            tail[m] = jnp.concatenate(blocks, axis=0).astype(BF16)
            copies.append(
                pltpu.make_async_copy(
                    tail.at[m], box.at[m, 0, pl.ds(cap, NOTE), :], box_sem.at[1 + m]
                )
            )
            copies[-1].start()
        else:
            note = notes[at // MOVE]
            for g in range(heads):
                note[m : m + 1, g * HD : (g + 1) * HD] = attended[at][g : g + 1, :]
            note[m : m + 1, heads * HD :] = residual
    for copy in copies + loads:
        copy.wait()


def attend_slots(cache, places, positions, query, attended_rows, heads):
    slots = len(places)
    for first in range(0, slots, BATCH):
        span = range(first, first + BATCH)
        got = attend(
            cache,
            [places[s] for s in span],
            [positions[s] for s in span],
            [query[s * GROUP : (s + 1) * GROUP, :] for s in span],
        )
        for s, rows in zip(span, got):
            attended_rows[s * GROUP : (s + 1) * GROUP, :] = rows
    return jnp.concatenate(
        [attended_rows[pl.ds(g, slots, stride=GROUP), :] for g in range(heads)], axis=1
    )


def attend_kernel(
    slots, heads, meta, lengths_s, query, newkey, newvalue, _, out, cache, attended_rows,
):
    low = meta[0] * slots
    positions = [lengths_s[low + s] for s in range(slots)]
    for s, p in enumerate(positions):
        put_row(cache, s, p, newkey[s : s + 1, :], newvalue[s : s + 1, :])
    out[...] = attend_slots(
        cache, list(range(slots)), positions, query, attended_rows, heads
    ).astype(BF16)


def project_out(attended, wo, residual, own, sends, me_tp, peers_tp):
    shard = own.shape[1]
    for k in list(range(peers_tp - 1, 0, -1)) + [0]:
        column = pl.multiple_of(jnp.bitwise_xor(me_tp, k) * shard, shard)
        part = jnp.dot(attended, wo[:, pl.ds(column, shard)], preferred_element_type=F32)
        if k == 0:
            own[...] = residual + part
        else:
            sends[k - 1][...] = part.astype(BF16)


def out_kernel(
    peers, peers_tp, meta, plan, attended, wo, hidden, box_hbm, *rest,
):
    notes, rest = rest[: peers - 2], rest[peers - 2 :]
    own, sends, (tail, sem) = rest[0], rest[1:peers_tp], rest[peers_tp:]
    shard = own.shape[1]
    cap = box_hbm.shape[2] - NOTE
    copy = pltpu.make_async_copy(box_hbm.at[:, 0, pl.ds(cap, NOTE), :], tail, sem.at[0])
    copy.start()
    rows = attended[...].astype(F32)
    heads = rows.shape[1] // HD
    column = pl.multiple_of(meta[1] * shard, shard)
    residual = hidden[:, pl.ds(column, shard)].astype(F32)
    row_index = lax.broadcasted_iota(I32, rows.shape, 0)
    residual_index = lax.broadcasted_iota(I32, residual.shape, 0)
    copy.wait()
    for at in range((peers - 1) * MOVE):
        m = at % MOVE
        if at < MOVE:
            blocks = tail[m].astype(F32)
            blocks = [blocks[b : b + 1, :] for b in range(heads + shard // HD)]
            note = jnp.concatenate(blocks, axis=1)
        else:
            note = notes[at // MOVE - 1][m : m + 1, :]
        rows = jnp.where(row_index == plan[at], note[:, : heads * HD], rows)
        residual = jnp.where(residual_index == plan[at], note[:, heads * HD :], residual)
    project_out(rows.astype(BF16), wo, residual, own, sends, meta[1], peers_tp)


def pack_kernel(plan, cache, _own, *rest):
    boxes, out_sem = rest[:-1], rest[-1]
    moving = plan.shape[0] // 2
    packs = [
        pltpu.make_async_copy(
            cache.at[plan[moving + at]], boxes[at // MOVE - 1].at[at % MOVE], out_sem.at[at - MOVE]
        )
        for at in range(MOVE, moving)
    ]
    for pack in packs:
        pack.start()
    for pack in packs:
        pack.wait()


def sum_kernel(own, *rest):
    total = own[...]
    for part in rest[:-1]:
        total = total + part[...].astype(F32)
    rest[-1][...] = total.astype(BF16)


def map_places(slots, peers, plan, place):
    for s in range(slots):
        place[s] = s
    for at in range((peers - 1) * MOVE):
        taker = plan[at]

        @pl.when(taker >= 0)
        def _():
            place[taker] = slots + at


def prepare_kernel(
    peers, slots, meta, source_s, lengths_s, plan, cos_ref, sin_ref, wkv, _,
    weight, cos_rows, sin_rows, place,
):
    map_places(slots, peers, plan, place)
    low = meta[0] * slots
    gather_angles(
        lambda s: lengths_s[source_s[low + s]] + 1, slots, cos_ref, sin_ref, cos_rows, sin_rows
    )
    row = lax.broadcasted_iota(I32, (2 * HD, 2 * HD), 0)
    col = lax.broadcasted_iota(I32, (2 * HD, 2 * HD), 1)
    goal = jnp.where(row < HD, 2 * row, 2 * (row - HD) + 1)
    places = jnp.where(col == goal, 1.0, 0.0).astype(BF16)
    for b in range(weight.shape[0] // HD):
        apart = jnp.dot(
            places, wkv[b * 2 * HD : (b + 1) * 2 * HD, :], preferred_element_type=F32
        ).astype(BF16)
        weight[b * HD : (b + 1) * HD, :HD] = apart[:HD]
        weight[b * HD : (b + 1) * HD, HD:] = apart[HD:]


def second_kernel(
    peers, peers_tp, slots, heads,
    meta, source_s, lengths_s, place, gain, cos_rows, sin_rows, wq, wkv, wo, _, *rest,
):
    blocks, rest = rest[:peers_tp], rest[peers_tp:]
    box_hbm, rest = rest[: peers - 1], rest[peers - 1 :]
    own, sends, cache = rest[0], rest[1:peers_tp], rest[peers_tp]
    normed3, query_rows, attended_rows, in_sem = rest[peers_tp + 1 :]
    me, me_tp = meta[0], meta[1]
    low = me * slots
    width = gain.shape[1]
    shard = own.shape[1]
    loads = [
        pltpu.make_async_copy(
            box.at[:, :, pl.ds(0, cache.shape[2]), :],
            cache.at[pl.ds(slots + k * MOVE, MOVE)],
            in_sem.at[k],
        )
        for k, box in enumerate(box_hbm)
    ]
    for copy in loads:
        copy.start()

    firsts = [jnp.bitwise_xor(me_tp, k) for k in range(peers_tp)]
    norm_into(
        normed3,
        [block[...].astype(F32) for block in blocks],
        [gain[:, pl.ds(pl.multiple_of(first * shard, shard), shard)] for first in firsts],
        [first * (shard // HD) for first in firsts],
        width,
    )
    positions = [lengths_s[source_s[low + s]] + 1 for s in range(slots)]
    query = project_from(normed3, wq)
    pair = project_from(normed3, wkv)
    key, value = pair[:, :HD], pair[:, HD:]
    cosine, sine = cos_rows[...], sin_rows[...]
    query_rows[...] = jnp.zeros(query_rows.shape, F32)
    for g in range(heads):
        turned = turn(query[:, g * HD : (g + 1) * HD], cosine, sine)
        query_rows[pl.ds(g, slots, stride=GROUP), :] = turned.astype(BF16).astype(F32)
    newkey = turn(key, cosine, sine).astype(BF16).astype(F32)
    newvalue = value.astype(BF16).astype(F32)

    for copy in loads:
        copy.wait()
    places = [place[s] for s in range(slots)]
    for s, (at, p) in enumerate(zip(places, positions)):
        put_row(cache, at, p, newkey[s : s + 1, :], newvalue[s : s + 1, :])
    attended = attend_slots(cache, places, positions, query_rows, attended_rows, heads)
    project_out(
        attended.astype(BF16), wo, blocks[0][...].astype(F32), own, sends, me_tp, peers_tp
    )


def cache_kernel(slots, place, cache, out_hbm, out_sem):
    copies = [
        pltpu.make_async_copy(cache.at[place[s]], out_hbm.at[s], out_sem.at[s])
        for s in range(slots)
    ]
    for copy in copies:
        copy.start()
    for copy in copies:
        copy.wait()


def join_kernel(peers_tp, meta, *rest):
    blocks, out, sem = rest[:-2], rest[-2], rest[-1]
    shard = blocks[0].shape[1]
    copies = []
    for k, block in enumerate(blocks):
        column = pl.multiple_of(jnp.bitwise_xor(meta[1], k) * shard, shard)
        copies.append(pltpu.make_async_copy(block, out.at[:, pl.ds(column, shard)], sem.at[k]))
        copies[-1].start()
    for copy in copies:
        copy.wait()


def swapped(x, axis, size, k):
    return lax.ppermute(x, axis, [(i, i ^ k) for i in range(size)])


def local(
    tables, kv_cache, hidden, lengths, source, norm_gain, query_weight, keyval_weight, out_weight
):
    peers, peers_tp = lax.axis_size("inst"), lax.axis_size("tp")
    slots, cap = kv_cache.shape[0], kv_cache.shape[2]
    width = hidden.shape[1]
    heads = query_weight.shape[1] // HD
    shard = width // peers_tp
    others, moving = peers - 1, (peers - 1) * MOVE
    blocks = width // HD
    meta = jnp.stack([lax.axis_index("inst"), lax.axis_index("tp")]).astype(I32)
    gain = norm_gain.reshape(1, width)
    wkv = keyval_weight.reshape(2 * width, HD)
    cosine, sine = (jnp.asarray(table) for table in tables)
    row32 = jax.ShapeDtypeStruct((slots, HD), F32)
    note_width = heads * HD + shard
    dma = pltpu.SemaphoreType.DMA
    weights = [
        pltpu.VMEM(query_weight.shape, BF16),
        pltpu.VMEM(wkv.shape, BF16),
    ]
    stages = [
        pltpu.VMEM((blocks, slots, HD), BF16),
        pltpu.VMEM((blocks, 2 * slots, 2 * HD), BF16),
        pltpu.VMEM((slots, HD), F32),
        pltpu.VMEM((slots, HD), F32),
    ]
    flops = 2 * slots * width * (heads + 2) * HD
    cache_bytes = kv_cache.size * 2
    held = jax.ShapeDtypeStruct((slots + moving,) + kv_cache.shape[1:], BF16)

    query, newkey1, newvalue1, plan, cache, *notes = pl.pallas_call(
        functools.partial(first_kernel, peers, slots, heads, shard),
        out_shape=[
            jax.ShapeDtypeStruct((slots * GROUP, HD), F32),
            row32,
            row32,
            jax.ShapeDtypeStruct((2 * moving,), I32),
            held,
        ]
        + [jax.ShapeDtypeStruct((MOVE, 2, cap + NOTE, HD), BF16)]
        + [jax.ShapeDtypeStruct((MOVE, note_width), F32)] * (others - 1),
        in_specs=[SMEM] + [HBM] * 9,
        out_specs=[VMEM] * 3 + [SMEM, VMEM, ANY] + [VMEM] * (others - 1),
        scratch_shapes=weights
        + stages
        + [
            pltpu.VMEM((moving,) + kv_cache.shape[1:], BF16),
            pltpu.VMEM((slots, width), F32),
            pltpu.SMEM((1, source.shape[0]), I32),
            pltpu.SMEM((1, source.shape[0]), I32),
            pltpu.VMEM((1, source.shape[0]), I32),
            pltpu.VMEM(hidden.shape, BF16),
            pltpu.VMEM((1, width), F32),
            pltpu.VMEM(cosine.shape, F32),
            pltpu.VMEM(cosine.shape, F32),
            pltpu.VMEM((MOVE, NOTE, HD), BF16),
            dma((7,)),
            dma((4,)),
            dma((4,)),
            dma((moving,)),
            dma((1 + MOVE,)),
            dma((slots // CHUNK,)),
        ],
        compiler_params=params(24),
        cost_estimate=cost(flops, (query_weight.size + wkv.size) * 2),
        name="first_step",
    )(meta, *(
        pltpu.with_memory_space_constraint(x, pltpu.HBM)
        for x in (source.reshape(1, -1), lengths.reshape(1, -1), hidden, gain, cosine, sine,
                  query_weight, wkv, kv_cache)
    ))
    got_notes = [swapped(note, "inst", peers, k + 1) for k, note in enumerate(notes)]

    attended, cache = pl.pallas_call(
        functools.partial(attend_kernel, slots, heads),
        out_shape=[jax.ShapeDtypeStruct((slots, heads * HD), BF16), held],
        in_specs=[SMEM] * 2 + [VMEM] * 4,
        out_specs=[VMEM] * 2,
        scratch_shapes=[pltpu.VMEM((slots * GROUP, HD), F32)],
        input_output_aliases={5: 1},
        compiler_params=params(12),
        cost_estimate=cost(4 * slots * cap * HD * heads, cache_bytes),
        name="attention",
    )(meta, lengths, query, newkey1, newvalue1, cache)

    sent = [jax.ShapeDtypeStruct((slots, shard), F32)]
    sent += [jax.ShapeDtypeStruct((slots, shard), BF16)] * (peers_tp - 1)
    own, *sends = pl.pallas_call(
        functools.partial(out_kernel, peers, peers_tp),
        out_shape=sent,
        in_specs=[SMEM] * 2 + [VMEM] * 3 + [ANY] + [VMEM] * (others - 1),
        out_specs=[VMEM] * peers_tp,
        scratch_shapes=[pltpu.VMEM((MOVE, NOTE, HD), BF16), dma((1,))],
        compiler_params=params(16),
        cost_estimate=cost(2 * slots * width * heads * HD, out_weight.size * 2),
        name="out_projection",
    )(meta, plan, attended, out_weight, hidden, *got_notes)
    boxes = pl.pallas_call(
        pack_kernel,
        out_shape=[jax.ShapeDtypeStruct((MOVE,) + kv_cache.shape[1:], BF16)] * (others - 1),
        in_specs=[SMEM, VMEM, ANY],
        out_specs=[ANY] * (others - 1),
        scratch_shapes=[dma((moving - MOVE,))],
        compiler_params=params(16),
        cost_estimate=cost(1, 1 * cache_bytes),
        name="pack",
    )(plan, cache, own)
    got_boxes = got_notes[:1] + [swapped(box, "inst", peers, k + 2) for k, box in enumerate(boxes)]

    def summed(own, sends, passed_on):
        got = [swapped(sends[k - 1], "tp", peers_tp, k) for k in range(peers_tp - 1, 0, -1)]
        shard_rows = pl.pallas_call(
            sum_kernel,
            out_shape=jax.ShapeDtypeStruct((slots, shard), BF16),
            in_specs=[VMEM] * peers_tp,
            out_specs=VMEM,
            compiler_params=params(16),
            name="sum_terms",
        )(own, *got)
        blocks = {0: shard_rows}
        if not passed_on:
            blocks |= {k: swapped(shard_rows, "tp", peers_tp, k) for k in range(1, peers_tp)}
        far = peers_tp // 2 if passed_on else 0
        while far:
            blocks |= {k + far: swapped(blocks[k], "tp", peers_tp, far) for k in blocks}
            far //= 2
        return [blocks[k] for k in range(peers_tp)]

    pieces = summed(own, sends, False)

    weight, cos_rows, sin_rows, place = pl.pallas_call(
        functools.partial(prepare_kernel, peers, slots),
        out_shape=[
            jax.ShapeDtypeStruct((width, 2 * HD), BF16),
            row32,
            row32,
            jax.ShapeDtypeStruct((slots,), I32),
        ],
        in_specs=[SMEM] * 4 + [VMEM] * 3 + [ANY],
        out_specs=[VMEM] * 3 + [SMEM],
        compiler_params=params(16),
        cost_estimate=cost(100*flops, wkv.size * 40),
        name="prepare",
    )(meta, source, lengths, plan, cosine, sine, wkv, own)

    own, *sends, cache = pl.pallas_call(
        functools.partial(second_kernel, peers, peers_tp, slots, heads),
        out_shape=sent + [held],
        in_specs=[SMEM] * 4 + [VMEM] * (7 + peers_tp) + [ANY] * others,
        out_specs=[VMEM] * (1 + peers_tp),
        scratch_shapes=[
            pltpu.VMEM((blocks, slots, HD), BF16),
            pltpu.VMEM((slots * GROUP, HD), F32),
            pltpu.VMEM((slots * GROUP, HD), F32),
            dma((others,)),
        ],
        input_output_aliases={10: peers_tp},
        compiler_params=params(16),
        cost_estimate=cost(3 * flops, cache_bytes + (query_weight.size + wkv.size) * 4),
        name="second_step",
    )(meta, source, lengths, place, gain, cos_rows, sin_rows, query_weight, weight, out_weight, cache,
      *pieces, *got_boxes)

    pieces = summed(own, sends, False)
    final_cache = pl.pallas_call(
        functools.partial(cache_kernel, slots),
        out_shape=jax.ShapeDtypeStruct(kv_cache.shape, BF16),
        in_specs=[SMEM, VMEM],
        out_specs=ANY,
        scratch_shapes=[dma((slots,))],
        compiler_params=params(16),
        cost_estimate=cost(0, 2 * cache_bytes),
        name="write_cache",
    )(place, cache)
    final_hidden = pl.pallas_call(
        functools.partial(join_kernel, peers_tp),
        out_shape=jax.ShapeDtypeStruct(hidden.shape, BF16),
        in_specs=[SMEM] + [ANY] * peers_tp,
        out_specs=ANY,
        scratch_shapes=[dma((peers_tp,))],
        compiler_params=params(16),
        name="join",
    )(meta, *pieces)
    return (final_hidden, final_cache)


def solution(mesh):
    def whole(kv_cache, *rest):
        tables = angle_tables(kv_cache.shape[2])
        return jax.shard_map(
            functools.partial(local, tables),
            mesh=mesh,
            in_specs=(
                P(("groups", "inst"), None, None, "tp"),
                P(("groups", "inst"), None),
                P("groups"),
                P("groups"),
                P(),
                P(None, "tp"),
                P(None, None, "tp"),
                P("tp", None),
            ),
            out_specs=(P(("groups", "inst"), None), P(("groups", "inst"), None, None, "tp")),
            check_vma=False,
        )(kv_cache, *rest)

    return whole
```

```python
import functools

import jax
import jax.numpy as jnp
import numpy as np
from jax import lax
from jax.experimental import pallas as pl
from jax.experimental.pallas import tpu as pltpu
from jax.sharding import PartitionSpec as P

MOVE = 2
EPS = 1e-05
THETA = 500000.0
HD = 128
GROUP = 8
PIECE = 16
CHUNK = 8
BATCH = 16
NOTE = 16

F32 = jnp.float32
BF16 = jnp.bfloat16
I32 = jnp.int32

ANY = pl.BlockSpec(memory_space=pl.ANY)
VMEM = pl.BlockSpec(memory_space=pltpu.VMEM)
SMEM = pl.BlockSpec(memory_space=pltpu.SMEM)
HBM = pl.BlockSpec(memory_space=pltpu.HBM)


def params(mib):
    return pltpu.CompilerParams(vmem_limit_bytes=mib * 1024 * 1024)


def cost(flops, nbytes):
    return pl.CostEstimate(flops=flops, bytes_accessed=nbytes, transcendentals=0)


def angle_tables(positions):
    frequency = THETA ** (-(np.arange(HD // 2, dtype=np.float64) * 2.0) / HD)
    angles = np.arange(positions, dtype=np.float64)[:, None] * frequency[None, :]
    cosine = np.concatenate([np.cos(angles), np.cos(angles)], axis=-1)
    sine = np.concatenate([-np.sin(angles), np.sin(angles)], axis=-1)
    return cosine.astype(np.float32), sine.astype(np.float32)


def turn(x, cosine, sine):
    return x * cosine + pltpu.roll(x, HD // 2, 1) * sine


def gather_angles(position_of, slots, cos_ref, sin_ref, cos_rows, sin_rows):
    for s in range(slots):
        p = position_of(s)
        cos_rows[s : s + 1, :] = cos_ref[pl.ds(p, 1), :]
        sin_rows[s : s + 1, :] = sin_ref[pl.ds(p, 1), :]


def spread_normed(normed3, spread, slots, width):
    blocks = width // HD
    row = lax.broadcasted_iota(I32, (HD, 4 * HD), 0)
    col = lax.broadcasted_iota(I32, (HD, 4 * HD), 1)
    goal = jnp.where(col < 2 * HD, 2 * row, 2 * row + 1 + 2 * HD)
    places = jnp.where(col == goal, 1.0, 0.0).astype(BF16)
    spread_all = jnp.dot(
        normed3[...].reshape(blocks * slots, HD), places, preferred_element_type=F32
    ).astype(BF16)
    spread[:, 0:slots, :] = spread_all[:, : 2 * HD].reshape(blocks, slots, 2 * HD)
    spread[:, slots:, :] = spread_all[:, 2 * HD :].reshape(blocks, slots, 2 * HD)


def project_from(normed3, weight, copies=()):
    total = None
    pairs = normed3.shape[0] // 2
    pieces = max(len(copies), 1)
    for b in range(pairs):
        if copies and b % (pairs // pieces) == 0:
            copies[b // (pairs // pieces)].wait()
        block = jnp.concatenate([normed3[2 * b], normed3[2 * b + 1]], axis=1)
        part = jnp.dot(
            block, weight[b * 2 * HD : (b + 1) * 2 * HD, :], preferred_element_type=F32
        )
        total = part if total is None else total + part
    return total


def project_spread(spread, wkv, copies):
    total = None
    blocks = spread.shape[0]
    for b in range(blocks):
        if b % (blocks // len(copies)) == 0:
            copies[b // (blocks // len(copies))].wait()
        part = jnp.dot(
            spread[b], wkv[b * 2 * HD : (b + 1) * 2 * HD, :], preferred_element_type=F32
        )
        total = part if total is None else total + part
    slots = spread.shape[1] // 2
    return total[:slots], total[slots:]


def weight_copies(src, dst, sem, pieces):
    depth = src.shape[0] // pieces
    copies = [
        pltpu.make_async_copy(
            src.at[pl.ds(c * depth, depth)], dst.at[pl.ds(c * depth, depth)], sem.at[c]
        )
        for c in range(pieces)
    ]
    return copies


def put_row(cache, place, p, key_row, value_row):
    base = pl.multiple_of((jnp.maximum(p, 0) // PIECE) * PIECE, PIECE)
    hit = lax.broadcasted_iota(I32, (PIECE, HD), 0) + base == p
    for which, new in ((0, key_row), (1, value_row)):
        old = cache[place, which, pl.ds(base, PIECE), :].astype(F32)
        cache[place, which, pl.ds(base, PIECE), :] = jnp.where(hit, new, old).astype(BF16)


def attend(cache, places, positions, query_rows):
    cap = cache.shape[2]
    col = lax.broadcasted_iota(I32, (GROUP, cap), 1)
    scores = [
        lax.dot_general(
            rows.astype(BF16),
            cache[place, 0],
            (((1,), (1,)), ((), ())),
            preferred_element_type=F32,
        )
        for place, rows in zip(places, query_rows)
    ]
    probs = []
    for score, p in zip(scores, positions):
        score = jnp.where(col <= p, score * HD**-0.5, -jnp.inf)
        weight = jnp.exp(score - jnp.max(score, axis=-1, keepdims=True))
        weight = weight / jnp.sum(weight, axis=-1, keepdims=True)
        probs.append(weight.astype(BF16))
    return [
        jnp.dot(prob, cache[place, 1], preferred_element_type=F32)
        for place, prob in zip(places, probs)
    ]


def norm_into(normed3, pieces, gains, firsts, total_width):
    square = None
    for piece in pieces:
        part = jnp.sum(piece * piece, axis=-1, keepdims=True)
        square = part if square is None else square + part
    factor = lax.rsqrt(square / total_width + EPS)
    for piece, gain, first in zip(pieces, gains, firsts):
        normed = (piece * factor * gain).astype(BF16)
        for i in range(piece.shape[1] // HD):
            normed3[first + i] = normed[:, i * HD : (i + 1) * HD]


def first_kernel(
    peers, slots, heads, shard,
    meta, source_hbm, lengths_hbm, hidden_hbm, gain_hbm, cos_hbm, sin_hbm, wq_hbm, wkv_hbm,
    cache_hbm, query_out, newkey_out, newvalue_out, plan, *rest,
):
    others = peers - 1
    moving = others * MOVE
    cache, box, notes = rest[0], rest[1], (None,) + rest[2 : others + 1]
    (wq, wkv, normed3, spread, cos_rows, sin_rows, hidden32, source_s, lengths_s, source_v,
     hidden, gain, cos_ref, sin_ref, small_sem, wq_sem, wkv_sem,
     box_sem, cache_sem) = rest[others + 1 :]
    width = hidden.shape[1]
    me, me_tp = meta[0], meta[1]
    wq_copies = weight_copies(wq_hbm, wq, wq_sem, 4)
    wkv_copies = weight_copies(wkv_hbm, wkv, wkv_sem, 4)
    small = [
        pltpu.make_async_copy(src, dst, small_sem.at[i])
        for i, (src, dst) in enumerate((
            (source_hbm, source_v), (source_hbm, source_s), (hidden_hbm, hidden), (gain_hbm, gain),
            (lengths_hbm, lengths_s), (cos_hbm, cos_ref), (sin_hbm, sin_ref),
        ))
    ]
    loads = [
        pltpu.make_async_copy(
            cache_hbm.at[pl.ds(c * CHUNK, CHUNK)], cache.at[pl.ds(c * CHUNK, CHUNK)], cache_sem.at[c]
        )
        for c in range(slots // CHUNK)
    ]
    for copy in small[:4] + wkv_copies + wq_copies + small[4:] + loads:
        copy.start()
    for copy in small[:2]:
        copy.wait()

    low = me * slots
    src = source_v[...]
    index = lax.broadcasted_iota(I32, src.shape, 1)
    mine_goes = (src >= low) & (src < low + slots)
    mine_comes = (index >= low) & (index < low + slots)
    index_f = index.astype(F32)
    send_slots = []
    for k in range(1, peers):
        other = jnp.bitwise_xor(me, k) * slots
        sent = mine_goes & (index >= other) & (index < other + slots)
        taken = mine_comes & (src >= other) & (src < other + slots)
        for m in range(MOVE):
            at = (k - 1) * MOVE + m
            if m == 0:
                j = jnp.min(jnp.where(sent, index_f, 1e6)).astype(I32)
                r = jnp.min(jnp.where(taken, index_f, 1e6)).astype(I32)
            else:
                j = jnp.max(jnp.where(sent, index_f, -1.0)).astype(I32)
                r = jnp.max(jnp.where(taken, index_f, -1.0)).astype(I32)
            known = (j >= 0) & (j < src.shape[1])
            slot = source_s[0, jnp.where(known, j, 0)] - low
            slot = jnp.where(known, slot, 0)
            send_slots.append(slot)
            plan[at] = jnp.where((r >= 0) & (r < src.shape[1]), r - low, -1)
            plan[moving + at] = slot

    for copy in small[2:4]:
        copy.wait()
    wide = hidden[...].astype(F32)
    hidden32[...] = wide
    norm_into(normed3, [wide], [gain[...]], [0], width)
    spread_normed(normed3, spread, slots, width)
    for copy in small[4:]:
        copy.wait()
    gather_angles(lambda s: lengths_s[0, low + s], slots, cos_ref, sin_ref, cos_rows, sin_rows)
    key, value = project_spread(spread, wkv, wkv_copies)
    query = project_from(normed3, wq, wq_copies)
    cosine, sine = cos_rows[...], sin_rows[...]
    query_out[...] = jnp.zeros(query_out.shape, F32)
    for g in range(heads):
        turned = turn(query[:, g * HD : (g + 1) * HD], cosine, sine)
        query_out[pl.ds(g, slots, stride=GROUP), :] = turned.astype(BF16).astype(F32)
    newkey_out[...] = turn(key, cosine, sine).astype(BF16).astype(F32)
    newvalue_out[...] = value.astype(BF16).astype(F32)

    positions = [lengths_s[0, low + slot] for slot in send_slots]
    for copy in loads:
        copy.wait()
    for slot, p in zip(send_slots, positions):
        put_row(cache, slot, p, newkey_out[pl.ds(slot, 1), :], newvalue_out[pl.ds(slot, 1), :])
    cap = cache.shape[2]
    copies = [
        pltpu.make_async_copy(cache.at[slot], box.at[m, :, pl.ds(0, cap), :], box_sem.at[m])
        for m, slot in enumerate(send_slots[:MOVE])
    ]
    for copy in copies:
        copy.start()
    rows = [query_out[pl.ds(pl.multiple_of(slot * GROUP, GROUP), GROUP), :] for slot in send_slots]
    attended = attend(cache, send_slots, positions, rows)
    column = pl.multiple_of(me_tp * shard, shard)
    for at, slot in enumerate(send_slots):
        m = at % MOVE
        residual = hidden32[pl.ds(slot, 1), pl.ds(column, shard)]
        if at < MOVE:
            blocks = [attended[at][g : g + 1, :] for g in range(heads)]
            blocks += [residual[:, b * HD : (b + 1) * HD] for b in range(shard // HD)]
            blocks += [jnp.zeros((1, HD), F32)] * (NOTE - len(blocks))
            box[m, 0, cap : cap + NOTE, :] = jnp.concatenate(blocks, axis=0).astype(BF16)
        else:
            note = notes[at // MOVE]
            for g in range(heads):
                note[m : m + 1, g * HD : (g + 1) * HD] = attended[at][g : g + 1, :]
            note[m : m + 1, heads * HD :] = residual
    for copy in copies:
        copy.wait()


def attend_slots(cache, places, positions, query, attended_rows, heads):
    slots = len(places)
    for first in range(0, slots, BATCH):
        span = range(first, first + BATCH)
        got = attend(
            cache,
            [places[s] for s in span],
            [positions[s] for s in span],
            [query[s * GROUP : (s + 1) * GROUP, :] for s in span],
        )
        for s, rows in zip(span, got):
            attended_rows[s * GROUP : (s + 1) * GROUP, :] = rows
    return jnp.concatenate(
        [attended_rows[pl.ds(g, slots, stride=GROUP), :] for g in range(heads)], axis=1
    )


def attend_kernel(
    slots, heads, meta, lengths_s, query, newkey, newvalue, _, out, cache, attended_rows,
):
    low = meta[0] * slots
    positions = [lengths_s[low + s] for s in range(slots)]
    for s, p in enumerate(positions):
        put_row(cache, s, p, newkey[s : s + 1, :], newvalue[s : s + 1, :])
    out[...] = attend_slots(
        cache, list(range(slots)), positions, query, attended_rows, heads
    ).astype(BF16)


def project_out(attended, wo, residual, own, sends, me_tp, peers_tp):
    shard = own.shape[1]
    for k in list(range(peers_tp - 1, 0, -1)) + [0]:
        column = pl.multiple_of(jnp.bitwise_xor(me_tp, k) * shard, shard)
        part = jnp.dot(attended, wo[:, pl.ds(column, shard)], preferred_element_type=F32)
        if k == 0:
            own[...] = residual + part
        else:
            sends[k - 1][...] = part.astype(BF16)


def out_kernel(
    peers, peers_tp, meta, plan, attended, wo, hidden, box_hbm, *rest,
):
    notes, rest = rest[: peers - 2], rest[peers - 2 :]
    own, sends, (tail, sem) = rest[0], rest[1:peers_tp], rest[peers_tp:]
    shard = own.shape[1]
    cap = box_hbm.shape[2] - NOTE
    copy = pltpu.make_async_copy(box_hbm.at[:, 0, pl.ds(cap, NOTE), :], tail, sem.at[0])
    copy.start()
    rows = attended[...].astype(F32)
    heads = rows.shape[1] // HD
    column = pl.multiple_of(meta[1] * shard, shard)
    residual = hidden[:, pl.ds(column, shard)].astype(F32)
    row_index = lax.broadcasted_iota(I32, rows.shape, 0)
    residual_index = lax.broadcasted_iota(I32, residual.shape, 0)
    copy.wait()
    for at in range((peers - 1) * MOVE):
        m = at % MOVE
        if at < MOVE:
            blocks = tail[m].astype(F32)
            blocks = [blocks[b : b + 1, :] for b in range(heads + shard // HD)]
            note = jnp.concatenate(blocks, axis=1)
        else:
            note = notes[at // MOVE - 1][m : m + 1, :]
        rows = jnp.where(row_index == plan[at], note[:, : heads * HD], rows)
        residual = jnp.where(residual_index == plan[at], note[:, heads * HD :], residual)
    project_out(rows.astype(BF16), wo, residual, own, sends, meta[1], peers_tp)


def pack_kernel(plan, cache, _own, *rest):
    boxes, out_sem = rest[:-1], rest[-1]
    moving = plan.shape[0] // 2
    packs = [
        pltpu.make_async_copy(
            cache.at[plan[moving + at]], boxes[at // MOVE - 1].at[at % MOVE], out_sem.at[at - MOVE]
        )
        for at in range(MOVE, moving)
    ]
    for pack in packs:
        pack.start()
    for pack in packs:
        pack.wait()


def sum_kernel(own, *rest):
    total = own[...]
    for part in rest[:-1]:
        total = total + part[...].astype(F32)
    rest[-1][...] = total.astype(BF16)


def map_places(slots, peers, plan, place):
    for s in range(slots):
        place[s] = s
    for at in range((peers - 1) * MOVE):
        taker = plan[at]

        @pl.when(taker >= 0)
        def _():
            place[taker] = slots + at


def prepare_kernel(
    peers, slots, meta, source_s, lengths_s, plan, cos_ref, sin_ref, wkv, _,
    weight, cos_rows, sin_rows, place,
):
    map_places(slots, peers, plan, place)
    low = meta[0] * slots
    gather_angles(
        lambda s: lengths_s[source_s[low + s]] + 1, slots, cos_ref, sin_ref, cos_rows, sin_rows
    )
    row = lax.broadcasted_iota(I32, (2 * HD, 2 * HD), 0)
    col = lax.broadcasted_iota(I32, (2 * HD, 2 * HD), 1)
    goal = jnp.where(row < HD, 2 * row, 2 * (row - HD) + 1)
    places = jnp.where(col == goal, 1.0, 0.0).astype(BF16)
    for b in range(weight.shape[0] // HD):
        apart = jnp.dot(
            places, wkv[b * 2 * HD : (b + 1) * 2 * HD, :], preferred_element_type=F32
        ).astype(BF16)
        weight[b * HD : (b + 1) * HD, :HD] = apart[:HD]
        weight[b * HD : (b + 1) * HD, HD:] = apart[HD:]


def second_kernel(
    peers, peers_tp, slots, heads,
    meta, source_s, lengths_s, place, gain, cos_rows, sin_rows, wq, wkv, wo, _, *rest,
):
    blocks, rest = rest[:peers_tp], rest[peers_tp:]
    box_hbm, rest = rest[: peers - 1], rest[peers - 1 :]
    own, sends, cache = rest[0], rest[1:peers_tp], rest[peers_tp]
    normed3, query_rows, attended_rows, in_sem = rest[peers_tp + 1 :]
    me, me_tp = meta[0], meta[1]
    low = me * slots
    width = gain.shape[1]
    shard = own.shape[1]
    loads = [
        pltpu.make_async_copy(
            box.at[:, :, pl.ds(0, cache.shape[2]), :],
            cache.at[pl.ds(slots + k * MOVE, MOVE)],
            in_sem.at[k],
        )
        for k, box in enumerate(box_hbm)
    ]
    for copy in loads:
        copy.start()

    firsts = [jnp.bitwise_xor(me_tp, k) for k in range(peers_tp)]
    norm_into(
        normed3,
        [block[...].astype(F32) for block in blocks],
        [gain[:, pl.ds(pl.multiple_of(first * shard, shard), shard)] for first in firsts],
        [first * (shard // HD) for first in firsts],
        width,
    )
    positions = [lengths_s[source_s[low + s]] + 1 for s in range(slots)]
    query = project_from(normed3, wq)
    pair = project_from(normed3, wkv)
    key, value = pair[:, :HD], pair[:, HD:]
    cosine, sine = cos_rows[...], sin_rows[...]
    query_rows[...] = jnp.zeros(query_rows.shape, F32)
    for g in range(heads):
        turned = turn(query[:, g * HD : (g + 1) * HD], cosine, sine)
        query_rows[pl.ds(g, slots, stride=GROUP), :] = turned.astype(BF16).astype(F32)
    newkey = turn(key, cosine, sine).astype(BF16).astype(F32)
    newvalue = value.astype(BF16).astype(F32)

    for copy in loads:
        copy.wait()
    places = [place[s] for s in range(slots)]
    for s, (at, p) in enumerate(zip(places, positions)):
        put_row(cache, at, p, newkey[s : s + 1, :], newvalue[s : s + 1, :])
    attended = attend_slots(cache, places, positions, query_rows, attended_rows, heads)
    project_out(
        attended.astype(BF16), wo, blocks[0][...].astype(F32), own, sends, me_tp, peers_tp
    )


def cache_kernel(slots, place, cache, out_hbm, out_sem):
    copies = [
        pltpu.make_async_copy(cache.at[place[s]], out_hbm.at[s], out_sem.at[s])
        for s in range(slots)
    ]
    for copy in copies:
        copy.start()
    for copy in copies:
        copy.wait()


def join_kernel(peers_tp, meta, *rest):
    blocks, out, sem = rest[:-2], rest[-2], rest[-1]
    shard = blocks[0].shape[1]
    copies = []
    for k, block in enumerate(blocks):
        column = pl.multiple_of(jnp.bitwise_xor(meta[1], k) * shard, shard)
        copies.append(pltpu.make_async_copy(block, out.at[:, pl.ds(column, shard)], sem.at[k]))
        copies[-1].start()
    for copy in copies:
        copy.wait()


def swapped(x, axis, size, k):
    return lax.ppermute(x, axis, [(i, i ^ k) for i in range(size)])


def local(
    tables, kv_cache, hidden, lengths, source, norm_gain, query_weight, keyval_weight, out_weight
):
    peers, peers_tp = lax.axis_size("inst"), lax.axis_size("tp")
    slots, cap = kv_cache.shape[0], kv_cache.shape[2]
    width = hidden.shape[1]
    heads = query_weight.shape[1] // HD
    shard = width // peers_tp
    others, moving = peers - 1, (peers - 1) * MOVE
    blocks = width // HD
    meta = jnp.stack([lax.axis_index("inst"), lax.axis_index("tp")]).astype(I32)
    gain = norm_gain.reshape(1, width)
    wkv = keyval_weight.reshape(2 * width, HD)
    cosine, sine = (jnp.asarray(table) for table in tables)
    row32 = jax.ShapeDtypeStruct((slots, HD), F32)
    note_width = heads * HD + shard
    dma = pltpu.SemaphoreType.DMA
    weights = [
        pltpu.VMEM(query_weight.shape, BF16),
        pltpu.VMEM(wkv.shape, BF16),
    ]
    stages = [
        pltpu.VMEM((blocks, slots, HD), BF16),
        pltpu.VMEM((blocks, 2 * slots, 2 * HD), BF16),
        pltpu.VMEM((slots, HD), F32),
        pltpu.VMEM((slots, HD), F32),
    ]
    flops = 2 * slots * width * (heads + 2) * HD
    cache_bytes = kv_cache.size * 2
    held = jax.ShapeDtypeStruct((slots + moving,) + kv_cache.shape[1:], BF16)

    query, newkey1, newvalue1, plan, cache, *notes = pl.pallas_call(
        functools.partial(first_kernel, peers, slots, heads, shard),
        out_shape=[
            jax.ShapeDtypeStruct((slots * GROUP, HD), F32),
            row32,
            row32,
            jax.ShapeDtypeStruct((2 * moving,), I32),
            held,
        ]
        + [jax.ShapeDtypeStruct((MOVE, 2, cap + NOTE, HD), BF16)]
        + [jax.ShapeDtypeStruct((MOVE, note_width), F32)] * (others - 1),
        in_specs=[SMEM] + [HBM] * 9,
        out_specs=[VMEM] * 3 + [SMEM] + [VMEM] * (others + 1),
        scratch_shapes=weights
        + stages
        + [
            pltpu.VMEM((slots, width), F32),
            pltpu.SMEM((1, source.shape[0]), I32),
            pltpu.SMEM((1, source.shape[0]), I32),
            pltpu.VMEM((1, source.shape[0]), I32),
            pltpu.VMEM(hidden.shape, BF16),
            pltpu.VMEM((1, width), F32),
            pltpu.VMEM(cosine.shape, F32),
            pltpu.VMEM(cosine.shape, F32),
            dma((7,)),
            dma((4,)),
            dma((4,)),
            dma((MOVE,)),
            dma((slots // CHUNK,)),
        ],
        compiler_params=params(24),
        cost_estimate=cost(flops, (query_weight.size + wkv.size) * 2),
        name="first_step",
    )(meta, *(
        pltpu.with_memory_space_constraint(x, pltpu.HBM)
        for x in (source.reshape(1, -1), lengths.reshape(1, -1), hidden, gain, cosine, sine,
                  query_weight, wkv, kv_cache)
    ))
    got_notes = [swapped(note, "inst", peers, k + 1) for k, note in enumerate(notes)]

    attended, cache = pl.pallas_call(
        functools.partial(attend_kernel, slots, heads),
        out_shape=[jax.ShapeDtypeStruct((slots, heads * HD), BF16), held],
        in_specs=[SMEM] * 2 + [VMEM] * 4,
        out_specs=[VMEM] * 2,
        scratch_shapes=[pltpu.VMEM((slots * GROUP, HD), F32)],
        input_output_aliases={5: 1},
        compiler_params=params(12),
        cost_estimate=cost(4 * slots * cap * HD * heads, cache_bytes),
        name="attention",
    )(meta, lengths, query, newkey1, newvalue1, cache)

    sent = [jax.ShapeDtypeStruct((slots, shard), F32)]
    sent += [jax.ShapeDtypeStruct((slots, shard), BF16)] * (peers_tp - 1)
    own, *sends = pl.pallas_call(
        functools.partial(out_kernel, peers, peers_tp),
        out_shape=sent,
        in_specs=[SMEM] * 2 + [VMEM] * 3 + [ANY] + [VMEM] * (others - 1),
        out_specs=[VMEM] * peers_tp,
        scratch_shapes=[pltpu.VMEM((MOVE, NOTE, HD), BF16), dma((1,))],
        compiler_params=params(16),
        cost_estimate=cost(2 * slots * width * heads * HD, out_weight.size * 2),
        name="out_projection",
    )(meta, plan, attended, out_weight, hidden, *got_notes)
    boxes = pl.pallas_call(
        pack_kernel,
        out_shape=[jax.ShapeDtypeStruct((MOVE,) + kv_cache.shape[1:], BF16)] * (others - 1),
        in_specs=[SMEM, VMEM, ANY],
        out_specs=[ANY] * (others - 1),
        scratch_shapes=[dma((moving - MOVE,))],
        compiler_params=params(16),
        cost_estimate=cost(1, 1 * cache_bytes),
        name="pack",
    )(plan, cache, own)
    got_boxes = got_notes[:1] + [swapped(box, "inst", peers, k + 2) for k, box in enumerate(boxes)]

    def summed(own, sends, passed_on):
        got = [swapped(sends[k - 1], "tp", peers_tp, k) for k in range(peers_tp - 1, 0, -1)]
        shard_rows = pl.pallas_call(
            sum_kernel,
            out_shape=jax.ShapeDtypeStruct((slots, shard), BF16),
            in_specs=[VMEM] * peers_tp,
            out_specs=VMEM,
            compiler_params=params(16),
            name="sum_terms",
        )(own, *got)
        blocks = {0: shard_rows}
        if not passed_on:
            blocks |= {k: swapped(shard_rows, "tp", peers_tp, k) for k in range(1, peers_tp)}
        far = peers_tp // 2 if passed_on else 0
        while far:
            blocks |= {k + far: swapped(blocks[k], "tp", peers_tp, far) for k in blocks}
            far //= 2
        return [blocks[k] for k in range(peers_tp)]

    pieces = summed(own, sends, False)

    weight, cos_rows, sin_rows, place = pl.pallas_call(
        functools.partial(prepare_kernel, peers, slots),
        out_shape=[
            jax.ShapeDtypeStruct((width, 2 * HD), BF16),
            row32,
            row32,
            jax.ShapeDtypeStruct((slots,), I32),
        ],
        in_specs=[SMEM] * 4 + [VMEM] * 3 + [ANY],
        out_specs=[VMEM] * 3 + [SMEM],
        compiler_params=params(16),
        cost_estimate=cost(100*flops, wkv.size * 40),
        name="prepare",
    )(meta, source, lengths, plan, cosine, sine, wkv, own)

    own, *sends, cache = pl.pallas_call(
        functools.partial(second_kernel, peers, peers_tp, slots, heads),
        out_shape=sent + [held],
        in_specs=[SMEM] * 4 + [VMEM] * (7 + peers_tp) + [ANY] * others,
        out_specs=[VMEM] * (1 + peers_tp),
        scratch_shapes=[
            pltpu.VMEM((blocks, slots, HD), BF16),
            pltpu.VMEM((slots * GROUP, HD), F32),
            pltpu.VMEM((slots * GROUP, HD), F32),
            dma((others,)),
        ],
        input_output_aliases={10: peers_tp},
        compiler_params=params(16),
        cost_estimate=cost(3 * flops, cache_bytes + (query_weight.size + wkv.size) * 4),
        name="second_step",
    )(meta, source, lengths, place, gain, cos_rows, sin_rows, query_weight, weight, out_weight, cache,
      *pieces, *got_boxes)

    pieces = summed(own, sends, False)
    final_cache = pl.pallas_call(
        functools.partial(cache_kernel, slots),
        out_shape=jax.ShapeDtypeStruct(kv_cache.shape, BF16),
        in_specs=[SMEM, VMEM],
        out_specs=ANY,
        scratch_shapes=[dma((slots,))],
        compiler_params=params(16),
        cost_estimate=cost(0, 2 * cache_bytes),
        name="write_cache",
    )(place, cache)
    final_hidden = pl.pallas_call(
        functools.partial(join_kernel, peers_tp),
        out_shape=jax.ShapeDtypeStruct(hidden.shape, BF16),
        in_specs=[SMEM] + [ANY] * peers_tp,
        out_specs=ANY,
        scratch_shapes=[dma((peers_tp,))],
        compiler_params=params(16),
        name="join",
    )(meta, *pieces)
    return (final_hidden, final_cache)


def solution(mesh):
    def whole(kv_cache, *rest):
        tables = angle_tables(kv_cache.shape[2])
        return jax.shard_map(
            functools.partial(local, tables),
            mesh=mesh,
            in_specs=(
                P(("groups", "inst"), None, None, "tp"),
                P(("groups", "inst"), None),
                P("groups"),
                P("groups"),
                P(),
                P(None, "tp"),
                P(None, None, "tp"),
                P("tp", None),
            ),
            out_specs=(P(("groups", "inst"), None), P(("groups", "inst"), None, None, "tp")),
            check_vma=False,
        )(kv_cache, *rest)

    return whole
```

```python
import functools

import jax
import jax.numpy as jnp
import numpy as np
from jax import lax
from jax.experimental import pallas as pl
from jax.experimental.pallas import tpu as pltpu
from jax.sharding import PartitionSpec as P

MOVE = 2
EPS = 1e-05
THETA = 500000.0
HD = 128
GROUP = 8
PIECE = 16
CHUNK = 8
BATCH = 16
NOTE = 16

F32 = jnp.float32
BF16 = jnp.bfloat16
I32 = jnp.int32

ANY = pl.BlockSpec(memory_space=pl.ANY)
VMEM = pl.BlockSpec(memory_space=pltpu.VMEM)
SMEM = pl.BlockSpec(memory_space=pltpu.SMEM)
HBM = pl.BlockSpec(memory_space=pltpu.HBM)


def params(mib):
    return pltpu.CompilerParams(vmem_limit_bytes=mib * 1024 * 1024)


def cost(flops, nbytes):
    return pl.CostEstimate(flops=flops, bytes_accessed=nbytes, transcendentals=0)


def angle_tables(positions):
    frequency = THETA ** (-(np.arange(HD // 2, dtype=np.float64) * 2.0) / HD)
    angles = np.arange(positions, dtype=np.float64)[:, None] * frequency[None, :]
    cosine = np.concatenate([np.cos(angles), np.cos(angles)], axis=-1)
    sine = np.concatenate([-np.sin(angles), np.sin(angles)], axis=-1)
    return cosine.astype(np.float32), sine.astype(np.float32)


def turn(x, cosine, sine):
    return x * cosine + pltpu.roll(x, HD // 2, 1) * sine


def gather_angles(position_of, slots, cos_ref, sin_ref, cos_rows, sin_rows):
    for s in range(slots):
        p = position_of(s)
        cos_rows[s : s + 1, :] = cos_ref[pl.ds(p, 1), :]
        sin_rows[s : s + 1, :] = sin_ref[pl.ds(p, 1), :]


def spread_normed(normed3, spread, slots, width):
    blocks = width // HD
    row = lax.broadcasted_iota(I32, (HD, 4 * HD), 0)
    col = lax.broadcasted_iota(I32, (HD, 4 * HD), 1)
    goal = jnp.where(col < 2 * HD, 2 * row, 2 * row + 1 + 2 * HD)
    places = jnp.where(col == goal, 1.0, 0.0).astype(BF16)
    spread_all = jnp.dot(
        normed3[...].reshape(blocks * slots, HD), places, preferred_element_type=F32
    ).astype(BF16)
    spread[:, 0:slots, :] = spread_all[:, : 2 * HD].reshape(blocks, slots, 2 * HD)
    spread[:, slots:, :] = spread_all[:, 2 * HD :].reshape(blocks, slots, 2 * HD)


def project_from(normed3, weight, copies=()):
    total = None
    pairs = normed3.shape[0] // 2
    pieces = max(len(copies), 1)
    for b in range(pairs):
        if copies and b % (pairs // pieces) == 0:
            copies[b // (pairs // pieces)].wait()
        block = jnp.concatenate([normed3[2 * b], normed3[2 * b + 1]], axis=1)
        part = jnp.dot(
            block, weight[b * 2 * HD : (b + 1) * 2 * HD, :], preferred_element_type=F32
        )
        total = part if total is None else total + part
    return total


def project_spread(spread, wkv, copies):
    total = None
    blocks = spread.shape[0]
    for b in range(blocks):
        if b % (blocks // len(copies)) == 0:
            copies[b // (blocks // len(copies))].wait()
        part = jnp.dot(
            spread[b], wkv[b * 2 * HD : (b + 1) * 2 * HD, :], preferred_element_type=F32
        )
        total = part if total is None else total + part
    slots = spread.shape[1] // 2
    return total[:slots], total[slots:]


def weight_copies(src, dst, sem, pieces):
    depth = src.shape[0] // pieces
    copies = [
        pltpu.make_async_copy(
            src.at[pl.ds(c * depth, depth)], dst.at[pl.ds(c * depth, depth)], sem.at[c]
        )
        for c in range(pieces)
    ]
    return copies


def put_row(cache, place, p, key_row, value_row):
    base = pl.multiple_of((jnp.maximum(p, 0) // PIECE) * PIECE, PIECE)
    hit = lax.broadcasted_iota(I32, (PIECE, HD), 0) + base == p
    for which, new in ((0, key_row), (1, value_row)):
        old = cache[place, which, pl.ds(base, PIECE), :].astype(F32)
        cache[place, which, pl.ds(base, PIECE), :] = jnp.where(hit, new, old).astype(BF16)


def attend(cache, places, positions, query_rows):
    cap = cache.shape[2]
    col = lax.broadcasted_iota(I32, (GROUP, cap), 1)
    scores = [
        lax.dot_general(
            rows.astype(BF16),
            cache[place, 0],
            (((1,), (1,)), ((), ())),
            preferred_element_type=F32,
        )
        for place, rows in zip(places, query_rows)
    ]
    probs = []
    for score, p in zip(scores, positions):
        score = jnp.where(col <= p, score * HD**-0.5, -jnp.inf)
        weight = jnp.exp(score - jnp.max(score, axis=-1, keepdims=True))
        weight = weight / jnp.sum(weight, axis=-1, keepdims=True)
        probs.append(weight.astype(BF16))
    return [
        jnp.dot(prob, cache[place, 1], preferred_element_type=F32)
        for place, prob in zip(places, probs)
    ]


def norm_into(normed3, pieces, gains, firsts, total_width):
    square = None
    for piece in pieces:
        part = jnp.sum(piece * piece, axis=-1, keepdims=True)
        square = part if square is None else square + part
    factor = lax.rsqrt(square / total_width + EPS)
    for piece, gain, first in zip(pieces, gains, firsts):
        normed = (piece * factor * gain).astype(BF16)
        for i in range(piece.shape[1] // HD):
            normed3[first + i] = normed[:, i * HD : (i + 1) * HD]


def cache_copies(cache_hbm, cache, sem, first, last):
    return [
        pltpu.make_async_copy(
            cache_hbm.at[pl.ds(at, CHUNK)], cache.at[pl.ds(at, CHUNK)], sem.at[i]
        )
        for i, at in enumerate(range(first, last, CHUNK))
    ]


def first_kernel(
    peers, slots, heads, shard,
    meta, source_hbm, lengths_hbm, hidden_hbm, gain_hbm, cos_hbm, sin_hbm, wq_hbm, wkv_hbm,
    cache_hbm, query_out, newkey_out, newvalue_out, plan, *rest,
):
    others = peers - 1
    moving = others * MOVE
    cache, box, notes = rest[0], rest[1], (None,) + rest[2 : others + 1]
    (wq, wkv, normed3, spread, cos_rows, sin_rows, leaving, hidden32, source_s, lengths_s, source_v,
     hidden, gain, cos_ref, sin_ref, small_sem, wq_sem, wkv_sem, in_sem,
     box_sem, cache_sem) = rest[others + 1 :]
    width = hidden.shape[1]
    me, me_tp = meta[0], meta[1]
    wq_copies = weight_copies(wq_hbm, wq, wq_sem, 4)
    wkv_copies = weight_copies(wkv_hbm, wkv, wkv_sem, 4)
    small = [
        pltpu.make_async_copy(src, dst, small_sem.at[i])
        for i, (src, dst) in enumerate((
            (source_hbm, source_v), (source_hbm, source_s), (hidden_hbm, hidden), (gain_hbm, gain),
            (lengths_hbm, lengths_s), (cos_hbm, cos_ref), (sin_hbm, sin_ref),
        ))
    ]
    for copy in small[:4] + wkv_copies + wq_copies + small[4:]:
        copy.start()
    loads = cache_copies(cache_hbm, cache, cache_sem, 0, slots - BATCH)
    for copy in small[:2]:
        copy.wait()

    low = me * slots
    src = source_v[...]
    index = lax.broadcasted_iota(I32, src.shape, 1)
    mine_goes = (src >= low) & (src < low + slots)
    mine_comes = (index >= low) & (index < low + slots)
    index_f = index.astype(F32)
    send_slots = []
    for k in range(1, peers):
        other = jnp.bitwise_xor(me, k) * slots
        sent = mine_goes & (index >= other) & (index < other + slots)
        taken = mine_comes & (src >= other) & (src < other + slots)
        for m in range(MOVE):
            at = (k - 1) * MOVE + m
            if m == 0:
                j = jnp.min(jnp.where(sent, index_f, 1e6)).astype(I32)
                r = jnp.min(jnp.where(taken, index_f, 1e6)).astype(I32)
            else:
                j = jnp.max(jnp.where(sent, index_f, -1.0)).astype(I32)
                r = jnp.max(jnp.where(taken, index_f, -1.0)).astype(I32)
            known = (j >= 0) & (j < src.shape[1])
            slot = source_s[0, jnp.where(known, j, 0)] - low
            slot = jnp.where(known, slot, 0)
            send_slots.append(slot)
            plan[at] = jnp.where((r >= 0) & (r < src.shape[1]), r - low, -1)
            plan[moving + at] = slot
            pltpu.make_async_copy(cache_hbm.at[slot], leaving.at[at], in_sem.at[at]).start()
    for copy in loads:
        copy.start()

    for copy in small[2:4]:
        copy.wait()
    wide = hidden[...].astype(F32)
    hidden32[...] = wide
    norm_into(normed3, [wide], [gain[...]], [0], width)
    spread_normed(normed3, spread, slots, width)
    for copy in small[4:]:
        copy.wait()
    gather_angles(lambda s: lengths_s[0, low + s], slots, cos_ref, sin_ref, cos_rows, sin_rows)
    key, value = project_spread(spread, wkv, wkv_copies)
    query = project_from(normed3, wq, wq_copies)
    cosine, sine = cos_rows[...], sin_rows[...]
    query_out[...] = jnp.zeros(query_out.shape, F32)
    for g in range(heads):
        turned = turn(query[:, g * HD : (g + 1) * HD], cosine, sine)
        query_out[pl.ds(g, slots, stride=GROUP), :] = turned.astype(BF16).astype(F32)
    newkey_out[...] = turn(key, cosine, sine).astype(BF16).astype(F32)
    newvalue_out[...] = value.astype(BF16).astype(F32)

    positions = [lengths_s[0, low + slot] for slot in send_slots]
    for at, slot in enumerate(send_slots):
        pltpu.make_async_copy(cache_hbm.at[slot], leaving.at[at], in_sem.at[at]).wait()
        put_row(
            leaving, at, positions[at],
            newkey_out[pl.ds(slot, 1), :], newvalue_out[pl.ds(slot, 1), :],
        )
    cap = leaving.shape[2]
    copies = [
        pltpu.make_async_copy(
            leaving.at[pl.ds(0, MOVE)], box.at[:, :, pl.ds(0, cap), :], box_sem.at[0]
        )
    ]
    copies[0].start()
    rows = [query_out[pl.ds(pl.multiple_of(slot * GROUP, GROUP), GROUP), :] for slot in send_slots]
    attended = attend(leaving, list(range(moving)), positions, rows)
    column = pl.multiple_of(me_tp * shard, shard)
    for at, slot in enumerate(send_slots):
        m = at % MOVE
        residual = hidden32[pl.ds(slot, 1), pl.ds(column, shard)]
        if at < MOVE:
            blocks = [attended[at][g : g + 1, :] for g in range(heads)]
            blocks += [residual[:, b * HD : (b + 1) * HD] for b in range(shard // HD)]
            blocks += [jnp.zeros((1, HD), F32)] * (NOTE - len(blocks))
            box[m, 0, cap : cap + NOTE, :] = jnp.concatenate(blocks, axis=0).astype(BF16)
        else:
            note = notes[at // MOVE]
            for g in range(heads):
                note[m : m + 1, g * HD : (g + 1) * HD] = attended[at][g : g + 1, :]
            note[m : m + 1, heads * HD :] = residual
    for copy in copies + loads:
        copy.wait()


def attend_slots(cache, places, positions, query, attended_rows, first, last):
    for start in range(first, last, BATCH):
        span = range(start, start + BATCH)
        got = attend(
            cache,
            [places[s] for s in span],
            [positions[s] for s in span],
            [query[s * GROUP : (s + 1) * GROUP, :] for s in span],
        )
        for s, rows in zip(span, got):
            attended_rows[s * GROUP : (s + 1) * GROUP, :] = rows


def side_by_side(attended_rows, slots, heads):
    return jnp.concatenate(
        [attended_rows[pl.ds(g, slots, stride=GROUP), :] for g in range(heads)], axis=1
    ).astype(BF16)


def attend_kernel(
    slots, heads, meta, lengths_s, query, newkey, newvalue, cache_hbm, _,
    out, cache, attended_rows, in_sem,
):
    low = meta[0] * slots
    early = slots - BATCH
    loads = cache_copies(cache_hbm, cache, in_sem, early, slots)
    for copy in loads:
        copy.start()
    positions = [lengths_s[low + s] for s in range(slots)]
    for first, last in ((0, early), (early, slots)):
        if first:
            for copy in loads:
                copy.wait()
        for s in range(first, last):
            put_row(cache, s, positions[s], newkey[s : s + 1, :], newvalue[s : s + 1, :])
        attend_slots(cache, list(range(slots)), positions, query, attended_rows, first, last)
    out[...] = side_by_side(attended_rows, slots, heads)


def project_out(attended, wo, residual, own, sends, me_tp, peers_tp):
    shard = own.shape[1]
    for k in list(range(peers_tp - 1, 0, -1)) + [0]:
        column = pl.multiple_of(jnp.bitwise_xor(me_tp, k) * shard, shard)
        part = jnp.dot(attended, wo[:, pl.ds(column, shard)], preferred_element_type=F32)
        if k == 0:
            own[...] = residual + part
        else:
            sends[k - 1][...] = part.astype(BF16)


def out_kernel(
    peers, peers_tp, meta, plan, attended, wo, hidden, box_hbm, *rest,
):
    notes, rest = rest[: peers - 2], rest[peers - 2 :]
    own, sends, (tail, sem) = rest[0], rest[1:peers_tp], rest[peers_tp:]
    shard = own.shape[1]
    cap = box_hbm.shape[2] - NOTE
    copy = pltpu.make_async_copy(box_hbm.at[:, 0, pl.ds(cap, NOTE), :], tail, sem.at[0])
    copy.start()
    rows = attended[...].astype(F32)
    heads = rows.shape[1] // HD
    column = pl.multiple_of(meta[1] * shard, shard)
    residual = hidden[:, pl.ds(column, shard)].astype(F32)
    row_index = lax.broadcasted_iota(I32, rows.shape, 0)
    residual_index = lax.broadcasted_iota(I32, residual.shape, 0)
    copy.wait()
    for at in range((peers - 1) * MOVE):
        m = at % MOVE
        if at < MOVE:
            blocks = tail[m].astype(F32)
            blocks = [blocks[b : b + 1, :] for b in range(heads + shard // HD)]
            note = jnp.concatenate(blocks, axis=1)
        else:
            note = notes[at // MOVE - 1][m : m + 1, :]
        rows = jnp.where(row_index == plan[at], note[:, : heads * HD], rows)
        residual = jnp.where(residual_index == plan[at], note[:, heads * HD :], residual)
    project_out(rows.astype(BF16), wo, residual, own, sends, meta[1], peers_tp)


def pack_kernel(plan, cache, _own, *rest):
    boxes, out_sem = rest[:-1], rest[-1]
    moving = plan.shape[0] // 2
    packs = [
        pltpu.make_async_copy(
            cache.at[plan[moving + at]], boxes[at // MOVE - 1].at[at % MOVE], out_sem.at[at - MOVE]
        )
        for at in range(MOVE, moving)
    ]
    for pack in packs:
        pack.start()
    for pack in packs:
        pack.wait()


def sum_kernel(own, *rest):
    total = own[...]
    for part in rest[:-1]:
        total = total + part[...].astype(F32)
    rest[-1][...] = total.astype(BF16)


def map_places(slots, peers, plan, place):
    for s in range(slots):
        place[s] = s
    for at in range((peers - 1) * MOVE):
        taker = plan[at]

        @pl.when(taker >= 0)
        def _():
            place[taker] = slots + at


def prepare_kernel(
    peers, slots, meta, source_s, lengths_s, plan, cos_ref, sin_ref, wkv, _,
    weight, cos_rows, sin_rows, place,
):
    map_places(slots, peers, plan, place)
    low = meta[0] * slots
    gather_angles(
        lambda s: lengths_s[source_s[low + s]] + 1, slots, cos_ref, sin_ref, cos_rows, sin_rows
    )
    row = lax.broadcasted_iota(I32, (2 * HD, 2 * HD), 0)
    col = lax.broadcasted_iota(I32, (2 * HD, 2 * HD), 1)
    goal = jnp.where(row < HD, 2 * row, 2 * (row - HD) + 1)
    places = jnp.where(col == goal, 1.0, 0.0).astype(BF16)
    for b in range(weight.shape[0] // HD):
        apart = jnp.dot(
            places, wkv[b * 2 * HD : (b + 1) * 2 * HD, :], preferred_element_type=F32
        ).astype(BF16)
        weight[b * HD : (b + 1) * HD, :HD] = apart[:HD]
        weight[b * HD : (b + 1) * HD, HD:] = apart[HD:]


def second_kernel(
    peers, peers_tp, slots, heads,
    meta, source_s, lengths_s, place, gain, cos_rows, sin_rows, wq, wkv, wo, _, *rest,
):
    blocks, rest = rest[:peers_tp], rest[peers_tp:]
    box_hbm, rest = rest[: peers - 1], rest[peers - 1 :]
    own, sends, cache = rest[0], rest[1:peers_tp], rest[peers_tp]
    normed3, query_rows, attended_rows, in_sem = rest[peers_tp + 1 :]
    me, me_tp = meta[0], meta[1]
    low = me * slots
    width = gain.shape[1]
    shard = own.shape[1]
    loads = [
        pltpu.make_async_copy(
            box.at[:, :, pl.ds(0, cache.shape[2]), :],
            cache.at[pl.ds(slots + k * MOVE, MOVE)],
            in_sem.at[k],
        )
        for k, box in enumerate(box_hbm)
    ]
    for copy in loads:
        copy.start()

    firsts = [jnp.bitwise_xor(me_tp, k) for k in range(peers_tp)]
    norm_into(
        normed3,
        [block[...].astype(F32) for block in blocks],
        [gain[:, pl.ds(pl.multiple_of(first * shard, shard), shard)] for first in firsts],
        [first * (shard // HD) for first in firsts],
        width,
    )
    positions = [lengths_s[source_s[low + s]] + 1 for s in range(slots)]
    query = project_from(normed3, wq)
    pair = project_from(normed3, wkv)
    key, value = pair[:, :HD], pair[:, HD:]
    cosine, sine = cos_rows[...], sin_rows[...]
    query_rows[...] = jnp.zeros(query_rows.shape, F32)
    for g in range(heads):
        turned = turn(query[:, g * HD : (g + 1) * HD], cosine, sine)
        query_rows[pl.ds(g, slots, stride=GROUP), :] = turned.astype(BF16).astype(F32)
    newkey = turn(key, cosine, sine).astype(BF16).astype(F32)
    newvalue = value.astype(BF16).astype(F32)

    for copy in loads:
        copy.wait()
    places = [place[s] for s in range(slots)]
    for s, (at, p) in enumerate(zip(places, positions)):
        put_row(cache, at, p, newkey[s : s + 1, :], newvalue[s : s + 1, :])
    attend_slots(cache, places, positions, query_rows, attended_rows, 0, slots)
    attended = side_by_side(attended_rows, slots, heads)
    project_out(attended, wo, blocks[0][...].astype(F32), own, sends, me_tp, peers_tp)


def cache_kernel(slots, place, cache, out_hbm, out_sem):
    copies = [
        pltpu.make_async_copy(cache.at[place[s]], out_hbm.at[s], out_sem.at[s])
        for s in range(slots)
    ]
    for copy in copies:
        copy.start()
    for copy in copies:
        copy.wait()


def join_kernel(peers_tp, meta, *rest):
    blocks, out, sem = rest[:-2], rest[-2], rest[-1]
    shard = blocks[0].shape[1]
    copies = []
    for k, block in enumerate(blocks):
        column = pl.multiple_of(jnp.bitwise_xor(meta[1], k) * shard, shard)
        copies.append(pltpu.make_async_copy(block, out.at[:, pl.ds(column, shard)], sem.at[k]))
        copies[-1].start()
    for copy in copies:
        copy.wait()


def swapped(x, axis, size, k):
    return lax.ppermute(x, axis, [(i, i ^ k) for i in range(size)])


def local(
    tables, kv_cache, hidden, lengths, source, norm_gain, query_weight, keyval_weight, out_weight
):
    peers, peers_tp = lax.axis_size("inst"), lax.axis_size("tp")
    slots, cap = kv_cache.shape[0], kv_cache.shape[2]
    width = hidden.shape[1]
    heads = query_weight.shape[1] // HD
    shard = width // peers_tp
    others, moving = peers - 1, (peers - 1) * MOVE
    blocks = width // HD
    meta = jnp.stack([lax.axis_index("inst"), lax.axis_index("tp")]).astype(I32)
    gain = norm_gain.reshape(1, width)
    wkv = keyval_weight.reshape(2 * width, HD)
    cosine, sine = (jnp.asarray(table) for table in tables)
    row32 = jax.ShapeDtypeStruct((slots, HD), F32)
    note_width = heads * HD + shard
    dma = pltpu.SemaphoreType.DMA
    weights = [
        pltpu.VMEM(query_weight.shape, BF16),
        pltpu.VMEM(wkv.shape, BF16),
    ]
    stages = [
        pltpu.VMEM((blocks, slots, HD), BF16),
        pltpu.VMEM((blocks, 2 * slots, 2 * HD), BF16),
        pltpu.VMEM((slots, HD), F32),
        pltpu.VMEM((slots, HD), F32),
    ]
    flops = 2 * slots * width * (heads + 2) * HD
    cache_bytes = kv_cache.size * 2
    held = jax.ShapeDtypeStruct((slots + moving,) + kv_cache.shape[1:], BF16)

    query, newkey1, newvalue1, plan, cache, *notes = pl.pallas_call(
        functools.partial(first_kernel, peers, slots, heads, shard),
        out_shape=[
            jax.ShapeDtypeStruct((slots * GROUP, HD), F32),
            row32,
            row32,
            jax.ShapeDtypeStruct((2 * moving,), I32),
            held,
        ]
        + [jax.ShapeDtypeStruct((MOVE, 2, cap + NOTE, HD), BF16)]
        + [jax.ShapeDtypeStruct((MOVE, note_width), F32)] * (others - 1),
        in_specs=[SMEM] + [HBM] * 9,
        out_specs=[VMEM] * 3 + [SMEM] + [VMEM] * (others + 1),
        scratch_shapes=weights
        + stages
        + [
            pltpu.VMEM((moving,) + kv_cache.shape[1:], BF16),
            pltpu.VMEM((slots, width), F32),
            pltpu.SMEM((1, source.shape[0]), I32),
            pltpu.SMEM((1, source.shape[0]), I32),
            pltpu.VMEM((1, source.shape[0]), I32),
            pltpu.VMEM(hidden.shape, BF16),
            pltpu.VMEM((1, width), F32),
            pltpu.VMEM(cosine.shape, F32),
            pltpu.VMEM(cosine.shape, F32),
            dma((7,)),
            dma((4,)),
            dma((4,)),
            dma((moving,)),
            dma((1,)),
            dma(((slots - BATCH) // CHUNK,)),
        ],
        compiler_params=params(24),
        cost_estimate=cost(flops, (query_weight.size + wkv.size) * 2),
        name="first_step",
    )(meta, *(
        pltpu.with_memory_space_constraint(x, pltpu.HBM)
        for x in (source.reshape(1, -1), lengths.reshape(1, -1), hidden, gain, cosine, sine,
                  query_weight, wkv, kv_cache)
    ))
    got_notes = [swapped(note, "inst", peers, k + 1) for k, note in enumerate(notes)]

    attended, cache = pl.pallas_call(
        functools.partial(attend_kernel, slots, heads),
        out_shape=[jax.ShapeDtypeStruct((slots, heads * HD), BF16), held],
        in_specs=[SMEM] * 2 + [VMEM] * 3 + [HBM, VMEM],
        out_specs=[VMEM] * 2,
        scratch_shapes=[pltpu.VMEM((slots * GROUP, HD), F32), dma((BATCH // CHUNK,))],
        input_output_aliases={6: 1},
        compiler_params=params(12),
        cost_estimate=cost(4 * slots * cap * HD * heads, cache_bytes),
        name="attention",
    )(meta, lengths, query, newkey1, newvalue1,
      pltpu.with_memory_space_constraint(kv_cache, pltpu.HBM), cache)

    sent = [jax.ShapeDtypeStruct((slots, shard), F32)]
    sent += [jax.ShapeDtypeStruct((slots, shard), BF16)] * (peers_tp - 1)
    own, *sends = pl.pallas_call(
        functools.partial(out_kernel, peers, peers_tp),
        out_shape=sent,
        in_specs=[SMEM] * 2 + [VMEM] * 3 + [ANY] + [VMEM] * (others - 1),
        out_specs=[VMEM] * peers_tp,
        scratch_shapes=[pltpu.VMEM((MOVE, NOTE, HD), BF16), dma((1,))],
        compiler_params=params(16),
        cost_estimate=cost(2 * slots * width * heads * HD, out_weight.size * 2),
        name="out_projection",
    )(meta, plan, attended, out_weight, hidden, *got_notes)
    boxes = pl.pallas_call(
        pack_kernel,
        out_shape=[jax.ShapeDtypeStruct((MOVE,) + kv_cache.shape[1:], BF16)] * (others - 1),
        in_specs=[SMEM, VMEM, ANY],
        out_specs=[ANY] * (others - 1),
        scratch_shapes=[dma((moving - MOVE,))],
        compiler_params=params(16),
        cost_estimate=cost(1, 1 * cache_bytes),
        name="pack",
    )(plan, cache, own)
    got_boxes = got_notes[:1] + [swapped(box, "inst", peers, k + 2) for k, box in enumerate(boxes)]

    def summed(own, sends, passed_on):
        got = [swapped(sends[k - 1], "tp", peers_tp, k) for k in range(peers_tp - 1, 0, -1)]
        shard_rows = pl.pallas_call(
            sum_kernel,
            out_shape=jax.ShapeDtypeStruct((slots, shard), BF16),
            in_specs=[VMEM] * peers_tp,
            out_specs=VMEM,
            compiler_params=params(16),
            name="sum_terms",
        )(own, *got)
        blocks = {0: shard_rows}
        if not passed_on:
            blocks |= {k: swapped(shard_rows, "tp", peers_tp, k) for k in range(1, peers_tp)}
        far = peers_tp // 2 if passed_on else 0
        while far:
            blocks |= {k + far: swapped(blocks[k], "tp", peers_tp, far) for k in blocks}
            far //= 2
        return [blocks[k] for k in range(peers_tp)]

    pieces = summed(own, sends, False)

    weight, cos_rows, sin_rows, place = pl.pallas_call(
        functools.partial(prepare_kernel, peers, slots),
        out_shape=[
            jax.ShapeDtypeStruct((width, 2 * HD), BF16),
            row32,
            row32,
            jax.ShapeDtypeStruct((slots,), I32),
        ],
        in_specs=[SMEM] * 4 + [VMEM] * 3 + [ANY],
        out_specs=[VMEM] * 3 + [SMEM],
        compiler_params=params(16),
        cost_estimate=cost(100*flops, wkv.size * 40),
        name="prepare",
    )(meta, source, lengths, plan, cosine, sine, wkv, own)

    own, *sends, cache = pl.pallas_call(
        functools.partial(second_kernel, peers, peers_tp, slots, heads),
        out_shape=sent + [held],
        in_specs=[SMEM] * 4 + [VMEM] * (7 + peers_tp) + [ANY] * others,
        out_specs=[VMEM] * (1 + peers_tp),
        scratch_shapes=[
            pltpu.VMEM((blocks, slots, HD), BF16),
            pltpu.VMEM((slots * GROUP, HD), F32),
            pltpu.VMEM((slots * GROUP, HD), F32),
            dma((others,)),
        ],
        input_output_aliases={10: peers_tp},
        compiler_params=params(16),
        cost_estimate=cost(3 * flops, cache_bytes + (query_weight.size + wkv.size) * 4),
        name="second_step",
    )(meta, source, lengths, place, gain, cos_rows, sin_rows, query_weight, weight, out_weight, cache,
      *pieces, *got_boxes)

    pieces = summed(own, sends, False)
    final_cache = pl.pallas_call(
        functools.partial(cache_kernel, slots),
        out_shape=jax.ShapeDtypeStruct(kv_cache.shape, BF16),
        in_specs=[SMEM, VMEM],
        out_specs=ANY,
        scratch_shapes=[dma((slots,))],
        compiler_params=params(16),
        cost_estimate=cost(0, 2 * cache_bytes),
        name="write_cache",
    )(place, cache)
    final_hidden = pl.pallas_call(
        functools.partial(join_kernel, peers_tp),
        out_shape=jax.ShapeDtypeStruct(hidden.shape, BF16),
        in_specs=[SMEM] + [ANY] * peers_tp,
        out_specs=ANY,
        scratch_shapes=[dma((peers_tp,))],
        compiler_params=params(16),
        name="join",
    )(meta, *pieces)
    return (final_hidden, final_cache)


def solution(mesh):
    def whole(kv_cache, *rest):
        tables = angle_tables(kv_cache.shape[2])
        return jax.shard_map(
            functools.partial(local, tables),
            mesh=mesh,
            in_specs=(
                P(("groups", "inst"), None, None, "tp"),
                P(("groups", "inst"), None),
                P("groups"),
                P("groups"),
                P(),
                P(None, "tp"),
                P(None, None, "tp"),
                P("tp", None),
            ),
            out_specs=(P(("groups", "inst"), None), P(("groups", "inst"), None, None, "tp")),
            check_vma=False,
        )(kv_cache, *rest)

    return whole
```

```python
import functools

import jax
import jax.numpy as jnp
import numpy as np
from jax import lax
from jax.experimental import pallas as pl
from jax.experimental.pallas import tpu as pltpu
from jax.sharding import PartitionSpec as P

MOVE = 2
EPS = 1e-05
THETA = 500000.0
HD = 128
GROUP = 8
PIECE = 16
CHUNK = 8
BATCH = 16
NOTE = 16

F32 = jnp.float32
BF16 = jnp.bfloat16
I32 = jnp.int32

ANY = pl.BlockSpec(memory_space=pl.ANY)
VMEM = pl.BlockSpec(memory_space=pltpu.VMEM)
SMEM = pl.BlockSpec(memory_space=pltpu.SMEM)
HBM = pl.BlockSpec(memory_space=pltpu.HBM)


def params(mib):
    return pltpu.CompilerParams(vmem_limit_bytes=mib * 1024 * 1024)


def cost(flops, nbytes):
    return pl.CostEstimate(flops=flops, bytes_accessed=nbytes, transcendentals=0)


def angle_tables(positions):
    frequency = THETA ** (-(np.arange(HD // 2, dtype=np.float64) * 2.0) / HD)
    angles = np.arange(positions, dtype=np.float64)[:, None] * frequency[None, :]
    cosine = np.concatenate([np.cos(angles), np.cos(angles)], axis=-1)
    sine = np.concatenate([-np.sin(angles), np.sin(angles)], axis=-1)
    return cosine.astype(np.float32), sine.astype(np.float32)


def turn(x, cosine, sine):
    return x * cosine + pltpu.roll(x, HD // 2, 1) * sine


def gather_angles(position_of, slots, cos_ref, sin_ref, cos_rows, sin_rows):
    for s in range(slots):
        p = position_of(s)
        cos_rows[s : s + 1, :] = cos_ref[pl.ds(p, 1), :]
        sin_rows[s : s + 1, :] = sin_ref[pl.ds(p, 1), :]


def spread_normed(normed3, spread, slots, width):
    blocks = width // HD
    row = lax.broadcasted_iota(I32, (HD, 4 * HD), 0)
    col = lax.broadcasted_iota(I32, (HD, 4 * HD), 1)
    goal = jnp.where(col < 2 * HD, 2 * row, 2 * row + 1 + 2 * HD)
    places = jnp.where(col == goal, 1.0, 0.0).astype(BF16)
    spread_all = jnp.dot(
        normed3[...].reshape(blocks * slots, HD), places, preferred_element_type=F32
    ).astype(BF16)
    spread[:, 0:slots, :] = spread_all[:, : 2 * HD].reshape(blocks, slots, 2 * HD)
    spread[:, slots:, :] = spread_all[:, 2 * HD :].reshape(blocks, slots, 2 * HD)


def project_from(normed3, weight, copies=()):
    total = None
    pairs = normed3.shape[0] // 2
    pieces = max(len(copies), 1)
    for b in range(pairs):
        if copies and b % (pairs // pieces) == 0:
            copies[b // (pairs // pieces)].wait()
        block = jnp.concatenate([normed3[2 * b], normed3[2 * b + 1]], axis=1)
        part = jnp.dot(
            block, weight[b * 2 * HD : (b + 1) * 2 * HD, :], preferred_element_type=F32
        )
        total = part if total is None else total + part
    return total


def project_spread(spread, wkv, copies):
    total = None
    blocks = spread.shape[0]
    for b in range(blocks):
        if b % (blocks // len(copies)) == 0:
            copies[b // (blocks // len(copies))].wait()
        part = jnp.dot(
            spread[b], wkv[b * 2 * HD : (b + 1) * 2 * HD, :], preferred_element_type=F32
        )
        total = part if total is None else total + part
    slots = spread.shape[1] // 2
    return total[:slots], total[slots:]


def weight_copies(src, dst, sem, pieces):
    depth = src.shape[0] // pieces
    copies = [
        pltpu.make_async_copy(
            src.at[pl.ds(c * depth, depth)], dst.at[pl.ds(c * depth, depth)], sem.at[c]
        )
        for c in range(pieces)
    ]
    return copies


def put_row(cache, place, p, key_row, value_row):
    base = pl.multiple_of((jnp.maximum(p, 0) // PIECE) * PIECE, PIECE)
    hit = lax.broadcasted_iota(I32, (PIECE, HD), 0) + base == p
    for which, new in ((0, key_row), (1, value_row)):
        old = cache[place, which, pl.ds(base, PIECE), :].astype(F32)
        cache[place, which, pl.ds(base, PIECE), :] = jnp.where(hit, new, old).astype(BF16)


def attend(cache, places, positions, query_rows):
    cap = cache.shape[2]
    col = lax.broadcasted_iota(I32, (GROUP, cap), 1)
    scores = [
        lax.dot_general(
            rows.astype(BF16),
            cache[place, 0],
            (((1,), (1,)), ((), ())),
            preferred_element_type=F32,
        )
        for place, rows in zip(places, query_rows)
    ]
    probs = []
    for score, p in zip(scores, positions):
        score = jnp.where(col <= p, score * HD**-0.5, -jnp.inf)
        weight = jnp.exp(score - jnp.max(score, axis=-1, keepdims=True))
        weight = weight / jnp.sum(weight, axis=-1, keepdims=True)
        probs.append(weight.astype(BF16))
    return [
        jnp.dot(prob, cache[place, 1], preferred_element_type=F32)
        for place, prob in zip(places, probs)
    ]


def norm_into(normed3, pieces, gains, firsts, total_width):
    square = None
    for piece in pieces:
        part = jnp.sum(piece * piece, axis=-1, keepdims=True)
        square = part if square is None else square + part
    factor = lax.rsqrt(square / total_width + EPS)
    for piece, gain, first in zip(pieces, gains, firsts):
        normed = (piece * factor * gain).astype(BF16)
        for i in range(piece.shape[1] // HD):
            normed3[first + i] = normed[:, i * HD : (i + 1) * HD]


def plan_moves(me, peers, slots, source):
    moving = (peers - 1) * MOVE
    shape = (2 * moving, source.shape[1])
    row = lax.broadcasted_iota(I32, shape, 0)
    index = lax.broadcasted_iota(I32, shape, 1)
    leaves = row < moving
    at = jnp.where(leaves, row, row - moving)
    other = jnp.bitwise_xor(me, at // MOVE + 1)
    here, there = me * slots, other * slots
    src = jnp.broadcast_to(source, shape)
    came, went = jnp.where(leaves, here, there), jnp.where(leaves, there, here)
    moved = (src >= came) & (src < came + slots) & (index >= went) & (index < went + slots)
    sign = jnp.where(at % MOVE == 0, -1.0, 1.0)
    index_f = index.astype(F32)
    best = jnp.max(jnp.where(moved, sign * index_f, -1e6), axis=1, keepdims=True)
    hit = moved & (sign * index_f == best)
    result = jnp.where(leaves, src, index) - here
    found = jnp.sum(jnp.where(hit, result.astype(F32), 0.0), axis=1, keepdims=True)
    none = jnp.where(leaves[:, :1], 0.0, -1.0)
    return jnp.where(best > -1e6, found, none).astype(I32)


def first_kernel(
    peers, slots, heads, shard,
    meta, source_hbm, lengths_hbm, hidden_hbm, gain_hbm, cos_hbm, sin_hbm, wq_hbm, wkv_hbm,
    cache_hbm, query_out, newkey_out, newvalue_out, plan, *rest,
):
    others = peers - 1
    moving = others * MOVE
    cache, box, notes = rest[0], rest[1], (None,) + rest[2 : others + 1]
    (wq, wkv, normed3, spread, cos_rows, sin_rows, leaving, hidden32, lengths_s, source_v,
     hidden, gain, cos_ref, sin_ref, small_sem, wq_sem, wkv_sem, in_sem,
     box_sem, cache_sem) = rest[others + 1 :]
    width = hidden.shape[1]
    me, me_tp = meta[0], meta[1]
    wq_copies = weight_copies(wq_hbm, wq, wq_sem, 4)
    wkv_copies = weight_copies(wkv_hbm, wkv, wkv_sem, 4)
    small = [
        pltpu.make_async_copy(src, dst, small_sem.at[i])
        for i, (src, dst) in enumerate((
            (source_hbm, source_v), (hidden_hbm, hidden), (gain_hbm, gain), (lengths_hbm, lengths_s),
            (cos_hbm, cos_ref), (sin_hbm, sin_ref),
        ))
    ]
    for copy in small[:3] + wkv_copies + wq_copies + small[3:]:
        copy.start()
    loads = [
        pltpu.make_async_copy(
            cache_hbm.at[pl.ds(c * CHUNK, CHUNK)], cache.at[pl.ds(c * CHUNK, CHUNK)], cache_sem.at[c]
        )
        for c in range(slots // CHUNK)
    ]
    for copy in small[:3]:
        copy.wait()
    low = me * slots
    moves = plan_moves(me, peers, slots, source_v[...])
    wide = hidden[...].astype(F32)
    hidden32[...] = wide
    norm_into(normed3, [wide], [gain[...]], [0], width)
    spread_normed(normed3, spread, slots, width)
    send_slots = []
    for at in range(moving):
        slot = moves[at, 0]
        send_slots.append(slot)
        plan[moving + at] = slot
        plan[at] = moves[moving + at, 0]
        pltpu.make_async_copy(cache_hbm.at[slot], leaving.at[at], in_sem.at[at]).start()
    for copy in loads:
        copy.start()
    for copy in small[3:]:
        copy.wait()
    gather_angles(lambda s: lengths_s[0, low + s], slots, cos_ref, sin_ref, cos_rows, sin_rows)
    key, value = project_spread(spread, wkv, wkv_copies)
    query = project_from(normed3, wq, wq_copies)
    cosine, sine = cos_rows[...], sin_rows[...]
    query_out[...] = jnp.zeros(query_out.shape, F32)
    for g in range(heads):
        turned = turn(query[:, g * HD : (g + 1) * HD], cosine, sine)
        query_out[pl.ds(g, slots, stride=GROUP), :] = turned.astype(BF16).astype(F32)
    newkey_out[...] = turn(key, cosine, sine).astype(BF16).astype(F32)
    newvalue_out[...] = value.astype(BF16).astype(F32)

    positions = [lengths_s[0, low + slot] for slot in send_slots]
    for at, slot in enumerate(send_slots):
        pltpu.make_async_copy(cache_hbm.at[slot], leaving.at[at], in_sem.at[at]).wait()
        put_row(
            leaving, at, positions[at],
            newkey_out[pl.ds(slot, 1), :], newvalue_out[pl.ds(slot, 1), :],
        )
    cap = leaving.shape[2]
    copies = [
        pltpu.make_async_copy(
            leaving.at[pl.ds(0, MOVE)], box.at[:, :, pl.ds(0, cap), :], box_sem.at[0]
        )
    ]
    copies[0].start()
    rows = [query_out[pl.ds(pl.multiple_of(slot * GROUP, GROUP), GROUP), :] for slot in send_slots]
    attended = attend(leaving, list(range(moving)), positions, rows)
    column = pl.multiple_of(me_tp * shard, shard)
    for at, slot in enumerate(send_slots):
        m = at % MOVE
        residual = hidden32[pl.ds(slot, 1), pl.ds(column, shard)]
        if at < MOVE:
            blocks = [attended[at][g : g + 1, :] for g in range(heads)]
            blocks += [residual[:, b * HD : (b + 1) * HD] for b in range(shard // HD)]
            blocks += [jnp.zeros((1, HD), F32)] * (NOTE - len(blocks))
            box[m, 0, cap : cap + NOTE, :] = jnp.concatenate(blocks, axis=0).astype(BF16)
        else:
            note = notes[at // MOVE]
            for g in range(heads):
                note[m : m + 1, g * HD : (g + 1) * HD] = attended[at][g : g + 1, :]
            note[m : m + 1, heads * HD :] = residual
    for copy in copies + loads:
        copy.wait()


def attend_slots(cache, places, positions, query, attended_rows, heads):
    slots = len(places)
    for first in range(0, slots, BATCH):
        span = range(first, first + BATCH)
        got = attend(
            cache,
            [places[s] for s in span],
            [positions[s] for s in span],
            [query[s * GROUP : (s + 1) * GROUP, :] for s in span],
        )
        for s, rows in zip(span, got):
            attended_rows[s * GROUP : (s + 1) * GROUP, :] = rows
    return jnp.concatenate(
        [attended_rows[pl.ds(g, slots, stride=GROUP), :] for g in range(heads)], axis=1
    )


def attend_kernel(
    slots, heads, meta, lengths_s, query, newkey, newvalue, _, out, cache, attended_rows,
):
    low = meta[0] * slots
    positions = [lengths_s[low + s] for s in range(slots)]
    for s, p in enumerate(positions):
        put_row(cache, s, p, newkey[s : s + 1, :], newvalue[s : s + 1, :])
    out[...] = attend_slots(
        cache, list(range(slots)), positions, query, attended_rows, heads
    ).astype(BF16)


def project_out(attended, wo, residual, own, sends, me_tp, peers_tp):
    shard = own.shape[1]
    for k in list(range(peers_tp - 1, 0, -1)) + [0]:
        column = pl.multiple_of(jnp.bitwise_xor(me_tp, k) * shard, shard)
        part = jnp.dot(attended, wo[:, pl.ds(column, shard)], preferred_element_type=F32)
        if k == 0:
            own[...] = residual + part
        else:
            sends[k - 1][...] = part.astype(BF16)


def out_kernel(
    peers, peers_tp, meta, plan, attended, wo, hidden, box_hbm, *rest,
):
    notes, rest = rest[: peers - 2], rest[peers - 2 :]
    own, sends, (tail, sem) = rest[0], rest[1:peers_tp], rest[peers_tp:]
    shard = own.shape[1]
    cap = box_hbm.shape[2] - NOTE
    copy = pltpu.make_async_copy(box_hbm.at[:, 0, pl.ds(cap, NOTE), :], tail, sem.at[0])
    copy.start()
    rows = attended[...].astype(F32)
    heads = rows.shape[1] // HD
    column = pl.multiple_of(meta[1] * shard, shard)
    residual = hidden[:, pl.ds(column, shard)].astype(F32)
    row_index = lax.broadcasted_iota(I32, rows.shape, 0)
    residual_index = lax.broadcasted_iota(I32, residual.shape, 0)
    copy.wait()
    for at in range((peers - 1) * MOVE):
        m = at % MOVE
        if at < MOVE:
            blocks = tail[m].astype(F32)
            blocks = [blocks[b : b + 1, :] for b in range(heads + shard // HD)]
            note = jnp.concatenate(blocks, axis=1)
        else:
            note = notes[at // MOVE - 1][m : m + 1, :]
        rows = jnp.where(row_index == plan[at], note[:, : heads * HD], rows)
        residual = jnp.where(residual_index == plan[at], note[:, heads * HD :], residual)
    project_out(rows.astype(BF16), wo, residual, own, sends, meta[1], peers_tp)


def pack_kernel(plan, cache, _own, *rest):
    boxes, out_sem = rest[:-1], rest[-1]
    moving = plan.shape[0] // 2
    packs = [
        pltpu.make_async_copy(
            cache.at[plan[moving + at]], boxes[at // MOVE - 1].at[at % MOVE], out_sem.at[at - MOVE]
        )
        for at in range(MOVE, moving)
    ]
    for pack in packs:
        pack.start()
    for pack in packs:
        pack.wait()


def sum_kernel(own, *rest):
    total = own[...]
    for part in rest[:-1]:
        total = total + part[...].astype(F32)
    rest[-1][...] = total.astype(BF16)


def map_places(slots, peers, plan, place):
    for s in range(slots):
        place[s] = s
    for at in range((peers - 1) * MOVE):
        taker = plan[at]

        @pl.when(taker >= 0)
        def _():
            place[taker] = slots + at


def prepare_kernel(
    peers, slots, meta, source_s, lengths_s, plan, cos_ref, sin_ref, wkv, _,
    weight, cos_rows, sin_rows, place,
):
    map_places(slots, peers, plan, place)
    low = meta[0] * slots
    gather_angles(
        lambda s: lengths_s[source_s[low + s]] + 1, slots, cos_ref, sin_ref, cos_rows, sin_rows
    )
    row = lax.broadcasted_iota(I32, (2 * HD, 2 * HD), 0)
    col = lax.broadcasted_iota(I32, (2 * HD, 2 * HD), 1)
    goal = jnp.where(row < HD, 2 * row, 2 * (row - HD) + 1)
    places = jnp.where(col == goal, 1.0, 0.0).astype(BF16)
    for b in range(weight.shape[0] // HD):
        apart = jnp.dot(
            places, wkv[b * 2 * HD : (b + 1) * 2 * HD, :], preferred_element_type=F32
        ).astype(BF16)
        weight[b * HD : (b + 1) * HD, :HD] = apart[:HD]
        weight[b * HD : (b + 1) * HD, HD:] = apart[HD:]


def second_kernel(
    peers, peers_tp, slots, heads,
    meta, source_s, lengths_s, place, gain, cos_rows, sin_rows, wq, wkv, wo, _, *rest,
):
    blocks, rest = rest[:peers_tp], rest[peers_tp:]
    box_hbm, rest = rest[: peers - 1], rest[peers - 1 :]
    own, sends, cache = rest[0], rest[1:peers_tp], rest[peers_tp]
    normed3, query_rows, attended_rows, in_sem = rest[peers_tp + 1 :]
    me, me_tp = meta[0], meta[1]
    low = me * slots
    width = gain.shape[1]
    shard = own.shape[1]
    loads = [
        pltpu.make_async_copy(
            box.at[:, :, pl.ds(0, cache.shape[2]), :],
            cache.at[pl.ds(slots + k * MOVE, MOVE)],
            in_sem.at[k],
        )
        for k, box in enumerate(box_hbm)
    ]
    for copy in loads:
        copy.start()

    firsts = [jnp.bitwise_xor(me_tp, k) for k in range(peers_tp)]
    norm_into(
        normed3,
        [block[...].astype(F32) for block in blocks],
        [gain[:, pl.ds(pl.multiple_of(first * shard, shard), shard)] for first in firsts],
        [first * (shard // HD) for first in firsts],
        width,
    )
    positions = [lengths_s[source_s[low + s]] + 1 for s in range(slots)]
    query = project_from(normed3, wq)
    pair = project_from(normed3, wkv)
    key, value = pair[:, :HD], pair[:, HD:]
    cosine, sine = cos_rows[...], sin_rows[...]
    query_rows[...] = jnp.zeros(query_rows.shape, F32)
    for g in range(heads):
        turned = turn(query[:, g * HD : (g + 1) * HD], cosine, sine)
        query_rows[pl.ds(g, slots, stride=GROUP), :] = turned.astype(BF16).astype(F32)
    newkey = turn(key, cosine, sine).astype(BF16).astype(F32)
    newvalue = value.astype(BF16).astype(F32)

    for copy in loads:
        copy.wait()
    places = [place[s] for s in range(slots)]
    for s, (at, p) in enumerate(zip(places, positions)):
        put_row(cache, at, p, newkey[s : s + 1, :], newvalue[s : s + 1, :])
    attended = attend_slots(cache, places, positions, query_rows, attended_rows, heads)
    project_out(
        attended.astype(BF16), wo, blocks[0][...].astype(F32), own, sends, me_tp, peers_tp
    )


def cache_kernel(slots, place, cache, out_hbm, out_sem):
    copies = [
        pltpu.make_async_copy(cache.at[place[s]], out_hbm.at[s], out_sem.at[s])
        for s in range(slots)
    ]
    for copy in copies:
        copy.start()
    for copy in copies:
        copy.wait()


def join_kernel(peers_tp, meta, *rest):
    blocks, out, sem = rest[:-2], rest[-2], rest[-1]
    shard = blocks[0].shape[1]
    copies = []
    for k, block in enumerate(blocks):
        column = pl.multiple_of(jnp.bitwise_xor(meta[1], k) * shard, shard)
        copies.append(pltpu.make_async_copy(block, out.at[:, pl.ds(column, shard)], sem.at[k]))
        copies[-1].start()
    for copy in copies:
        copy.wait()


def swapped(x, axis, size, k):
    return lax.ppermute(x, axis, [(i, i ^ k) for i in range(size)])


def local(
    tables, kv_cache, hidden, lengths, source, norm_gain, query_weight, keyval_weight, out_weight
):
    peers, peers_tp = lax.axis_size("inst"), lax.axis_size("tp")
    slots, cap = kv_cache.shape[0], kv_cache.shape[2]
    width = hidden.shape[1]
    heads = query_weight.shape[1] // HD
    shard = width // peers_tp
    others, moving = peers - 1, (peers - 1) * MOVE
    blocks = width // HD
    meta = jnp.stack([lax.axis_index("inst"), lax.axis_index("tp")]).astype(I32)
    gain = norm_gain.reshape(1, width)
    wkv = keyval_weight.reshape(2 * width, HD)
    cosine, sine = (jnp.asarray(table) for table in tables)
    row32 = jax.ShapeDtypeStruct((slots, HD), F32)
    note_width = heads * HD + shard
    dma = pltpu.SemaphoreType.DMA
    weights = [
        pltpu.VMEM(query_weight.shape, BF16),
        pltpu.VMEM(wkv.shape, BF16),
    ]
    stages = [
        pltpu.VMEM((blocks, slots, HD), BF16),
        pltpu.VMEM((blocks, 2 * slots, 2 * HD), BF16),
        pltpu.VMEM((slots, HD), F32),
        pltpu.VMEM((slots, HD), F32),
    ]
    flops = 2 * slots * width * (heads + 2) * HD
    cache_bytes = kv_cache.size * 2
    held = jax.ShapeDtypeStruct((slots + moving,) + kv_cache.shape[1:], BF16)

    query, newkey1, newvalue1, plan, cache, *notes = pl.pallas_call(
        functools.partial(first_kernel, peers, slots, heads, shard),
        out_shape=[
            jax.ShapeDtypeStruct((slots * GROUP, HD), F32),
            row32,
            row32,
            jax.ShapeDtypeStruct((2 * moving,), I32),
            held,
        ]
        + [jax.ShapeDtypeStruct((MOVE, 2, cap + NOTE, HD), BF16)]
        + [jax.ShapeDtypeStruct((MOVE, note_width), F32)] * (others - 1),
        in_specs=[SMEM] + [HBM] * 9,
        out_specs=[VMEM] * 3 + [SMEM] + [VMEM] * (others + 1),
        scratch_shapes=weights
        + stages
        + [
            pltpu.VMEM((moving,) + kv_cache.shape[1:], BF16),
            pltpu.VMEM((slots, width), F32),
            pltpu.SMEM((1, source.shape[0]), I32),
            pltpu.VMEM((1, source.shape[0]), I32),
            pltpu.VMEM(hidden.shape, BF16),
            pltpu.VMEM((1, width), F32),
            pltpu.VMEM(cosine.shape, F32),
            pltpu.VMEM(cosine.shape, F32),
            dma((6,)),
            dma((4,)),
            dma((4,)),
            dma((moving,)),
            dma((1,)),
            dma((slots // CHUNK,)),
        ],
        compiler_params=params(24),
        cost_estimate=cost(flops, (query_weight.size + wkv.size) * 2),
        name="first_step",
    )(meta, *(
        pltpu.with_memory_space_constraint(x, pltpu.HBM)
        for x in (source.reshape(1, -1), lengths.reshape(1, -1), hidden, gain, cosine, sine,
                  query_weight, wkv, kv_cache)
    ))
    got_notes = [swapped(note, "inst", peers, k + 1) for k, note in enumerate(notes)]

    attended, cache = pl.pallas_call(
        functools.partial(attend_kernel, slots, heads),
        out_shape=[jax.ShapeDtypeStruct((slots, heads * HD), BF16), held],
        in_specs=[SMEM] * 2 + [VMEM] * 4,
        out_specs=[VMEM] * 2,
        scratch_shapes=[pltpu.VMEM((slots * GROUP, HD), F32)],
        input_output_aliases={5: 1},
        compiler_params=params(12),
        cost_estimate=cost(4 * slots * cap * HD * heads, cache_bytes),
        name="attention",
    )(meta, lengths, query, newkey1, newvalue1, cache)

    sent = [jax.ShapeDtypeStruct((slots, shard), F32)]
    sent += [jax.ShapeDtypeStruct((slots, shard), BF16)] * (peers_tp - 1)
    own, *sends = pl.pallas_call(
        functools.partial(out_kernel, peers, peers_tp),
        out_shape=sent,
        in_specs=[SMEM] * 2 + [VMEM] * 3 + [ANY] + [VMEM] * (others - 1),
        out_specs=[VMEM] * peers_tp,
        scratch_shapes=[pltpu.VMEM((MOVE, NOTE, HD), BF16), dma((1,))],
        compiler_params=params(16),
        cost_estimate=cost(2 * slots * width * heads * HD, out_weight.size * 2),
        name="out_projection",
    )(meta, plan, attended, out_weight, hidden, *got_notes)
    boxes = pl.pallas_call(
        pack_kernel,
        out_shape=[jax.ShapeDtypeStruct((MOVE,) + kv_cache.shape[1:], BF16)] * (others - 1),
        in_specs=[SMEM, VMEM, ANY],
        out_specs=[ANY] * (others - 1),
        scratch_shapes=[dma((moving - MOVE,))],
        compiler_params=params(16),
        cost_estimate=cost(1, 1 * cache_bytes),
        name="pack",
    )(plan, cache, own)
    got_boxes = got_notes[:1] + [swapped(box, "inst", peers, k + 2) for k, box in enumerate(boxes)]

    def summed(own, sends, passed_on):
        got = [swapped(sends[k - 1], "tp", peers_tp, k) for k in range(peers_tp - 1, 0, -1)]
        shard_rows = pl.pallas_call(
            sum_kernel,
            out_shape=jax.ShapeDtypeStruct((slots, shard), BF16),
            in_specs=[VMEM] * peers_tp,
            out_specs=VMEM,
            compiler_params=params(16),
            name="sum_terms",
        )(own, *got)
        blocks = {0: shard_rows}
        if not passed_on:
            blocks |= {k: swapped(shard_rows, "tp", peers_tp, k) for k in range(1, peers_tp)}
        far = peers_tp // 2 if passed_on else 0
        while far:
            blocks |= {k + far: swapped(blocks[k], "tp", peers_tp, far) for k in blocks}
            far //= 2
        return [blocks[k] for k in range(peers_tp)]

    pieces = summed(own, sends, False)

    weight, cos_rows, sin_rows, place = pl.pallas_call(
        functools.partial(prepare_kernel, peers, slots),
        out_shape=[
            jax.ShapeDtypeStruct((width, 2 * HD), BF16),
            row32,
            row32,
            jax.ShapeDtypeStruct((slots,), I32),
        ],
        in_specs=[SMEM] * 4 + [VMEM] * 3 + [ANY],
        out_specs=[VMEM] * 3 + [SMEM],
        compiler_params=params(16),
        cost_estimate=cost(100*flops, wkv.size * 40),
        name="prepare",
    )(meta, source, lengths, plan, cosine, sine, wkv, own)

    own, *sends, cache = pl.pallas_call(
        functools.partial(second_kernel, peers, peers_tp, slots, heads),
        out_shape=sent + [held],
        in_specs=[SMEM] * 4 + [VMEM] * (7 + peers_tp) + [ANY] * others,
        out_specs=[VMEM] * (1 + peers_tp),
        scratch_shapes=[
            pltpu.VMEM((blocks, slots, HD), BF16),
            pltpu.VMEM((slots * GROUP, HD), F32),
            pltpu.VMEM((slots * GROUP, HD), F32),
            dma((others,)),
        ],
        input_output_aliases={10: peers_tp},
        compiler_params=params(16),
        cost_estimate=cost(3 * flops, cache_bytes + (query_weight.size + wkv.size) * 4),
        name="second_step",
    )(meta, source, lengths, place, gain, cos_rows, sin_rows, query_weight, weight, out_weight, cache,
      *pieces, *got_boxes)

    pieces = summed(own, sends, False)
    final_cache = pl.pallas_call(
        functools.partial(cache_kernel, slots),
        out_shape=jax.ShapeDtypeStruct(kv_cache.shape, BF16),
        in_specs=[SMEM, VMEM],
        out_specs=ANY,
        scratch_shapes=[dma((slots,))],
        compiler_params=params(16),
        cost_estimate=cost(0, 2 * cache_bytes),
        name="write_cache",
    )(place, cache)
    final_hidden = pl.pallas_call(
        functools.partial(join_kernel, peers_tp),
        out_shape=jax.ShapeDtypeStruct(hidden.shape, BF16),
        in_specs=[SMEM] + [ANY] * peers_tp,
        out_specs=ANY,
        scratch_shapes=[dma((peers_tp,))],
        compiler_params=params(16),
        name="join",
    )(meta, *pieces)
    return (final_hidden, final_cache)


def solution(mesh):
    def whole(kv_cache, *rest):
        tables = angle_tables(kv_cache.shape[2])
        return jax.shard_map(
            functools.partial(local, tables),
            mesh=mesh,
            in_specs=(
                P(("groups", "inst"), None, None, "tp"),
                P(("groups", "inst"), None),
                P("groups"),
                P("groups"),
                P(),
                P(None, "tp"),
                P(None, None, "tp"),
                P("tp", None),
            ),
            out_specs=(P(("groups", "inst"), None), P(("groups", "inst"), None, None, "tp")),
            check_vma=False,
        )(kv_cache, *rest)

    return whole
```

```python
import functools

import jax
import jax.numpy as jnp
import numpy as np
from jax import lax
from jax.experimental import pallas as pl
from jax.experimental.pallas import tpu as pltpu
from jax.sharding import PartitionSpec as P

MOVE = 2
EPS = 1e-05
THETA = 500000.0
HD = 128
GROUP = 8
PIECE = 16
CHUNK = 8
BATCH = 16
NOTE = 16

F32 = jnp.float32
BF16 = jnp.bfloat16
I32 = jnp.int32

ANY = pl.BlockSpec(memory_space=pl.ANY)
VMEM = pl.BlockSpec(memory_space=pltpu.VMEM)
SMEM = pl.BlockSpec(memory_space=pltpu.SMEM)
HBM = pl.BlockSpec(memory_space=pltpu.HBM)


def params(mib):
    return pltpu.CompilerParams(vmem_limit_bytes=mib * 1024 * 1024)


def cost(flops, nbytes):
    return pl.CostEstimate(flops=flops, bytes_accessed=nbytes, transcendentals=0)


def angle_tables(positions):
    frequency = THETA ** (-(np.arange(HD // 2, dtype=np.float64) * 2.0) / HD)
    angles = np.arange(positions, dtype=np.float64)[:, None] * frequency[None, :]
    cosine = np.concatenate([np.cos(angles), np.cos(angles)], axis=-1)
    sine = np.concatenate([-np.sin(angles), np.sin(angles)], axis=-1)
    return cosine.astype(np.float32), sine.astype(np.float32)


def turn(x, cosine, sine):
    return x * cosine + pltpu.roll(x, HD // 2, 1) * sine


def gather_angles(position_of, slots, cos_ref, sin_ref, cos_rows, sin_rows):
    for s in range(slots):
        p = position_of(s)
        cos_rows[s : s + 1, :] = cos_ref[pl.ds(p, 1), :]
        sin_rows[s : s + 1, :] = sin_ref[pl.ds(p, 1), :]


def spread_normed(normed3, spread, slots, width):
    blocks = width // HD
    row = lax.broadcasted_iota(I32, (HD, 4 * HD), 0)
    col = lax.broadcasted_iota(I32, (HD, 4 * HD), 1)
    goal = jnp.where(col < 2 * HD, 2 * row, 2 * row + 1 + 2 * HD)
    places = jnp.where(col == goal, 1.0, 0.0).astype(BF16)
    spread_all = jnp.dot(
        normed3[...].reshape(blocks * slots, HD), places, preferred_element_type=F32
    ).astype(BF16)
    spread[:, 0:slots, :] = spread_all[:, : 2 * HD].reshape(blocks, slots, 2 * HD)
    spread[:, slots:, :] = spread_all[:, 2 * HD :].reshape(blocks, slots, 2 * HD)


def project_from(normed3, weight, copies=()):
    total = None
    pairs = normed3.shape[0] // 2
    pieces = max(len(copies), 1)
    for b in range(pairs):
        if copies and b % (pairs // pieces) == 0:
            copies[b // (pairs // pieces)].wait()
        block = jnp.concatenate([normed3[2 * b], normed3[2 * b + 1]], axis=1)
        part = jnp.dot(
            block, weight[b * 2 * HD : (b + 1) * 2 * HD, :], preferred_element_type=F32
        )
        total = part if total is None else total + part
    return total


def project_spread(spread, wkv, copies):
    total = None
    blocks = spread.shape[0]
    for b in range(blocks):
        if b % (blocks // len(copies)) == 0:
            copies[b // (blocks // len(copies))].wait()
        part = jnp.dot(
            spread[b], wkv[b * 2 * HD : (b + 1) * 2 * HD, :], preferred_element_type=F32
        )
        total = part if total is None else total + part
    slots = spread.shape[1] // 2
    return total[:slots], total[slots:]


def weight_copies(src, dst, sem, pieces):
    depth = src.shape[0] // pieces
    copies = [
        pltpu.make_async_copy(
            src.at[pl.ds(c * depth, depth)], dst.at[pl.ds(c * depth, depth)], sem.at[c]
        )
        for c in range(pieces)
    ]
    return copies


def put_row(cache, place, p, key_row, value_row):
    base = pl.multiple_of((jnp.maximum(p, 0) // PIECE) * PIECE, PIECE)
    hit = lax.broadcasted_iota(I32, (PIECE, HD), 0) + base == p
    for which, new in ((0, key_row), (1, value_row)):
        old = cache[place, which, pl.ds(base, PIECE), :].astype(F32)
        cache[place, which, pl.ds(base, PIECE), :] = jnp.where(hit, new, old).astype(BF16)


def attend(cache, places, positions, query_rows):
    cap = cache.shape[2]
    col = lax.broadcasted_iota(I32, (GROUP, cap), 1)
    scores = [
        lax.dot_general(
            rows.astype(BF16),
            cache[place, 0],
            (((1,), (1,)), ((), ())),
            preferred_element_type=F32,
        )
        for place, rows in zip(places, query_rows)
    ]
    probs = []
    for score, p in zip(scores, positions):
        score = jnp.where(col <= p, score * HD**-0.5, -jnp.inf)
        weight = jnp.exp(score - jnp.max(score, axis=-1, keepdims=True))
        weight = weight / jnp.sum(weight, axis=-1, keepdims=True)
        probs.append(weight.astype(BF16))
    return [
        jnp.dot(prob, cache[place, 1], preferred_element_type=F32)
        for place, prob in zip(places, probs)
    ]


def norm_into(normed3, pieces, gains, firsts, total_width):
    square = None
    for piece in pieces:
        part = jnp.sum(piece * piece, axis=-1, keepdims=True)
        square = part if square is None else square + part
    factor = lax.rsqrt(square / total_width + EPS)
    for piece, gain, first in zip(pieces, gains, firsts):
        normed = (piece * factor * gain).astype(BF16)
        for i in range(piece.shape[1] // HD):
            normed3[first + i] = normed[:, i * HD : (i + 1) * HD]


def cache_copies(cache_hbm, cache, sem, first, last):
    return [
        pltpu.make_async_copy(
            cache_hbm.at[pl.ds(at, CHUNK)], cache.at[pl.ds(at, CHUNK)], sem.at[i]
        )
        for i, at in enumerate(range(first, last, CHUNK))
    ]


def plan_moves(me, peers, slots, source):
    moving = (peers - 1) * MOVE
    shape = (2 * moving, source.shape[1])
    row = lax.broadcasted_iota(I32, shape, 0)
    index = lax.broadcasted_iota(I32, shape, 1)
    leaves = row < moving
    at = jnp.where(leaves, row, row - moving)
    other = jnp.bitwise_xor(me, at // MOVE + 1)
    here, there = me * slots, other * slots
    src = jnp.broadcast_to(source, shape)
    came, went = jnp.where(leaves, here, there), jnp.where(leaves, there, here)
    moved = (src >= came) & (src < came + slots) & (index >= went) & (index < went + slots)
    sign = jnp.where(at % MOVE == 0, -1.0, 1.0)
    index_f = index.astype(F32)
    best = jnp.max(jnp.where(moved, sign * index_f, -1e6), axis=1, keepdims=True)
    hit = moved & (sign * index_f == best)
    result = jnp.where(leaves, src, index) - here
    found = jnp.sum(jnp.where(hit, result.astype(F32), 0.0), axis=1, keepdims=True)
    none = jnp.where(leaves[:, :1], 0.0, -1.0)
    return jnp.where(best > -1e6, found, none).astype(I32)


def first_kernel(
    peers, slots, heads, shard,
    meta, source_hbm, lengths_hbm, hidden_hbm, gain_hbm, cos_hbm, sin_hbm, wq_hbm, wkv_hbm,
    cache_hbm, query_out, newkey_out, newvalue_out, plan, *rest,
):
    others = peers - 1
    moving = others * MOVE
    cache, box, notes = rest[0], rest[1], (None,) + rest[2 : others + 1]
    (wq, wkv, normed3, spread, cos_rows, sin_rows, leaving, hidden32, lengths_s, source_v,
     hidden, gain, cos_ref, sin_ref, small_sem, wq_sem, wkv_sem, in_sem,
     box_sem, cache_sem) = rest[others + 1 :]
    width = hidden.shape[1]
    me, me_tp = meta[0], meta[1]
    wq_copies = weight_copies(wq_hbm, wq, wq_sem, 4)
    wkv_copies = weight_copies(wkv_hbm, wkv, wkv_sem, 4)
    small = [
        pltpu.make_async_copy(src, dst, small_sem.at[i])
        for i, (src, dst) in enumerate((
            (source_hbm, source_v), (hidden_hbm, hidden), (gain_hbm, gain), (lengths_hbm, lengths_s),
            (cos_hbm, cos_ref), (sin_hbm, sin_ref),
        ))
    ]
    for copy in small[:3] + wkv_copies + wq_copies + small[3:]:
        copy.start()
    loads = cache_copies(cache_hbm, cache, cache_sem, 0, slots - BATCH)
    for copy in small[:3]:
        copy.wait()
    low = me * slots
    moves = plan_moves(me, peers, slots, source_v[...])
    wide = hidden[...].astype(F32)
    hidden32[...] = wide
    norm_into(normed3, [wide], [gain[...]], [0], width)
    spread_normed(normed3, spread, slots, width)
    send_slots = []
    for at in range(moving):
        slot = moves[at, 0]
        send_slots.append(slot)
        plan[moving + at] = slot
        plan[at] = moves[moving + at, 0]
        pltpu.make_async_copy(cache_hbm.at[slot], leaving.at[at], in_sem.at[at]).start()
    for copy in loads:
        copy.start()
    for copy in small[3:]:
        copy.wait()
    gather_angles(lambda s: lengths_s[0, low + s], slots, cos_ref, sin_ref, cos_rows, sin_rows)
    key, value = project_spread(spread, wkv, wkv_copies)
    query = project_from(normed3, wq, wq_copies)
    cosine, sine = cos_rows[...], sin_rows[...]
    query_out[...] = jnp.zeros(query_out.shape, F32)
    for g in range(heads):
        turned = turn(query[:, g * HD : (g + 1) * HD], cosine, sine)
        query_out[pl.ds(g, slots, stride=GROUP), :] = turned.astype(BF16).astype(F32)
    newkey_out[...] = turn(key, cosine, sine).astype(BF16).astype(F32)
    newvalue_out[...] = value.astype(BF16).astype(F32)

    positions = [lengths_s[0, low + slot] for slot in send_slots]
    for at, slot in enumerate(send_slots):
        pltpu.make_async_copy(cache_hbm.at[slot], leaving.at[at], in_sem.at[at]).wait()
        put_row(
            leaving, at, positions[at],
            newkey_out[pl.ds(slot, 1), :], newvalue_out[pl.ds(slot, 1), :],
        )
    cap = leaving.shape[2]
    copies = [
        pltpu.make_async_copy(
            leaving.at[pl.ds(0, MOVE)], box.at[:, :, pl.ds(0, cap), :], box_sem.at[0]
        )
    ]
    copies[0].start()
    rows = [query_out[pl.ds(pl.multiple_of(slot * GROUP, GROUP), GROUP), :] for slot in send_slots]
    attended = attend(leaving, list(range(moving)), positions, rows)
    column = pl.multiple_of(me_tp * shard, shard)
    for at, slot in enumerate(send_slots):
        m = at % MOVE
        residual = hidden32[pl.ds(slot, 1), pl.ds(column, shard)]
        if at < MOVE:
            blocks = [attended[at][g : g + 1, :] for g in range(heads)]
            blocks += [residual[:, b * HD : (b + 1) * HD] for b in range(shard // HD)]
            blocks += [jnp.zeros((1, HD), F32)] * (NOTE - len(blocks))
            box[m, 0, cap : cap + NOTE, :] = jnp.concatenate(blocks, axis=0).astype(BF16)
        else:
            note = notes[at // MOVE]
            for g in range(heads):
                note[m : m + 1, g * HD : (g + 1) * HD] = attended[at][g : g + 1, :]
            note[m : m + 1, heads * HD :] = residual
    for copy in copies + loads:
        copy.wait()


def attend_slots(cache, places, positions, query, attended_rows, first, last):
    for start in range(first, last, BATCH):
        span = range(start, start + BATCH)
        got = attend(
            cache,
            [places[s] for s in span],
            [positions[s] for s in span],
            [query[s * GROUP : (s + 1) * GROUP, :] for s in span],
        )
        for s, rows in zip(span, got):
            attended_rows[s * GROUP : (s + 1) * GROUP, :] = rows


def side_by_side(attended_rows, slots, heads):
    return jnp.concatenate(
        [attended_rows[pl.ds(g, slots, stride=GROUP), :] for g in range(heads)], axis=1
    ).astype(BF16)


def attend_kernel(
    slots, heads, meta, lengths_s, query, newkey, newvalue, cache_hbm, _,
    out, cache, attended_rows, in_sem,
):
    low = meta[0] * slots
    early = slots - BATCH
    loads = cache_copies(cache_hbm, cache, in_sem, early, slots)
    for copy in loads:
        copy.start()
    positions = [lengths_s[low + s] for s in range(slots)]
    for first, last in ((0, early), (early, slots)):
        if first:
            for copy in loads:
                copy.wait()
        for s in range(first, last):
            put_row(cache, s, positions[s], newkey[s : s + 1, :], newvalue[s : s + 1, :])
        attend_slots(cache, list(range(slots)), positions, query, attended_rows, first, last)
    out[...] = side_by_side(attended_rows, slots, heads)


def project_out(attended, wo, residual, own, sends, me_tp, peers_tp):
    shard = own.shape[1]
    for k in list(range(peers_tp - 1, 0, -1)) + [0]:
        column = pl.multiple_of(jnp.bitwise_xor(me_tp, k) * shard, shard)
        part = jnp.dot(attended, wo[:, pl.ds(column, shard)], preferred_element_type=F32)
        if k == 0:
            own[...] = residual + part
        else:
            sends[k - 1][...] = part.astype(BF16)


def out_kernel(
    peers, peers_tp, meta, plan, attended, wo, hidden, box_hbm, *rest,
):
    notes, rest = rest[: peers - 2], rest[peers - 2 :]
    own, sends, (tail, sem) = rest[0], rest[1:peers_tp], rest[peers_tp:]
    shard = own.shape[1]
    cap = box_hbm.shape[2] - NOTE
    copy = pltpu.make_async_copy(box_hbm.at[:, 0, pl.ds(cap, NOTE), :], tail, sem.at[0])
    copy.start()
    rows = attended[...].astype(F32)
    heads = rows.shape[1] // HD
    column = pl.multiple_of(meta[1] * shard, shard)
    residual = hidden[:, pl.ds(column, shard)].astype(F32)
    row_index = lax.broadcasted_iota(I32, rows.shape, 0)
    residual_index = lax.broadcasted_iota(I32, residual.shape, 0)
    copy.wait()
    for at in range((peers - 1) * MOVE):
        m = at % MOVE
        if at < MOVE:
            blocks = tail[m].astype(F32)
            blocks = [blocks[b : b + 1, :] for b in range(heads + shard // HD)]
            note = jnp.concatenate(blocks, axis=1)
        else:
            note = notes[at // MOVE - 1][m : m + 1, :]
        rows = jnp.where(row_index == plan[at], note[:, : heads * HD], rows)
        residual = jnp.where(residual_index == plan[at], note[:, heads * HD :], residual)
    project_out(rows.astype(BF16), wo, residual, own, sends, meta[1], peers_tp)


def pack_kernel(plan, cache, _own, *rest):
    boxes, out_sem = rest[:-1], rest[-1]
    moving = plan.shape[0] // 2
    packs = [
        pltpu.make_async_copy(
            cache.at[plan[moving + at]], boxes[at // MOVE - 1].at[at % MOVE], out_sem.at[at - MOVE]
        )
        for at in range(MOVE, moving)
    ]
    for pack in packs:
        pack.start()
    for pack in packs:
        pack.wait()


def sum_kernel(own, *rest):
    total = own[...]
    for part in rest[:-1]:
        total = total + part[...].astype(F32)
    rest[-1][...] = total.astype(BF16)


def map_places(slots, peers, plan, place):
    for s in range(slots):
        place[s] = s
    for at in range((peers - 1) * MOVE):
        taker = plan[at]

        @pl.when(taker >= 0)
        def _():
            place[taker] = slots + at


def prepare_kernel(
    peers, slots, meta, source_s, lengths_s, plan, cos_ref, sin_ref, wkv, _,
    weight, cos_rows, sin_rows, place,
):
    map_places(slots, peers, plan, place)
    low = meta[0] * slots
    gather_angles(
        lambda s: lengths_s[source_s[low + s]] + 1, slots, cos_ref, sin_ref, cos_rows, sin_rows
    )
    row = lax.broadcasted_iota(I32, (2 * HD, 2 * HD), 0)
    col = lax.broadcasted_iota(I32, (2 * HD, 2 * HD), 1)
    goal = jnp.where(row < HD, 2 * row, 2 * (row - HD) + 1)
    places = jnp.where(col == goal, 1.0, 0.0).astype(BF16)
    for b in range(weight.shape[0] // HD):
        apart = jnp.dot(
            places, wkv[b * 2 * HD : (b + 1) * 2 * HD, :], preferred_element_type=F32
        ).astype(BF16)
        weight[b * HD : (b + 1) * HD, :HD] = apart[:HD]
        weight[b * HD : (b + 1) * HD, HD:] = apart[HD:]


def second_kernel(
    peers, peers_tp, slots, heads,
    meta, source_s, lengths_s, place, gain, cos_rows, sin_rows, wq, wkv, wo, _, *rest,
):
    blocks, rest = rest[:peers_tp], rest[peers_tp:]
    box_hbm, rest = rest[: peers - 1], rest[peers - 1 :]
    own, sends, cache = rest[0], rest[1:peers_tp], rest[peers_tp]
    normed3, query_rows, attended_rows, in_sem = rest[peers_tp + 1 :]
    me, me_tp = meta[0], meta[1]
    low = me * slots
    width = gain.shape[1]
    shard = own.shape[1]
    loads = [
        pltpu.make_async_copy(
            box.at[:, :, pl.ds(0, cache.shape[2]), :],
            cache.at[pl.ds(slots + k * MOVE, MOVE)],
            in_sem.at[k],
        )
        for k, box in enumerate(box_hbm)
    ]
    for copy in loads:
        copy.start()

    firsts = [jnp.bitwise_xor(me_tp, k) for k in range(peers_tp)]
    norm_into(
        normed3,
        [block[...].astype(F32) for block in blocks],
        [gain[:, pl.ds(pl.multiple_of(first * shard, shard), shard)] for first in firsts],
        [first * (shard // HD) for first in firsts],
        width,
    )
    positions = [lengths_s[source_s[low + s]] + 1 for s in range(slots)]
    query = project_from(normed3, wq)
    pair = project_from(normed3, wkv)
    key, value = pair[:, :HD], pair[:, HD:]
    cosine, sine = cos_rows[...], sin_rows[...]
    query_rows[...] = jnp.zeros(query_rows.shape, F32)
    for g in range(heads):
        turned = turn(query[:, g * HD : (g + 1) * HD], cosine, sine)
        query_rows[pl.ds(g, slots, stride=GROUP), :] = turned.astype(BF16).astype(F32)
    newkey = turn(key, cosine, sine).astype(BF16).astype(F32)
    newvalue = value.astype(BF16).astype(F32)

    for copy in loads:
        copy.wait()
    places = [place[s] for s in range(slots)]
    for s, (at, p) in enumerate(zip(places, positions)):
        put_row(cache, at, p, newkey[s : s + 1, :], newvalue[s : s + 1, :])
    attend_slots(cache, places, positions, query_rows, attended_rows, 0, slots)
    attended = side_by_side(attended_rows, slots, heads)
    project_out(attended, wo, blocks[0][...].astype(F32), own, sends, me_tp, peers_tp)


def cache_kernel(slots, place, cache, out_hbm, out_sem):
    copies = [
        pltpu.make_async_copy(cache.at[place[s]], out_hbm.at[s], out_sem.at[s])
        for s in range(slots)
    ]
    for copy in copies:
        copy.start()
    for copy in copies:
        copy.wait()


def join_kernel(peers_tp, meta, *rest):
    blocks, out, sem = rest[:-2], rest[-2], rest[-1]
    shard = blocks[0].shape[1]
    copies = []
    for k, block in enumerate(blocks):
        column = pl.multiple_of(jnp.bitwise_xor(meta[1], k) * shard, shard)
        copies.append(pltpu.make_async_copy(block, out.at[:, pl.ds(column, shard)], sem.at[k]))
        copies[-1].start()
    for copy in copies:
        copy.wait()


def swapped(x, axis, size, k):
    return lax.ppermute(x, axis, [(i, i ^ k) for i in range(size)])


def local(
    tables, kv_cache, hidden, lengths, source, norm_gain, query_weight, keyval_weight, out_weight
):
    peers, peers_tp = lax.axis_size("inst"), lax.axis_size("tp")
    slots, cap = kv_cache.shape[0], kv_cache.shape[2]
    width = hidden.shape[1]
    heads = query_weight.shape[1] // HD
    shard = width // peers_tp
    others, moving = peers - 1, (peers - 1) * MOVE
    blocks = width // HD
    meta = jnp.stack([lax.axis_index("inst"), lax.axis_index("tp")]).astype(I32)
    gain = norm_gain.reshape(1, width)
    wkv = keyval_weight.reshape(2 * width, HD)
    cosine, sine = (jnp.asarray(table) for table in tables)
    row32 = jax.ShapeDtypeStruct((slots, HD), F32)
    note_width = heads * HD + shard
    dma = pltpu.SemaphoreType.DMA
    weights = [
        pltpu.VMEM(query_weight.shape, BF16),
        pltpu.VMEM(wkv.shape, BF16),
    ]
    stages = [
        pltpu.VMEM((blocks, slots, HD), BF16),
        pltpu.VMEM((blocks, 2 * slots, 2 * HD), BF16),
        pltpu.VMEM((slots, HD), F32),
        pltpu.VMEM((slots, HD), F32),
    ]
    flops = 2 * slots * width * (heads + 2) * HD
    cache_bytes = kv_cache.size * 2
    held = jax.ShapeDtypeStruct((slots + moving,) + kv_cache.shape[1:], BF16)

    query, newkey1, newvalue1, plan, cache, *notes = pl.pallas_call(
        functools.partial(first_kernel, peers, slots, heads, shard),
        out_shape=[
            jax.ShapeDtypeStruct((slots * GROUP, HD), F32),
            row32,
            row32,
            jax.ShapeDtypeStruct((2 * moving,), I32),
            held,
        ]
        + [jax.ShapeDtypeStruct((MOVE, 2, cap + NOTE, HD), BF16)]
        + [jax.ShapeDtypeStruct((MOVE, note_width), F32)] * (others - 1),
        in_specs=[SMEM] + [HBM] * 9,
        out_specs=[VMEM] * 3 + [SMEM] + [VMEM] * (others + 1),
        scratch_shapes=weights
        + stages
        + [
            pltpu.VMEM((moving,) + kv_cache.shape[1:], BF16),
            pltpu.VMEM((slots, width), F32),
            pltpu.SMEM((1, source.shape[0]), I32),
            pltpu.VMEM((1, source.shape[0]), I32),
            pltpu.VMEM(hidden.shape, BF16),
            pltpu.VMEM((1, width), F32),
            pltpu.VMEM(cosine.shape, F32),
            pltpu.VMEM(cosine.shape, F32),
            dma((6,)),
            dma((4,)),
            dma((4,)),
            dma((moving,)),
            dma((1,)),
            dma(((slots - BATCH) // CHUNK,)),
        ],
        compiler_params=params(24),
        cost_estimate=cost(flops, (query_weight.size + wkv.size) * 2),
        name="first_step",
    )(meta, *(
        pltpu.with_memory_space_constraint(x, pltpu.HBM)
        for x in (source.reshape(1, -1), lengths.reshape(1, -1), hidden, gain, cosine, sine,
                  query_weight, wkv, kv_cache)
    ))
    got_notes = [swapped(note, "inst", peers, k + 1) for k, note in enumerate(notes)]

    attended, cache = pl.pallas_call(
        functools.partial(attend_kernel, slots, heads),
        out_shape=[jax.ShapeDtypeStruct((slots, heads * HD), BF16), held],
        in_specs=[SMEM] * 2 + [VMEM] * 3 + [HBM, VMEM],
        out_specs=[VMEM] * 2,
        scratch_shapes=[pltpu.VMEM((slots * GROUP, HD), F32), dma((BATCH // CHUNK,))],
        input_output_aliases={6: 1},
        compiler_params=params(12),
        cost_estimate=cost(4 * slots * cap * HD * heads, cache_bytes),
        name="attention",
    )(meta, lengths, query, newkey1, newvalue1,
      pltpu.with_memory_space_constraint(kv_cache, pltpu.HBM), cache)

    sent = [jax.ShapeDtypeStruct((slots, shard), F32)]
    sent += [jax.ShapeDtypeStruct((slots, shard), BF16)] * (peers_tp - 1)
    own, *sends = pl.pallas_call(
        functools.partial(out_kernel, peers, peers_tp),
        out_shape=sent,
        in_specs=[SMEM] * 2 + [VMEM] * 3 + [ANY] + [VMEM] * (others - 1),
        out_specs=[VMEM] * peers_tp,
        scratch_shapes=[pltpu.VMEM((MOVE, NOTE, HD), BF16), dma((1,))],
        compiler_params=params(16),
        cost_estimate=cost(2 * slots * width * heads * HD, out_weight.size * 2),
        name="out_projection",
    )(meta, plan, attended, out_weight, hidden, *got_notes)
    boxes = pl.pallas_call(
        pack_kernel,
        out_shape=[jax.ShapeDtypeStruct((MOVE,) + kv_cache.shape[1:], BF16)] * (others - 1),
        in_specs=[SMEM, VMEM, ANY],
        out_specs=[ANY] * (others - 1),
        scratch_shapes=[dma((moving - MOVE,))],
        compiler_params=params(16),
        cost_estimate=cost(1, 1 * cache_bytes),
        name="pack",
    )(plan, cache, own)
    got_boxes = got_notes[:1] + [swapped(box, "inst", peers, k + 2) for k, box in enumerate(boxes)]

    def summed(own, sends, passed_on):
        got = [swapped(sends[k - 1], "tp", peers_tp, k) for k in range(peers_tp - 1, 0, -1)]
        shard_rows = pl.pallas_call(
            sum_kernel,
            out_shape=jax.ShapeDtypeStruct((slots, shard), BF16),
            in_specs=[VMEM] * peers_tp,
            out_specs=VMEM,
            compiler_params=params(16),
            name="sum_terms",
        )(own, *got)
        blocks = {0: shard_rows}
        if not passed_on:
            blocks |= {k: swapped(shard_rows, "tp", peers_tp, k) for k in range(1, peers_tp)}
        far = peers_tp // 2 if passed_on else 0
        while far:
            blocks |= {k + far: swapped(blocks[k], "tp", peers_tp, far) for k in blocks}
            far //= 2
        return [blocks[k] for k in range(peers_tp)]

    pieces = summed(own, sends, False)

    weight, cos_rows, sin_rows, place = pl.pallas_call(
        functools.partial(prepare_kernel, peers, slots),
        out_shape=[
            jax.ShapeDtypeStruct((width, 2 * HD), BF16),
            row32,
            row32,
            jax.ShapeDtypeStruct((slots,), I32),
        ],
        in_specs=[SMEM] * 4 + [VMEM] * 3 + [ANY],
        out_specs=[VMEM] * 3 + [SMEM],
        compiler_params=params(16),
        cost_estimate=cost(100*flops, wkv.size * 40),
        name="prepare",
    )(meta, source, lengths, plan, cosine, sine, wkv, own)

    own, *sends, cache = pl.pallas_call(
        functools.partial(second_kernel, peers, peers_tp, slots, heads),
        out_shape=sent + [held],
        in_specs=[SMEM] * 4 + [VMEM] * (7 + peers_tp) + [ANY] * others,
        out_specs=[VMEM] * (1 + peers_tp),
        scratch_shapes=[
            pltpu.VMEM((blocks, slots, HD), BF16),
            pltpu.VMEM((slots * GROUP, HD), F32),
            pltpu.VMEM((slots * GROUP, HD), F32),
            dma((others,)),
        ],
        input_output_aliases={10: peers_tp},
        compiler_params=params(16),
        cost_estimate=cost(3 * flops, cache_bytes + (query_weight.size + wkv.size) * 4),
        name="second_step",
    )(meta, source, lengths, place, gain, cos_rows, sin_rows, query_weight, weight, out_weight, cache,
      *pieces, *got_boxes)

    pieces = summed(own, sends, False)
    final_cache = pl.pallas_call(
        functools.partial(cache_kernel, slots),
        out_shape=jax.ShapeDtypeStruct(kv_cache.shape, BF16),
        in_specs=[SMEM, VMEM],
        out_specs=ANY,
        scratch_shapes=[dma((slots,))],
        compiler_params=params(16),
        cost_estimate=cost(0, 2 * cache_bytes),
        name="write_cache",
    )(place, cache)
    final_hidden = pl.pallas_call(
        functools.partial(join_kernel, peers_tp),
        out_shape=jax.ShapeDtypeStruct(hidden.shape, BF16),
        in_specs=[SMEM] + [ANY] * peers_tp,
        out_specs=ANY,
        scratch_shapes=[dma((peers_tp,))],
        compiler_params=params(16),
        name="join",
    )(meta, *pieces)
    return (final_hidden, final_cache)


def solution(mesh):
    def whole(kv_cache, *rest):
        tables = angle_tables(kv_cache.shape[2])
        return jax.shard_map(
            functools.partial(local, tables),
            mesh=mesh,
            in_specs=(
                P(("groups", "inst"), None, None, "tp"),
                P(("groups", "inst"), None),
                P("groups"),
                P("groups"),
                P(),
                P(None, "tp"),
                P(None, None, "tp"),
                P("tp", None),
            ),
            out_specs=(P(("groups", "inst"), None), P(("groups", "inst"), None, None, "tp")),
            check_vma=False,
        )(kv_cache, *rest)

    return whole
```

```python
import functools

import jax
import jax.numpy as jnp
import numpy as np
from jax import lax
from jax.experimental import pallas as pl
from jax.experimental.pallas import tpu as pltpu
from jax.sharding import PartitionSpec as P

MOVE = 2
EPS = 1e-05
THETA = 500000.0
HD = 128
GROUP = 8
PIECE = 16
CHUNK = 8
BATCH = 16
NOTE = 16

F32 = jnp.float32
BF16 = jnp.bfloat16
I32 = jnp.int32

ANY = pl.BlockSpec(memory_space=pl.ANY)
VMEM = pl.BlockSpec(memory_space=pltpu.VMEM)
SMEM = pl.BlockSpec(memory_space=pltpu.SMEM)
HBM = pl.BlockSpec(memory_space=pltpu.HBM)


def params(mib):
    return pltpu.CompilerParams(vmem_limit_bytes=mib * 1024 * 1024)


def cost(flops, nbytes):
    return pl.CostEstimate(flops=flops, bytes_accessed=nbytes, transcendentals=0)


def angle_tables(positions):
    frequency = THETA ** (-(np.arange(HD // 2, dtype=np.float64) * 2.0) / HD)
    angles = np.arange(positions, dtype=np.float64)[:, None] * frequency[None, :]
    cosine = np.concatenate([np.cos(angles), np.cos(angles)], axis=-1)
    sine = np.concatenate([-np.sin(angles), np.sin(angles)], axis=-1)
    return cosine.astype(np.float32), sine.astype(np.float32)


def turn(x, cosine, sine):
    return x * cosine + pltpu.roll(x, HD // 2, 1) * sine


def gather_angles(position_of, slots, cos_ref, sin_ref, cos_rows, sin_rows):
    for s in range(slots):
        p = position_of(s)
        cos_rows[s : s + 1, :] = cos_ref[pl.ds(p, 1), :]
        sin_rows[s : s + 1, :] = sin_ref[pl.ds(p, 1), :]


def spread_normed(normed3, spread, slots, width):
    blocks = width // HD
    row = lax.broadcasted_iota(I32, (HD, 4 * HD), 0)
    col = lax.broadcasted_iota(I32, (HD, 4 * HD), 1)
    goal = jnp.where(col < 2 * HD, 2 * row, 2 * row + 1 + 2 * HD)
    places = jnp.where(col == goal, 1.0, 0.0).astype(BF16)
    spread_all = jnp.dot(
        normed3[...].reshape(blocks * slots, HD), places, preferred_element_type=F32
    ).astype(BF16)
    spread[:, 0:slots, :] = spread_all[:, : 2 * HD].reshape(blocks, slots, 2 * HD)
    spread[:, slots:, :] = spread_all[:, 2 * HD :].reshape(blocks, slots, 2 * HD)


def project_from(normed3, weight):
    total = None
    for b in range(normed3.shape[0] // 2):
        block = jnp.concatenate([normed3[2 * b], normed3[2 * b + 1]], axis=1)
        part = jnp.dot(
            block, weight[b * 2 * HD : (b + 1) * 2 * HD, :], preferred_element_type=F32
        )
        total = part if total is None else total + part
    return total


def project_spread(spread, wkv):
    total = None
    for b in range(spread.shape[0]):
        part = jnp.dot(
            spread[b], wkv[b * 2 * HD : (b + 1) * 2 * HD, :], preferred_element_type=F32
        )
        total = part if total is None else total + part
    slots = spread.shape[1] // 2
    return total[:slots], total[slots:]


def weight_copies(src, dst, sem, pieces):
    depth = src.shape[0] // pieces
    copies = [
        pltpu.make_async_copy(
            src.at[pl.ds(c * depth, depth)], dst.at[pl.ds(c * depth, depth)], sem.at[c]
        )
        for c in range(pieces)
    ]
    return copies


def put_row(cache, place, p, key_row, value_row):
    base = pl.multiple_of((jnp.maximum(p, 0) // PIECE) * PIECE, PIECE)
    hit = lax.broadcasted_iota(I32, (PIECE, HD), 0) + base == p
    for which, new in ((0, key_row), (1, value_row)):
        old = cache[place, which, pl.ds(base, PIECE), :].astype(F32)
        cache[place, which, pl.ds(base, PIECE), :] = jnp.where(hit, new, old).astype(BF16)


def attend(cache, places, positions, query_rows):
    cap = cache.shape[2]
    col = lax.broadcasted_iota(I32, (GROUP, cap), 1)
    scores = [
        lax.dot_general(
            rows.astype(BF16),
            cache[place, 0],
            (((1,), (1,)), ((), ())),
            preferred_element_type=F32,
        )
        for place, rows in zip(places, query_rows)
    ]
    probs = []
    for score, p in zip(scores, positions):
        score = jnp.where(col <= p, score * HD**-0.5, -jnp.inf)
        weight = jnp.exp(score - jnp.max(score, axis=-1, keepdims=True))
        weight = weight / jnp.sum(weight, axis=-1, keepdims=True)
        probs.append(weight.astype(BF16))
    return [
        jnp.dot(prob, cache[place, 1], preferred_element_type=F32)
        for place, prob in zip(places, probs)
    ]


def norm_into(normed3, pieces, gains, firsts, total_width):
    square = None
    for piece in pieces:
        part = jnp.sum(piece * piece, axis=-1, keepdims=True)
        square = part if square is None else square + part
    factor = lax.rsqrt(square / total_width + EPS)
    for piece, gain, first in zip(pieces, gains, firsts):
        normed = (piece * factor * gain).astype(BF16)
        for i in range(piece.shape[1] // HD):
            normed3[first + i] = normed[:, i * HD : (i + 1) * HD]


def plan_moves(me, peers, slots, source):
    moving = (peers - 1) * MOVE
    shape = (2 * moving, source.shape[1])
    row = lax.broadcasted_iota(I32, shape, 0)
    index = lax.broadcasted_iota(I32, shape, 1)
    leaves = row < moving
    at = jnp.where(leaves, row, row - moving)
    other = jnp.bitwise_xor(me, at // MOVE + 1)
    here, there = me * slots, other * slots
    src = jnp.broadcast_to(source, shape)
    came, went = jnp.where(leaves, here, there), jnp.where(leaves, there, here)
    moved = (src >= came) & (src < came + slots) & (index >= went) & (index < went + slots)
    sign = jnp.where(at % MOVE == 0, -1.0, 1.0)
    index_f = index.astype(F32)
    best = jnp.max(jnp.where(moved, sign * index_f, -1e6), axis=1, keepdims=True)
    hit = moved & (sign * index_f == best)
    result = jnp.where(leaves, src, index) - here
    found = jnp.sum(jnp.where(hit, result.astype(F32), 0.0), axis=1, keepdims=True)
    none = jnp.where(leaves[:, :1], 0.0, -1.0)
    return jnp.where(best > -1e6, found, none).astype(I32)


def first_kernel(
    peers, slots, heads, shard,
    meta, source_hbm, lengths_hbm, hidden_hbm, gain_hbm, cos_hbm, sin_hbm, wq_hbm, wkv_hbm,
    cache_hbm, query_out, newkey_out, newvalue_out, plan, *rest,
):
    others = peers - 1
    moving = others * MOVE
    cache, box, notes = rest[0], rest[1], (None,) + rest[2 : others + 1]
    (wq, wkv, normed3, spread, cos_rows, sin_rows, leaving, hidden32, lengths_s, source_v,
     hidden, gain, cos_ref, sin_ref, small_sem, wq_sem, wkv_sem, in_sem,
     box_sem, cache_sem) = rest[others + 1 :]
    width = hidden.shape[1]
    me, me_tp = meta[0], meta[1]
    wq_copies = weight_copies(wq_hbm, wq, wq_sem, 4)
    wkv_copies = weight_copies(wkv_hbm, wkv, wkv_sem, 4)
    small = [
        pltpu.make_async_copy(src, dst, small_sem.at[i])
        for i, (src, dst) in enumerate((
            (source_hbm, source_v), (hidden_hbm, hidden), (gain_hbm, gain), (lengths_hbm, lengths_s),
            (cos_hbm, cos_ref), (sin_hbm, sin_ref),
        ))
    ]
    for copy in small[:3] + wkv_copies + wq_copies + small[3:]:
        copy.start()
    loads = [
        pltpu.make_async_copy(
            cache_hbm.at[pl.ds(c * CHUNK, CHUNK)], cache.at[pl.ds(c * CHUNK, CHUNK)], cache_sem.at[c]
        )
        for c in range(slots // CHUNK)
    ]
    for copy in small[:3]:
        copy.wait()
    low = me * slots
    moves = plan_moves(me, peers, slots, source_v[...])
    wide = hidden[...].astype(F32)
    hidden32[...] = wide
    norm_into(normed3, [wide], [gain[...]], [0], width)
    spread_normed(normed3, spread, slots, width)
    send_slots = []
    for at in range(moving):
        slot = moves[at, 0]
        send_slots.append(slot)
        plan[moving + at] = slot
        plan[at] = moves[moving + at, 0]
        pltpu.make_async_copy(cache_hbm.at[slot], leaving.at[at], in_sem.at[at]).start()
    for copy in loads:
        copy.start()
    for copy in small[3:] + wkv_copies + wq_copies:
        copy.wait()
    gather_angles(lambda s: lengths_s[0, low + s], slots, cos_ref, sin_ref, cos_rows, sin_rows)
    key, value = project_spread(spread, wkv)
    query = project_from(normed3, wq)
    cosine, sine = cos_rows[...], sin_rows[...]
    query_out[...] = jnp.zeros(query_out.shape, F32)
    for g in range(heads):
        turned = turn(query[:, g * HD : (g + 1) * HD], cosine, sine)
        query_out[pl.ds(g, slots, stride=GROUP), :] = turned.astype(BF16).astype(F32)
    newkey_out[...] = turn(key, cosine, sine).astype(BF16).astype(F32)
    newvalue_out[...] = value.astype(BF16).astype(F32)

    positions = [lengths_s[0, low + slot] for slot in send_slots]
    for at, slot in enumerate(send_slots):
        pltpu.make_async_copy(cache_hbm.at[slot], leaving.at[at], in_sem.at[at]).wait()
        put_row(
            leaving, at, positions[at],
            newkey_out[pl.ds(slot, 1), :], newvalue_out[pl.ds(slot, 1), :],
        )
    cap = leaving.shape[2]
    copies = [
        pltpu.make_async_copy(
            leaving.at[pl.ds(0, MOVE)], box.at[:, :, pl.ds(0, cap), :], box_sem.at[0]
        )
    ]
    copies[0].start()
    rows = [query_out[pl.ds(pl.multiple_of(slot * GROUP, GROUP), GROUP), :] for slot in send_slots]
    attended = attend(leaving, list(range(moving)), positions, rows)
    column = pl.multiple_of(me_tp * shard, shard)
    for at, slot in enumerate(send_slots):
        m = at % MOVE
        residual = hidden32[pl.ds(slot, 1), pl.ds(column, shard)]
        if at < MOVE:
            blocks = [attended[at][g : g + 1, :] for g in range(heads)]
            blocks += [residual[:, b * HD : (b + 1) * HD] for b in range(shard // HD)]
            blocks += [jnp.zeros((1, HD), F32)] * (NOTE - len(blocks))
            box[m, 0, cap : cap + NOTE, :] = jnp.concatenate(blocks, axis=0).astype(BF16)
        else:
            note = notes[at // MOVE]
            for g in range(heads):
                note[m : m + 1, g * HD : (g + 1) * HD] = attended[at][g : g + 1, :]
            note[m : m + 1, heads * HD :] = residual
    for copy in copies + loads:
        copy.wait()


def attend_slots(cache, places, positions, query, attended_rows, heads):
    slots = len(places)
    for first in range(0, slots, BATCH):
        span = range(first, first + BATCH)
        got = attend(
            cache,
            [places[s] for s in span],
            [positions[s] for s in span],
            [query[s * GROUP : (s + 1) * GROUP, :] for s in span],
        )
        for s, rows in zip(span, got):
            attended_rows[s * GROUP : (s + 1) * GROUP, :] = rows
    return jnp.concatenate(
        [attended_rows[pl.ds(g, slots, stride=GROUP), :] for g in range(heads)], axis=1
    )


def attend_kernel(
    slots, heads, meta, lengths_s, query, newkey, newvalue, _, out, cache, attended_rows,
):
    low = meta[0] * slots
    positions = [lengths_s[low + s] for s in range(slots)]
    for s, p in enumerate(positions):
        put_row(cache, s, p, newkey[s : s + 1, :], newvalue[s : s + 1, :])
    out[...] = attend_slots(
        cache, list(range(slots)), positions, query, attended_rows, heads
    ).astype(BF16)


def project_out(attended, wo, residual, own, sends, me_tp, peers_tp):
    shard = own.shape[1]
    for k in list(range(peers_tp - 1, 0, -1)) + [0]:
        column = pl.multiple_of(jnp.bitwise_xor(me_tp, k) * shard, shard)
        part = jnp.dot(attended, wo[:, pl.ds(column, shard)], preferred_element_type=F32)
        if k == 0:
            own[...] = residual + part
        else:
            sends[k - 1][...] = part.astype(BF16)


def out_kernel(
    peers, peers_tp, meta, plan, attended, wo, hidden, box_hbm, *rest,
):
    notes, rest = rest[: peers - 2], rest[peers - 2 :]
    own, sends, (tail, sem) = rest[0], rest[1:peers_tp], rest[peers_tp:]
    shard = own.shape[1]
    cap = box_hbm.shape[2] - NOTE
    copy = pltpu.make_async_copy(box_hbm.at[:, 0, pl.ds(cap, NOTE), :], tail, sem.at[0])
    copy.start()
    rows = attended[...].astype(F32)
    heads = rows.shape[1] // HD
    column = pl.multiple_of(meta[1] * shard, shard)
    residual = hidden[:, pl.ds(column, shard)].astype(F32)
    row_index = lax.broadcasted_iota(I32, rows.shape, 0)
    residual_index = lax.broadcasted_iota(I32, residual.shape, 0)
    copy.wait()
    for at in range((peers - 1) * MOVE):
        m = at % MOVE
        if at < MOVE:
            blocks = tail[m].astype(F32)
            blocks = [blocks[b : b + 1, :] for b in range(heads + shard // HD)]
            note = jnp.concatenate(blocks, axis=1)
        else:
            note = notes[at // MOVE - 1][m : m + 1, :]
        rows = jnp.where(row_index == plan[at], note[:, : heads * HD], rows)
        residual = jnp.where(residual_index == plan[at], note[:, heads * HD :], residual)
    project_out(rows.astype(BF16), wo, residual, own, sends, meta[1], peers_tp)


def pack_kernel(plan, cache, _own, *rest):
    boxes, out_sem = rest[:-1], rest[-1]
    moving = plan.shape[0] // 2
    packs = [
        pltpu.make_async_copy(
            cache.at[plan[moving + at]], boxes[at // MOVE - 1].at[at % MOVE], out_sem.at[at - MOVE]
        )
        for at in range(MOVE, moving)
    ]
    for pack in packs:
        pack.start()
    for pack in packs:
        pack.wait()


def sum_kernel(own, *rest):
    total = own[...]
    for part in rest[:-1]:
        total = total + part[...].astype(F32)
    rest[-1][...] = total.astype(BF16)


def map_places(slots, peers, plan, place):
    for s in range(slots):
        place[s] = s
    for at in range((peers - 1) * MOVE):
        taker = plan[at]

        @pl.when(taker >= 0)
        def _():
            place[taker] = slots + at


def prepare_kernel(
    peers, slots, meta, source_s, lengths_s, plan, cos_ref, sin_ref, wkv, _,
    weight, cos_rows, sin_rows, place,
):
    map_places(slots, peers, plan, place)
    low = meta[0] * slots
    gather_angles(
        lambda s: lengths_s[source_s[low + s]] + 1, slots, cos_ref, sin_ref, cos_rows, sin_rows
    )
    row = lax.broadcasted_iota(I32, (2 * HD, 2 * HD), 0)
    col = lax.broadcasted_iota(I32, (2 * HD, 2 * HD), 1)
    goal = jnp.where(row < HD, 2 * row, 2 * (row - HD) + 1)
    places = jnp.where(col == goal, 1.0, 0.0).astype(BF16)
    for b in range(weight.shape[0] // HD):
        apart = jnp.dot(
            places, wkv[b * 2 * HD : (b + 1) * 2 * HD, :], preferred_element_type=F32
        ).astype(BF16)
        weight[b * HD : (b + 1) * HD, :HD] = apart[:HD]
        weight[b * HD : (b + 1) * HD, HD:] = apart[HD:]


def second_kernel(
    peers, peers_tp, slots, heads,
    meta, source_s, lengths_s, place, gain, cos_rows, sin_rows, wq, wkv, wo, _, *rest,
):
    blocks, rest = rest[:peers_tp], rest[peers_tp:]
    box_hbm, rest = rest[: peers - 1], rest[peers - 1 :]
    own, sends, cache = rest[0], rest[1:peers_tp], rest[peers_tp]
    normed3, query_rows, attended_rows, in_sem = rest[peers_tp + 1 :]
    me, me_tp = meta[0], meta[1]
    low = me * slots
    width = gain.shape[1]
    shard = own.shape[1]
    loads = [
        pltpu.make_async_copy(
            box.at[:, :, pl.ds(0, cache.shape[2]), :],
            cache.at[pl.ds(slots + k * MOVE, MOVE)],
            in_sem.at[k],
        )
        for k, box in enumerate(box_hbm)
    ]
    for copy in loads:
        copy.start()

    firsts = [jnp.bitwise_xor(me_tp, k) for k in range(peers_tp)]
    norm_into(
        normed3,
        [block[...].astype(F32) for block in blocks],
        [gain[:, pl.ds(pl.multiple_of(first * shard, shard), shard)] for first in firsts],
        [first * (shard // HD) for first in firsts],
        width,
    )
    positions = [lengths_s[source_s[low + s]] + 1 for s in range(slots)]
    query = project_from(normed3, wq)
    pair = project_from(normed3, wkv)
    key, value = pair[:, :HD], pair[:, HD:]
    cosine, sine = cos_rows[...], sin_rows[...]
    query_rows[...] = jnp.zeros(query_rows.shape, F32)
    for g in range(heads):
        turned = turn(query[:, g * HD : (g + 1) * HD], cosine, sine)
        query_rows[pl.ds(g, slots, stride=GROUP), :] = turned.astype(BF16).astype(F32)
    newkey = turn(key, cosine, sine).astype(BF16).astype(F32)
    newvalue = value.astype(BF16).astype(F32)

    for copy in loads:
        copy.wait()
    places = [place[s] for s in range(slots)]
    for s, (at, p) in enumerate(zip(places, positions)):
        put_row(cache, at, p, newkey[s : s + 1, :], newvalue[s : s + 1, :])
    attended = attend_slots(cache, places, positions, query_rows, attended_rows, heads)
    project_out(
        attended.astype(BF16), wo, blocks[0][...].astype(F32), own, sends, me_tp, peers_tp
    )


def cache_kernel(slots, place, cache, out_hbm, out_sem):
    copies = [
        pltpu.make_async_copy(cache.at[place[s]], out_hbm.at[s], out_sem.at[s])
        for s in range(slots)
    ]
    for copy in copies:
        copy.start()
    for copy in copies:
        copy.wait()


def join_kernel(peers_tp, meta, *rest):
    blocks, out, sem = rest[:-2], rest[-2], rest[-1]
    shard = blocks[0].shape[1]
    copies = []
    for k, block in enumerate(blocks):
        column = pl.multiple_of(jnp.bitwise_xor(meta[1], k) * shard, shard)
        copies.append(pltpu.make_async_copy(block, out.at[:, pl.ds(column, shard)], sem.at[k]))
        copies[-1].start()
    for copy in copies:
        copy.wait()


def swapped(x, axis, size, k):
    return lax.ppermute(x, axis, [(i, i ^ k) for i in range(size)])


def local(
    tables, kv_cache, hidden, lengths, source, norm_gain, query_weight, keyval_weight, out_weight
):
    peers, peers_tp = lax.axis_size("inst"), lax.axis_size("tp")
    slots, cap = kv_cache.shape[0], kv_cache.shape[2]
    width = hidden.shape[1]
    heads = query_weight.shape[1] // HD
    shard = width // peers_tp
    others, moving = peers - 1, (peers - 1) * MOVE
    blocks = width // HD
    meta = jnp.stack([lax.axis_index("inst"), lax.axis_index("tp")]).astype(I32)
    gain = norm_gain.reshape(1, width)
    wkv = keyval_weight.reshape(2 * width, HD)
    cosine, sine = (jnp.asarray(table) for table in tables)
    row32 = jax.ShapeDtypeStruct((slots, HD), F32)
    note_width = heads * HD + shard
    dma = pltpu.SemaphoreType.DMA
    weights = [
        pltpu.VMEM(query_weight.shape, BF16),
        pltpu.VMEM(wkv.shape, BF16),
    ]
    stages = [
        pltpu.VMEM((blocks, slots, HD), BF16),
        pltpu.VMEM((blocks, 2 * slots, 2 * HD), BF16),
        pltpu.VMEM((slots, HD), F32),
        pltpu.VMEM((slots, HD), F32),
    ]
    flops = 2 * slots * width * (heads + 2) * HD
    cache_bytes = kv_cache.size * 2
    held = jax.ShapeDtypeStruct((slots + moving,) + kv_cache.shape[1:], BF16)

    query, newkey1, newvalue1, plan, cache, *notes = pl.pallas_call(
        functools.partial(first_kernel, peers, slots, heads, shard),
        out_shape=[
            jax.ShapeDtypeStruct((slots * GROUP, HD), F32),
            row32,
            row32,
            jax.ShapeDtypeStruct((2 * moving,), I32),
            held,
        ]
        + [jax.ShapeDtypeStruct((MOVE, 2, cap + NOTE, HD), BF16)]
        + [jax.ShapeDtypeStruct((MOVE, note_width), F32)] * (others - 1),
        in_specs=[SMEM] + [HBM] * 9,
        out_specs=[VMEM] * 3 + [SMEM] + [VMEM] * (others + 1),
        scratch_shapes=weights
        + stages
        + [
            pltpu.VMEM((moving,) + kv_cache.shape[1:], BF16),
            pltpu.VMEM((slots, width), F32),
            pltpu.SMEM((1, source.shape[0]), I32),
            pltpu.VMEM((1, source.shape[0]), I32),
            pltpu.VMEM(hidden.shape, BF16),
            pltpu.VMEM((1, width), F32),
            pltpu.VMEM(cosine.shape, F32),
            pltpu.VMEM(cosine.shape, F32),
            dma((6,)),
            dma((4,)),
            dma((4,)),
            dma((moving,)),
            dma((1,)),
            dma((slots // CHUNK,)),
        ],
        compiler_params=params(24),
        cost_estimate=cost(flops, (query_weight.size + wkv.size) * 2),
        name="first_step",
    )(meta, *(
        pltpu.with_memory_space_constraint(x, pltpu.HBM)
        for x in (source.reshape(1, -1), lengths.reshape(1, -1), hidden, gain, cosine, sine,
                  query_weight, wkv, kv_cache)
    ))
    got_notes = [swapped(note, "inst", peers, k + 1) for k, note in enumerate(notes)]

    attended, cache = pl.pallas_call(
        functools.partial(attend_kernel, slots, heads),
        out_shape=[jax.ShapeDtypeStruct((slots, heads * HD), BF16), held],
        in_specs=[SMEM] * 2 + [VMEM] * 4,
        out_specs=[VMEM] * 2,
        scratch_shapes=[pltpu.VMEM((slots * GROUP, HD), F32)],
        input_output_aliases={5: 1},
        compiler_params=params(12),
        cost_estimate=cost(4 * slots * cap * HD * heads, cache_bytes),
        name="attention",
    )(meta, lengths, query, newkey1, newvalue1, cache)

    sent = [jax.ShapeDtypeStruct((slots, shard), F32)]
    sent += [jax.ShapeDtypeStruct((slots, shard), BF16)] * (peers_tp - 1)
    own, *sends = pl.pallas_call(
        functools.partial(out_kernel, peers, peers_tp),
        out_shape=sent,
        in_specs=[SMEM] * 2 + [VMEM] * 3 + [ANY] + [VMEM] * (others - 1),
        out_specs=[VMEM] * peers_tp,
        scratch_shapes=[pltpu.VMEM((MOVE, NOTE, HD), BF16), dma((1,))],
        compiler_params=params(16),
        cost_estimate=cost(2 * slots * width * heads * HD, out_weight.size * 2),
        name="out_projection",
    )(meta, plan, attended, out_weight, hidden, *got_notes)
    boxes = pl.pallas_call(
        pack_kernel,
        out_shape=[jax.ShapeDtypeStruct((MOVE,) + kv_cache.shape[1:], BF16)] * (others - 1),
        in_specs=[SMEM, VMEM, ANY],
        out_specs=[ANY] * (others - 1),
        scratch_shapes=[dma((moving - MOVE,))],
        compiler_params=params(16),
        cost_estimate=cost(1, 1 * cache_bytes),
        name="pack",
    )(plan, cache, own)
    got_boxes = got_notes[:1] + [swapped(box, "inst", peers, k + 2) for k, box in enumerate(boxes)]

    def summed(own, sends, passed_on):
        got = [swapped(sends[k - 1], "tp", peers_tp, k) for k in range(peers_tp - 1, 0, -1)]
        shard_rows = pl.pallas_call(
            sum_kernel,
            out_shape=jax.ShapeDtypeStruct((slots, shard), BF16),
            in_specs=[VMEM] * peers_tp,
            out_specs=VMEM,
            compiler_params=params(16),
            name="sum_terms",
        )(own, *got)
        blocks = {0: shard_rows}
        if not passed_on:
            blocks |= {k: swapped(shard_rows, "tp", peers_tp, k) for k in range(1, peers_tp)}
        far = peers_tp // 2 if passed_on else 0
        while far:
            blocks |= {k + far: swapped(blocks[k], "tp", peers_tp, far) for k in blocks}
            far //= 2
        return [blocks[k] for k in range(peers_tp)]

    pieces = summed(own, sends, False)

    weight, cos_rows, sin_rows, place = pl.pallas_call(
        functools.partial(prepare_kernel, peers, slots),
        out_shape=[
            jax.ShapeDtypeStruct((width, 2 * HD), BF16),
            row32,
            row32,
            jax.ShapeDtypeStruct((slots,), I32),
        ],
        in_specs=[SMEM] * 4 + [VMEM] * 3 + [ANY],
        out_specs=[VMEM] * 3 + [SMEM],
        compiler_params=params(16),
        cost_estimate=cost(100*flops, wkv.size * 40),
        name="prepare",
    )(meta, source, lengths, plan, cosine, sine, wkv, own)

    own, *sends, cache = pl.pallas_call(
        functools.partial(second_kernel, peers, peers_tp, slots, heads),
        out_shape=sent + [held],
        in_specs=[SMEM] * 4 + [VMEM] * (7 + peers_tp) + [ANY] * others,
        out_specs=[VMEM] * (1 + peers_tp),
        scratch_shapes=[
            pltpu.VMEM((blocks, slots, HD), BF16),
            pltpu.VMEM((slots * GROUP, HD), F32),
            pltpu.VMEM((slots * GROUP, HD), F32),
            dma((others,)),
        ],
        input_output_aliases={10: peers_tp},
        compiler_params=params(16),
        cost_estimate=cost(3 * flops, cache_bytes + (query_weight.size + wkv.size) * 4),
        name="second_step",
    )(meta, source, lengths, place, gain, cos_rows, sin_rows, query_weight, weight, out_weight, cache,
      *pieces, *got_boxes)

    pieces = summed(own, sends, False)
    final_cache = pl.pallas_call(
        functools.partial(cache_kernel, slots),
        out_shape=jax.ShapeDtypeStruct(kv_cache.shape, BF16),
        in_specs=[SMEM, VMEM],
        out_specs=ANY,
        scratch_shapes=[dma((slots,))],
        compiler_params=params(16),
        cost_estimate=cost(0, 2 * cache_bytes),
        name="write_cache",
    )(place, cache)
    final_hidden = pl.pallas_call(
        functools.partial(join_kernel, peers_tp),
        out_shape=jax.ShapeDtypeStruct(hidden.shape, BF16),
        in_specs=[SMEM] + [ANY] * peers_tp,
        out_specs=ANY,
        scratch_shapes=[dma((peers_tp,))],
        compiler_params=params(16),
        name="join",
    )(meta, *pieces)
    return (final_hidden, final_cache)


def solution(mesh):
    def whole(kv_cache, *rest):
        tables = angle_tables(kv_cache.shape[2])
        return jax.shard_map(
            functools.partial(local, tables),
            mesh=mesh,
            in_specs=(
                P(("groups", "inst"), None, None, "tp"),
                P(("groups", "inst"), None),
                P("groups"),
                P("groups"),
                P(),
                P(None, "tp"),
                P(None, None, "tp"),
                P("tp", None),
            ),
            out_specs=(P(("groups", "inst"), None), P(("groups", "inst"), None, None, "tp")),
            check_vma=False,
        )(kv_cache, *rest)

    return whole
```

```python
import functools

import jax
import jax.numpy as jnp
import numpy as np
from jax import lax
from jax.experimental import pallas as pl
from jax.experimental.pallas import tpu as pltpu
from jax.sharding import PartitionSpec as P

MOVE = 2
EPS = 1e-05
THETA = 500000.0
HD = 128
GROUP = 8
PIECE = 16
CHUNK = 8
BATCH = 16
NOTE = 16

F32 = jnp.float32
BF16 = jnp.bfloat16
I32 = jnp.int32

ANY = pl.BlockSpec(memory_space=pl.ANY)
VMEM = pl.BlockSpec(memory_space=pltpu.VMEM)
SMEM = pl.BlockSpec(memory_space=pltpu.SMEM)
HBM = pl.BlockSpec(memory_space=pltpu.HBM)


def params(mib):
    return pltpu.CompilerParams(vmem_limit_bytes=mib * 1024 * 1024)


def cost(flops, nbytes):
    return pl.CostEstimate(flops=flops, bytes_accessed=nbytes, transcendentals=0)


def angle_tables(positions):
    frequency = THETA ** (-(np.arange(HD // 2, dtype=np.float64) * 2.0) / HD)
    angles = np.arange(positions, dtype=np.float64)[:, None] * frequency[None, :]
    cosine = np.concatenate([np.cos(angles), np.cos(angles)], axis=-1)
    sine = np.concatenate([-np.sin(angles), np.sin(angles)], axis=-1)
    return cosine.astype(np.float32), sine.astype(np.float32)


def turn(x, cosine, sine):
    return x * cosine + pltpu.roll(x, HD // 2, 1) * sine


def gather_angles(position_of, slots, cos_ref, sin_ref, cos_rows, sin_rows):
    for s in range(slots):
        p = position_of(s)
        cos_rows[s : s + 1, :] = cos_ref[pl.ds(p, 1), :]
        sin_rows[s : s + 1, :] = sin_ref[pl.ds(p, 1), :]


def spread_normed(normed3, spread, slots, width):
    blocks = width // HD
    row = lax.broadcasted_iota(I32, (HD, 4 * HD), 0)
    col = lax.broadcasted_iota(I32, (HD, 4 * HD), 1)
    goal = jnp.where(col < 2 * HD, 2 * row, 2 * row + 1 + 2 * HD)
    places = jnp.where(col == goal, 1.0, 0.0).astype(BF16)
    spread_all = jnp.dot(
        normed3[...].reshape(blocks * slots, HD), places, preferred_element_type=F32
    ).astype(BF16)
    spread[:, 0:slots, :] = spread_all[:, : 2 * HD].reshape(blocks, slots, 2 * HD)
    spread[:, slots:, :] = spread_all[:, 2 * HD :].reshape(blocks, slots, 2 * HD)


def project_from(normed3, weight):
    total = None
    for b in range(normed3.shape[0] // 2):
        block = jnp.concatenate([normed3[2 * b], normed3[2 * b + 1]], axis=1)
        part = jnp.dot(
            block, weight[b * 2 * HD : (b + 1) * 2 * HD, :], preferred_element_type=F32
        )
        total = part if total is None else total + part
    return total


def project_spread(spread, wkv):
    total = None
    for b in range(spread.shape[0]):
        part = jnp.dot(
            spread[b], wkv[b * 2 * HD : (b + 1) * 2 * HD, :], preferred_element_type=F32
        )
        total = part if total is None else total + part
    slots = spread.shape[1] // 2
    return total[:slots], total[slots:]


def weight_copies(src, dst, sem, pieces):
    depth = src.shape[0] // pieces
    copies = [
        pltpu.make_async_copy(
            src.at[pl.ds(c * depth, depth)], dst.at[pl.ds(c * depth, depth)], sem.at[c]
        )
        for c in range(pieces)
    ]
    return copies


def put_row(cache, place, p, key_row, value_row):
    base = pl.multiple_of((jnp.maximum(p, 0) // PIECE) * PIECE, PIECE)
    hit = lax.broadcasted_iota(I32, (PIECE, HD), 0) + base == p
    for which, new in ((0, key_row), (1, value_row)):
        old = cache[place, which, pl.ds(base, PIECE), :].astype(F32)
        cache[place, which, pl.ds(base, PIECE), :] = jnp.where(hit, new, old).astype(BF16)


def attend(cache, places, positions, query_rows):
    cap = cache.shape[2]
    col = lax.broadcasted_iota(I32, (GROUP, cap), 1)
    scores = [
        lax.dot_general(
            rows.astype(BF16),
            cache[place, 0],
            (((1,), (1,)), ((), ())),
            preferred_element_type=F32,
        )
        for place, rows in zip(places, query_rows)
    ]
    probs = []
    for score, p in zip(scores, positions):
        score = jnp.where(col <= p, score * HD**-0.5, -jnp.inf)
        weight = jnp.exp(score - jnp.max(score, axis=-1, keepdims=True))
        weight = weight / jnp.sum(weight, axis=-1, keepdims=True)
        probs.append(weight.astype(BF16))
    return [
        jnp.dot(prob, cache[place, 1], preferred_element_type=F32)
        for place, prob in zip(places, probs)
    ]


def norm_into(normed3, pieces, gains, firsts, total_width):
    square = None
    for piece in pieces:
        part = jnp.sum(piece * piece, axis=-1, keepdims=True)
        square = part if square is None else square + part
    factor = lax.rsqrt(square / total_width + EPS)
    for piece, gain, first in zip(pieces, gains, firsts):
        normed = (piece * factor * gain).astype(BF16)
        for i in range(piece.shape[1] // HD):
            normed3[first + i] = normed[:, i * HD : (i + 1) * HD]


def plan_moves(me, peers, slots, source):
    moving = (peers - 1) * MOVE
    shape = (2 * moving, source.shape[1])
    row = lax.broadcasted_iota(I32, shape, 0)
    index = lax.broadcasted_iota(I32, shape, 1)
    leaves = row < moving
    at = jnp.where(leaves, row, row - moving)
    other = jnp.bitwise_xor(me, at // MOVE + 1)
    here, there = me * slots, other * slots
    src = jnp.broadcast_to(source, shape)
    came, went = jnp.where(leaves, here, there), jnp.where(leaves, there, here)
    moved = (src >= came) & (src < came + slots) & (index >= went) & (index < went + slots)
    sign = jnp.where(at % MOVE == 0, -1.0, 1.0)
    index_f = index.astype(F32)
    best = jnp.max(jnp.where(moved, sign * index_f, -1e6), axis=1, keepdims=True)
    hit = moved & (sign * index_f == best)
    result = jnp.where(leaves, src, index) - here
    found = jnp.sum(jnp.where(hit, result.astype(F32), 0.0), axis=1, keepdims=True)
    none = jnp.where(leaves[:, :1], 0.0, -1.0)
    return jnp.where(best > -1e6, found, none).astype(I32)


def first_kernel(
    peers, slots, heads, shard,
    meta, source_hbm, lengths_hbm, hidden_hbm, gain_hbm, cos_hbm, sin_hbm, wq_hbm, wkv_hbm,
    cache_hbm, query_out, newkey_out, newvalue_out, plan, *rest,
):
    others = peers - 1
    moving = others * MOVE
    cache, box, notes = rest[0], rest[1], (None,) + rest[2 : others + 1]
    (wq, wkv, normed3, spread, cos_rows, sin_rows, leaving, hidden32, lengths_s, source_v,
     hidden, gain, cos_ref, sin_ref, small_sem, wq_sem, wkv_sem, in_sem,
     box_sem, cache_sem) = rest[others + 1 :]
    width = hidden.shape[1]
    me, me_tp = meta[0], meta[1]
    wq_copies = weight_copies(wq_hbm, wq, wq_sem, 4)
    wkv_copies = weight_copies(wkv_hbm, wkv, wkv_sem, 4)
    small = [
        pltpu.make_async_copy(src, dst, small_sem.at[i])
        for i, (src, dst) in enumerate((
            (source_hbm, source_v), (hidden_hbm, hidden), (gain_hbm, gain), (lengths_hbm, lengths_s),
            (cos_hbm, cos_ref), (sin_hbm, sin_ref),
        ))
    ]
    for copy in small[:3] + wkv_copies + wq_copies + small[3:]:
        copy.start()
    loads = [
        pltpu.make_async_copy(
            cache_hbm.at[pl.ds(c * CHUNK, CHUNK)], cache.at[pl.ds(c * CHUNK, CHUNK)], cache_sem.at[c]
        )
        for c in range(slots // CHUNK)
    ]
    for copy in small[:3]:
        copy.wait()
    low = me * slots
    moves = plan_moves(me, peers, slots, source_v[...])
    wide = hidden[...].astype(F32)
    hidden32[...] = wide
    norm_into(normed3, [wide], [gain[...]], [0], width)
    spread_normed(normed3, spread, slots, width)
    send_slots = [moves[at, 0] for at in range(moving)]
    fetches = [
        pltpu.make_async_copy(cache_hbm.at[slot], leaving.at[at], in_sem.at[at])
        for at, slot in enumerate(send_slots)
    ]
    for copy in fetches:
        copy.start()
    for at, slot in enumerate(send_slots):
        plan[moving + at] = slot
        plan[at] = moves[moving + at, 0]
    for copy in loads:
        copy.start()
    for copy in small[3:] + wkv_copies + wq_copies + fetches:
        copy.wait()
    gather_angles(lambda s: lengths_s[0, low + s], slots, cos_ref, sin_ref, cos_rows, sin_rows)
    key, value = project_spread(spread, wkv)
    query = project_from(normed3, wq)
    cosine, sine = cos_rows[...], sin_rows[...]
    query_out[...] = jnp.zeros(query_out.shape, F32)
    for g in range(heads):
        turned = turn(query[:, g * HD : (g + 1) * HD], cosine, sine)
        query_out[pl.ds(g, slots, stride=GROUP), :] = turned.astype(BF16).astype(F32)
    newkey_out[...] = turn(key, cosine, sine).astype(BF16).astype(F32)
    newvalue_out[...] = value.astype(BF16).astype(F32)

    positions = [lengths_s[0, low + slot] for slot in send_slots]
    for at, slot in enumerate(send_slots):
        put_row(
            leaving, at, positions[at],
            newkey_out[pl.ds(slot, 1), :], newvalue_out[pl.ds(slot, 1), :],
        )
    cap = leaving.shape[2]
    copies = [
        pltpu.make_async_copy(
            leaving.at[pl.ds(0, MOVE)], box.at[:, :, pl.ds(0, cap), :], box_sem.at[0]
        )
    ]
    copies[0].start()
    rows = [query_out[pl.ds(pl.multiple_of(slot * GROUP, GROUP), GROUP), :] for slot in send_slots]
    attended = attend(leaving, list(range(moving)), positions, rows)
    column = pl.multiple_of(me_tp * shard, shard)
    for at, slot in enumerate(send_slots):
        m = at % MOVE
        residual = hidden32[pl.ds(slot, 1), pl.ds(column, shard)]
        if at < MOVE:
            blocks = [attended[at][g : g + 1, :] for g in range(heads)]
            blocks += [residual[:, b * HD : (b + 1) * HD] for b in range(shard // HD)]
            blocks += [jnp.zeros((1, HD), F32)] * (NOTE - len(blocks))
            box[m, 0, cap : cap + NOTE, :] = jnp.concatenate(blocks, axis=0).astype(BF16)
        else:
            note = notes[at // MOVE]
            for g in range(heads):
                note[m : m + 1, g * HD : (g + 1) * HD] = attended[at][g : g + 1, :]
            note[m : m + 1, heads * HD :] = residual
    for copy in copies + loads:
        copy.wait()


def attend_slots(cache, places, positions, query, attended_rows, heads):
    slots = len(places)
    for first in range(0, slots, BATCH):
        span = range(first, first + BATCH)
        got = attend(
            cache,
            [places[s] for s in span],
            [positions[s] for s in span],
            [query[s * GROUP : (s + 1) * GROUP, :] for s in span],
        )
        for s, rows in zip(span, got):
            attended_rows[s * GROUP : (s + 1) * GROUP, :] = rows
    return jnp.concatenate(
        [attended_rows[pl.ds(g, slots, stride=GROUP), :] for g in range(heads)], axis=1
    )


def attend_kernel(
    slots, heads, meta, lengths_s, query, newkey, newvalue, _, out, cache, attended_rows,
):
    low = meta[0] * slots
    positions = [lengths_s[low + s] for s in range(slots)]
    for s, p in enumerate(positions):
        put_row(cache, s, p, newkey[s : s + 1, :], newvalue[s : s + 1, :])
    out[...] = attend_slots(
        cache, list(range(slots)), positions, query, attended_rows, heads
    ).astype(BF16)


def project_out(attended, wo, residual, own, sends, me_tp, peers_tp):
    shard = own.shape[1]
    for k in list(range(peers_tp - 1, 0, -1)) + [0]:
        column = pl.multiple_of(jnp.bitwise_xor(me_tp, k) * shard, shard)
        part = jnp.dot(attended, wo[:, pl.ds(column, shard)], preferred_element_type=F32)
        if k == 0:
            own[...] = residual + part
        else:
            sends[k - 1][...] = part.astype(BF16)


def out_kernel(
    peers, peers_tp, meta, plan, attended, wo, hidden, box, *rest,
):
    notes, rest = rest[: peers - 2], rest[peers - 2 :]
    own, sends = rest[0], rest[1:peers_tp]
    shard = own.shape[1]
    cap = box.shape[2] - NOTE
    rows = attended[...].astype(F32)
    heads = rows.shape[1] // HD
    column = pl.multiple_of(meta[1] * shard, shard)
    residual = hidden[:, pl.ds(column, shard)].astype(F32)
    row_index = lax.broadcasted_iota(I32, rows.shape, 0)
    residual_index = lax.broadcasted_iota(I32, residual.shape, 0)
    for at in range((peers - 1) * MOVE):
        m = at % MOVE
        if at < MOVE:
            blocks = box[m, 0, cap : cap + NOTE, :].astype(F32)
            blocks = [blocks[b : b + 1, :] for b in range(heads + shard // HD)]
            note = jnp.concatenate(blocks, axis=1)
        else:
            note = notes[at // MOVE - 1][m : m + 1, :]
        rows = jnp.where(row_index == plan[at], note[:, : heads * HD], rows)
        residual = jnp.where(residual_index == plan[at], note[:, heads * HD :], residual)
    project_out(rows.astype(BF16), wo, residual, own, sends, meta[1], peers_tp)


def pack_kernel(plan, cache, _own, *rest):
    boxes, out_sem = rest[:-1], rest[-1]
    moving = plan.shape[0] // 2
    packs = [
        pltpu.make_async_copy(
            cache.at[plan[moving + at]], boxes[at // MOVE - 1].at[at % MOVE], out_sem.at[at - MOVE]
        )
        for at in range(MOVE, moving)
    ]
    for pack in packs:
        pack.start()
    for pack in packs:
        pack.wait()


def sum_kernel(own, *rest):
    total = own[...]
    for part in rest[:-1]:
        total = total + part[...].astype(F32)
    rest[-1][...] = total.astype(BF16)


def map_places(slots, peers, plan, place):
    for s in range(slots):
        place[s] = s
    for at in range((peers - 1) * MOVE):
        taker = plan[at]

        @pl.when(taker >= 0)
        def _():
            place[taker] = slots + at


def prepare_kernel(
    peers, slots, meta, source_s, lengths_s, plan, cos_ref, sin_ref, wkv, _,
    weight, cos_rows, sin_rows, place,
):
    map_places(slots, peers, plan, place)
    low = meta[0] * slots
    gather_angles(
        lambda s: lengths_s[source_s[low + s]] + 1, slots, cos_ref, sin_ref, cos_rows, sin_rows
    )
    row = lax.broadcasted_iota(I32, (2 * HD, 2 * HD), 0)
    col = lax.broadcasted_iota(I32, (2 * HD, 2 * HD), 1)
    goal = jnp.where(row < HD, 2 * row, 2 * (row - HD) + 1)
    places = jnp.where(col == goal, 1.0, 0.0).astype(BF16)
    for b in range(weight.shape[0] // HD):
        apart = jnp.dot(
            places, wkv[b * 2 * HD : (b + 1) * 2 * HD, :], preferred_element_type=F32
        ).astype(BF16)
        weight[b * HD : (b + 1) * HD, :HD] = apart[:HD]
        weight[b * HD : (b + 1) * HD, HD:] = apart[HD:]


def second_kernel(
    peers, peers_tp, slots, heads,
    meta, source_s, lengths_s, place, gain, cos_rows, sin_rows, wq, wkv, wo, _, *rest,
):
    blocks, rest = rest[:peers_tp], rest[peers_tp:]
    box_hbm, rest = rest[: peers - 1], rest[peers - 1 :]
    own, sends, cache = rest[0], rest[1:peers_tp], rest[peers_tp]
    normed3, query_rows, attended_rows, in_sem = rest[peers_tp + 1 :]
    me, me_tp = meta[0], meta[1]
    low = me * slots
    width = gain.shape[1]
    shard = own.shape[1]
    loads = [
        pltpu.make_async_copy(
            box.at[:, :, pl.ds(0, cache.shape[2]), :],
            cache.at[pl.ds(slots + k * MOVE, MOVE)],
            in_sem.at[k],
        )
        for k, box in enumerate(box_hbm)
    ]
    for copy in loads:
        copy.start()

    firsts = [jnp.bitwise_xor(me_tp, k) for k in range(peers_tp)]
    norm_into(
        normed3,
        [block[...].astype(F32) for block in blocks],
        [gain[:, pl.ds(pl.multiple_of(first * shard, shard), shard)] for first in firsts],
        [first * (shard // HD) for first in firsts],
        width,
    )
    positions = [lengths_s[source_s[low + s]] + 1 for s in range(slots)]
    for copy in loads:
        copy.wait()
    query = project_from(normed3, wq)
    pair = project_from(normed3, wkv)
    key, value = pair[:, :HD], pair[:, HD:]
    cosine, sine = cos_rows[...], sin_rows[...]
    query_rows[...] = jnp.zeros(query_rows.shape, F32)
    for g in range(heads):
        turned = turn(query[:, g * HD : (g + 1) * HD], cosine, sine)
        query_rows[pl.ds(g, slots, stride=GROUP), :] = turned.astype(BF16).astype(F32)
    newkey = turn(key, cosine, sine).astype(BF16).astype(F32)
    newvalue = value.astype(BF16).astype(F32)

    places = [place[s] for s in range(slots)]
    for s, (at, p) in enumerate(zip(places, positions)):
        put_row(cache, at, p, newkey[s : s + 1, :], newvalue[s : s + 1, :])
    attended = attend_slots(cache, places, positions, query_rows, attended_rows, heads)
    project_out(
        attended.astype(BF16), wo, blocks[0][...].astype(F32), own, sends, me_tp, peers_tp
    )


def cache_kernel(slots, place, cache, out_hbm, out_sem):
    copies = [
        pltpu.make_async_copy(cache.at[place[s]], out_hbm.at[s], out_sem.at[s])
        for s in range(slots)
    ]
    for copy in copies:
        copy.start()
    for copy in copies:
        copy.wait()


def join_kernel(peers_tp, meta, *rest):
    blocks, out, sem = rest[:-2], rest[-2], rest[-1]
    shard = blocks[0].shape[1]
    copies = []
    for k, block in enumerate(blocks):
        column = pl.multiple_of(jnp.bitwise_xor(meta[1], k) * shard, shard)
        copies.append(pltpu.make_async_copy(block, out.at[:, pl.ds(column, shard)], sem.at[k]))
        copies[-1].start()
    for copy in copies:
        copy.wait()


def swapped(x, axis, size, k):
    return lax.ppermute(x, axis, [(i, i ^ k) for i in range(size)])


def local(
    tables, kv_cache, hidden, lengths, source, norm_gain, query_weight, keyval_weight, out_weight
):
    peers, peers_tp = lax.axis_size("inst"), lax.axis_size("tp")
    slots, cap = kv_cache.shape[0], kv_cache.shape[2]
    width = hidden.shape[1]
    heads = query_weight.shape[1] // HD
    shard = width // peers_tp
    others, moving = peers - 1, (peers - 1) * MOVE
    blocks = width // HD
    meta = jnp.stack([lax.axis_index("inst"), lax.axis_index("tp")]).astype(I32)
    gain = norm_gain.reshape(1, width)
    wkv = keyval_weight.reshape(2 * width, HD)
    cosine, sine = (jnp.asarray(table) for table in tables)
    row32 = jax.ShapeDtypeStruct((slots, HD), F32)
    note_width = heads * HD + shard
    dma = pltpu.SemaphoreType.DMA
    weights = [
        pltpu.VMEM(query_weight.shape, BF16),
        pltpu.VMEM(wkv.shape, BF16),
    ]
    stages = [
        pltpu.VMEM((blocks, slots, HD), BF16),
        pltpu.VMEM((blocks, 2 * slots, 2 * HD), BF16),
        pltpu.VMEM((slots, HD), F32),
        pltpu.VMEM((slots, HD), F32),
    ]
    flops = 2 * slots * width * (heads + 2) * HD
    cache_bytes = kv_cache.size * 2
    held = jax.ShapeDtypeStruct((slots + moving,) + kv_cache.shape[1:], BF16)

    query, newkey1, newvalue1, plan, cache, *notes = pl.pallas_call(
        functools.partial(first_kernel, peers, slots, heads, shard),
        out_shape=[
            jax.ShapeDtypeStruct((slots * GROUP, HD), F32),
            row32,
            row32,
            jax.ShapeDtypeStruct((2 * moving,), I32),
            held,
        ]
        + [jax.ShapeDtypeStruct((MOVE, 2, cap + NOTE, HD), BF16)]
        + [jax.ShapeDtypeStruct((MOVE, note_width), F32)] * (others - 1),
        in_specs=[SMEM] + [HBM] * 9,
        out_specs=[VMEM] * 3 + [SMEM] + [VMEM] * (others + 1),
        scratch_shapes=weights
        + stages
        + [
            pltpu.VMEM((moving,) + kv_cache.shape[1:], BF16),
            pltpu.VMEM((slots, width), F32),
            pltpu.SMEM((1, source.shape[0]), I32),
            pltpu.VMEM((1, source.shape[0]), I32),
            pltpu.VMEM(hidden.shape, BF16),
            pltpu.VMEM((1, width), F32),
            pltpu.VMEM(cosine.shape, F32),
            pltpu.VMEM(cosine.shape, F32),
            dma((6,)),
            dma((4,)),
            dma((4,)),
            dma((moving,)),
            dma((1,)),
            dma((slots // CHUNK,)),
        ],
        compiler_params=params(24),
        cost_estimate=cost(flops, (query_weight.size + wkv.size) * 2),
        name="first_step",
    )(meta, *(
        pltpu.with_memory_space_constraint(x, pltpu.HBM)
        for x in (source.reshape(1, -1), lengths.reshape(1, -1), hidden, gain, cosine, sine,
                  query_weight, wkv, kv_cache)
    ))
    got_notes = [swapped(note, "inst", peers, k + 1) for k, note in enumerate(notes)]

    attended, cache = pl.pallas_call(
        functools.partial(attend_kernel, slots, heads),
        out_shape=[jax.ShapeDtypeStruct((slots, heads * HD), BF16), held],
        in_specs=[SMEM] * 2 + [VMEM] * 4,
        out_specs=[VMEM] * 2,
        scratch_shapes=[pltpu.VMEM((slots * GROUP, HD), F32)],
        input_output_aliases={5: 1},
        compiler_params=params(12),
        cost_estimate=cost(4 * slots * cap * HD * heads, cache_bytes),
        name="attention",
    )(meta, lengths, query, newkey1, newvalue1, cache)

    sent = [jax.ShapeDtypeStruct((slots, shard), F32)]
    sent += [jax.ShapeDtypeStruct((slots, shard), BF16)] * (peers_tp - 1)
    own, *sends = pl.pallas_call(
        functools.partial(out_kernel, peers, peers_tp),
        out_shape=sent,
        in_specs=[SMEM] * 2 + [VMEM] * (3 + others),
        out_specs=[VMEM] * peers_tp,
        compiler_params=params(16),
        cost_estimate=cost(2 * slots * width * heads * HD, out_weight.size * 2),
        name="out_projection",
    )(meta, plan, attended, out_weight, hidden, *got_notes)
    boxes = pl.pallas_call(
        pack_kernel,
        out_shape=[jax.ShapeDtypeStruct((MOVE,) + kv_cache.shape[1:], BF16)] * (others - 1),
        in_specs=[SMEM, VMEM, ANY],
        out_specs=[ANY] * (others - 1),
        scratch_shapes=[dma((moving - MOVE,))],
        compiler_params=params(16),
        cost_estimate=cost(1, 1 * cache_bytes),
        name="pack",
    )(plan, cache, own)
    got_boxes = got_notes[:1] + [swapped(box, "inst", peers, k + 2) for k, box in enumerate(boxes)]

    def summed(own, sends, passed_on):
        got = [swapped(sends[k - 1], "tp", peers_tp, k) for k in range(peers_tp - 1, 0, -1)]
        shard_rows = pl.pallas_call(
            sum_kernel,
            out_shape=jax.ShapeDtypeStruct((slots, shard), BF16),
            in_specs=[VMEM] * peers_tp,
            out_specs=VMEM,
            compiler_params=params(16),
            name="sum_terms",
        )(own, *got)
        blocks = {0: shard_rows}
        if not passed_on:
            blocks |= {k: swapped(shard_rows, "tp", peers_tp, k) for k in range(1, peers_tp)}
        far = peers_tp // 2 if passed_on else 0
        while far:
            blocks |= {k + far: swapped(blocks[k], "tp", peers_tp, far) for k in blocks}
            far //= 2
        return [blocks[k] for k in range(peers_tp)]

    pieces = summed(own, sends, False)

    weight, cos_rows, sin_rows, place = pl.pallas_call(
        functools.partial(prepare_kernel, peers, slots),
        out_shape=[
            jax.ShapeDtypeStruct((width, 2 * HD), BF16),
            row32,
            row32,
            jax.ShapeDtypeStruct((slots,), I32),
        ],
        in_specs=[SMEM] * 4 + [VMEM] * 3 + [ANY],
        out_specs=[VMEM] * 3 + [SMEM],
        compiler_params=params(16),
        cost_estimate=cost(100*flops, wkv.size * 40),
        name="prepare",
    )(meta, source, lengths, plan, cosine, sine, wkv, own)

    own, *sends, cache = pl.pallas_call(
        functools.partial(second_kernel, peers, peers_tp, slots, heads),
        out_shape=sent + [held],
        in_specs=[SMEM] * 4 + [VMEM] * (7 + peers_tp) + [ANY] * others,
        out_specs=[VMEM] * (1 + peers_tp),
        scratch_shapes=[
            pltpu.VMEM((blocks, slots, HD), BF16),
            pltpu.VMEM((slots * GROUP, HD), F32),
            pltpu.VMEM((slots * GROUP, HD), F32),
            dma((others,)),
        ],
        input_output_aliases={10: peers_tp},
        compiler_params=params(16),
        cost_estimate=cost(3 * flops, cache_bytes + (query_weight.size + wkv.size) * 4),
        name="second_step",
    )(meta, source, lengths, place, gain, cos_rows, sin_rows, query_weight, weight, out_weight, cache,
      *pieces, *got_boxes)

    pieces = summed(own, sends, False)
    final_cache = pl.pallas_call(
        functools.partial(cache_kernel, slots),
        out_shape=jax.ShapeDtypeStruct(kv_cache.shape, BF16),
        in_specs=[SMEM, VMEM],
        out_specs=ANY,
        scratch_shapes=[dma((slots,))],
        compiler_params=params(16),
        cost_estimate=cost(0, 2 * cache_bytes),
        name="write_cache",
    )(place, cache)
    final_hidden = pl.pallas_call(
        functools.partial(join_kernel, peers_tp),
        out_shape=jax.ShapeDtypeStruct(hidden.shape, BF16),
        in_specs=[SMEM] + [ANY] * peers_tp,
        out_specs=ANY,
        scratch_shapes=[dma((peers_tp,))],
        compiler_params=params(16),
        name="join",
    )(meta, *pieces)
    return (final_hidden, final_cache)


def solution(mesh):
    def whole(kv_cache, *rest):
        tables = angle_tables(kv_cache.shape[2])
        return jax.shard_map(
            functools.partial(local, tables),
            mesh=mesh,
            in_specs=(
                P(("groups", "inst"), None, None, "tp"),
                P(("groups", "inst"), None),
                P("groups"),
                P("groups"),
                P(),
                P(None, "tp"),
                P(None, None, "tp"),
                P("tp", None),
            ),
            out_specs=(P(("groups", "inst"), None), P(("groups", "inst"), None, None, "tp")),
            check_vma=False,
        )(kv_cache, *rest)

    return whole
```

```python
import functools

import jax
import jax.numpy as jnp
import numpy as np
from jax import lax
from jax.experimental import pallas as pl
from jax.experimental.pallas import tpu as pltpu
from jax.sharding import PartitionSpec as P

MOVE = 2
EPS = 1e-05
THETA = 500000.0
HD = 128
GROUP = 8
PIECE = 16
CHUNK = 8
BATCH = 16
NOTE = 16

F32 = jnp.float32
BF16 = jnp.bfloat16
I32 = jnp.int32

ANY = pl.BlockSpec(memory_space=pl.ANY)
VMEM = pl.BlockSpec(memory_space=pltpu.VMEM)
SMEM = pl.BlockSpec(memory_space=pltpu.SMEM)
HBM = pl.BlockSpec(memory_space=pltpu.HBM)


def params(mib):
    return pltpu.CompilerParams(vmem_limit_bytes=mib * 1024 * 1024)


def cost(flops, nbytes):
    return pl.CostEstimate(flops=flops, bytes_accessed=nbytes, transcendentals=0)


def angle_tables(positions):
    frequency = THETA ** (-(np.arange(HD // 2, dtype=np.float64) * 2.0) / HD)
    angles = np.arange(positions, dtype=np.float64)[:, None] * frequency[None, :]
    cosine = np.concatenate([np.cos(angles), np.cos(angles)], axis=-1)
    sine = np.concatenate([-np.sin(angles), np.sin(angles)], axis=-1)
    return cosine.astype(np.float32), sine.astype(np.float32)


def turn(x, cosine, sine):
    return x * cosine + pltpu.roll(x, HD // 2, 1) * sine


def gather_angles(position_of, slots, cos_ref, sin_ref, cos_rows, sin_rows):
    for s in range(slots):
        p = position_of(s)
        cos_rows[s : s + 1, :] = cos_ref[pl.ds(p, 1), :]
        sin_rows[s : s + 1, :] = sin_ref[pl.ds(p, 1), :]


def spread_normed(normed3, spread, slots, width):
    blocks = width // HD
    row = lax.broadcasted_iota(I32, (HD, 4 * HD), 0)
    col = lax.broadcasted_iota(I32, (HD, 4 * HD), 1)
    goal = jnp.where(col < 2 * HD, 2 * row, 2 * row + 1 + 2 * HD)
    places = jnp.where(col == goal, 1.0, 0.0).astype(BF16)
    spread_all = jnp.dot(
        normed3[...].reshape(blocks * slots, HD), places, preferred_element_type=F32
    ).astype(BF16)
    spread[:, 0:slots, :] = spread_all[:, : 2 * HD].reshape(blocks, slots, 2 * HD)
    spread[:, slots:, :] = spread_all[:, 2 * HD :].reshape(blocks, slots, 2 * HD)


def project_from(normed3, weight):
    total = None
    for b in range(normed3.shape[0] // 2):
        block = jnp.concatenate([normed3[2 * b], normed3[2 * b + 1]], axis=1)
        part = jnp.dot(
            block, weight[b * 2 * HD : (b + 1) * 2 * HD, :], preferred_element_type=F32
        )
        total = part if total is None else total + part
    return total


def project_spread(spread, wkv):
    total = None
    for b in range(spread.shape[0]):
        part = jnp.dot(
            spread[b], wkv[b * 2 * HD : (b + 1) * 2 * HD, :], preferred_element_type=F32
        )
        total = part if total is None else total + part
    slots = spread.shape[1] // 2
    return total[:slots], total[slots:]


def weight_copies(src, dst, sem, pieces):
    depth = src.shape[0] // pieces
    copies = [
        pltpu.make_async_copy(
            src.at[pl.ds(c * depth, depth)], dst.at[pl.ds(c * depth, depth)], sem.at[c]
        )
        for c in range(pieces)
    ]
    return copies


def put_row(cache, place, p, key_row, value_row):
    base = pl.multiple_of((jnp.maximum(p, 0) // PIECE) * PIECE, PIECE)
    hit = lax.broadcasted_iota(I32, (PIECE, HD), 0) + base == p
    for which, new in ((0, key_row), (1, value_row)):
        old = cache[place, which, pl.ds(base, PIECE), :]
        new = jnp.broadcast_to(new, old.shape).astype(BF16)
        cache[place, which, pl.ds(base, PIECE), :] = jnp.where(hit, new, old)


def attend(cache, places, positions, query_rows):
    cap = cache.shape[2]
    col = lax.broadcasted_iota(I32, (GROUP, cap), 1)
    scores = [
        lax.dot_general(
            rows.astype(BF16),
            cache[place, 0],
            (((1,), (1,)), ((), ())),
            preferred_element_type=F32,
        )
        for place, rows in zip(places, query_rows)
    ]
    probs = []
    for score, p in zip(scores, positions):
        score = jnp.where(col <= p, score * HD**-0.5, -jnp.inf)
        weight = jnp.exp(score - jnp.max(score, axis=-1, keepdims=True))
        weight = weight / jnp.sum(weight, axis=-1, keepdims=True)
        probs.append(weight.astype(BF16))
    return [
        jnp.dot(prob, cache[place, 1], preferred_element_type=F32)
        for place, prob in zip(places, probs)
    ]


def norm_into(normed3, pieces, gains, firsts, total_width):
    square = None
    for piece in pieces:
        part = jnp.sum(piece * piece, axis=-1, keepdims=True)
        square = part if square is None else square + part
    factor = lax.rsqrt(square / total_width + EPS)
    for piece, gain, first in zip(pieces, gains, firsts):
        normed = (piece * factor * gain).astype(BF16)
        for i in range(piece.shape[1] // HD):
            normed3[first + i] = normed[:, i * HD : (i + 1) * HD]


def plan_moves(me, peers, slots, source):
    moving = (peers - 1) * MOVE
    shape = (2 * moving, source.shape[1])
    row = lax.broadcasted_iota(I32, shape, 0)
    index = lax.broadcasted_iota(I32, shape, 1)
    leaves = row < moving
    at = jnp.where(leaves, row, row - moving)
    other = jnp.bitwise_xor(me, at // MOVE + 1)
    here, there = me * slots, other * slots
    src = jnp.broadcast_to(source, shape)
    came, went = jnp.where(leaves, here, there), jnp.where(leaves, there, here)
    moved = (src >= came) & (src < came + slots) & (index >= went) & (index < went + slots)
    sign = jnp.where(at % MOVE == 0, -1.0, 1.0)
    index_f = index.astype(F32)
    best = jnp.max(jnp.where(moved, sign * index_f, -1e6), axis=1, keepdims=True)
    hit = moved & (sign * index_f == best)
    result = jnp.where(leaves, src, index) - here
    found = jnp.sum(jnp.where(hit, result.astype(F32), 0.0), axis=1, keepdims=True)
    none = jnp.where(leaves[:, :1], 0.0, -1.0)
    return jnp.where(best > -1e6, found, none).astype(I32)


def first_kernel(
    peers, slots, heads, shard,
    meta, source_hbm, lengths_hbm, hidden_hbm, gain_hbm, cos_hbm, sin_hbm, wq_hbm, wkv_hbm,
    cache_hbm, query_out, newkey_out, newvalue_out, plan, *rest,
):
    others = peers - 1
    moving = others * MOVE
    cache, box, notes = rest[0], rest[1], (None,) + rest[2 : others + 1]
    (wq, wkv, normed3, spread, cos_rows, sin_rows, leaving, hidden32, lengths_s, source_v,
     hidden, gain, cos_ref, sin_ref, small_sem, wq_sem, wkv_sem, in_sem,
     box_sem, cache_sem) = rest[others + 1 :]
    width = hidden.shape[1]
    me, me_tp = meta[0], meta[1]
    wq_copies = weight_copies(wq_hbm, wq, wq_sem, 4)
    wkv_copies = weight_copies(wkv_hbm, wkv, wkv_sem, 4)
    small = [
        pltpu.make_async_copy(src, dst, small_sem.at[i])
        for i, (src, dst) in enumerate((
            (source_hbm, source_v), (hidden_hbm, hidden), (gain_hbm, gain), (lengths_hbm, lengths_s),
            (cos_hbm, cos_ref), (sin_hbm, sin_ref),
        ))
    ]
    for copy in small[:3] + wkv_copies + wq_copies + small[3:]:
        copy.start()
    loads = [
        pltpu.make_async_copy(
            cache_hbm.at[pl.ds(c * CHUNK, CHUNK)], cache.at[pl.ds(c * CHUNK, CHUNK)], cache_sem.at[c]
        )
        for c in range(slots // CHUNK)
    ]
    for copy in small[:3]:
        copy.wait()
    low = me * slots
    moves = plan_moves(me, peers, slots, source_v[...])
    wide = hidden[...].astype(F32)
    hidden32[...] = wide
    norm_into(normed3, [wide], [gain[...]], [0], width)
    spread_normed(normed3, spread, slots, width)
    send_slots = [moves[at, 0] for at in range(moving)]
    fetches = [
        pltpu.make_async_copy(cache_hbm.at[slot], leaving.at[at], in_sem.at[at])
        for at, slot in enumerate(send_slots)
    ]
    for copy in fetches:
        copy.start()
    for at, slot in enumerate(send_slots):
        plan[moving + at] = slot
        plan[at] = moves[moving + at, 0]
    for copy in loads:
        copy.start()
    for copy in small[3:] + wkv_copies + wq_copies + fetches:
        copy.wait()
    gather_angles(lambda s: lengths_s[0, low + s], slots, cos_ref, sin_ref, cos_rows, sin_rows)
    key, value = project_spread(spread, wkv)
    cosine, sine = cos_rows[...], sin_rows[...]
    newkey_out[...] = turn(key, cosine, sine).astype(BF16).astype(F32)
    newvalue_out[...] = value.astype(BF16).astype(F32)
    positions = [lengths_s[0, low + slot] for slot in send_slots]
    for at, slot in enumerate(send_slots):
        put_row(
            leaving, at, positions[at],
            newkey_out[pl.ds(slot, 1), :], newvalue_out[pl.ds(slot, 1), :],
        )
    query = project_from(normed3, wq)
    query_out[...] = jnp.zeros(query_out.shape, F32)
    for g in range(heads):
        turned = turn(query[:, g * HD : (g + 1) * HD], cosine, sine)
        query_out[pl.ds(g, slots, stride=GROUP), :] = turned.astype(BF16).astype(F32)
    cap = leaving.shape[2]
    copies = [
        pltpu.make_async_copy(
            leaving.at[pl.ds(0, MOVE)], box.at[:, :, pl.ds(0, cap), :], box_sem.at[0]
        )
    ]
    copies[0].start()
    rows = [query_out[pl.ds(pl.multiple_of(slot * GROUP, GROUP), GROUP), :] for slot in send_slots]
    attended = attend(leaving, list(range(moving)), positions, rows)
    column = pl.multiple_of(me_tp * shard, shard)
    for at, slot in enumerate(send_slots):
        m = at % MOVE
        residual = hidden32[pl.ds(slot, 1), pl.ds(column, shard)]
        if at < MOVE:
            blocks = [attended[at][g : g + 1, :] for g in range(heads)]
            blocks += [residual[:, b * HD : (b + 1) * HD] for b in range(shard // HD)]
            blocks += [jnp.zeros((1, HD), F32)] * (NOTE - len(blocks))
            box[m, 0, cap : cap + NOTE, :] = jnp.concatenate(blocks, axis=0).astype(BF16)
        else:
            note = notes[at // MOVE]
            for g in range(heads):
                note[m : m + 1, g * HD : (g + 1) * HD] = attended[at][g : g + 1, :]
            note[m : m + 1, heads * HD :] = residual
    for copy in copies + loads:
        copy.wait()


def attend_slots(cache, places, positions, query, attended_rows, heads):
    slots = len(places)
    for first in range(0, slots, BATCH):
        span = range(first, first + BATCH)
        got = attend(
            cache,
            [places[s] for s in span],
            [positions[s] for s in span],
            [query[s * GROUP : (s + 1) * GROUP, :] for s in span],
        )
        for s, rows in zip(span, got):
            attended_rows[s * GROUP : (s + 1) * GROUP, :] = rows
    return jnp.concatenate(
        [attended_rows[pl.ds(g, slots, stride=GROUP), :] for g in range(heads)], axis=1
    )


def attend_kernel(
    slots, heads, meta, lengths_s, query, newkey, newvalue, _, out, cache, attended_rows,
):
    low = meta[0] * slots
    positions = [lengths_s[low + s] for s in range(slots)]
    for s, p in enumerate(positions):
        put_row(cache, s, p, newkey[s : s + 1, :], newvalue[s : s + 1, :])
    out[...] = attend_slots(
        cache, list(range(slots)), positions, query, attended_rows, heads
    ).astype(BF16)


def project_out(attended, wo, residual, own, sends, me_tp, peers_tp):
    shard = own.shape[1]
    for k in list(range(peers_tp - 1, 0, -1)) + [0]:
        column = pl.multiple_of(jnp.bitwise_xor(me_tp, k) * shard, shard)
        part = jnp.dot(attended, wo[:, pl.ds(column, shard)], preferred_element_type=F32)
        if k == 0:
            own[...] = residual + part
        else:
            sends[k - 1][...] = part.astype(BF16)


def out_kernel(
    peers, peers_tp, meta, plan, attended, wo, hidden, box, *rest,
):
    notes, rest = rest[: peers - 2], rest[peers - 2 :]
    own, sends = rest[0], rest[1:peers_tp]
    shard = own.shape[1]
    cap = box.shape[2] - NOTE
    rows = attended[...].astype(F32)
    heads = rows.shape[1] // HD
    column = pl.multiple_of(meta[1] * shard, shard)
    residual = hidden[:, pl.ds(column, shard)].astype(F32)
    row_index = lax.broadcasted_iota(I32, rows.shape, 0)
    residual_index = lax.broadcasted_iota(I32, residual.shape, 0)
    for at in range((peers - 1) * MOVE):
        m = at % MOVE
        if at < MOVE:
            blocks = box[m, 0, cap : cap + NOTE, :].astype(F32)
            blocks = [blocks[b : b + 1, :] for b in range(heads + shard // HD)]
            note = jnp.concatenate(blocks, axis=1)
        else:
            note = notes[at // MOVE - 1][m : m + 1, :]
        rows = jnp.where(row_index == plan[at], note[:, : heads * HD], rows)
        residual = jnp.where(residual_index == plan[at], note[:, heads * HD :], residual)
    project_out(rows.astype(BF16), wo, residual, own, sends, meta[1], peers_tp)


def pack_kernel(plan, cache, _own, *rest):
    boxes, out_sem = rest[:-1], rest[-1]
    moving = plan.shape[0] // 2
    packs = [
        pltpu.make_async_copy(
            cache.at[plan[moving + at]], boxes[at // MOVE - 1].at[at % MOVE], out_sem.at[at - MOVE]
        )
        for at in range(MOVE, moving)
    ]
    for pack in packs:
        pack.start()
    for pack in packs:
        pack.wait()


def sum_kernel(own, *rest):
    total = own[...]
    for part in rest[:-1]:
        total = total + part[...].astype(F32)
    rest[-1][...] = total.astype(BF16)


def map_places(slots, peers, plan, place):
    for s in range(slots):
        place[s] = s
    for at in range((peers - 1) * MOVE):
        taker = plan[at]

        @pl.when(taker >= 0)
        def _():
            place[taker] = slots + at


def prepare_kernel(
    peers, slots, meta, source_s, lengths_s, plan, cos_ref, sin_ref, wkv, _,
    weight, cos_rows, sin_rows, place,
):
    map_places(slots, peers, plan, place)
    low = meta[0] * slots
    gather_angles(
        lambda s: lengths_s[source_s[low + s]] + 1, slots, cos_ref, sin_ref, cos_rows, sin_rows
    )
    row = lax.broadcasted_iota(I32, (2 * HD, 2 * HD), 0)
    col = lax.broadcasted_iota(I32, (2 * HD, 2 * HD), 1)
    goal = jnp.where(row < HD, 2 * row, 2 * (row - HD) + 1)
    places = jnp.where(col == goal, 1.0, 0.0).astype(BF16)
    for b in range(weight.shape[0] // HD):
        apart = jnp.dot(
            places, wkv[b * 2 * HD : (b + 1) * 2 * HD, :], preferred_element_type=F32
        ).astype(BF16)
        weight[b * HD : (b + 1) * HD, :HD] = apart[:HD]
        weight[b * HD : (b + 1) * HD, HD:] = apart[HD:]


def second_kernel(
    peers, peers_tp, slots, heads,
    meta, source_s, lengths_s, place, gain, cos_rows, sin_rows, wq, wkv, wo, _, *rest,
):
    blocks, rest = rest[:peers_tp], rest[peers_tp:]
    box_hbm, rest = rest[: peers - 1], rest[peers - 1 :]
    own, sends, cache = rest[0], rest[1:peers_tp], rest[peers_tp]
    normed3, query_rows, attended_rows, in_sem = rest[peers_tp + 1 :]
    me, me_tp = meta[0], meta[1]
    low = me * slots
    width = gain.shape[1]
    shard = own.shape[1]
    loads = [
        pltpu.make_async_copy(
            box.at[:, :, pl.ds(0, cache.shape[2]), :],
            cache.at[pl.ds(slots + k * MOVE, MOVE)],
            in_sem.at[k],
        )
        for k, box in enumerate(box_hbm)
    ]
    for copy in loads:
        copy.start()

    firsts = [jnp.bitwise_xor(me_tp, k) for k in range(peers_tp)]
    norm_into(
        normed3,
        [block[...].astype(F32) for block in blocks],
        [gain[:, pl.ds(pl.multiple_of(first * shard, shard), shard)] for first in firsts],
        [first * (shard // HD) for first in firsts],
        width,
    )
    positions = [lengths_s[source_s[low + s]] + 1 for s in range(slots)]
    for copy in loads:
        copy.wait()
    pair = project_from(normed3, wkv)
    cosine, sine = cos_rows[...], sin_rows[...]
    newkey = turn(pair[:, :HD], cosine, sine).astype(BF16).astype(F32)
    newvalue = pair[:, HD:].astype(BF16).astype(F32)
    places = [place[s] for s in range(slots)]
    for s, (at, p) in enumerate(zip(places, positions)):
        put_row(cache, at, p, newkey[s : s + 1, :], newvalue[s : s + 1, :])
    query = project_from(normed3, wq)
    query_rows[...] = jnp.zeros(query_rows.shape, F32)
    for g in range(heads):
        turned = turn(query[:, g * HD : (g + 1) * HD], cosine, sine)
        query_rows[pl.ds(g, slots, stride=GROUP), :] = turned.astype(BF16).astype(F32)
    attended = attend_slots(cache, places, positions, query_rows, attended_rows, heads)
    project_out(
        attended.astype(BF16), wo, blocks[0][...].astype(F32), own, sends, me_tp, peers_tp
    )


def cache_kernel(slots, place, cache, out_hbm, out_sem):
    copies = [
        pltpu.make_async_copy(cache.at[place[s]], out_hbm.at[s], out_sem.at[s])
        for s in range(slots)
    ]
    for copy in copies:
        copy.start()
    for copy in copies:
        copy.wait()


def join_kernel(peers_tp, meta, *rest):
    blocks, out, sem = rest[:-2], rest[-2], rest[-1]
    shard = blocks[0].shape[1]
    copies = []
    for k, block in enumerate(blocks):
        column = pl.multiple_of(jnp.bitwise_xor(meta[1], k) * shard, shard)
        copies.append(pltpu.make_async_copy(block, out.at[:, pl.ds(column, shard)], sem.at[k]))
        copies[-1].start()
    for copy in copies:
        copy.wait()


def swapped(x, axis, size, k):
    return lax.ppermute(x, axis, [(i, i ^ k) for i in range(size)])


def local(
    tables, kv_cache, hidden, lengths, source, norm_gain, query_weight, keyval_weight, out_weight
):
    peers, peers_tp = lax.axis_size("inst"), lax.axis_size("tp")
    slots, cap = kv_cache.shape[0], kv_cache.shape[2]
    width = hidden.shape[1]
    heads = query_weight.shape[1] // HD
    shard = width // peers_tp
    others, moving = peers - 1, (peers - 1) * MOVE
    blocks = width // HD
    meta = jnp.stack([lax.axis_index("inst"), lax.axis_index("tp")]).astype(I32)
    gain = norm_gain.reshape(1, width)
    wkv = keyval_weight.reshape(2 * width, HD)
    cosine, sine = (jnp.asarray(table) for table in tables)
    row32 = jax.ShapeDtypeStruct((slots, HD), F32)
    note_width = heads * HD + shard
    dma = pltpu.SemaphoreType.DMA
    weights = [
        pltpu.VMEM(query_weight.shape, BF16),
        pltpu.VMEM(wkv.shape, BF16),
    ]
    stages = [
        pltpu.VMEM((blocks, slots, HD), BF16),
        pltpu.VMEM((blocks, 2 * slots, 2 * HD), BF16),
        pltpu.VMEM((slots, HD), F32),
        pltpu.VMEM((slots, HD), F32),
    ]
    flops = 2 * slots * width * (heads + 2) * HD
    cache_bytes = kv_cache.size * 2
    held = jax.ShapeDtypeStruct((slots + moving,) + kv_cache.shape[1:], BF16)

    query, newkey1, newvalue1, plan, cache, *notes = pl.pallas_call(
        functools.partial(first_kernel, peers, slots, heads, shard),
        out_shape=[
            jax.ShapeDtypeStruct((slots * GROUP, HD), F32),
            row32,
            row32,
            jax.ShapeDtypeStruct((2 * moving,), I32),
            held,
        ]
        + [jax.ShapeDtypeStruct((MOVE, 2, cap + NOTE, HD), BF16)]
        + [jax.ShapeDtypeStruct((MOVE, note_width), F32)] * (others - 1),
        in_specs=[SMEM] + [HBM] * 9,
        out_specs=[VMEM] * 3 + [SMEM] + [VMEM] * (others + 1),
        scratch_shapes=weights
        + stages
        + [
            pltpu.VMEM((moving,) + kv_cache.shape[1:], BF16),
            pltpu.VMEM((slots, width), F32),
            pltpu.SMEM((1, source.shape[0]), I32),
            pltpu.VMEM((1, source.shape[0]), I32),
            pltpu.VMEM(hidden.shape, BF16),
            pltpu.VMEM((1, width), F32),
            pltpu.VMEM(cosine.shape, F32),
            pltpu.VMEM(cosine.shape, F32),
            dma((6,)),
            dma((4,)),
            dma((4,)),
            dma((moving,)),
            dma((1,)),
            dma((slots // CHUNK,)),
        ],
        compiler_params=params(24),
        cost_estimate=cost(flops, (query_weight.size + wkv.size) * 2),
        name="first_step",
    )(meta, *(
        pltpu.with_memory_space_constraint(x, pltpu.HBM)
        for x in (source.reshape(1, -1), lengths.reshape(1, -1), hidden, gain, cosine, sine,
                  query_weight, wkv, kv_cache)
    ))
    got_notes = [swapped(note, "inst", peers, k + 1) for k, note in enumerate(notes)]

    attended, cache = pl.pallas_call(
        functools.partial(attend_kernel, slots, heads),
        out_shape=[jax.ShapeDtypeStruct((slots, heads * HD), BF16), held],
        in_specs=[SMEM] * 2 + [VMEM] * 4,
        out_specs=[VMEM] * 2,
        scratch_shapes=[pltpu.VMEM((slots * GROUP, HD), F32)],
        input_output_aliases={5: 1},
        compiler_params=params(12),
        cost_estimate=cost(4 * slots * cap * HD * heads, cache_bytes),
        name="attention",
    )(meta, lengths, query, newkey1, newvalue1, cache)

    sent = [jax.ShapeDtypeStruct((slots, shard), F32)]
    sent += [jax.ShapeDtypeStruct((slots, shard), BF16)] * (peers_tp - 1)
    own, *sends = pl.pallas_call(
        functools.partial(out_kernel, peers, peers_tp),
        out_shape=sent,
        in_specs=[SMEM] * 2 + [VMEM] * (3 + others),
        out_specs=[VMEM] * peers_tp,
        compiler_params=params(16),
        cost_estimate=cost(2 * slots * width * heads * HD, out_weight.size * 2),
        name="out_projection",
    )(meta, plan, attended, out_weight, hidden, *got_notes)
    boxes = pl.pallas_call(
        pack_kernel,
        out_shape=[jax.ShapeDtypeStruct((MOVE,) + kv_cache.shape[1:], BF16)] * (others - 1),
        in_specs=[SMEM, VMEM, ANY],
        out_specs=[ANY] * (others - 1),
        scratch_shapes=[dma((moving - MOVE,))],
        compiler_params=params(16),
        cost_estimate=cost(1, 1 * cache_bytes),
        name="pack",
    )(plan, cache, own)
    got_boxes = got_notes[:1] + [swapped(box, "inst", peers, k + 2) for k, box in enumerate(boxes)]

    def summed(own, sends, passed_on):
        got = [swapped(sends[k - 1], "tp", peers_tp, k) for k in range(peers_tp - 1, 0, -1)]
        shard_rows = pl.pallas_call(
            sum_kernel,
            out_shape=jax.ShapeDtypeStruct((slots, shard), BF16),
            in_specs=[VMEM] * peers_tp,
            out_specs=VMEM,
            compiler_params=params(16),
            name="sum_terms",
        )(own, *got)
        blocks = {0: shard_rows}
        if not passed_on:
            blocks |= {k: swapped(shard_rows, "tp", peers_tp, k) for k in range(1, peers_tp)}
        far = peers_tp // 2 if passed_on else 0
        while far:
            blocks |= {k + far: swapped(blocks[k], "tp", peers_tp, far) for k in blocks}
            far //= 2
        return [blocks[k] for k in range(peers_tp)]

    pieces = summed(own, sends, False)

    weight, cos_rows, sin_rows, place = pl.pallas_call(
        functools.partial(prepare_kernel, peers, slots),
        out_shape=[
            jax.ShapeDtypeStruct((width, 2 * HD), BF16),
            row32,
            row32,
            jax.ShapeDtypeStruct((slots,), I32),
        ],
        in_specs=[SMEM] * 4 + [VMEM] * 3 + [ANY],
        out_specs=[VMEM] * 3 + [SMEM],
        compiler_params=params(16),
        cost_estimate=cost(100*flops, wkv.size * 40),
        name="prepare",
    )(meta, source, lengths, plan, cosine, sine, wkv, own)

    own, *sends, cache = pl.pallas_call(
        functools.partial(second_kernel, peers, peers_tp, slots, heads),
        out_shape=sent + [held],
        in_specs=[SMEM] * 4 + [VMEM] * (7 + peers_tp) + [ANY] * others,
        out_specs=[VMEM] * (1 + peers_tp),
        scratch_shapes=[
            pltpu.VMEM((blocks, slots, HD), BF16),
            pltpu.VMEM((slots * GROUP, HD), F32),
            pltpu.VMEM((slots * GROUP, HD), F32),
            dma((others,)),
        ],
        input_output_aliases={10: peers_tp},
        compiler_params=params(16),
        cost_estimate=cost(3 * flops, cache_bytes + (query_weight.size + wkv.size) * 4),
        name="second_step",
    )(meta, source, lengths, place, gain, cos_rows, sin_rows, query_weight, weight, out_weight, cache,
      *pieces, *got_boxes)

    pieces = summed(own, sends, False)
    final_cache = pl.pallas_call(
        functools.partial(cache_kernel, slots),
        out_shape=jax.ShapeDtypeStruct(kv_cache.shape, BF16),
        in_specs=[SMEM, VMEM],
        out_specs=ANY,
        scratch_shapes=[dma((slots,))],
        compiler_params=params(16),
        cost_estimate=cost(0, 2 * cache_bytes),
        name="write_cache",
    )(place, cache)
    final_hidden = pl.pallas_call(
        functools.partial(join_kernel, peers_tp),
        out_shape=jax.ShapeDtypeStruct(hidden.shape, BF16),
        in_specs=[SMEM] + [ANY] * peers_tp,
        out_specs=ANY,
        scratch_shapes=[dma((peers_tp,))],
        compiler_params=params(16),
        name="join",
    )(meta, *pieces)
    return (final_hidden, final_cache)


def solution(mesh):
    def whole(kv_cache, *rest):
        tables = angle_tables(kv_cache.shape[2])
        return jax.shard_map(
            functools.partial(local, tables),
            mesh=mesh,
            in_specs=(
                P(("groups", "inst"), None, None, "tp"),
                P(("groups", "inst"), None),
                P("groups"),
                P("groups"),
                P(),
                P(None, "tp"),
                P(None, None, "tp"),
                P("tp", None),
            ),
            out_specs=(P(("groups", "inst"), None), P(("groups", "inst"), None, None, "tp")),
            check_vma=False,
        )(kv_cache, *rest)

    return whole
```

```python
import functools

import jax
import jax.numpy as jnp
import numpy as np
from jax import lax
from jax.experimental import pallas as pl
from jax.experimental.pallas import tpu as pltpu
from jax.sharding import PartitionSpec as P

MOVE = 2
EPS = 1e-05
THETA = 500000.0
HD = 128
GROUP = 8
PIECE = 16
CHUNK = 8
BATCH = 16
NOTE = 16

F32 = jnp.float32
BF16 = jnp.bfloat16
I32 = jnp.int32

ANY = pl.BlockSpec(memory_space=pl.ANY)
VMEM = pl.BlockSpec(memory_space=pltpu.VMEM)
SMEM = pl.BlockSpec(memory_space=pltpu.SMEM)
HBM = pl.BlockSpec(memory_space=pltpu.HBM)


def params(mib):
    return pltpu.CompilerParams(vmem_limit_bytes=mib * 1024 * 1024)


def cost(flops, nbytes):
    return pl.CostEstimate(flops=flops, bytes_accessed=nbytes, transcendentals=0)


def angle_tables(positions):
    frequency = THETA ** (-(np.arange(HD // 2, dtype=np.float64) * 2.0) / HD)
    angles = np.arange(positions, dtype=np.float64)[:, None] * frequency[None, :]
    cosine = np.concatenate([np.cos(angles), np.cos(angles)], axis=-1)
    sine = np.concatenate([-np.sin(angles), np.sin(angles)], axis=-1)
    return cosine.astype(np.float32), sine.astype(np.float32)


def turn(x, cosine, sine):
    return x * cosine + pltpu.roll(x, HD // 2, 1) * sine


def gather_angles(position_of, slots, cos_ref, sin_ref, cos_rows, sin_rows):
    for s in range(slots):
        p = position_of(s)
        cos_rows[s : s + 1, :] = cos_ref[pl.ds(p, 1), :]
        sin_rows[s : s + 1, :] = sin_ref[pl.ds(p, 1), :]


def spread_normed(normed3, spread, slots, width):
    blocks = width // HD
    row = lax.broadcasted_iota(I32, (HD, 4 * HD), 0)
    col = lax.broadcasted_iota(I32, (HD, 4 * HD), 1)
    goal = jnp.where(col < 2 * HD, 2 * row, 2 * row + 1 + 2 * HD)
    places = jnp.where(col == goal, 1.0, 0.0).astype(BF16)
    spread_all = jnp.dot(
        normed3[...].reshape(blocks * slots, HD), places, preferred_element_type=F32
    ).astype(BF16)
    spread[:, 0:slots, :] = spread_all[:, : 2 * HD].reshape(blocks, slots, 2 * HD)
    spread[:, slots:, :] = spread_all[:, 2 * HD :].reshape(blocks, slots, 2 * HD)


def project_from(normed3, weight):
    total = None
    for b in range(normed3.shape[0] // 2):
        block = jnp.concatenate([normed3[2 * b], normed3[2 * b + 1]], axis=1)
        part = jnp.dot(
            block, weight[b * 2 * HD : (b + 1) * 2 * HD, :], preferred_element_type=F32
        )
        total = part if total is None else total + part
    return total


def project_spread(spread, wkv):
    total = None
    for b in range(spread.shape[0]):
        part = jnp.dot(
            spread[b], wkv[b * 2 * HD : (b + 1) * 2 * HD, :], preferred_element_type=F32
        )
        total = part if total is None else total + part
    slots = spread.shape[1] // 2
    return total[:slots], total[slots:]


def weight_copies(src, dst, sem, pieces):
    depth = src.shape[0] // pieces
    copies = [
        pltpu.make_async_copy(
            src.at[pl.ds(c * depth, depth)], dst.at[pl.ds(c * depth, depth)], sem.at[c]
        )
        for c in range(pieces)
    ]
    return copies


def put_row(cache, place, p, key_row, value_row):
    base = pl.multiple_of((jnp.maximum(p, 0) // PIECE) * PIECE, PIECE)
    hit = lax.broadcasted_iota(I32, (PIECE, HD), 0) + base == p
    for which, new in ((0, key_row), (1, value_row)):
        old = cache[place, which, pl.ds(base, PIECE), :]
        new = jnp.broadcast_to(new, old.shape).astype(BF16)
        cache[place, which, pl.ds(base, PIECE), :] = jnp.where(hit, new, old)


def attend(cache, places, positions, query_rows):
    cap = cache.shape[2]
    col = lax.broadcasted_iota(I32, (GROUP, cap), 1)
    scores = [
        lax.dot_general(
            rows.astype(BF16),
            cache[place, 0],
            (((1,), (1,)), ((), ())),
            preferred_element_type=F32,
        )
        for place, rows in zip(places, query_rows)
    ]
    probs = []
    for score, p in zip(scores, positions):
        score = jnp.where(col <= p, score * HD**-0.5, -jnp.inf)
        weight = jnp.exp(score - jnp.max(score, axis=-1, keepdims=True))
        weight = weight / jnp.sum(weight, axis=-1, keepdims=True)
        probs.append(weight.astype(BF16))
    return [
        jnp.dot(prob, cache[place, 1], preferred_element_type=F32)
        for place, prob in zip(places, probs)
    ]


def norm_into(normed3, pieces, gains, firsts, total_width):
    square = None
    for piece in pieces:
        part = jnp.sum(piece * piece, axis=-1, keepdims=True)
        square = part if square is None else square + part
    factor = lax.rsqrt(square / total_width + EPS)
    for piece, gain, first in zip(pieces, gains, firsts):
        normed = (piece * factor * gain).astype(BF16)
        for i in range(piece.shape[1] // HD):
            normed3[first + i] = normed[:, i * HD : (i + 1) * HD]


def plan_moves(me, peers, slots, source):
    moving = (peers - 1) * MOVE
    shape = (2 * moving, source.shape[1])
    row = lax.broadcasted_iota(I32, shape, 0)
    index = lax.broadcasted_iota(I32, shape, 1)
    leaves = row < moving
    at = jnp.where(leaves, row, row - moving)
    other = jnp.bitwise_xor(me, at // MOVE + 1)
    here, there = me * slots, other * slots
    src = jnp.broadcast_to(source, shape)
    came, went = jnp.where(leaves, here, there), jnp.where(leaves, there, here)
    moved = (src >= came) & (src < came + slots) & (index >= went) & (index < went + slots)
    sign = jnp.where(at % MOVE == 0, -1.0, 1.0)
    index_f = index.astype(F32)
    best = jnp.max(jnp.where(moved, sign * index_f, -1e6), axis=1, keepdims=True)
    hit = moved & (sign * index_f == best)
    result = jnp.where(leaves, src, index) - here
    found = jnp.sum(jnp.where(hit, result.astype(F32), 0.0), axis=1, keepdims=True)
    none = jnp.where(leaves[:, :1], 0.0, -1.0)
    return jnp.where(best > -1e6, found, none).astype(I32)


def first_kernel(
    peers, slots, heads, shard,
    meta, source_hbm, lengths_hbm, hidden_hbm, gain_hbm, cos_hbm, sin_hbm, wq_hbm, wkv_hbm,
    cache_hbm, query_out, newkey_out, newvalue_out, plan, *rest,
):
    others = peers - 1
    moving = others * MOVE
    cache, box, notes = rest[0], rest[1], (None,) + rest[2 : others + 1]
    (wq, wkv, normed3, spread, cos_rows, sin_rows, leaving, hidden32, lengths_s, source_v,
     hidden, gain, cos_ref, sin_ref, small_sem, wq_sem, wkv_sem, in_sem,
     box_sem, cache_sem) = rest[others + 1 :]
    width = hidden.shape[1]
    me, me_tp = meta[0], meta[1]
    wq_copies = weight_copies(wq_hbm, wq, wq_sem, 4)
    wkv_copies = weight_copies(wkv_hbm, wkv, wkv_sem, 4)
    small = [
        pltpu.make_async_copy(src, dst, small_sem.at[i])
        for i, (src, dst) in enumerate((
            (source_hbm, source_v), (hidden_hbm, hidden), (gain_hbm, gain), (lengths_hbm, lengths_s),
            (cos_hbm, cos_ref), (sin_hbm, sin_ref),
        ))
    ]
    for copy in small[:3] + wkv_copies + wq_copies + small[3:]:
        copy.start()
    loads = [
        pltpu.make_async_copy(
            cache_hbm.at[pl.ds(c * CHUNK, CHUNK)], cache.at[pl.ds(c * CHUNK, CHUNK)], cache_sem.at[c]
        )
        for c in range(slots // CHUNK)
    ]
    for copy in small[:3]:
        copy.wait()
    low = me * slots
    moves = plan_moves(me, peers, slots, source_v[...])
    wide = hidden[...].astype(F32)
    hidden32[...] = wide
    norm_into(normed3, [wide], [gain[...]], [0], width)
    spread_normed(normed3, spread, slots, width)
    send_slots = [moves[at, 0] for at in range(moving)]
    fetches = [
        pltpu.make_async_copy(cache_hbm.at[slot], leaving.at[at], in_sem.at[at])
        for at, slot in enumerate(send_slots)
    ]
    for copy in fetches:
        copy.start()
    for at, slot in enumerate(send_slots):
        plan[moving + at] = slot
        plan[at] = moves[moving + at, 0]
    for copy in loads:
        copy.start()
    for copy in small[3:] + wkv_copies + wq_copies + fetches:
        copy.wait()
    gather_angles(lambda s: lengths_s[0, low + s], slots, cos_ref, sin_ref, cos_rows, sin_rows)
    key, value = project_spread(spread, wkv)
    cosine, sine = cos_rows[...], sin_rows[...]
    newkey_out[...] = turn(key, cosine, sine).astype(BF16).astype(F32)
    newvalue_out[...] = value.astype(BF16).astype(F32)
    positions = [lengths_s[0, low + slot] for slot in send_slots]
    for at, slot in enumerate(send_slots):
        put_row(
            leaving, at, positions[at],
            newkey_out[pl.ds(slot, 1), :], newvalue_out[pl.ds(slot, 1), :],
        )
    query = project_from(normed3, wq)
    query_out[...] = jnp.zeros(query_out.shape, F32)
    for g in range(heads):
        turned = turn(query[:, g * HD : (g + 1) * HD], cosine, sine)
        query_out[pl.ds(g, slots, stride=GROUP), :] = turned.astype(BF16).astype(F32)
    cap = leaving.shape[2]
    copies = [
        pltpu.make_async_copy(
            leaving.at[pl.ds(0, MOVE)], box.at[:, :, pl.ds(0, cap), :], box_sem.at[0]
        )
    ]
    copies[0].start()
    rows = [query_out[pl.ds(pl.multiple_of(slot * GROUP, GROUP), GROUP), :] for slot in send_slots]
    attended = attend(leaving, list(range(moving)), positions, rows)
    column = pl.multiple_of(me_tp * shard, shard)
    for at, slot in enumerate(send_slots):
        m = at % MOVE
        residual = hidden32[pl.ds(slot, 1), pl.ds(column, shard)]
        if at < MOVE:
            blocks = [attended[at][g : g + 1, :] for g in range(heads)]
            blocks += [residual[:, b * HD : (b + 1) * HD] for b in range(shard // HD)]
            blocks += [jnp.zeros((1, HD), F32)] * (NOTE - len(blocks))
            box[m, 0, cap : cap + NOTE, :] = jnp.concatenate(blocks, axis=0).astype(BF16)
        else:
            note = notes[at // MOVE]
            for g in range(heads):
                note[m : m + 1, g * HD : (g + 1) * HD] = attended[at][g : g + 1, :]
            note[m : m + 1, heads * HD :] = residual
    for copy in copies + loads:
        copy.wait()


def attend_slots(cache, places, positions, query, attended_rows, heads):
    slots = len(places)
    for first in range(0, slots, BATCH):
        span = range(first, first + BATCH)
        got = attend(
            cache,
            [places[s] for s in span],
            [positions[s] for s in span],
            [query[s * GROUP : (s + 1) * GROUP, :] for s in span],
        )
        for s, rows in zip(span, got):
            attended_rows[s * GROUP : (s + 1) * GROUP, :] = rows
    return jnp.concatenate(
        [attended_rows[pl.ds(g, slots, stride=GROUP), :] for g in range(heads)], axis=1
    )


def attend_kernel(
    slots, heads, meta, lengths_s, query, newkey, newvalue, _, out, cache, attended_rows,
):
    low = meta[0] * slots
    positions = [lengths_s[low + s] for s in range(slots)]
    for s, p in enumerate(positions):
        put_row(cache, s, p, newkey[s : s + 1, :], newvalue[s : s + 1, :])
    out[...] = attend_slots(
        cache, list(range(slots)), positions, query, attended_rows, heads
    ).astype(BF16)


def project_out(attended, wo, sends, me_tp):
    for k in range(len(sends), 0, -1):
        shard = sends[k - 1].shape[1]
        column = pl.multiple_of(jnp.bitwise_xor(me_tp, k) * shard, shard)
        part = jnp.dot(attended, wo[:, pl.ds(column, shard)], preferred_element_type=F32)
        sends[k - 1][...] = part.astype(BF16)


def own_kernel(meta, attended, wo, residual, own):
    shard = own.shape[1]
    column = pl.multiple_of(meta[1] * shard, shard)
    part = jnp.dot(attended[...], wo[:, pl.ds(column, shard)], preferred_element_type=F32)
    own[...] = residual[...].astype(F32) + part


def out_kernel(
    peers, peers_tp, meta, plan, attended, wo, hidden, box, *rest,
):
    notes, rest = rest[: peers - 2], rest[peers - 2 :]
    residual_out, rows_out, sends = rest[0], rest[1], rest[2:]
    shard = residual_out.shape[1]
    cap = box.shape[2] - NOTE
    rows = attended[...].astype(F32)
    heads = rows.shape[1] // HD
    column = pl.multiple_of(meta[1] * shard, shard)
    residual = hidden[:, pl.ds(column, shard)].astype(F32)
    row_index = lax.broadcasted_iota(I32, rows.shape, 0)
    residual_index = lax.broadcasted_iota(I32, residual.shape, 0)
    for at in range((peers - 1) * MOVE):
        m = at % MOVE
        if at < MOVE:
            blocks = box[m, 0, cap : cap + NOTE, :].astype(F32)
            blocks = [blocks[b : b + 1, :] for b in range(heads + shard // HD)]
            note = jnp.concatenate(blocks, axis=1)
        else:
            note = notes[at // MOVE - 1][m : m + 1, :]
        rows = jnp.where(row_index == plan[at], note[:, : heads * HD], rows)
        residual = jnp.where(residual_index == plan[at], note[:, heads * HD :], residual)
    residual_out[...] = residual
    rows_out[...] = rows.astype(BF16)
    project_out(rows.astype(BF16), wo, sends, meta[1])


def pack_kernel(plan, cache, _own, *rest):
    boxes, out_sem = rest[:-1], rest[-1]
    moving = plan.shape[0] // 2
    packs = [
        pltpu.make_async_copy(
            cache.at[plan[moving + at]], boxes[at // MOVE - 1].at[at % MOVE], out_sem.at[at - MOVE]
        )
        for at in range(MOVE, moving)
    ]
    for pack in packs:
        pack.start()
    for pack in packs:
        pack.wait()


def sum_kernel(own, *rest):
    total = own[...]
    for part in rest[:-1]:
        total = total + part[...].astype(F32)
    rest[-1][...] = total.astype(BF16)


def map_places(slots, peers, plan, place):
    for s in range(slots):
        place[s] = s
    for at in range((peers - 1) * MOVE):
        taker = plan[at]

        @pl.when(taker >= 0)
        def _():
            place[taker] = slots + at


def prepare_kernel(
    peers, slots, meta, source_s, lengths_s, plan, cos_ref, sin_ref, wkv, _,
    weight, cos_rows, sin_rows, place,
):
    map_places(slots, peers, plan, place)
    low = meta[0] * slots
    gather_angles(
        lambda s: lengths_s[source_s[low + s]] + 1, slots, cos_ref, sin_ref, cos_rows, sin_rows
    )
    row = lax.broadcasted_iota(I32, (2 * HD, 2 * HD), 0)
    col = lax.broadcasted_iota(I32, (2 * HD, 2 * HD), 1)
    goal = jnp.where(row < HD, 2 * row, 2 * (row - HD) + 1)
    places = jnp.where(col == goal, 1.0, 0.0).astype(BF16)
    for b in range(weight.shape[0] // HD):
        apart = jnp.dot(
            places, wkv[b * 2 * HD : (b + 1) * 2 * HD, :], preferred_element_type=F32
        ).astype(BF16)
        weight[b * HD : (b + 1) * HD, :HD] = apart[:HD]
        weight[b * HD : (b + 1) * HD, HD:] = apart[HD:]


def second_kernel(
    peers, peers_tp, slots, heads,
    meta, source_s, lengths_s, place, gain, cos_rows, sin_rows, wq, wkv, wo, _, *rest,
):
    blocks, rest = rest[:peers_tp], rest[peers_tp:]
    box_hbm, rest = rest[: peers - 1], rest[peers - 1 :]
    attended_out, sends, cache = rest[0], rest[1:peers_tp], rest[peers_tp]
    normed3, query_rows, attended_rows, in_sem = rest[peers_tp + 1 :]
    me, me_tp = meta[0], meta[1]
    low = me * slots
    width = gain.shape[1]
    shard = blocks[0].shape[1]
    loads = [
        pltpu.make_async_copy(
            box.at[:, :, pl.ds(0, cache.shape[2]), :],
            cache.at[pl.ds(slots + k * MOVE, MOVE)],
            in_sem.at[k],
        )
        for k, box in enumerate(box_hbm)
    ]
    for copy in loads:
        copy.start()

    firsts = [jnp.bitwise_xor(me_tp, k) for k in range(peers_tp)]
    norm_into(
        normed3,
        [block[...].astype(F32) for block in blocks],
        [gain[:, pl.ds(pl.multiple_of(first * shard, shard), shard)] for first in firsts],
        [first * (shard // HD) for first in firsts],
        width,
    )
    positions = [lengths_s[source_s[low + s]] + 1 for s in range(slots)]
    for copy in loads:
        copy.wait()
    pair = project_from(normed3, wkv)
    cosine, sine = cos_rows[...], sin_rows[...]
    newkey = turn(pair[:, :HD], cosine, sine).astype(BF16).astype(F32)
    newvalue = pair[:, HD:].astype(BF16).astype(F32)
    places = [place[s] for s in range(slots)]
    for s, (at, p) in enumerate(zip(places, positions)):
        put_row(cache, at, p, newkey[s : s + 1, :], newvalue[s : s + 1, :])
    query = project_from(normed3, wq)
    query_rows[...] = jnp.zeros(query_rows.shape, F32)
    for g in range(heads):
        turned = turn(query[:, g * HD : (g + 1) * HD], cosine, sine)
        query_rows[pl.ds(g, slots, stride=GROUP), :] = turned.astype(BF16).astype(F32)
    attended = attend_slots(cache, places, positions, query_rows, attended_rows, heads)
    attended_out[...] = attended.astype(BF16)
    project_out(attended.astype(BF16), wo, sends, me_tp)


def cache_kernel(slots, place, cache, out_hbm, out_sem):
    copies = [
        pltpu.make_async_copy(cache.at[place[s]], out_hbm.at[s], out_sem.at[s])
        for s in range(slots)
    ]
    for copy in copies:
        copy.start()
    for copy in copies:
        copy.wait()


def join_kernel(peers_tp, meta, *rest):
    blocks, out, sem = rest[:-2], rest[-2], rest[-1]
    shard = blocks[0].shape[1]
    copies = []
    for k, block in enumerate(blocks):
        column = pl.multiple_of(jnp.bitwise_xor(meta[1], k) * shard, shard)
        copies.append(pltpu.make_async_copy(block, out.at[:, pl.ds(column, shard)], sem.at[k]))
        copies[-1].start()
    for copy in copies:
        copy.wait()


def swapped(x, axis, size, k):
    return lax.ppermute(x, axis, [(i, i ^ k) for i in range(size)])


def local(
    tables, kv_cache, hidden, lengths, source, norm_gain, query_weight, keyval_weight, out_weight
):
    peers, peers_tp = lax.axis_size("inst"), lax.axis_size("tp")
    slots, cap = kv_cache.shape[0], kv_cache.shape[2]
    width = hidden.shape[1]
    heads = query_weight.shape[1] // HD
    shard = width // peers_tp
    others, moving = peers - 1, (peers - 1) * MOVE
    blocks = width // HD
    meta = jnp.stack([lax.axis_index("inst"), lax.axis_index("tp")]).astype(I32)
    gain = norm_gain.reshape(1, width)
    wkv = keyval_weight.reshape(2 * width, HD)
    cosine, sine = (jnp.asarray(table) for table in tables)
    row32 = jax.ShapeDtypeStruct((slots, HD), F32)
    note_width = heads * HD + shard
    dma = pltpu.SemaphoreType.DMA
    weights = [
        pltpu.VMEM(query_weight.shape, BF16),
        pltpu.VMEM(wkv.shape, BF16),
    ]
    stages = [
        pltpu.VMEM((blocks, slots, HD), BF16),
        pltpu.VMEM((blocks, 2 * slots, 2 * HD), BF16),
        pltpu.VMEM((slots, HD), F32),
        pltpu.VMEM((slots, HD), F32),
    ]
    flops = 2 * slots * width * (heads + 2) * HD
    cache_bytes = kv_cache.size * 2
    held = jax.ShapeDtypeStruct((slots + moving,) + kv_cache.shape[1:], BF16)

    query, newkey1, newvalue1, plan, cache, *notes = pl.pallas_call(
        functools.partial(first_kernel, peers, slots, heads, shard),
        out_shape=[
            jax.ShapeDtypeStruct((slots * GROUP, HD), F32),
            row32,
            row32,
            jax.ShapeDtypeStruct((2 * moving,), I32),
            held,
        ]
        + [jax.ShapeDtypeStruct((MOVE, 2, cap + NOTE, HD), BF16)]
        + [jax.ShapeDtypeStruct((MOVE, note_width), F32)] * (others - 1),
        in_specs=[SMEM] + [HBM] * 9,
        out_specs=[VMEM] * 3 + [SMEM] + [VMEM] * (others + 1),
        scratch_shapes=weights
        + stages
        + [
            pltpu.VMEM((moving,) + kv_cache.shape[1:], BF16),
            pltpu.VMEM((slots, width), F32),
            pltpu.SMEM((1, source.shape[0]), I32),
            pltpu.VMEM((1, source.shape[0]), I32),
            pltpu.VMEM(hidden.shape, BF16),
            pltpu.VMEM((1, width), F32),
            pltpu.VMEM(cosine.shape, F32),
            pltpu.VMEM(cosine.shape, F32),
            dma((6,)),
            dma((4,)),
            dma((4,)),
            dma((moving,)),
            dma((1,)),
            dma((slots // CHUNK,)),
        ],
        compiler_params=params(24),
        cost_estimate=cost(flops, (query_weight.size + wkv.size) * 2),
        name="first_step",
    )(meta, *(
        pltpu.with_memory_space_constraint(x, pltpu.HBM)
        for x in (source.reshape(1, -1), lengths.reshape(1, -1), hidden, gain, cosine, sine,
                  query_weight, wkv, kv_cache)
    ))
    got_notes = [swapped(note, "inst", peers, k + 1) for k, note in enumerate(notes)]

    attended, cache = pl.pallas_call(
        functools.partial(attend_kernel, slots, heads),
        out_shape=[jax.ShapeDtypeStruct((slots, heads * HD), BF16), held],
        in_specs=[SMEM] * 2 + [VMEM] * 4,
        out_specs=[VMEM] * 2,
        scratch_shapes=[pltpu.VMEM((slots * GROUP, HD), F32)],
        input_output_aliases={5: 1},
        compiler_params=params(12),
        cost_estimate=cost(4 * slots * cap * HD * heads, cache_bytes),
        name="attention",
    )(meta, lengths, query, newkey1, newvalue1, cache)

    own32 = jax.ShapeDtypeStruct((slots, shard), F32)
    rows16 = jax.ShapeDtypeStruct((slots, heads * HD), BF16)
    sent = [jax.ShapeDtypeStruct((slots, shard), BF16)] * (peers_tp - 1)

    def own_term(rows, residual):
        return pl.pallas_call(
            own_kernel,
            out_shape=own32,
            in_specs=[SMEM] + [VMEM] * 3,
            out_specs=VMEM,
            compiler_params=params(16),
            cost_estimate=cost(2 * slots * shard * heads * HD, out_weight.size // 2),
            name="own_term",
        )(meta, rows, out_weight, residual)

    residual, rows, *sends = pl.pallas_call(
        functools.partial(out_kernel, peers, peers_tp),
        out_shape=[own32, rows16] + sent,
        in_specs=[SMEM] * 2 + [VMEM] * (3 + others),
        out_specs=[VMEM] * (1 + peers_tp),
        compiler_params=params(16),
        cost_estimate=cost(2 * slots * width * heads * HD, out_weight.size * 2),
        name="out_projection",
    )(meta, plan, attended, out_weight, hidden, *got_notes)
    own = own_term(rows, residual)
    boxes = pl.pallas_call(
        pack_kernel,
        out_shape=[jax.ShapeDtypeStruct((MOVE,) + kv_cache.shape[1:], BF16)] * (others - 1),
        in_specs=[SMEM, VMEM, ANY],
        out_specs=[ANY] * (others - 1),
        scratch_shapes=[dma((moving - MOVE,))],
        compiler_params=params(16),
        cost_estimate=cost(1, 1 * cache_bytes),
        name="pack",
    )(plan, cache, rows)
    got_boxes = got_notes[:1] + [swapped(box, "inst", peers, k + 2) for k, box in enumerate(boxes)]

    def summed(own, sends, passed_on):
        got = [swapped(sends[k - 1], "tp", peers_tp, k) for k in range(peers_tp - 1, 0, -1)]
        shard_rows = pl.pallas_call(
            sum_kernel,
            out_shape=jax.ShapeDtypeStruct((slots, shard), BF16),
            in_specs=[VMEM] * peers_tp,
            out_specs=VMEM,
            compiler_params=params(16),
            name="sum_terms",
        )(own, *got)
        blocks = {0: shard_rows}
        if not passed_on:
            blocks |= {k: swapped(shard_rows, "tp", peers_tp, k) for k in range(1, peers_tp)}
        far = peers_tp // 2 if passed_on else 0
        while far:
            blocks |= {k + far: swapped(blocks[k], "tp", peers_tp, far) for k in blocks}
            far //= 2
        return [blocks[k] for k in range(peers_tp)]

    pieces = summed(own, sends, False)

    weight, cos_rows, sin_rows, place = pl.pallas_call(
        functools.partial(prepare_kernel, peers, slots),
        out_shape=[
            jax.ShapeDtypeStruct((width, 2 * HD), BF16),
            row32,
            row32,
            jax.ShapeDtypeStruct((slots,), I32),
        ],
        in_specs=[SMEM] * 4 + [VMEM] * 3 + [ANY],
        out_specs=[VMEM] * 3 + [SMEM],
        compiler_params=params(16),
        cost_estimate=cost(100*flops, wkv.size * 40),
        name="prepare",
    )(meta, source, lengths, plan, cosine, sine, wkv, rows)

    rows, *sends, cache = pl.pallas_call(
        functools.partial(second_kernel, peers, peers_tp, slots, heads),
        out_shape=[rows16] + sent + [held],
        in_specs=[SMEM] * 4 + [VMEM] * (7 + peers_tp) + [ANY] * others,
        out_specs=[VMEM] * (1 + peers_tp),
        scratch_shapes=[
            pltpu.VMEM((blocks, slots, HD), BF16),
            pltpu.VMEM((slots * GROUP, HD), F32),
            pltpu.VMEM((slots * GROUP, HD), F32),
            dma((others,)),
        ],
        input_output_aliases={10: peers_tp},
        compiler_params=params(16),
        cost_estimate=cost(3 * flops, cache_bytes + (query_weight.size + wkv.size) * 4),
        name="second_step",
    )(meta, source, lengths, place, gain, cos_rows, sin_rows, query_weight, weight, out_weight, cache,
      *pieces, *got_boxes)
    own = own_term(rows, pieces[0])

    pieces = summed(own, sends, False)
    final_cache = pl.pallas_call(
        functools.partial(cache_kernel, slots),
        out_shape=jax.ShapeDtypeStruct(kv_cache.shape, BF16),
        in_specs=[SMEM, VMEM],
        out_specs=ANY,
        scratch_shapes=[dma((slots,))],
        compiler_params=params(16),
        cost_estimate=cost(0, 2 * cache_bytes),
        name="write_cache",
    )(place, cache)
    final_hidden = pl.pallas_call(
        functools.partial(join_kernel, peers_tp),
        out_shape=jax.ShapeDtypeStruct(hidden.shape, BF16),
        in_specs=[SMEM] + [ANY] * peers_tp,
        out_specs=ANY,
        scratch_shapes=[dma((peers_tp,))],
        compiler_params=params(16),
        name="join",
    )(meta, *pieces)
    return (final_hidden, final_cache)


def solution(mesh):
    def whole(kv_cache, *rest):
        tables = angle_tables(kv_cache.shape[2])
        return jax.shard_map(
            functools.partial(local, tables),
            mesh=mesh,
            in_specs=(
                P(("groups", "inst"), None, None, "tp"),
                P(("groups", "inst"), None),
                P("groups"),
                P("groups"),
                P(),
                P(None, "tp"),
                P(None, None, "tp"),
                P("tp", None),
            ),
            out_specs=(P(("groups", "inst"), None), P(("groups", "inst"), None, None, "tp")),
            check_vma=False,
        )(kv_cache, *rest)

    return whole
```

```python
import functools

import jax
import jax.numpy as jnp
import numpy as np
from jax import lax
from jax.experimental import pallas as pl
from jax.experimental.pallas import tpu as pltpu
from jax.sharding import PartitionSpec as P

MOVE = 2
EPS = 1e-05
THETA = 500000.0
HD = 128
GROUP = 8
PIECE = 16
CHUNK = 8
BATCH = 24
NOTE = 16

F32 = jnp.float32
BF16 = jnp.bfloat16
I32 = jnp.int32

ANY = pl.BlockSpec(memory_space=pl.ANY)
VMEM = pl.BlockSpec(memory_space=pltpu.VMEM)
SMEM = pl.BlockSpec(memory_space=pltpu.SMEM)
HBM = pl.BlockSpec(memory_space=pltpu.HBM)


def params(mib):
    return pltpu.CompilerParams(vmem_limit_bytes=mib * 1024 * 1024)


def cost(flops, nbytes):
    return pl.CostEstimate(flops=flops, bytes_accessed=nbytes, transcendentals=0)


def angle_tables(positions):
    frequency = THETA ** (-(np.arange(HD // 2, dtype=np.float64) * 2.0) / HD)
    angles = np.arange(positions, dtype=np.float64)[:, None] * frequency[None, :]
    cosine = np.concatenate([np.cos(angles), np.cos(angles)], axis=-1)
    sine = np.concatenate([-np.sin(angles), np.sin(angles)], axis=-1)
    return cosine.astype(np.float32), sine.astype(np.float32)


def turn(x, cosine, sine):
    return x * cosine + pltpu.roll(x, HD // 2, 1) * sine


def gather_angles(position_of, slots, cos_ref, sin_ref, cos_rows, sin_rows):
    for s in range(slots):
        p = position_of(s)
        cos_rows[s : s + 1, :] = cos_ref[pl.ds(p, 1), :]
        sin_rows[s : s + 1, :] = sin_ref[pl.ds(p, 1), :]


def spread_normed(normed3, spread, slots, width):
    blocks = width // HD
    row = lax.broadcasted_iota(I32, (HD, 4 * HD), 0)
    col = lax.broadcasted_iota(I32, (HD, 4 * HD), 1)
    goal = jnp.where(col < 2 * HD, 2 * row, 2 * row + 1 + 2 * HD)
    places = jnp.where(col == goal, 1.0, 0.0).astype(BF16)
    spread_all = jnp.dot(
        normed3[...].reshape(blocks * slots, HD), places, preferred_element_type=F32
    ).astype(BF16)
    spread[:, 0:slots, :] = spread_all[:, : 2 * HD].reshape(blocks, slots, 2 * HD)
    spread[:, slots:, :] = spread_all[:, 2 * HD :].reshape(blocks, slots, 2 * HD)


def project_from(normed3, weight):
    total = None
    for b in range(normed3.shape[0] // 2):
        block = jnp.concatenate([normed3[2 * b], normed3[2 * b + 1]], axis=1)
        part = jnp.dot(
            block, weight[b * 2 * HD : (b + 1) * 2 * HD, :], preferred_element_type=F32
        )
        total = part if total is None else total + part
    return total


def project_spread(spread, wkv):
    total = None
    for b in range(spread.shape[0]):
        part = jnp.dot(
            spread[b], wkv[b * 2 * HD : (b + 1) * 2 * HD, :], preferred_element_type=F32
        )
        total = part if total is None else total + part
    slots = spread.shape[1] // 2
    return total[:slots], total[slots:]


def weight_copies(src, dst, sem, pieces):
    depth = src.shape[0] // pieces
    copies = [
        pltpu.make_async_copy(
            src.at[pl.ds(c * depth, depth)], dst.at[pl.ds(c * depth, depth)], sem.at[c]
        )
        for c in range(pieces)
    ]
    return copies


def put_row(cache, place, p, key_row, value_row):
    base = pl.multiple_of((jnp.maximum(p, 0) // PIECE) * PIECE, PIECE)
    hit = lax.broadcasted_iota(I32, (PIECE, HD), 0) + base == p
    for which, new in ((0, key_row), (1, value_row)):
        old = cache[place, which, pl.ds(base, PIECE), :]
        new = jnp.broadcast_to(new, old.shape).astype(BF16)
        cache[place, which, pl.ds(base, PIECE), :] = jnp.where(hit, new, old)


def attend(cache, places, positions, query_rows):
    cap = cache.shape[2]
    col = lax.broadcasted_iota(I32, (GROUP, cap), 1)
    scores = [
        lax.dot_general(
            rows.astype(BF16),
            cache[place, 0],
            (((1,), (1,)), ((), ())),
            preferred_element_type=F32,
        )
        for place, rows in zip(places, query_rows)
    ]
    probs = []
    for score, p in zip(scores, positions):
        score = jnp.where(col <= p, score * HD**-0.5, -jnp.inf)
        weight = jnp.exp(score - jnp.max(score, axis=-1, keepdims=True))
        weight = weight / jnp.sum(weight, axis=-1, keepdims=True)
        probs.append(weight.astype(BF16))
    return [
        jnp.dot(prob, cache[place, 1], preferred_element_type=F32)
        for place, prob in zip(places, probs)
    ]


def norm_into(normed3, pieces, gains, firsts, total_width):
    square = None
    for piece in pieces:
        part = jnp.sum(piece * piece, axis=-1, keepdims=True)
        square = part if square is None else square + part
    factor = lax.rsqrt(square / total_width + EPS)
    for piece, gain, first in zip(pieces, gains, firsts):
        normed = (piece * factor * gain).astype(BF16)
        for i in range(piece.shape[1] // HD):
            normed3[first + i] = normed[:, i * HD : (i + 1) * HD]


def plan_moves(me, peers, slots, source):
    moving = (peers - 1) * MOVE
    shape = (2 * moving, source.shape[1])
    row = lax.broadcasted_iota(I32, shape, 0)
    index = lax.broadcasted_iota(I32, shape, 1)
    leaves = row < moving
    at = jnp.where(leaves, row, row - moving)
    other = jnp.bitwise_xor(me, at // MOVE + 1)
    here, there = me * slots, other * slots
    src = jnp.broadcast_to(source, shape)
    came, went = jnp.where(leaves, here, there), jnp.where(leaves, there, here)
    moved = (src >= came) & (src < came + slots) & (index >= went) & (index < went + slots)
    sign = jnp.where(at % MOVE == 0, -1.0, 1.0)
    index_f = index.astype(F32)
    best = jnp.max(jnp.where(moved, sign * index_f, -1e6), axis=1, keepdims=True)
    hit = moved & (sign * index_f == best)
    result = jnp.where(leaves, src, index) - here
    found = jnp.sum(jnp.where(hit, result.astype(F32), 0.0), axis=1, keepdims=True)
    none = jnp.where(leaves[:, :1], 0.0, -1.0)
    return jnp.where(best > -1e6, found, none).astype(I32)


def first_kernel(
    peers, slots, heads, shard,
    meta, source_hbm, lengths_hbm, hidden_hbm, gain_hbm, cos_hbm, sin_hbm, wq_hbm, wkv_hbm,
    cache_hbm, query_out, newkey_out, newvalue_out, plan, *rest,
):
    others = peers - 1
    moving = others * MOVE
    cache, box, notes = rest[0], rest[1], (None,) + rest[2 : others + 1]
    (wq, wkv, normed3, spread, cos_rows, sin_rows, leaving, hidden32, lengths_s, source_v,
     hidden, gain, cos_ref, sin_ref, small_sem, wq_sem, wkv_sem, in_sem,
     box_sem, cache_sem) = rest[others + 1 :]
    width = hidden.shape[1]
    me, me_tp = meta[0], meta[1]
    wq_copies = weight_copies(wq_hbm, wq, wq_sem, 4)
    wkv_copies = weight_copies(wkv_hbm, wkv, wkv_sem, 4)
    small = [
        pltpu.make_async_copy(src, dst, small_sem.at[i])
        for i, (src, dst) in enumerate((
            (source_hbm, source_v), (hidden_hbm, hidden), (gain_hbm, gain), (lengths_hbm, lengths_s),
            (cos_hbm, cos_ref), (sin_hbm, sin_ref),
        ))
    ]
    for copy in small[:3] + wkv_copies + wq_copies + small[3:]:
        copy.start()
    loads = [
        pltpu.make_async_copy(
            cache_hbm.at[pl.ds(c * CHUNK, CHUNK)], cache.at[pl.ds(c * CHUNK, CHUNK)], cache_sem.at[c]
        )
        for c in range(slots // CHUNK)
    ]
    for copy in small[:3]:
        copy.wait()
    low = me * slots
    moves = plan_moves(me, peers, slots, source_v[...])
    wide = hidden[...].astype(F32)
    hidden32[...] = wide
    norm_into(normed3, [wide], [gain[...]], [0], width)
    spread_normed(normed3, spread, slots, width)
    send_slots = [moves[at, 0] for at in range(moving)]
    fetches = [
        pltpu.make_async_copy(cache_hbm.at[slot], leaving.at[at], in_sem.at[at])
        for at, slot in enumerate(send_slots)
    ]
    for copy in fetches:
        copy.start()
    for at, slot in enumerate(send_slots):
        plan[moving + at] = slot
        plan[at] = moves[moving + at, 0]
    for copy in loads:
        copy.start()
    for copy in small[3:] + wkv_copies + wq_copies + fetches:
        copy.wait()
    gather_angles(lambda s: lengths_s[0, low + s], slots, cos_ref, sin_ref, cos_rows, sin_rows)
    key, value = project_spread(spread, wkv)
    cosine, sine = cos_rows[...], sin_rows[...]
    newkey_out[...] = turn(key, cosine, sine).astype(BF16).astype(F32)
    newvalue_out[...] = value.astype(BF16).astype(F32)
    positions = [lengths_s[0, low + slot] for slot in send_slots]
    for at, slot in enumerate(send_slots):
        put_row(
            leaving, at, positions[at],
            newkey_out[pl.ds(slot, 1), :], newvalue_out[pl.ds(slot, 1), :],
        )
    query = project_from(normed3, wq)
    query_out[...] = jnp.zeros(query_out.shape, F32)
    for g in range(heads):
        turned = turn(query[:, g * HD : (g + 1) * HD], cosine, sine)
        query_out[pl.ds(g, slots, stride=GROUP), :] = turned.astype(BF16).astype(F32)
    cap = leaving.shape[2]
    copies = [
        pltpu.make_async_copy(
            leaving.at[pl.ds(0, MOVE)], box.at[:, :, pl.ds(0, cap), :], box_sem.at[0]
        )
    ]
    copies[0].start()
    rows = [query_out[pl.ds(pl.multiple_of(slot * GROUP, GROUP), GROUP), :] for slot in send_slots]
    attended = attend(leaving, list(range(moving)), positions, rows)
    column = pl.multiple_of(me_tp * shard, shard)
    for at, slot in enumerate(send_slots):
        m = at % MOVE
        residual = hidden32[pl.ds(slot, 1), pl.ds(column, shard)]
        if at < MOVE:
            blocks = [attended[at][g : g + 1, :] for g in range(heads)]
            blocks += [residual[:, b * HD : (b + 1) * HD] for b in range(shard // HD)]
            blocks += [jnp.zeros((1, HD), F32)] * (NOTE - len(blocks))
            box[m, 0, cap : cap + NOTE, :] = jnp.concatenate(blocks, axis=0).astype(BF16)
        else:
            note = notes[at // MOVE]
            for g in range(heads):
                note[m : m + 1, g * HD : (g + 1) * HD] = attended[at][g : g + 1, :]
            note[m : m + 1, heads * HD :] = residual
    for copy in copies + loads:
        copy.wait()


def attend_slots(cache, places, positions, query, attended_rows, heads):
    slots = len(places)
    for first in range(0, slots, BATCH):
        span = range(first, first + BATCH)
        got = attend(
            cache,
            [places[s] for s in span],
            [positions[s] for s in span],
            [query[s * GROUP : (s + 1) * GROUP, :] for s in span],
        )
        for s, rows in zip(span, got):
            attended_rows[s * GROUP : (s + 1) * GROUP, :] = rows
    return jnp.concatenate(
        [attended_rows[pl.ds(g, slots, stride=GROUP), :] for g in range(heads)], axis=1
    )


def attend_kernel(
    slots, heads, meta, lengths_s, query, newkey, newvalue, _, out, cache, attended_rows,
):
    low = meta[0] * slots
    positions = [lengths_s[low + s] for s in range(slots)]
    for s, p in enumerate(positions):
        put_row(cache, s, p, newkey[s : s + 1, :], newvalue[s : s + 1, :])
    out[...] = attend_slots(
        cache, list(range(slots)), positions, query, attended_rows, heads
    ).astype(BF16)


def project_out(attended, wo, sends, me_tp):
    for k in range(len(sends), 0, -1):
        shard = sends[k - 1].shape[1]
        column = pl.multiple_of(jnp.bitwise_xor(me_tp, k) * shard, shard)
        part = jnp.dot(attended, wo[:, pl.ds(column, shard)], preferred_element_type=F32)
        sends[k - 1][...] = part.astype(BF16)


def own_kernel(meta, attended, wo, residual, own):
    shard = own.shape[1]
    column = pl.multiple_of(meta[1] * shard, shard)
    part = jnp.dot(attended[...], wo[:, pl.ds(column, shard)], preferred_element_type=F32)
    own[...] = residual[...].astype(F32) + part


def out_kernel(
    peers, peers_tp, meta, plan, attended, wo, hidden, box, *rest,
):
    notes, rest = rest[: peers - 2], rest[peers - 2 :]
    residual_out, rows_out, sends = rest[0], rest[1], rest[2:]
    shard = residual_out.shape[1]
    cap = box.shape[2] - NOTE
    rows = attended[...].astype(F32)
    heads = rows.shape[1] // HD
    column = pl.multiple_of(meta[1] * shard, shard)
    residual = hidden[:, pl.ds(column, shard)].astype(F32)
    row_index = lax.broadcasted_iota(I32, rows.shape, 0)
    residual_index = lax.broadcasted_iota(I32, residual.shape, 0)
    for at in range((peers - 1) * MOVE):
        m = at % MOVE
        if at < MOVE:
            blocks = box[m, 0, cap : cap + NOTE, :].astype(F32)
            blocks = [blocks[b : b + 1, :] for b in range(heads + shard // HD)]
            note = jnp.concatenate(blocks, axis=1)
        else:
            note = notes[at // MOVE - 1][m : m + 1, :]
        rows = jnp.where(row_index == plan[at], note[:, : heads * HD], rows)
        residual = jnp.where(residual_index == plan[at], note[:, heads * HD :], residual)
    residual_out[...] = residual
    rows_out[...] = rows.astype(BF16)
    project_out(rows.astype(BF16), wo, sends, meta[1])


def pack_kernel(plan, cache, _own, *rest):
    boxes, out_sem = rest[:-1], rest[-1]
    moving = plan.shape[0] // 2
    packs = [
        pltpu.make_async_copy(
            cache.at[plan[moving + at]], boxes[at // MOVE - 1].at[at % MOVE], out_sem.at[at - MOVE]
        )
        for at in range(MOVE, moving)
    ]
    for pack in packs:
        pack.start()
    for pack in packs:
        pack.wait()


def sum_kernel(own, *rest):
    total = own[...]
    for part in rest[:-1]:
        total = total + part[...].astype(F32)
    rest[-1][...] = total.astype(BF16)


def map_places(slots, peers, plan, place):
    for s in range(slots):
        place[s] = s
    for at in range((peers - 1) * MOVE):
        taker = plan[at]

        @pl.when(taker >= 0)
        def _():
            place[taker] = slots + at


def prepare_kernel(
    peers, slots, meta, source_s, lengths_s, plan, cos_ref, sin_ref, wkv, _,
    weight, cos_rows, sin_rows, place,
):
    map_places(slots, peers, plan, place)
    low = meta[0] * slots
    positions = [lengths_s[source_s[low + s]] + 1 for s in range(slots)]
    for s, p in enumerate(positions):
        place[slots + s] = p
    gather_angles(lambda s: positions[s], slots, cos_ref, sin_ref, cos_rows, sin_rows)
    row = lax.broadcasted_iota(I32, (2 * HD, 2 * HD), 0)
    col = lax.broadcasted_iota(I32, (2 * HD, 2 * HD), 1)
    goal = jnp.where(row < HD, 2 * row, 2 * (row - HD) + 1)
    places = jnp.where(col == goal, 1.0, 0.0).astype(BF16)
    for b in range(weight.shape[0] // HD):
        apart = jnp.dot(
            places, wkv[b * 2 * HD : (b + 1) * 2 * HD, :], preferred_element_type=F32
        ).astype(BF16)
        weight[b * HD : (b + 1) * HD, :HD] = apart[:HD]
        weight[b * HD : (b + 1) * HD, HD:] = apart[HD:]


def second_kernel(
    peers, peers_tp, slots, heads,
    meta, place, gain, cos_rows, sin_rows, wq, wkv, wo, _, *rest,
):
    blocks, rest = rest[:peers_tp], rest[peers_tp:]
    box_hbm, rest = rest[: peers - 1], rest[peers - 1 :]
    attended_out, sends, cache = rest[0], rest[1:peers_tp], rest[peers_tp]
    normed3, query_rows, attended_rows, in_sem = rest[peers_tp + 1 :]
    me_tp = meta[1]
    width = gain.shape[1]
    shard = blocks[0].shape[1]
    loads = [
        pltpu.make_async_copy(
            box.at[:, :, pl.ds(0, cache.shape[2]), :],
            cache.at[pl.ds(slots + k * MOVE, MOVE)],
            in_sem.at[k],
        )
        for k, box in enumerate(box_hbm)
    ]
    for copy in loads:
        copy.start()

    firsts = [jnp.bitwise_xor(me_tp, k) for k in range(peers_tp)]
    norm_into(
        normed3,
        [block[...].astype(F32) for block in blocks],
        [gain[:, pl.ds(pl.multiple_of(first * shard, shard), shard)] for first in firsts],
        [first * (shard // HD) for first in firsts],
        width,
    )
    positions = [place[slots + s] for s in range(slots)]
    for copy in loads:
        copy.wait()
    pair = project_from(normed3, wkv)
    cosine, sine = cos_rows[...], sin_rows[...]
    newkey = turn(pair[:, :HD], cosine, sine).astype(BF16).astype(F32)
    newvalue = pair[:, HD:].astype(BF16).astype(F32)
    places = [place[s] for s in range(slots)]
    for s, (at, p) in enumerate(zip(places, positions)):
        put_row(cache, at, p, newkey[s : s + 1, :], newvalue[s : s + 1, :])
    query = project_from(normed3, wq)
    query_rows[...] = jnp.zeros(query_rows.shape, F32)
    for g in range(heads):
        turned = turn(query[:, g * HD : (g + 1) * HD], cosine, sine)
        query_rows[pl.ds(g, slots, stride=GROUP), :] = turned.astype(BF16).astype(F32)
    attended = attend_slots(cache, places, positions, query_rows, attended_rows, heads)
    attended_out[...] = attended.astype(BF16)
    project_out(attended.astype(BF16), wo, sends, me_tp)


def cache_kernel(slots, place, cache, out_hbm, out_sem):
    copies = [
        pltpu.make_async_copy(cache.at[place[s]], out_hbm.at[s], out_sem.at[s])
        for s in range(slots)
    ]
    for copy in copies:
        copy.start()
    for copy in copies:
        copy.wait()


def join_kernel(peers_tp, meta, *rest):
    blocks, out, sem = rest[:-2], rest[-2], rest[-1]
    shard = blocks[0].shape[1]
    copies = []
    for k, block in enumerate(blocks):
        column = pl.multiple_of(jnp.bitwise_xor(meta[1], k) * shard, shard)
        copies.append(pltpu.make_async_copy(block, out.at[:, pl.ds(column, shard)], sem.at[k]))
        copies[-1].start()
    for copy in copies:
        copy.wait()


def swapped(x, axis, size, k):
    return lax.ppermute(x, axis, [(i, i ^ k) for i in range(size)])


def local(
    tables, kv_cache, hidden, lengths, source, norm_gain, query_weight, keyval_weight, out_weight
):
    peers, peers_tp = lax.axis_size("inst"), lax.axis_size("tp")
    slots, cap = kv_cache.shape[0], kv_cache.shape[2]
    width = hidden.shape[1]
    heads = query_weight.shape[1] // HD
    shard = width // peers_tp
    others, moving = peers - 1, (peers - 1) * MOVE
    blocks = width // HD
    meta = jnp.stack([lax.axis_index("inst"), lax.axis_index("tp")]).astype(I32)
    gain = norm_gain.reshape(1, width)
    wkv = keyval_weight.reshape(2 * width, HD)
    cosine, sine = (jnp.asarray(table) for table in tables)
    row32 = jax.ShapeDtypeStruct((slots, HD), F32)
    note_width = heads * HD + shard
    dma = pltpu.SemaphoreType.DMA
    weights = [
        pltpu.VMEM(query_weight.shape, BF16),
        pltpu.VMEM(wkv.shape, BF16),
    ]
    stages = [
        pltpu.VMEM((blocks, slots, HD), BF16),
        pltpu.VMEM((blocks, 2 * slots, 2 * HD), BF16),
        pltpu.VMEM((slots, HD), F32),
        pltpu.VMEM((slots, HD), F32),
    ]
    flops = 2 * slots * width * (heads + 2) * HD
    cache_bytes = kv_cache.size * 2
    held = jax.ShapeDtypeStruct((slots + moving,) + kv_cache.shape[1:], BF16)

    query, newkey1, newvalue1, plan, cache, *notes = pl.pallas_call(
        functools.partial(first_kernel, peers, slots, heads, shard),
        out_shape=[
            jax.ShapeDtypeStruct((slots * GROUP, HD), F32),
            row32,
            row32,
            jax.ShapeDtypeStruct((2 * moving,), I32),
            held,
        ]
        + [jax.ShapeDtypeStruct((MOVE, 2, cap + NOTE, HD), BF16)]
        + [jax.ShapeDtypeStruct((MOVE, note_width), F32)] * (others - 1),
        in_specs=[SMEM] + [HBM] * 9,
        out_specs=[VMEM] * 3 + [SMEM] + [VMEM] * (others + 1),
        scratch_shapes=weights
        + stages
        + [
            pltpu.VMEM((moving,) + kv_cache.shape[1:], BF16),
            pltpu.VMEM((slots, width), F32),
            pltpu.SMEM((1, source.shape[0]), I32),
            pltpu.VMEM((1, source.shape[0]), I32),
            pltpu.VMEM(hidden.shape, BF16),
            pltpu.VMEM((1, width), F32),
            pltpu.VMEM(cosine.shape, F32),
            pltpu.VMEM(cosine.shape, F32),
            dma((6,)),
            dma((4,)),
            dma((4,)),
            dma((moving,)),
            dma((1,)),
            dma((slots // CHUNK,)),
        ],
        compiler_params=params(24),
        cost_estimate=cost(flops, (query_weight.size + wkv.size) * 2),
        name="first_step",
    )(meta, *(
        pltpu.with_memory_space_constraint(x, pltpu.HBM)
        for x in (source.reshape(1, -1), lengths.reshape(1, -1), hidden, gain, cosine, sine,
                  query_weight, wkv, kv_cache)
    ))
    got_notes = [swapped(note, "inst", peers, k + 1) for k, note in enumerate(notes)]

    attended, cache = pl.pallas_call(
        functools.partial(attend_kernel, slots, heads),
        out_shape=[jax.ShapeDtypeStruct((slots, heads * HD), BF16), held],
        in_specs=[SMEM] * 2 + [VMEM] * 4,
        out_specs=[VMEM] * 2,
        scratch_shapes=[pltpu.VMEM((slots * GROUP, HD), F32)],
        input_output_aliases={5: 1},
        compiler_params=params(12),
        cost_estimate=cost(4 * slots * cap * HD * heads, cache_bytes),
        name="attention",
    )(meta, lengths, query, newkey1, newvalue1, cache)

    own32 = jax.ShapeDtypeStruct((slots, shard), F32)
    rows16 = jax.ShapeDtypeStruct((slots, heads * HD), BF16)
    sent = [jax.ShapeDtypeStruct((slots, shard), BF16)] * (peers_tp - 1)

    def own_term(rows, residual):
        return pl.pallas_call(
            own_kernel,
            out_shape=own32,
            in_specs=[SMEM] + [VMEM] * 3,
            out_specs=VMEM,
            compiler_params=params(16),
            cost_estimate=cost(2 * slots * shard * heads * HD, out_weight.size // 2),
            name="own_term",
        )(meta, rows, out_weight, residual)

    residual, rows, *sends = pl.pallas_call(
        functools.partial(out_kernel, peers, peers_tp),
        out_shape=[own32, rows16] + sent,
        in_specs=[SMEM] * 2 + [VMEM] * (3 + others),
        out_specs=[VMEM] * (1 + peers_tp),
        compiler_params=params(16),
        cost_estimate=cost(2 * slots * width * heads * HD, out_weight.size * 2),
        name="out_projection",
    )(meta, plan, attended, out_weight, hidden, *got_notes)
    own = own_term(rows, residual)
    boxes = pl.pallas_call(
        pack_kernel,
        out_shape=[jax.ShapeDtypeStruct((MOVE,) + kv_cache.shape[1:], BF16)] * (others - 1),
        in_specs=[SMEM, VMEM, ANY],
        out_specs=[ANY] * (others - 1),
        scratch_shapes=[dma((moving - MOVE,))],
        compiler_params=params(16),
        cost_estimate=cost(1, 1 * cache_bytes),
        name="pack",
    )(plan, cache, rows)
    got_boxes = got_notes[:1] + [swapped(box, "inst", peers, k + 2) for k, box in enumerate(boxes)]

    def summed(own, sends, passed_on):
        got = [swapped(sends[k - 1], "tp", peers_tp, k) for k in range(peers_tp - 1, 0, -1)]
        shard_rows = pl.pallas_call(
            sum_kernel,
            out_shape=jax.ShapeDtypeStruct((slots, shard), BF16),
            in_specs=[VMEM] * peers_tp,
            out_specs=VMEM,
            compiler_params=params(16),
            name="sum_terms",
        )(own, *got)
        blocks = {0: shard_rows}
        if not passed_on:
            blocks |= {k: swapped(shard_rows, "tp", peers_tp, k) for k in range(1, peers_tp)}
        far = peers_tp // 2 if passed_on else 0
        while far:
            blocks |= {k + far: swapped(blocks[k], "tp", peers_tp, far) for k in blocks}
            far //= 2
        return [blocks[k] for k in range(peers_tp)]

    pieces = summed(own, sends, False)

    weight, cos_rows, sin_rows, place = pl.pallas_call(
        functools.partial(prepare_kernel, peers, slots),
        out_shape=[
            jax.ShapeDtypeStruct((width, 2 * HD), BF16),
            row32,
            row32,
            jax.ShapeDtypeStruct((2 * slots,), I32),
        ],
        in_specs=[SMEM] * 4 + [VMEM] * 3 + [ANY],
        out_specs=[VMEM] * 3 + [SMEM],
        compiler_params=params(16),
        cost_estimate=cost(100*flops, wkv.size * 40),
        name="prepare",
    )(meta, source, lengths, plan, cosine, sine, wkv, rows)

    rows, *sends, cache = pl.pallas_call(
        functools.partial(second_kernel, peers, peers_tp, slots, heads),
        out_shape=[rows16] + sent + [held],
        in_specs=[SMEM] * 2 + [VMEM] * (7 + peers_tp) + [ANY] * others,
        out_specs=[VMEM] * (1 + peers_tp),
        scratch_shapes=[
            pltpu.VMEM((blocks, slots, HD), BF16),
            pltpu.VMEM((slots * GROUP, HD), F32),
            pltpu.VMEM((slots * GROUP, HD), F32),
            dma((others,)),
        ],
        input_output_aliases={8: peers_tp},
        compiler_params=params(16),
        cost_estimate=cost(3 * flops, cache_bytes + (query_weight.size + wkv.size) * 4),
        name="second_step",
    )(meta, place, gain, cos_rows, sin_rows, query_weight, weight, out_weight, cache,
      *pieces, *got_boxes)
    own = own_term(rows, pieces[0])

    pieces = summed(own, sends, False)
    final_cache = pl.pallas_call(
        functools.partial(cache_kernel, slots),
        out_shape=jax.ShapeDtypeStruct(kv_cache.shape, BF16),
        in_specs=[SMEM, VMEM],
        out_specs=ANY,
        scratch_shapes=[dma((slots,))],
        compiler_params=params(16),
        cost_estimate=cost(0, 2 * cache_bytes),
        name="write_cache",
    )(place, cache)
    final_hidden = pl.pallas_call(
        functools.partial(join_kernel, peers_tp),
        out_shape=jax.ShapeDtypeStruct(hidden.shape, BF16),
        in_specs=[SMEM] + [ANY] * peers_tp,
        out_specs=ANY,
        scratch_shapes=[dma((peers_tp,))],
        compiler_params=params(16),
        name="join",
    )(meta, *pieces)
    return (final_hidden, final_cache)


def solution(mesh):
    def whole(kv_cache, *rest):
        tables = angle_tables(kv_cache.shape[2])
        return jax.shard_map(
            functools.partial(local, tables),
            mesh=mesh,
            in_specs=(
                P(("groups", "inst"), None, None, "tp"),
                P(("groups", "inst"), None),
                P("groups"),
                P("groups"),
                P(),
                P(None, "tp"),
                P(None, None, "tp"),
                P("tp", None),
            ),
            out_specs=(P(("groups", "inst"), None), P(("groups", "inst"), None, None, "tp")),
            check_vma=False,
        )(kv_cache, *rest)

    return whole
```

```python
import functools

import jax
import jax.numpy as jnp
import numpy as np
from jax import lax
from jax.experimental import pallas as pl
from jax.experimental.pallas import tpu as pltpu
from jax.sharding import PartitionSpec as P

MOVE = 2
EPS = 1e-05
THETA = 500000.0
HD = 128
GROUP = 8
PIECE = 16
CHUNK = 8
BATCH = 48
NOTE = 16

F32 = jnp.float32
BF16 = jnp.bfloat16
I32 = jnp.int32

ANY = pl.BlockSpec(memory_space=pl.ANY)
VMEM = pl.BlockSpec(memory_space=pltpu.VMEM)
SMEM = pl.BlockSpec(memory_space=pltpu.SMEM)
HBM = pl.BlockSpec(memory_space=pltpu.HBM)


def params(mib):
    return pltpu.CompilerParams(vmem_limit_bytes=mib * 1024 * 1024)


def cost(flops, nbytes):
    return pl.CostEstimate(flops=flops, bytes_accessed=nbytes, transcendentals=0)


def angle_tables(positions):
    frequency = THETA ** (-(np.arange(HD // 2, dtype=np.float64) * 2.0) / HD)
    angles = np.arange(positions, dtype=np.float64)[:, None] * frequency[None, :]
    cosine = np.concatenate([np.cos(angles), np.cos(angles)], axis=-1)
    sine = np.concatenate([-np.sin(angles), np.sin(angles)], axis=-1)
    return cosine.astype(np.float32), sine.astype(np.float32)


def turn(x, cosine, sine):
    return x * cosine + pltpu.roll(x, HD // 2, 1) * sine


def gather_angles(position_of, slots, cos_ref, sin_ref, cos_rows, sin_rows):
    for s in range(slots):
        p = position_of(s)
        cos_rows[s : s + 1, :] = cos_ref[pl.ds(p, 1), :]
        sin_rows[s : s + 1, :] = sin_ref[pl.ds(p, 1), :]


def spread_normed(normed3, spread, slots, width):
    blocks = width // HD
    row = lax.broadcasted_iota(I32, (HD, 4 * HD), 0)
    col = lax.broadcasted_iota(I32, (HD, 4 * HD), 1)
    goal = jnp.where(col < 2 * HD, 2 * row, 2 * row + 1 + 2 * HD)
    places = jnp.where(col == goal, 1.0, 0.0).astype(BF16)
    spread_all = jnp.dot(
        normed3[...].reshape(blocks * slots, HD), places, preferred_element_type=F32
    ).astype(BF16)
    spread[:, 0:slots, :] = spread_all[:, : 2 * HD].reshape(blocks, slots, 2 * HD)
    spread[:, slots:, :] = spread_all[:, 2 * HD :].reshape(blocks, slots, 2 * HD)


def project_from(normed3, weight):
    total = None
    for b in range(normed3.shape[0] // 2):
        block = jnp.concatenate([normed3[2 * b], normed3[2 * b + 1]], axis=1)
        part = jnp.dot(
            block, weight[b * 2 * HD : (b + 1) * 2 * HD, :], preferred_element_type=F32
        )
        total = part if total is None else total + part
    return total


def project_spread(spread, wkv):
    total = None
    for b in range(spread.shape[0]):
        part = jnp.dot(
            spread[b], wkv[b * 2 * HD : (b + 1) * 2 * HD, :], preferred_element_type=F32
        )
        total = part if total is None else total + part
    slots = spread.shape[1] // 2
    return total[:slots], total[slots:]


def weight_copies(src, dst, sem, pieces):
    depth = src.shape[0] // pieces
    copies = [
        pltpu.make_async_copy(
            src.at[pl.ds(c * depth, depth)], dst.at[pl.ds(c * depth, depth)], sem.at[c]
        )
        for c in range(pieces)
    ]
    return copies


def put_row(cache, place, p, key_row, value_row):
    base = pl.multiple_of((jnp.maximum(p, 0) // PIECE) * PIECE, PIECE)
    hit = lax.broadcasted_iota(I32, (PIECE, HD), 0) + base == p
    for which, new in ((0, key_row), (1, value_row)):
        old = cache[place, which, pl.ds(base, PIECE), :]
        new = jnp.broadcast_to(new, old.shape).astype(BF16)
        cache[place, which, pl.ds(base, PIECE), :] = jnp.where(hit, new, old)


def attend(cache, places, positions, query_rows):
    cap = cache.shape[2]
    col = lax.broadcasted_iota(I32, (GROUP, cap), 1)
    scores = [
        lax.dot_general(
            rows.astype(BF16),
            cache[place, 0],
            (((1,), (1,)), ((), ())),
            preferred_element_type=F32,
        )
        for place, rows in zip(places, query_rows)
    ]
    probs = []
    for score, p in zip(scores, positions):
        score = jnp.where(col <= p, score * HD**-0.5, -jnp.inf)
        weight = jnp.exp(score - jnp.max(score, axis=-1, keepdims=True))
        weight = weight / jnp.sum(weight, axis=-1, keepdims=True)
        probs.append(weight.astype(BF16))
    return [
        jnp.dot(prob, cache[place, 1], preferred_element_type=F32)
        for place, prob in zip(places, probs)
    ]


def norm_into(normed3, pieces, gains, firsts, total_width):
    square = None
    for piece in pieces:
        part = jnp.sum(piece * piece, axis=-1, keepdims=True)
        square = part if square is None else square + part
    factor = lax.rsqrt(square / total_width + EPS)
    for piece, gain, first in zip(pieces, gains, firsts):
        normed = (piece * factor * gain).astype(BF16)
        for i in range(piece.shape[1] // HD):
            normed3[first + i] = normed[:, i * HD : (i + 1) * HD]


def plan_moves(me, peers, slots, source):
    moving = (peers - 1) * MOVE
    shape = (2 * moving, source.shape[1])
    row = lax.broadcasted_iota(I32, shape, 0)
    index = lax.broadcasted_iota(I32, shape, 1)
    leaves = row < moving
    at = jnp.where(leaves, row, row - moving)
    other = jnp.bitwise_xor(me, at // MOVE + 1)
    here, there = me * slots, other * slots
    src = jnp.broadcast_to(source, shape)
    came, went = jnp.where(leaves, here, there), jnp.where(leaves, there, here)
    moved = (src >= came) & (src < came + slots) & (index >= went) & (index < went + slots)
    sign = jnp.where(at % MOVE == 0, -1.0, 1.0)
    index_f = index.astype(F32)
    best = jnp.max(jnp.where(moved, sign * index_f, -1e6), axis=1, keepdims=True)
    hit = moved & (sign * index_f == best)
    result = jnp.where(leaves, src, index) - here
    found = jnp.sum(jnp.where(hit, result.astype(F32), 0.0), axis=1, keepdims=True)
    none = jnp.where(leaves[:, :1], 0.0, -1.0)
    return jnp.where(best > -1e6, found, none).astype(I32)


def first_kernel(
    peers, slots, heads, shard,
    meta, source_hbm, lengths_hbm, hidden_hbm, gain_hbm, cos_hbm, sin_hbm, wq_hbm, wkv_hbm,
    cache_hbm, query_out, newkey_out, newvalue_out, plan, *rest,
):
    others = peers - 1
    moving = others * MOVE
    cache, box, notes = rest[0], rest[1], (None,) + rest[2 : others + 1]
    (wq, wkv, normed3, spread, cos_rows, sin_rows, leaving, hidden32, lengths_s, source_v,
     hidden, gain, cos_ref, sin_ref, small_sem, wq_sem, wkv_sem, in_sem,
     box_sem, cache_sem) = rest[others + 1 :]
    width = hidden.shape[1]
    me, me_tp = meta[0], meta[1]
    wq_copies = weight_copies(wq_hbm, wq, wq_sem, 4)
    wkv_copies = weight_copies(wkv_hbm, wkv, wkv_sem, 4)
    small = [
        pltpu.make_async_copy(src, dst, small_sem.at[i])
        for i, (src, dst) in enumerate((
            (source_hbm, source_v), (hidden_hbm, hidden), (gain_hbm, gain), (lengths_hbm, lengths_s),
            (cos_hbm, cos_ref), (sin_hbm, sin_ref),
        ))
    ]
    for copy in small[:3] + wkv_copies + wq_copies + small[3:]:
        copy.start()
    loads = [
        pltpu.make_async_copy(
            cache_hbm.at[pl.ds(c * CHUNK, CHUNK)], cache.at[pl.ds(c * CHUNK, CHUNK)], cache_sem.at[c]
        )
        for c in range(slots // CHUNK)
    ]
    for copy in small[:3]:
        copy.wait()
    low = me * slots
    moves = plan_moves(me, peers, slots, source_v[...])
    wide = hidden[...].astype(F32)
    hidden32[...] = wide
    norm_into(normed3, [wide], [gain[...]], [0], width)
    spread_normed(normed3, spread, slots, width)
    send_slots = [moves[at, 0] for at in range(moving)]
    fetches = [
        pltpu.make_async_copy(cache_hbm.at[slot], leaving.at[at], in_sem.at[at])
        for at, slot in enumerate(send_slots)
    ]
    for copy in fetches:
        copy.start()
    for at, slot in enumerate(send_slots):
        plan[moving + at] = slot
        plan[at] = moves[moving + at, 0]
    for copy in loads:
        copy.start()
    for copy in small[3:] + wkv_copies + wq_copies + fetches:
        copy.wait()
    gather_angles(lambda s: lengths_s[0, low + s], slots, cos_ref, sin_ref, cos_rows, sin_rows)
    key, value = project_spread(spread, wkv)
    cosine, sine = cos_rows[...], sin_rows[...]
    newkey_out[...] = turn(key, cosine, sine).astype(BF16).astype(F32)
    newvalue_out[...] = value.astype(BF16).astype(F32)
    positions = [lengths_s[0, low + slot] for slot in send_slots]
    for at, slot in enumerate(send_slots):
        put_row(
            leaving, at, positions[at],
            newkey_out[pl.ds(slot, 1), :], newvalue_out[pl.ds(slot, 1), :],
        )
    query = project_from(normed3, wq)
    query_out[...] = jnp.zeros(query_out.shape, F32)
    for g in range(heads):
        turned = turn(query[:, g * HD : (g + 1) * HD], cosine, sine)
        query_out[pl.ds(g, slots, stride=GROUP), :] = turned.astype(BF16).astype(F32)
    cap = leaving.shape[2]
    copies = [
        pltpu.make_async_copy(
            leaving.at[pl.ds(0, MOVE)], box.at[:, :, pl.ds(0, cap), :], box_sem.at[0]
        )
    ]
    copies[0].start()
    rows = [query_out[pl.ds(pl.multiple_of(slot * GROUP, GROUP), GROUP), :] for slot in send_slots]
    attended = attend(leaving, list(range(moving)), positions, rows)
    column = pl.multiple_of(me_tp * shard, shard)
    for at, slot in enumerate(send_slots):
        m = at % MOVE
        residual = hidden32[pl.ds(slot, 1), pl.ds(column, shard)]
        if at < MOVE:
            blocks = [attended[at][g : g + 1, :] for g in range(heads)]
            blocks += [residual[:, b * HD : (b + 1) * HD] for b in range(shard // HD)]
            blocks += [jnp.zeros((1, HD), F32)] * (NOTE - len(blocks))
            box[m, 0, cap : cap + NOTE, :] = jnp.concatenate(blocks, axis=0).astype(BF16)
        else:
            note = notes[at // MOVE]
            for g in range(heads):
                note[m : m + 1, g * HD : (g + 1) * HD] = attended[at][g : g + 1, :]
            note[m : m + 1, heads * HD :] = residual
    for copy in copies + loads:
        copy.wait()


def attend_slots(cache, places, positions, query, attended_rows, heads):
    slots = len(places)
    for first in range(0, slots, BATCH):
        span = range(first, first + BATCH)
        got = attend(
            cache,
            [places[s] for s in span],
            [positions[s] for s in span],
            [query[s * GROUP : (s + 1) * GROUP, :] for s in span],
        )
        for s, rows in zip(span, got):
            attended_rows[s * GROUP : (s + 1) * GROUP, :] = rows
    return jnp.concatenate(
        [attended_rows[pl.ds(g, slots, stride=GROUP), :] for g in range(heads)], axis=1
    )


def attend_kernel(
    slots, heads, meta, lengths_s, query, newkey, newvalue, _, out, cache, attended_rows,
):
    low = meta[0] * slots
    positions = [lengths_s[low + s] for s in range(slots)]
    for s, p in enumerate(positions):
        put_row(cache, s, p, newkey[s : s + 1, :], newvalue[s : s + 1, :])
    out[...] = attend_slots(
        cache, list(range(slots)), positions, query, attended_rows, heads
    ).astype(BF16)


def project_out(attended, wo, sends, me_tp):
    for k in range(len(sends), 0, -1):
        shard = sends[k - 1].shape[1]
        column = pl.multiple_of(jnp.bitwise_xor(me_tp, k) * shard, shard)
        part = jnp.dot(attended, wo[:, pl.ds(column, shard)], preferred_element_type=F32)
        sends[k - 1][...] = part.astype(BF16)


def own_kernel(meta, attended, wo, residual, own):
    shard = own.shape[1]
    column = pl.multiple_of(meta[1] * shard, shard)
    part = jnp.dot(attended[...], wo[:, pl.ds(column, shard)], preferred_element_type=F32)
    own[...] = residual[...].astype(F32) + part


def out_kernel(
    peers, peers_tp, meta, plan, attended, wo, hidden, box, *rest,
):
    notes, rest = rest[: peers - 2], rest[peers - 2 :]
    residual_out, rows_out, sends = rest[0], rest[1], rest[2:]
    shard = residual_out.shape[1]
    cap = box.shape[2] - NOTE
    rows = attended[...].astype(F32)
    heads = rows.shape[1] // HD
    column = pl.multiple_of(meta[1] * shard, shard)
    residual = hidden[:, pl.ds(column, shard)].astype(F32)
    row_index = lax.broadcasted_iota(I32, rows.shape, 0)
    residual_index = lax.broadcasted_iota(I32, residual.shape, 0)
    for at in range((peers - 1) * MOVE):
        m = at % MOVE
        if at < MOVE:
            blocks = box[m, 0, cap : cap + NOTE, :].astype(F32)
            blocks = [blocks[b : b + 1, :] for b in range(heads + shard // HD)]
            note = jnp.concatenate(blocks, axis=1)
        else:
            note = notes[at // MOVE - 1][m : m + 1, :]
        rows = jnp.where(row_index == plan[at], note[:, : heads * HD], rows)
        residual = jnp.where(residual_index == plan[at], note[:, heads * HD :], residual)
    residual_out[...] = residual
    rows_out[...] = rows.astype(BF16)
    project_out(rows.astype(BF16), wo, sends, meta[1])


def pack_kernel(plan, cache, _own, *rest):
    boxes, out_sem = rest[:-1], rest[-1]
    moving = plan.shape[0] // 2
    packs = [
        pltpu.make_async_copy(
            cache.at[plan[moving + at]], boxes[at // MOVE - 1].at[at % MOVE], out_sem.at[at - MOVE]
        )
        for at in range(MOVE, moving)
    ]
    for pack in packs:
        pack.start()
    for pack in packs:
        pack.wait()


def sum_kernel(own, *rest):
    total = own[...]
    for part in rest[:-1]:
        total = total + part[...].astype(F32)
    rest[-1][...] = total.astype(BF16)


def map_places(slots, peers, plan, place):
    for s in range(slots):
        place[s] = s
    for at in range((peers - 1) * MOVE):
        taker = plan[at]

        @pl.when(taker >= 0)
        def _():
            place[taker] = slots + at


def prepare_kernel(
    peers, slots, meta, source_s, lengths_s, plan, cos_ref, sin_ref, wkv, _,
    weight, cos_rows, sin_rows, place,
):
    map_places(slots, peers, plan, place)
    low = meta[0] * slots
    positions = [lengths_s[source_s[low + s]] + 1 for s in range(slots)]
    for s, p in enumerate(positions):
        place[slots + s] = p
    gather_angles(lambda s: positions[s], slots, cos_ref, sin_ref, cos_rows, sin_rows)
    row = lax.broadcasted_iota(I32, (2 * HD, 2 * HD), 0)
    col = lax.broadcasted_iota(I32, (2 * HD, 2 * HD), 1)
    goal = jnp.where(row < HD, 2 * row, 2 * (row - HD) + 1)
    places = jnp.where(col == goal, 1.0, 0.0).astype(BF16)
    for b in range(weight.shape[0] // HD):
        apart = jnp.dot(
            places, wkv[b * 2 * HD : (b + 1) * 2 * HD, :], preferred_element_type=F32
        ).astype(BF16)
        weight[b * HD : (b + 1) * HD, :HD] = apart[:HD]
        weight[b * HD : (b + 1) * HD, HD:] = apart[HD:]


def second_kernel(
    peers, peers_tp, slots, heads,
    meta, place, gain, cos_rows, sin_rows, wq, wkv, wo, _, *rest,
):
    blocks, rest = rest[:peers_tp], rest[peers_tp:]
    box_hbm, rest = rest[: peers - 1], rest[peers - 1 :]
    attended_out, sends, cache = rest[0], rest[1:peers_tp], rest[peers_tp]
    normed3, query_rows, attended_rows, in_sem = rest[peers_tp + 1 :]
    me_tp = meta[1]
    width = gain.shape[1]
    shard = blocks[0].shape[1]
    loads = [
        pltpu.make_async_copy(
            box.at[:, :, pl.ds(0, cache.shape[2]), :],
            cache.at[pl.ds(slots + k * MOVE, MOVE)],
            in_sem.at[k],
        )
        for k, box in enumerate(box_hbm)
    ]
    for copy in loads:
        copy.start()

    firsts = [jnp.bitwise_xor(me_tp, k) for k in range(peers_tp)]
    norm_into(
        normed3,
        [block[...].astype(F32) for block in blocks],
        [gain[:, pl.ds(pl.multiple_of(first * shard, shard), shard)] for first in firsts],
        [first * (shard // HD) for first in firsts],
        width,
    )
    positions = [place[slots + s] for s in range(slots)]
    for copy in loads:
        copy.wait()
    pair = project_from(normed3, wkv)
    cosine, sine = cos_rows[...], sin_rows[...]
    newkey = turn(pair[:, :HD], cosine, sine).astype(BF16).astype(F32)
    newvalue = pair[:, HD:].astype(BF16).astype(F32)
    places = [place[s] for s in range(slots)]
    for s, (at, p) in enumerate(zip(places, positions)):
        put_row(cache, at, p, newkey[s : s + 1, :], newvalue[s : s + 1, :])
    query = project_from(normed3, wq)
    query_rows[...] = jnp.zeros(query_rows.shape, F32)
    for g in range(heads):
        turned = turn(query[:, g * HD : (g + 1) * HD], cosine, sine)
        query_rows[pl.ds(g, slots, stride=GROUP), :] = turned.astype(BF16).astype(F32)
    attended = attend_slots(cache, places, positions, query_rows, attended_rows, heads)
    attended_out[...] = attended.astype(BF16)
    project_out(attended.astype(BF16), wo, sends, me_tp)


def cache_kernel(slots, place, cache, out_hbm, out_sem):
    copies = [
        pltpu.make_async_copy(cache.at[place[s]], out_hbm.at[s], out_sem.at[s])
        for s in range(slots)
    ]
    for copy in copies:
        copy.start()
    for copy in copies:
        copy.wait()


def join_kernel(peers_tp, meta, *rest):
    blocks, out, sem = rest[:-2], rest[-2], rest[-1]
    shard = blocks[0].shape[1]
    copies = []
    for k, block in enumerate(blocks):
        column = pl.multiple_of(jnp.bitwise_xor(meta[1], k) * shard, shard)
        copies.append(pltpu.make_async_copy(block, out.at[:, pl.ds(column, shard)], sem.at[k]))
        copies[-1].start()
    for copy in copies:
        copy.wait()


def swapped(x, axis, size, k):
    return lax.ppermute(x, axis, [(i, i ^ k) for i in range(size)])


def local(
    tables, kv_cache, hidden, lengths, source, norm_gain, query_weight, keyval_weight, out_weight
):
    peers, peers_tp = lax.axis_size("inst"), lax.axis_size("tp")
    slots, cap = kv_cache.shape[0], kv_cache.shape[2]
    width = hidden.shape[1]
    heads = query_weight.shape[1] // HD
    shard = width // peers_tp
    others, moving = peers - 1, (peers - 1) * MOVE
    blocks = width // HD
    meta = jnp.stack([lax.axis_index("inst"), lax.axis_index("tp")]).astype(I32)
    gain = norm_gain.reshape(1, width)
    wkv = keyval_weight.reshape(2 * width, HD)
    cosine, sine = (jnp.asarray(table) for table in tables)
    row32 = jax.ShapeDtypeStruct((slots, HD), F32)
    note_width = heads * HD + shard
    dma = pltpu.SemaphoreType.DMA
    weights = [
        pltpu.VMEM(query_weight.shape, BF16),
        pltpu.VMEM(wkv.shape, BF16),
    ]
    stages = [
        pltpu.VMEM((blocks, slots, HD), BF16),
        pltpu.VMEM((blocks, 2 * slots, 2 * HD), BF16),
        pltpu.VMEM((slots, HD), F32),
        pltpu.VMEM((slots, HD), F32),
    ]
    flops = 2 * slots * width * (heads + 2) * HD
    cache_bytes = kv_cache.size * 2
    held = jax.ShapeDtypeStruct((slots + moving,) + kv_cache.shape[1:], BF16)

    query, newkey1, newvalue1, plan, cache, *notes = pl.pallas_call(
        functools.partial(first_kernel, peers, slots, heads, shard),
        out_shape=[
            jax.ShapeDtypeStruct((slots * GROUP, HD), F32),
            row32,
            row32,
            jax.ShapeDtypeStruct((2 * moving,), I32),
            held,
        ]
        + [jax.ShapeDtypeStruct((MOVE, 2, cap + NOTE, HD), BF16)]
        + [jax.ShapeDtypeStruct((MOVE, note_width), F32)] * (others - 1),
        in_specs=[SMEM] + [HBM] * 9,
        out_specs=[VMEM] * 3 + [SMEM] + [VMEM] * (others + 1),
        scratch_shapes=weights
        + stages
        + [
            pltpu.VMEM((moving,) + kv_cache.shape[1:], BF16),
            pltpu.VMEM((slots, width), F32),
            pltpu.SMEM((1, source.shape[0]), I32),
            pltpu.VMEM((1, source.shape[0]), I32),
            pltpu.VMEM(hidden.shape, BF16),
            pltpu.VMEM((1, width), F32),
            pltpu.VMEM(cosine.shape, F32),
            pltpu.VMEM(cosine.shape, F32),
            dma((6,)),
            dma((4,)),
            dma((4,)),
            dma((moving,)),
            dma((1,)),
            dma((slots // CHUNK,)),
        ],
        compiler_params=params(24),
        cost_estimate=cost(flops, (query_weight.size + wkv.size) * 2),
        name="first_step",
    )(meta, *(
        pltpu.with_memory_space_constraint(x, pltpu.HBM)
        for x in (source.reshape(1, -1), lengths.reshape(1, -1), hidden, gain, cosine, sine,
                  query_weight, wkv, kv_cache)
    ))
    got_notes = [swapped(note, "inst", peers, k + 1) for k, note in enumerate(notes)]

    attended, cache = pl.pallas_call(
        functools.partial(attend_kernel, slots, heads),
        out_shape=[jax.ShapeDtypeStruct((slots, heads * HD), BF16), held],
        in_specs=[SMEM] * 2 + [VMEM] * 4,
        out_specs=[VMEM] * 2,
        scratch_shapes=[pltpu.VMEM((slots * GROUP, HD), F32)],
        input_output_aliases={5: 1},
        compiler_params=params(12),
        cost_estimate=cost(4 * slots * cap * HD * heads, cache_bytes),
        name="attention",
    )(meta, lengths, query, newkey1, newvalue1, cache)

    own32 = jax.ShapeDtypeStruct((slots, shard), F32)
    rows16 = jax.ShapeDtypeStruct((slots, heads * HD), BF16)
    sent = [jax.ShapeDtypeStruct((slots, shard), BF16)] * (peers_tp - 1)

    def own_term(rows, residual):
        return pl.pallas_call(
            own_kernel,
            out_shape=own32,
            in_specs=[SMEM] + [VMEM] * 3,
            out_specs=VMEM,
            compiler_params=params(16),
            cost_estimate=cost(2 * slots * shard * heads * HD, out_weight.size // 2),
            name="own_term",
        )(meta, rows, out_weight, residual)

    residual, rows, *sends = pl.pallas_call(
        functools.partial(out_kernel, peers, peers_tp),
        out_shape=[own32, rows16] + sent,
        in_specs=[SMEM] * 2 + [VMEM] * (3 + others),
        out_specs=[VMEM] * (1 + peers_tp),
        compiler_params=params(16),
        cost_estimate=cost(2 * slots * width * heads * HD, out_weight.size * 2),
        name="out_projection",
    )(meta, plan, attended, out_weight, hidden, *got_notes)
    own = own_term(rows, residual)
    boxes = pl.pallas_call(
        pack_kernel,
        out_shape=[jax.ShapeDtypeStruct((MOVE,) + kv_cache.shape[1:], BF16)] * (others - 1),
        in_specs=[SMEM, VMEM, ANY],
        out_specs=[ANY] * (others - 1),
        scratch_shapes=[dma((moving - MOVE,))],
        compiler_params=params(16),
        cost_estimate=cost(1, 1 * cache_bytes),
        name="pack",
    )(plan, cache, rows)
    got_boxes = got_notes[:1] + [swapped(box, "inst", peers, k + 2) for k, box in enumerate(boxes)]

    def summed(own, sends, passed_on):
        got = [swapped(sends[k - 1], "tp", peers_tp, k) for k in range(peers_tp - 1, 0, -1)]
        shard_rows = pl.pallas_call(
            sum_kernel,
            out_shape=jax.ShapeDtypeStruct((slots, shard), BF16),
            in_specs=[VMEM] * peers_tp,
            out_specs=VMEM,
            compiler_params=params(16),
            name="sum_terms",
        )(own, *got)
        blocks = {0: shard_rows}
        if not passed_on:
            blocks |= {k: swapped(shard_rows, "tp", peers_tp, k) for k in range(1, peers_tp)}
        far = peers_tp // 2 if passed_on else 0
        while far:
            blocks |= {k + far: swapped(blocks[k], "tp", peers_tp, far) for k in blocks}
            far //= 2
        return [blocks[k] for k in range(peers_tp)]

    pieces = summed(own, sends, False)

    weight, cos_rows, sin_rows, place = pl.pallas_call(
        functools.partial(prepare_kernel, peers, slots),
        out_shape=[
            jax.ShapeDtypeStruct((width, 2 * HD), BF16),
            row32,
            row32,
            jax.ShapeDtypeStruct((2 * slots,), I32),
        ],
        in_specs=[SMEM] * 4 + [VMEM] * 3 + [ANY],
        out_specs=[VMEM] * 3 + [SMEM],
        compiler_params=params(16),
        cost_estimate=cost(100*flops, wkv.size * 40),
        name="prepare",
    )(meta, source, lengths, plan, cosine, sine, wkv, rows)

    rows, *sends, cache = pl.pallas_call(
        functools.partial(second_kernel, peers, peers_tp, slots, heads),
        out_shape=[rows16] + sent + [held],
        in_specs=[SMEM] * 2 + [VMEM] * (7 + peers_tp) + [ANY] * others,
        out_specs=[VMEM] * (1 + peers_tp),
        scratch_shapes=[
            pltpu.VMEM((blocks, slots, HD), BF16),
            pltpu.VMEM((slots * GROUP, HD), F32),
            pltpu.VMEM((slots * GROUP, HD), F32),
            dma((others,)),
        ],
        input_output_aliases={8: peers_tp},
        compiler_params=params(16),
        cost_estimate=cost(3 * flops, cache_bytes + (query_weight.size + wkv.size) * 4),
        name="second_step",
    )(meta, place, gain, cos_rows, sin_rows, query_weight, weight, out_weight, cache,
      *pieces, *got_boxes)
    own = own_term(rows, pieces[0])

    pieces = summed(own, sends, False)
    final_cache = pl.pallas_call(
        functools.partial(cache_kernel, slots),
        out_shape=jax.ShapeDtypeStruct(kv_cache.shape, BF16),
        in_specs=[SMEM, VMEM],
        out_specs=ANY,
        scratch_shapes=[dma((slots,))],
        compiler_params=params(16),
        cost_estimate=cost(0, 2 * cache_bytes),
        name="write_cache",
    )(place, cache)
    final_hidden = pl.pallas_call(
        functools.partial(join_kernel, peers_tp),
        out_shape=jax.ShapeDtypeStruct(hidden.shape, BF16),
        in_specs=[SMEM] + [ANY] * peers_tp,
        out_specs=ANY,
        scratch_shapes=[dma((peers_tp,))],
        compiler_params=params(16),
        name="join",
    )(meta, *pieces)
    return (final_hidden, final_cache)


def solution(mesh):
    def whole(kv_cache, *rest):
        tables = angle_tables(kv_cache.shape[2])
        return jax.shard_map(
            functools.partial(local, tables),
            mesh=mesh,
            in_specs=(
                P(("groups", "inst"), None, None, "tp"),
                P(("groups", "inst"), None),
                P("groups"),
                P("groups"),
                P(),
                P(None, "tp"),
                P(None, None, "tp"),
                P("tp", None),
            ),
            out_specs=(P(("groups", "inst"), None), P(("groups", "inst"), None, None, "tp")),
            check_vma=False,
        )(kv_cache, *rest)

    return whole
```
